32 devices in a mesh: gx: 8 (over y, x, core), gy: 4 (over z).
Axes of the slice: x: 2, y: 2, z: 4, core: 2. Of those that a mesh axis runs over, the one named last changes fastest.
Arguments:
- tokens: bfloat16 [16384, 2048], P(('gx', 'gy')), may hold values from -6 to 6
- reset_mask: int32 [16384], P(('gx', 'gy')), may hold values from 0 to 1, as said below
- weight: bfloat16 [2048, 6144], P(('gx', 'gy')), may hold values from -0.125 to 0.125
- vectors: bfloat16 [6, 2048], P(None, ('gx', 'gy')), may hold values from -2 to 15, as said below
- cotangent: bfloat16 [16384, 2048], P(('gx', 'gy')), may hold values from -6 to 6
Outputs:
- output: bfloat16 [16384, 2048], P(('gx', 'gy'))
- input_grad: float32 [16384, 2048], P(('gx', 'gy'))
- weight_grad: float32 [2048, 6144], P(('gx', 'gy'))
- vector_grad: float32 [6, 2048], P(None, ('gx', 'gy'))
The draws below stay inside these ranges and needn't reach their ends.
Inputs may be any that keep to these rules, and one draw needn't show every extreme that they name: `vectors`: the gain row lies in 0.6 to 1.4, the forget bias row in 1 to 15, the other rows in -2 to 2. `reset_mask`: ones fall only among the first 512 and the last 512 tokens of the stream, with at least one among tokens 1 to 511 and at least one among the last 512.
All inputs are finite; a program needn't handle non-finite values.
Results may differ from the reference program's by a relative error of at most 0.005.
Values may be sent and summed in bfloat16 or wider, within the bound.
A program may use at most 256 MiB of HBM per device.

```python
import math
import jax
import jax.numpy as jnp
from jax import lax

D = 2048
TOK_DEV = 512
TOKENS = 16384


def draw_vectors(key, part):
    key = jax.random.fold_in(key, 7)
    keys = jax.random.split(key, 8)
    slow_share = 0.5
    gain = 1.0 + 0.4 * jax.random.uniform(keys[0], (D,), jnp.float32, -1.0, 1.0)
    shift_bias = jax.random.uniform(keys[1], (D,), jnp.float32, -0.8, 0.8)
    forget_peep = jax.random.uniform(keys[2], (D,), jnp.float32, -1.0, 1.0)
    fast_bias = jax.random.uniform(keys[3], (D,), jnp.float32, 1.0, 8.0)
    slow_bias = jnp.log(jnp.float32(TOKENS)) + jax.random.uniform(keys[6], (D,), jnp.float32, 0.5, 2.5)
    slow_pick = jax.random.uniform(keys[7], (D,), jnp.float32) < slow_share
    forget_bias = jnp.where(slow_pick, slow_bias, fast_bias)
    reset_peep = jax.random.uniform(keys[4], (D,), jnp.float32, -2.0, 2.0)
    reset_bias = jax.random.uniform(keys[5], (D,), jnp.float32, -1.0, 1.0)
    return jnp.stack([gain, shift_bias, forget_peep, forget_bias, reset_peep, reset_bias], 0).astype(jnp.bfloat16)


def draw_reset_mask(key, part):
    key = jax.random.fold_in(key, 11)
    keys = jax.random.split(key, 3)
    position = jnp.arange(TOKENS, dtype=jnp.int32)
    border = (position < TOK_DEV) | (position >= TOKENS - TOK_DEV)
    coins = jax.random.randint(keys[0], (TOKENS,), 0, 16) == 0
    first_start = jax.random.randint(keys[1], (), 1, TOK_DEV)
    last_start = TOKENS - TOK_DEV + jax.random.randint(keys[2], (), 0, TOK_DEV)
    marked = border & coins | (position == first_start) | (position == last_start)
    return marked.astype(jnp.int32)


def block_levels(own_key, extent, cuts, low, top_value):
    level = 1.0
    for dim, parts in cuts:
        steps = jax.random.uniform(jax.random.fold_in(jax.random.fold_in(own_key, 6), dim), (parts,), jnp.float32, low / len(cuts), top_value / len(cuts))
        level = level * jnp.repeat(jnp.exp(steps), extent[dim] // parts).reshape((-1,) + (1,) * (len(extent) - 1 - dim))
    return level


def normal_values(key, dims, spread, bound, shards=(), held_as=jnp.bfloat16):
    array = spread * jax.random.normal(key, dims, jnp.float32)
    if shards:
        array = array * block_levels(key, dims, shards, -0.22, 0.18)
    return jnp.clip(array, -bound, bound).astype(held_as)


def setup_inputs(seed: int = 0) -> dict:
    streams_of = jax.random.split(jax.random.key(seed), 6)
    tokens = normal_values(streams_of[0], (TOKENS, D), 1.0, 6.0, ((0, 32),))
    reset_mask = draw_reset_mask(jax.random.fold_in(streams_of[5], 71), 0)
    weight = normal_values(streams_of[2], (D, 3 * D), D ** -0.5, 0.125, ((0, 32),))
    vectors = draw_vectors(jax.random.fold_in(streams_of[5], 71), 0)
    cotangent = normal_values(streams_of[4], (TOKENS, D), 1.0, 6.0, ((0, 32),))
    return dict(tokens=tokens, reset_mask=reset_mask, weight=weight, vectors=vectors, cotangent=cotangent)


@jax.custom_vjp
def low(v):
    return lax.optimization_barrier(v.astype(jnp.bfloat16)).astype(jnp.float32)

@jax.custom_vjp
def low_back(v):
    return v

def low_keep(v):
    return (low(v), None)

def low_pass(kept, grad):
    return (grad,)

def back_keep(v):
    return (v, None)

def back_low(kept, grad):
    return (low(grad),)
low.defvjp(low_keep, low_pass)
low_back.defvjp(back_keep, back_low)

def forward(inputs, weight, vectors, keep):
    gain, shift_bias, forget_peep, forget_bias, reset_peep, reset_bias = [vectors[k] for k in range(6)]
    block_len = math.gcd(TOKENS, 4096)
    block_count = TOKENS // block_len

    def one_block(carry, pieces):
        block_in, block_keep = pieces
        centred = block_in - lax.optimization_barrier(jnp.mean(block_in, axis=1, keepdims=True))
        inv_std = lax.rsqrt(lax.optimization_barrier(jnp.mean(centred * centred, axis=1, keepdims=True)) + 1e-05)
        scaled = centred * inv_std * gain + shift_bias
        projected = low_back(jnp.dot(low(scaled), weight, precision=lax.Precision.HIGHEST))
        candidate = projected[:, :D]
        forget_pre = projected[:, D:2 * D]
        reset_pre = projected[:, 2 * D:]
        forget = jax.nn.sigmoid(forget_pre + forget_peep * scaled + forget_bias)

        def step(state, item):
            forget_t, cand_t, keep_t = item
            prior = keep_t * state
            fresh = forget_t * prior + (1.0 - forget_t) * cand_t
            return (fresh, (prior, fresh))
        last, (previous, states) = lax.scan(step, carry, (forget, candidate, block_keep))
        reset = jax.nn.sigmoid(reset_pre + reset_peep * previous + reset_bias)
        return (last, reset * states + (1.0 - reset) * block_in)
    start = jnp.zeros((D,), jnp.float32)
    blocks_in = inputs.reshape(block_count, block_len, D)
    blocks_keep = keep.reshape(block_count, block_len, 1)
    final, outs = lax.scan(jax.checkpoint(one_block), start, (blocks_in, blocks_keep))
    return outs.reshape(TOKENS, D)

def reference(tokens, reset_mask, weight, vectors, cotangent):
    inputs = tokens.astype(jnp.float32)
    keep = (1 - reset_mask).astype(jnp.float32)
    weight_full = weight.astype(jnp.float32)
    vector_full = vectors.astype(jnp.float32)
    output, pullback = jax.vjp(lambda a, b, c: forward(a, b, c, keep), inputs, weight_full, vector_full)
    input_grad, weight_grad, vector_grad = pullback(cotangent.astype(jnp.float32))
    return (output.astype(jnp.bfloat16), input_grad, weight_grad, vector_grad)
```

```python
import functools

import jax
import jax.numpy as jnp
from jax import lax
from jax.experimental import pallas as pl
from jax.experimental.pallas import tpu as pltpu
from jax.sharding import PartitionSpec as P

MESH = pl.DeviceIdType.MESH
F32, BF16 = jnp.float32, jnp.bfloat16
LANES, RUNS, GROUP, HALF = 128, 8, 4, 2
EPS = 1e-05


def place(ny):
    gx, gy = lax.axis_index("gx"), lax.axis_index("gy")
    core, xx, yy = lax.rem(gx, 2), lax.rem(gx // 2, 2), gx // 4
    return gx, gy, core, gx + 1 - 2 * core, gx + 2 - 4 * xx, gx + 4 - 8 * yy


def remote(src, dst, send, recv, to):
    return pltpu.make_async_remote_copy(
        src_ref=src, dst_ref=dst, send_sem=send, recv_sem=recv, device_id=to, device_id_type=MESH
    )


def lanes_of(b):
    return pl.ds(pl.multiple_of(b * LANES, LANES), LANES)


def run_matrix(tokens, back):
    steps = tokens // RUNS
    row = lax.broadcasted_iota(jnp.int32, (tokens, tokens), 0)
    col = lax.broadcasted_iota(jnp.int32, (tokens, tokens), 1)
    if back:
        hit = col == lax.rem(row, steps) * RUNS + row // steps
    else:
        hit = col == lax.rem(row, RUNS) * steps + row // RUNS
    return jnp.where(hit, 1.0, 0.0).astype(BF16)


def entering(value, axis, join, neutral, backward):
    count, mine = (lax.axis_size(axis), lax.axis_index(axis))
    pieces = jax.tree.map(lambda part: lax.all_gather(part, axis), value)
    if backward:
        pieces = jax.tree.map(lambda part: part[::-1], pieces)
        mine = count - 1 - mine
    subtotal = jax.tree.map(
        lambda part, zero: jnp.full_like(part, 0) + jnp.asarray(zero, part.dtype), value, neutral
    )

    def lap(position, subtotal):
        longer = join(subtotal, jax.tree.map(lambda part: part[position], pieces))
        return jax.tree.map(lambda new, old: jnp.where(position < mine, new, old), longer, subtotal)

    return lax.fori_loop(0, count - 1, lap, subtotal)


def from_behind(block, axis, distance):
    devices = range(lax.axis_size(axis))
    route = [(i - distance, i) for i in devices if i - distance in devices]
    return lax.ppermute(block, axis, route)


def compose(earlier, later):
    return (earlier[0] * later[0], later[0] * earlier[1] + later[1])


def local(tokens, reset_mask, weight, vectors, cotangent):
    width = weight.shape[1] // 3
    whole_weight, whole_vectors = (
        lax.all_gather(weight, ("gx", "gy"), axis=0, tiled=True),
        lax.all_gather(vectors, ("gx", "gy"), axis=1, tiled=True),
    )
    params = whole_vectors.astype(jnp.float32)
    gain = params[0]
    shift_bias = params[1]
    forget_peep = params[2]
    forget_bias = params[3]
    reset_peep = params[4]
    reset_bias = params[5]
    inputs = tokens.astype(jnp.float32)
    keep = (1 - reset_mask).astype(jnp.float32)[:, None]
    centred = inputs - jnp.mean(inputs, axis=1, keepdims=True)
    inv_std = lax.rsqrt(jnp.mean(centred * centred, axis=1, keepdims=True) + 1e-05)
    normed = centred * inv_std
    scaled = normed * gain + shift_bias
    rounded = scaled.astype(jnp.bfloat16)
    projected = jnp.dot(rounded, whole_weight, preferred_element_type=jnp.float32)
    candidate = projected[:, :width]
    forget_pre = projected[:, width : 2 * width]
    reset_pre = projected[:, 2 * width :]
    forget = jax.nn.sigmoid(forget_pre + forget_peep * scaled + forget_bias)
    decay = forget * keep
    inflow = (1.0 - forget) * candidate
    cum_decay, cum_state = lax.associative_scan(compose, (decay, inflow), axis=0)
    unit = (jnp.ones_like(cum_decay[-1]), jnp.zeros_like(cum_state[-1]))
    before = entering((cum_decay[-1], cum_state[-1]), ("gx", "gy"), compose, unit, False)
    state_in = before[1]
    state = cum_decay * state_in + cum_state
    previous = keep * jnp.concatenate([state_in[None], state[:-1]], 0)
    reset = jax.nn.sigmoid(reset_pre + reset_peep * previous + reset_bias)
    output = reset * state + (1.0 - reset) * inputs
    upstream = cotangent.astype(jnp.float32)
    reset_grad = upstream * (state - inputs) * reset * (1.0 - reset)
    through = keep * reset_peep * reset_grad
    next_decay, next_through = from_behind((decay[0], through[0]), ("gx", "gy"), -1)
    ahead = jnp.concatenate([decay[1:], next_decay[None]], 0)
    local_term = upstream * reset + jnp.concatenate([through[1:], next_through[None]], 0)
    flip_mult, flip_sum = lax.associative_scan(compose, (ahead[::-1], local_term[::-1]), axis=0)
    mult_back = flip_mult[::-1]
    sum_back = flip_sum[::-1]
    after = entering((mult_back[0], sum_back[0]), ("gx", "gy"), compose, unit, True)
    state_grad = mult_back * after[1] + sum_back
    candidate_grad = state_grad * (1.0 - forget)
    forget_grad = state_grad * (previous - candidate) * forget * (1.0 - forget)
    proj_grad = jnp.concatenate([candidate_grad, forget_grad, reset_grad], 1).astype(jnp.bfloat16)
    weight_grad = lax.psum_scatter(
        lax.dot_general(
            rounded, proj_grad, (((0,), (0,)), ((), ())), preferred_element_type=jnp.float32
        ),
        ("gx", "gy"),
        scatter_dimension=0,
        tiled=True,
    )
    scaled_grad = lax.dot_general(
        proj_grad,
        lax.all_gather(weight, ("gx", "gy"), axis=0, tiled=True),
        (((1,), (1,)), ((), ())),
        preferred_element_type=jnp.float32,
    )
    scaled_grad = scaled_grad + forget_grad * forget_peep
    vector_terms = jnp.stack(
        [
            jnp.sum(scaled_grad * normed, axis=0),
            jnp.sum(scaled_grad, axis=0),
            jnp.sum(forget_grad * scaled, axis=0),
            jnp.sum(forget_grad, axis=0),
            jnp.sum(reset_grad * previous, axis=0),
            jnp.sum(reset_grad, axis=0),
        ],
        0,
    )
    vector_grad = lax.psum_scatter(vector_terms, ("gx", "gy"), scatter_dimension=1, tiled=True)
    normed_grad = scaled_grad * gain
    input_grad = upstream * (1.0 - reset) + inv_std * (
        normed_grad
        - jnp.mean(normed_grad, axis=1, keepdims=True)
        - normed * jnp.mean(normed_grad * normed, axis=1, keepdims=True)
    )
    return (output.astype(jnp.bfloat16), input_grad, weight_grad, vector_grad)


def front_kernel(
    nx, ny, units,
    tok, cot, keep, wsrc, vsrc,
    wall, pg, rcat, outp, grest, nrmo, invo, vecs, vsum,
    wv, vbuf, xs, gs, nrm, rnd, pj, pv, grs, outs, pgs, perm, stage,
    ach, bch, qch, sin, cin, m1a, m1b, m2a, m2b,
    zs, zr, os, bs, br, dsn, dr, cs, cr, ws,
    vzs, vzr, vxs, vxr, vo, sts, rs, rr, ro, ps, pr, po, gos, e1as, e1ar, e1bs, e1br, e2as, e2ar, e2bs, e2br,
):
    gx, gy, core, mate, xn, yn = place(ny)
    tokens, width = xs.shape
    rows = wsrc.shape[1]
    block = rows * ny
    groups = units // GROUP
    glanes = GROUP * LANES
    diag = xn + yn - gx
    first = gx * block
    mine = first + gy * rows

    def peer_y(j):
        return lax.rem(gy + j, ny)

    def peer_x(j):
        return lax.rem(gx + j, nx)

    barrier = pltpu.get_barrier_semaphore()
    for j in range(1, ny):
        pl.semaphore_signal(barrier, inc=1, device_id=(gx, peer_y(j)), device_id_type=MESH)
    for j in range(1, nx):
        pl.semaphore_signal(barrier, inc=1, device_id=(peer_x(j), gy), device_id_type=MESH)

    def band(b, n=block):
        return pl.ds(pl.multiple_of(b, 16), n)

    def stage_copy(i):
        src = tok if i < 4 else cot
        c = i % 4
        return pltpu.make_async_copy(src.at[:, pl.ds(c * glanes, glanes)], stage.at[i % 2], sts.at[i % 2])

    stage_copy(0).start()
    stage_copy(1).start()

    def vz(j):
        return remote(vsrc, vbuf.at[band(mine, rows)], vzs.at[j - 1], vzr.at[j - 1], (gx, peer_y(j)))

    def vx(j):
        return remote(vbuf.at[band(first)], vbuf.at[band(first)], vxs.at[j - 1], vxr.at[j - 1], (peer_x(j), gy))

    own_vec = pltpu.make_async_copy(vsrc, vbuf.at[band(mine, rows)], vo)

    def z_copy(u, j):
        return remote(wsrc.at[u], wv.at[u, band(mine, rows)], zs.at[u, j - 1], zr.at[u, j - 1], (gx, peer_y(j)))

    def own_copy(u):
        return pltpu.make_async_copy(wsrc.at[u], wv.at[u, band(mine, rows)], os.at[u])

    def band_copy(u, i):
        to = (mate, xn, yn)[i]
        recv = cr.at[u, 0] if i == 0 else br.at[u, i - 1]
        part = wv.at[u, band(first)]
        return remote(part, part, bs.at[u, i], recv, (to, gy))

    def diag_copy(u, i):
        at = (xn * block, yn * block + block // 2)[i]
        part = wv.at[u, band(at, block // 2)]
        return remote(part, part, dsn.at[u, i], dr.at[u, i], ((yn, xn)[i], gy))

    def core_copy(u, i):
        part = wv.at[u, band((None, xn, yn, diag)[i] * block)]
        return remote(part, part, cs.at[u, i - 1], cr.at[u, i], (mate, gy))

    def keep_copy(u):
        return pltpu.make_async_copy(wv.at[u], wall.at[u], ws.at[u])

    def z_start(u):
        own_copy(u).start()
        for j in range(1, ny):
            z_copy(u, j).start()

    def z_wait(u):
        own_copy(u).wait()
        for j in range(1, ny):
            z_copy(u, j).wait_recv()
        for i in (1, 2, 0):
            band_copy(u, i).start()

    def xy_wait(u):
        for i in (1, 2):
            band_copy(u, i).wait_recv()
        for i in (0, 1):
            diag_copy(u, i).start()
        for i in (1, 2):
            core_copy(u, i).start()

    def diag_wait(u):
        for i in (0, 1):
            diag_copy(u, i).wait_recv()
        core_copy(u, 3).start()

    def core_wait(u):
        band_copy(u, 0).wait_recv()
        for i in (1, 2, 3):
            core_copy(u, i).wait_recv()

    pl.semaphore_wait(barrier, nx + ny - 2)
    own_vec.start()
    for j in range(1, ny):
        vz(j).start()
    AHEAD_Z, AHEAD_B = 5, 3
    for u in range(AHEAD_Z):
        z_start(u)

    perm[...] = run_matrix(tokens, False)

    def to_runs(i, into):
        stage_copy(i).wait()
        c = i % 4
        into[:, c * glanes:(c + 1) * glanes] = jnp.dot(
            perm[...], stage[i % 2], preferred_element_type=F32
        ).astype(BF16)
        if i + 2 < 8:
            stage_copy(i + 2).start()

    for i in range(4):
        to_runs(i, xs)
    z_wait(0)
    own_vec.wait()
    for j in range(1, ny):
        vz(j).wait_recv()
    for j in range(1, nx):
        vx(j).start()
    z_wait(1)

    BAND = 32

    def moments(i, _):
        r = pl.ds(pl.multiple_of(i * BAND, BAND), BAND)
        x = xs[r, :].astype(F32)
        centred = x - jnp.mean(x, axis=1, keepdims=True)
        inv = lax.rsqrt(jnp.mean(centred * centred, axis=1, keepdims=True) + EPS)
        nrm[r, :] = centred * inv
        invo[r, :] = jnp.broadcast_to(inv, (BAND, LANES))
        return 0

    lax.fori_loop(0, tokens // BAND, moments, 0)
    nrm_copy = pltpu.make_async_copy(nrm, nrmo, gos.at[0, 2])
    nrm_copy.start()
    for u in range(2, AHEAD_B):
        z_wait(u)
    for i in range(4, 8):
        to_runs(i, gs)
    perm[...] = run_matrix(tokens, True)
    for j in range(1, nx):
        vx(j).wait_recv()

    for c in range(width // LANES):
        part = vbuf[c * LANES:(c + 1) * LANES, :].astype(F32)
        vecs[:, c * LANES:(c + 1) * LANES] = part.T[0:8, :]

    def rounding(i, _):
        r = pl.ds(pl.multiple_of(i * BAND, BAND), BAND)
        rnd[r, :] = (nrm[r, :] * vecs[0:1, :] + vecs[1:2, :]).astype(BF16)
        return 0

    lax.fori_loop(0, tokens // BAND, rounding, 0)

    quads = nx // 2

    def r_own(i):
        src = rnd.at[:, pl.ds(pl.multiple_of((2 * i + core) * block, LANES), block)]
        return pltpu.make_async_copy(src, rcat.at[0:tokens, pl.ds(i * block, block)], ro.at[i])

    def r_mate(i):
        src = rnd.at[:, pl.ds(pl.multiple_of((2 * i + 1 - core) * block, LANES), block)]
        dst = rcat.at[tokens:2 * tokens, pl.ds(i * block, block)]
        return remote(src, dst, rs.at[i], rr.at[i], (mate, gy))

    for i in range(quads):
        r_own(i).start()
        r_mate(i).start()

    def e_copies(buf, send, recv, q, level):
        if level == 0:
            return [
                remote(buf.at[q, gy], buf.at[q, gy], send.at[q, j - 1], recv.at[q, j - 1], (gx, peer_y(j)))
                for j in range(1, ny)
            ]
        return [
            remote(buf.at[q, gx], buf.at[q, gx], send.at[q, j - 1], recv.at[q, j - 1], (peer_x(j), gy))
            for j in range(1, nx)
        ]

    def e_start(*a):
        for c in e_copies(*a):
            c.start()

    def e_wait(*a):
        for c in e_copies(*a):
            c.wait_recv()

    double = tokens // (2 * RUNS)

    def project(u):
        slot = lax.rem(u, 2 * GROUP)
        pj[slot] = jnp.dot(rnd[...], wv[u], preferred_element_type=F32)

    def vec(i, u):
        return vecs[i:i + 1, lanes_of(u)]

    def gates(u):
        slot = lax.rem(u, 2 * GROUP)
        gain, shift, vf, bf = (vec(i, u) for i in range(4))

        def step(i, carry):
            a, b = carry
            r = pl.ds(pl.multiple_of(i * 16, 16), 16)
            scaled = nrm[r, lanes_of(u)] * gain + shift
            f = jax.nn.sigmoid(pj[slot, r, LANES:2 * LANES] + vf * scaled + bf)
            pj[slot, r, LANES:2 * LANES] = f
            d = f * keep[r, :]
            inflow = (1.0 - f) * pj[slot, r, 0:LANES]
            for h in (0, 8):
                a = a * d[h:h + 8]
                b = d[h:h + 8] * b + inflow[h:h + 8]
            return a, b

        a, b = lax.fori_loop(0, double, step, (jnp.ones((RUNS, LANES), F32), jnp.zeros((RUNS, LANES), F32)), unroll=4)
        g, j = lax.rem(u // GROUP, 2), lax.rem(u, GROUP)
        ach[g, :, lanes_of(j)] = a
        bch[g, :, lanes_of(j)] = b

    def totals(q):
        g = lax.rem(q, 2)
        a, b = jnp.ones((1, glanes), F32), jnp.zeros((1, glanes), F32)
        for s in range(RUNS):
            one = ach[g, s:s + 1, :]
            a = a * one
            b = one * b + bch[g, s:s + 1, :]
        m1a[q, gy, 0:1, :] = a
        m1a[q, gy, 1:2, :] = b
        e_start(m1a, e1as, e1ar, q, 0)

    def totals_x(q):
        e_wait(m1a, e1as, e1ar, q, 0)
        a, b = jnp.ones((1, glanes), F32), jnp.zeros((1, glanes), F32)
        for s in range(ny):
            one = m1a[q, s, 0:1, :]
            a = a * one
            b = one * b + m1a[q, s, 1:2, :]
        m1b[q, gx, 0:1, :] = a
        m1b[q, gx, 1:2, :] = b
        e_start(m1b, e1bs, e1br, q, 1)

    def enter(q):
        e_wait(m1b, e1bs, e1br, q, 1)
        g = lax.rem(q, 2)
        s = jnp.zeros((1, glanes), F32)
        s = lax.fori_loop(0, gx, lambda i, s: m1b[q, i, 0:1, :] * s + m1b[q, i, 1:2, :], s)
        s = lax.fori_loop(0, gy, lambda i, s: m1a[q, i, 0:1, :] * s + m1a[q, i, 1:2, :], s)
        for r in range(RUNS):
            sin[g, r:r + 1, :] = s
            s = ach[g, r:r + 1, :] * s + bch[g, r:r + 1, :]

    def forward(u):
        slot = lax.rem(u, 2 * GROUP)
        g, j = lax.rem(u // GROUP, 2), lax.rem(u, GROUP)
        vr, br_ = vec(4, u), vec(5, u)
        zero = jnp.zeros((RUNS, LANES), F32)

        def step(i, carry):
            s, run, q, v4, v5 = carry
            r = pl.ds(pl.multiple_of(i * 16, 16), 16)
            f = pj[slot, r, LANES:2 * LANES]
            k = keep[r, :]
            inflow = (1.0 - f) * pj[slot, r, 0:LANES]
            prevs, states = [], []
            for h in (0, 8):
                prev = k[h:h + 8] * s
                s = f[h:h + 8] * prev + inflow[h:h + 8]
                prevs.append(prev)
                states.append(s)
            prev, state = jnp.concatenate(prevs, 0), jnp.concatenate(states, 0)
            x = xs[r, lanes_of(u)].astype(F32)
            up = gs[r, lanes_of(u)].astype(F32)
            reset = jax.nn.sigmoid(pj[slot, r, 2 * LANES:3 * LANES] + vr * prev + br_)
            rest = 1.0 - reset
            outs[r, lanes_of(j)] = (reset * state + rest * x).astype(BF16)
            rg = up * (state - x) * reset * rest
            gr = up * rest
            pj[slot, r, 2 * LANES:3 * LANES] = rg
            pv[slot, r, :] = prev
            grs[g, r, lanes_of(j)] = gr
            local = up * reset
            d, through = f * k, k * vr * rg
            for h in (0, 8):
                q = q + run * through[h:h + 8]
                run = run * d[h:h + 8]
                q = q + run * local[h:h + 8]
                v4 = v4 + rg[h:h + 8] * prev[h:h + 8]
                v5 = v5 + rg[h:h + 8]
            return s, run, q, v4, v5

        init = (sin[g, :, lanes_of(j)], jnp.ones((RUNS, LANES), F32), zero, zero, zero)
        _, _, q, v4, v5 = lax.fori_loop(0, double, step, init, unroll=4)
        qch[g, :, lanes_of(j)] = q
        vsum[4:5, lanes_of(u)] = jnp.sum(v4, axis=0, keepdims=True)
        vsum[5:6, lanes_of(u)] = jnp.sum(v5, axis=0, keepdims=True)

    def out_copy(q):
        c = pl.ds(pl.multiple_of(q * glanes, LANES), glanes)
        return pltpu.make_async_copy(stage.at[lax.rem(q, 2)], outp.at[:, c], gos.at[q, 0])

    def rest_copy(q):
        c = pl.ds(pl.multiple_of(q * glanes, LANES), glanes)
        return pltpu.make_async_copy(grs.at[lax.rem(q, 2)], grest.at[:, c], gos.at[q, 1])

    def forward_group(q):
        enter(q)
        pl.when(q >= 2)(lambda: (rest_copy(q - 2).wait(), out_copy(q - 2).wait())[0])
        lax.fori_loop(0, GROUP, lambda j, _: (forward(q * GROUP + j), 0)[1], 0)
        g = lax.rem(q, 2)
        s = jnp.zeros((1, glanes), F32)
        for r in reversed(range(RUNS)):
            s = ach[g, r:r + 1, :] * s + qch[g, r:r + 1, :]
        m2a[q, gy, 0:1, :] = s
        e_start(m2a, e2as, e2ar, q, 0)
        rest_copy(q).start()
        stage[g] = jnp.dot(perm[...], outs[...], preferred_element_type=F32).astype(BF16)
        out_copy(q).start()

    def grads_x(q):
        e_wait(m2a, e2as, e2ar, q, 0)
        s = jnp.zeros((1, glanes), F32)
        for r in reversed(range(ny)):
            s = m1a[q, r, 0:1, :] * s + m2a[q, r, 0:1, :]
        m2b[q, gx, 0:1, :] = s
        e_start(m2b, e2bs, e2br, q, 1)

    def enter_back(q):
        e_wait(m2b, e2bs, e2br, q, 1)
        g = lax.rem(q, 2)
        s = jnp.zeros((1, glanes), F32)

        def over_x(i, s):
            return m1b[q, nx - 1 - i, 0:1, :] * s + m2b[q, nx - 1 - i, 0:1, :]

        def over_y(i, s):
            return m1a[q, ny - 1 - i, 0:1, :] * s + m2a[q, ny - 1 - i, 0:1, :]

        s = lax.fori_loop(0, nx - 1 - gx, over_x, s)
        s = lax.fori_loop(0, ny - 1 - gy, over_y, s)
        for r in reversed(range(RUNS)):
            cin[g, r:r + 1, :] = s
            s = ach[g, r:r + 1, :] * s + qch[g, r:r + 1, :]

    def pg_own(u):
        return pltpu.make_async_copy(pgs.at[u], pg.at[u, 0:tokens], po.at[u])

    def pg_mate(u):
        return remote(pgs.at[u], pg.at[u, tokens:2 * tokens], ps.at[u], pr.at[u], (mate, gy))

    def backward(u):
        slot = lax.rem(u, 2 * GROUP)
        g, j = lax.rem(u // GROUP, 2), lax.rem(u, GROUP)
        gain, shift, vr = vec(0, u), vec(1, u), vec(4, u)
        zero = jnp.zeros((RUNS, LANES), F32)

        def step(i, carry):
            c, v2, v3 = carry
            r = pl.ds(pl.multiple_of((double - 1 - i) * 16, 16), 16)
            f = pj[slot, r, LANES:2 * LANES]
            k = keep[r, :]
            rg = pj[slot, r, 2 * LANES:3 * LANES]
            local = gs[r, lanes_of(u)].astype(F32) - grs[g, r, lanes_of(j)]
            d, through = f * k, k * vr * rg
            grads = [None, None]
            for h in (1, 0):
                part = slice(8 * h, 8 * h + 8)
                grads[h] = local[part] + c
                c = d[part] * grads[h] + through[part]
            grad = jnp.concatenate(grads, 0)
            cg = grad * (1.0 - f)
            fg = cg * (pv[slot, r, :] - pj[slot, r, 0:LANES]) * f
            scaled = nrm[r, lanes_of(u)] * gain + shift
            pgs[u, r, 0:LANES] = cg.astype(BF16)
            pgs[u, r, LANES:2 * LANES] = fg.astype(BF16)
            pgs[u, r, 2 * LANES:3 * LANES] = rg.astype(BF16)
            fs = fg * scaled
            return c, v2 + fs[0:8] + fs[8:16], v3 + fg[0:8] + fg[8:16]

        _, v2, v3 = lax.fori_loop(0, double, step, (cin[g, :, lanes_of(j)], zero, zero), unroll=4)
        vsum[2:3, lanes_of(u)] = jnp.sum(v2, axis=0, keepdims=True)
        vsum[3:4, lanes_of(u)] = jnp.sum(v3, axis=0, keepdims=True)
        pg_own(u).start()
        pg_mate(u).start()

    def backward_group(q):
        enter_back(q)
        lax.fori_loop(0, GROUP, lambda j, _: (backward(q * GROUP + j), 0)[1], 0)

    vsum[...] = jnp.zeros_like(vsum)

    def tick(k, _):
        u = k - 2
        q, m = u // GROUP, lax.rem(u, GROUP)
        pl.when(k + AHEAD_Z < units)(lambda: z_start(k + AHEAD_Z))
        pl.when(k + AHEAD_B < units)(lambda: z_wait(k + AHEAD_B))
        pl.when(k < units)(lambda: xy_wait(k))
        pl.when((k >= 1) & (k <= units))(lambda: diag_wait(k - 1))
        late = (u >= GROUP)
        pl.when(late & (m == 0))(lambda: totals_x(q - 1))
        pl.when(late & (m == 1))(lambda: forward_group(q - 1))
        pl.when(late & (m == 2))(lambda: grads_x(q - 1))
        pl.when(late & (m == 3))(lambda: backward_group(q - 1))

        @pl.when((u >= 0) & (u < units))
        def _():
            core_wait(u)
            keep_copy(u).start()
            project(u)
            gates(u)
            pl.when(m == GROUP - 1)(lambda: totals(q))

        return 0

    lax.fori_loop(0, units + 2 + GROUP, tick, 0)

    def drain(u, _):
        for j in range(1, ny):
            z_copy(u, j).wait_send()
        for i in range(3):
            band_copy(u, i).wait_send()
        for i in (0, 1):
            diag_copy(u, i).wait_send()
        for i in (1, 2, 3):
            core_copy(u, i).wait_send()
        keep_copy(u).wait()
        pg_own(u).wait()
        pg_mate(u).wait()
        return 0

    lax.fori_loop(0, units, drain, 0)

    def drain_group(q, _):
        for a in ((m1a, e1as, e1ar, q, 0), (m1b, e1bs, e1br, q, 1), (m2a, e2as, e2ar, q, 0), (m2b, e2bs, e2br, q, 1)):
            for c in e_copies(*a):
                c.wait_send()
        return 0

    lax.fori_loop(0, groups, drain_group, 0)
    for q in range(groups - 2, groups):
        rest_copy(q).wait()
        out_copy(q).wait()
    nrm_copy.wait()
    for j in range(1, ny):
        vz(j).wait_send()
    for j in range(1, nx):
        vx(j).wait_send()
    for i in range(quads):
        r_own(i).wait()
        r_mate(i).wait()


def front(nx, ny, tok, cot, keep, wsrc, vsrc):
    tokens, width = tok.shape
    units, rows, cols = wsrc.shape
    groups, glanes, block = units // GROUP, GROUP * LANES, rows * ny
    dma = pltpu.SemaphoreType.DMA
    any_, vmem = pl.BlockSpec(memory_space=pl.ANY), pl.BlockSpec(memory_space=pltpu.VMEM)
    msg = RUNS, glanes
    s = jax.ShapeDtypeStruct
    return pl.pallas_call(
        functools.partial(front_kernel, nx, ny, units),
        out_shape=(
            s((units, width, cols), BF16), s((units, 2 * tokens, cols), BF16), s((2 * tokens, width // 2), BF16),
            s((tokens, width), BF16), s((tokens, width), F32), s((tokens, width), F32), s((tokens, LANES), F32),
            s((8, width), F32), s((8, width), F32),
        ),
        in_specs=[any_, any_, vmem, any_, any_],
        out_specs=(any_,) * 6 + (vmem,) * 3,
        scratch_shapes=[
            pltpu.VMEM((units, width, cols), BF16),
            pltpu.VMEM((width, LANES), BF16),
            pltpu.VMEM((tokens, width), BF16),
            pltpu.VMEM((tokens, width), BF16),
            pltpu.VMEM((tokens, width), F32),
            pltpu.VMEM((tokens, width), BF16),
            pltpu.VMEM((2 * GROUP, tokens, cols), F32),
            pltpu.VMEM((2 * GROUP, tokens, LANES), F32),
            pltpu.VMEM((2, tokens, glanes), F32),
            pltpu.VMEM((tokens, glanes), BF16),
            pltpu.VMEM((units, tokens, cols), BF16),
            pltpu.VMEM((tokens, tokens), BF16),
            pltpu.VMEM((2, tokens, glanes), BF16),
            pltpu.VMEM((2,) + msg, F32), pltpu.VMEM((2,) + msg, F32), pltpu.VMEM((2,) + msg, F32),
            pltpu.VMEM((2,) + msg, F32), pltpu.VMEM((2,) + msg, F32),
            pltpu.VMEM((groups, ny) + msg, F32), pltpu.VMEM((groups, nx) + msg, F32),
            pltpu.VMEM((groups, ny) + msg, F32), pltpu.VMEM((groups, nx) + msg, F32),
            dma((units, ny - 1)), dma((units, ny - 1)), dma((units,)), dma((units, 3)), dma((units, 2)),
            dma((units, 2)), dma((units, 2)), dma((units, 3)), dma((units, 4)), dma((units,)),
            dma((ny - 1,)), dma((ny - 1,)), dma((nx - 1,)), dma((nx - 1,)), dma, dma((2,)),
            dma((nx // 2,)), dma((nx // 2,)), dma((nx // 2,)), dma((units,)), dma((units,)), dma((units,)),
            dma((groups, 3)),
            dma((groups, ny - 1)), dma((groups, ny - 1)), dma((groups, nx - 1)), dma((groups, nx - 1)),
            dma((groups, ny - 1)), dma((groups, ny - 1)), dma((groups, nx - 1)), dma((groups, nx - 1)),
        ],
        compiler_params=pltpu.CompilerParams(
            collective_id=0, has_side_effects=True, vmem_limit_bytes=61 * 2**20
        ),
        cost_estimate=pl.CostEstimate(
            flops=2 * tokens * width * units * cols, bytes_accessed=2 * width * units * cols, transcendentals=0
        ),
    )(tok, cot, keep, wsrc, vsrc)


def fast(nx, ny, tokens, reset_mask, weight, vectors, cotangent):
    count, width = tokens.shape
    rows = weight.shape[0]
    units, steps = width // LANES, count // RUNS
    keep = (1 - reset_mask).astype(F32).reshape(RUNS, steps).T.reshape(count, 1)
    keep = jnp.broadcast_to(keep, (count, LANES))
    wsrc = weight.reshape(rows, 3, units, LANES).transpose(2, 0, 1, 3).reshape(units, rows, 3 * LANES)
    vsrc = jnp.pad(vectors.T, ((0, 0), (0, LANES - 6)))
    wall, pg, rcat, outp, grest, nrm, inv, vecs, vsum = front(nx, ny, tokens, cotangent, keep, wsrc, vsrc)
    rounded = (nrm * vecs[0] + vecs[1]).astype(BF16)
    own = pg[:, :count].transpose(1, 0, 2).reshape(count, units, 3, LANES).transpose(0, 2, 1, 3).reshape(count, 3 * width)
    weight_grad = lax.psum_scatter(
        lax.dot_general(rounded, own, (((0,), (0,)), ((), ())), preferred_element_type=F32),
        ("gx", "gy"), scatter_dimension=0, tiled=True,
    )
    flat = pg[:, :count].transpose(1, 0, 2).reshape(count, 3 * width)
    wflat = wall.transpose(1, 0, 2).reshape(width, 3 * width)
    scaled_grad = lax.dot_general(flat, wflat, (((1,), (1,)), ((), ())), preferred_element_type=F32)
    scaled_grad = scaled_grad + own[:, width:2 * width].astype(F32) * vecs[2]
    terms = jnp.concatenate([
        jnp.sum(scaled_grad * nrm, axis=0)[None], jnp.sum(scaled_grad, axis=0)[None], vsum[2:6],
    ], 0)
    vector_grad = lax.psum_scatter(terms, ("gx", "gy"), scatter_dimension=1, tiled=True)
    n = scaled_grad * vecs[0]
    grad = grest + inv[:, :1] * (
        n - jnp.mean(n, axis=1, keepdims=True) - nrm * jnp.mean(n * nrm, axis=1, keepdims=True)
    )
    grad = grad.reshape(steps, RUNS, width).transpose(1, 0, 2).reshape(count, width)
    return outp, grad, weight_grad, vector_grad


def solution(mesh):
    placed = (
        P(("gx", "gy"), None),
        P(("gx", "gy")),
        P(("gx", "gy"), None),
        P(None, ("gx", "gy")),
        P(("gx", "gy"), None),
    )
    nx, ny = mesh.shape["gx"], mesh.shape["gy"]

    def body(tokens, reset_mask, weight, vectors, cotangent):
        whole_tiles = weight.shape[0] % 16 == 0 and tokens.shape[0] % 256 == 0
        if nx == 8 and whole_tiles and (weight.shape[0] * ny) % 256 == 0 and tokens.shape[1] % 2048 == 0:
            return fast(nx, ny, tokens, reset_mask, weight, vectors, cotangent)
        return local(tokens, reset_mask, weight, vectors, cotangent)

    return jax.shard_map(
        body,
        mesh=mesh,
        in_specs=placed,
        out_specs=(
            P(("gx", "gy"), None),
            P(("gx", "gy"), None),
            P(("gx", "gy"), None),
            P(None, ("gx", "gy")),
        ),
        check_vma=False,
    )
```

```python
import functools

import jax
import jax.numpy as jnp
from jax import lax
from jax.experimental import pallas as pl
from jax.experimental.pallas import tpu as pltpu
from jax.sharding import PartitionSpec as P

MESH = pl.DeviceIdType.MESH
F32, BF16 = jnp.float32, jnp.bfloat16
LANES, RUNS, GROUP, HALF = 128, 8, 4, 2
EPS = 1e-05


def place(ny):
    gx, gy = lax.axis_index("gx"), lax.axis_index("gy")
    core, xx, yy = lax.rem(gx, 2), lax.rem(gx // 2, 2), gx // 4
    return gx, gy, core, gx + 1 - 2 * core, gx + 2 - 4 * xx, gx + 4 - 8 * yy


def remote(src, dst, send, recv, to):
    return pltpu.make_async_remote_copy(
        src_ref=src, dst_ref=dst, send_sem=send, recv_sem=recv, device_id=to, device_id_type=MESH
    )


def lanes_of(b):
    return pl.ds(pl.multiple_of(b * LANES, LANES), LANES)


def run_matrix(tokens, back):
    steps = tokens // RUNS
    row = lax.broadcasted_iota(jnp.int32, (tokens, tokens), 0)
    col = lax.broadcasted_iota(jnp.int32, (tokens, tokens), 1)
    if back:
        hit = col == lax.rem(row, steps) * RUNS + row // steps
    else:
        hit = col == lax.rem(row, RUNS) * steps + row // RUNS
    return jnp.where(hit, 1.0, 0.0).astype(BF16)


def entering(value, axis, join, neutral, backward):
    count, mine = (lax.axis_size(axis), lax.axis_index(axis))
    pieces = jax.tree.map(lambda part: lax.all_gather(part, axis), value)
    if backward:
        pieces = jax.tree.map(lambda part: part[::-1], pieces)
        mine = count - 1 - mine
    subtotal = jax.tree.map(
        lambda part, zero: jnp.full_like(part, 0) + jnp.asarray(zero, part.dtype), value, neutral
    )

    def lap(position, subtotal):
        longer = join(subtotal, jax.tree.map(lambda part: part[position], pieces))
        return jax.tree.map(lambda new, old: jnp.where(position < mine, new, old), longer, subtotal)

    return lax.fori_loop(0, count - 1, lap, subtotal)


def from_behind(block, axis, distance):
    devices = range(lax.axis_size(axis))
    route = [(i - distance, i) for i in devices if i - distance in devices]
    return lax.ppermute(block, axis, route)


def compose(earlier, later):
    return (earlier[0] * later[0], later[0] * earlier[1] + later[1])


def local(tokens, reset_mask, weight, vectors, cotangent):
    width = weight.shape[1] // 3
    whole_weight, whole_vectors = (
        lax.all_gather(weight, ("gx", "gy"), axis=0, tiled=True),
        lax.all_gather(vectors, ("gx", "gy"), axis=1, tiled=True),
    )
    params = whole_vectors.astype(jnp.float32)
    gain = params[0]
    shift_bias = params[1]
    forget_peep = params[2]
    forget_bias = params[3]
    reset_peep = params[4]
    reset_bias = params[5]
    inputs = tokens.astype(jnp.float32)
    keep = (1 - reset_mask).astype(jnp.float32)[:, None]
    centred = inputs - jnp.mean(inputs, axis=1, keepdims=True)
    inv_std = lax.rsqrt(jnp.mean(centred * centred, axis=1, keepdims=True) + 1e-05)
    normed = centred * inv_std
    scaled = normed * gain + shift_bias
    rounded = scaled.astype(jnp.bfloat16)
    projected = jnp.dot(rounded, whole_weight, preferred_element_type=jnp.float32)
    candidate = projected[:, :width]
    forget_pre = projected[:, width : 2 * width]
    reset_pre = projected[:, 2 * width :]
    forget = jax.nn.sigmoid(forget_pre + forget_peep * scaled + forget_bias)
    decay = forget * keep
    inflow = (1.0 - forget) * candidate
    cum_decay, cum_state = lax.associative_scan(compose, (decay, inflow), axis=0)
    unit = (jnp.ones_like(cum_decay[-1]), jnp.zeros_like(cum_state[-1]))
    before = entering((cum_decay[-1], cum_state[-1]), ("gx", "gy"), compose, unit, False)
    state_in = before[1]
    state = cum_decay * state_in + cum_state
    previous = keep * jnp.concatenate([state_in[None], state[:-1]], 0)
    reset = jax.nn.sigmoid(reset_pre + reset_peep * previous + reset_bias)
    output = reset * state + (1.0 - reset) * inputs
    upstream = cotangent.astype(jnp.float32)
    reset_grad = upstream * (state - inputs) * reset * (1.0 - reset)
    through = keep * reset_peep * reset_grad
    next_decay, next_through = from_behind((decay[0], through[0]), ("gx", "gy"), -1)
    ahead = jnp.concatenate([decay[1:], next_decay[None]], 0)
    local_term = upstream * reset + jnp.concatenate([through[1:], next_through[None]], 0)
    flip_mult, flip_sum = lax.associative_scan(compose, (ahead[::-1], local_term[::-1]), axis=0)
    mult_back = flip_mult[::-1]
    sum_back = flip_sum[::-1]
    after = entering((mult_back[0], sum_back[0]), ("gx", "gy"), compose, unit, True)
    state_grad = mult_back * after[1] + sum_back
    candidate_grad = state_grad * (1.0 - forget)
    forget_grad = state_grad * (previous - candidate) * forget * (1.0 - forget)
    proj_grad = jnp.concatenate([candidate_grad, forget_grad, reset_grad], 1).astype(jnp.bfloat16)
    weight_grad = lax.psum_scatter(
        lax.dot_general(
            rounded, proj_grad, (((0,), (0,)), ((), ())), preferred_element_type=jnp.float32
        ),
        ("gx", "gy"),
        scatter_dimension=0,
        tiled=True,
    )
    scaled_grad = lax.dot_general(
        proj_grad,
        lax.all_gather(weight, ("gx", "gy"), axis=0, tiled=True),
        (((1,), (1,)), ((), ())),
        preferred_element_type=jnp.float32,
    )
    scaled_grad = scaled_grad + forget_grad * forget_peep
    vector_terms = jnp.stack(
        [
            jnp.sum(scaled_grad * normed, axis=0),
            jnp.sum(scaled_grad, axis=0),
            jnp.sum(forget_grad * scaled, axis=0),
            jnp.sum(forget_grad, axis=0),
            jnp.sum(reset_grad * previous, axis=0),
            jnp.sum(reset_grad, axis=0),
        ],
        0,
    )
    vector_grad = lax.psum_scatter(vector_terms, ("gx", "gy"), scatter_dimension=1, tiled=True)
    normed_grad = scaled_grad * gain
    input_grad = upstream * (1.0 - reset) + inv_std * (
        normed_grad
        - jnp.mean(normed_grad, axis=1, keepdims=True)
        - normed * jnp.mean(normed_grad * normed, axis=1, keepdims=True)
    )
    return (output.astype(jnp.bfloat16), input_grad, weight_grad, vector_grad)


def front_kernel(
    nx, ny, units,
    tok, cot, keep, wsrc, vsrc,
    wall, pg, rcat, outp, grest, nrmo, invo, vecs, vsum,
    wv, vbuf, xs, gs, nrm, rnd, pj, pv, grs, outs, pgs, perm, stage,
    ach, bch, qch, sin, cin, m1a, m1b, m2a, m2b,
    zs, zr, os, bs, br, dsn, dr, cs, cr, ws,
    vzs, vzr, vxs, vxr, vo, sts, rs, rr, ro, ps, pr, po, gos, e1as, e1ar, e1bs, e1br, e2as, e2ar, e2bs, e2br,
):
    gx, gy, core, mate, xn, yn = place(ny)
    tokens, width = xs.shape
    rows = wsrc.shape[1]
    block = rows * ny
    groups = units // GROUP
    glanes = GROUP * LANES
    diag = xn + yn - gx
    first = gx * block
    mine = first + gy * rows

    def peer_y(j):
        return lax.rem(gy + j, ny)

    def peer_x(j):
        return lax.rem(gx + j, nx)

    barrier = pltpu.get_barrier_semaphore()
    for j in range(1, ny):
        pl.semaphore_signal(barrier, inc=1, device_id=(gx, peer_y(j)), device_id_type=MESH)
    for j in range(1, nx):
        pl.semaphore_signal(barrier, inc=1, device_id=(peer_x(j), gy), device_id_type=MESH)

    def band(b, n=block):
        return pl.ds(pl.multiple_of(b, 16), n)

    def stage_copy(i):
        src = tok if i < 4 else cot
        c = i % 4
        return pltpu.make_async_copy(src.at[:, pl.ds(c * glanes, glanes)], stage.at[i % 2], sts.at[i % 2])

    stage_copy(0).start()
    stage_copy(1).start()

    def vz(j):
        return remote(vsrc, vbuf.at[band(mine, rows)], vzs.at[j - 1], vzr.at[j - 1], (gx, peer_y(j)))

    def vx(j):
        return remote(vbuf.at[band(first)], vbuf.at[band(first)], vxs.at[j - 1], vxr.at[j - 1], (peer_x(j), gy))

    own_vec = pltpu.make_async_copy(vsrc, vbuf.at[band(mine, rows)], vo)

    def z_copy(u, j):
        return remote(wsrc.at[u], wv.at[u, band(mine, rows)], zs.at[u, j - 1], zr.at[u, j - 1], (gx, peer_y(j)))

    def own_copy(u):
        return pltpu.make_async_copy(wsrc.at[u], wv.at[u, band(mine, rows)], os.at[u])

    def band_copy(u, i):
        to = (mate, xn, yn)[i]
        recv = cr.at[u, 0] if i == 0 else br.at[u, i - 1]
        part = wv.at[u, band(first)]
        return remote(part, part, bs.at[u, i], recv, (to, gy))

    def diag_copy(u, i):
        at = (xn * block, yn * block + block // 2)[i]
        part = wv.at[u, band(at, block // 2)]
        return remote(part, part, dsn.at[u, i], dr.at[u, i], ((yn, xn)[i], gy))

    def core_copy(u, i):
        part = wv.at[u, band((None, xn, yn, diag)[i] * block)]
        return remote(part, part, cs.at[u, i - 1], cr.at[u, i], (mate, gy))

    def keep_copy(u):
        return pltpu.make_async_copy(wv.at[u], wall.at[u], ws.at[u])

    def z_start(u):
        own_copy(u).start()
        for j in range(1, ny):
            z_copy(u, j).start()

    def z_wait(u):
        own_copy(u).wait()
        for j in range(1, ny):
            z_copy(u, j).wait_recv()
        for i in (1, 2, 0):
            band_copy(u, i).start()

    def xy_wait(u):
        for i in (1, 2):
            band_copy(u, i).wait_recv()
        for i in (0, 1):
            diag_copy(u, i).start()
        for i in (1, 2):
            core_copy(u, i).start()

    def diag_wait(u):
        for i in (0, 1):
            diag_copy(u, i).wait_recv()
        core_copy(u, 3).start()

    def core_wait(u):
        band_copy(u, 0).wait_recv()
        for i in (1, 2, 3):
            core_copy(u, i).wait_recv()

    pl.semaphore_wait(barrier, nx + ny - 2)
    own_vec.start()
    for j in range(1, ny):
        vz(j).start()
    AHEAD_Z, AHEAD_B = 5, 3
    for u in range(AHEAD_Z):
        z_start(u)

    perm[...] = run_matrix(tokens, False)

    def to_runs(i, into):
        stage_copy(i).wait()
        c = i % 4
        into[:, c * glanes:(c + 1) * glanes] = jnp.dot(
            perm[...], stage[i % 2], preferred_element_type=F32
        ).astype(BF16)
        if i + 2 < 8:
            stage_copy(i + 2).start()

    for i in range(4):
        to_runs(i, xs)
    z_wait(0)
    own_vec.wait()
    for j in range(1, ny):
        vz(j).wait_recv()
    for j in range(1, nx):
        vx(j).start()
    z_wait(1)

    BAND = 32

    def moments(i, _):
        r = pl.ds(pl.multiple_of(i * BAND, BAND), BAND)
        x = xs[r, :].astype(F32)
        centred = x - jnp.mean(x, axis=1, keepdims=True)
        inv = lax.rsqrt(jnp.mean(centred * centred, axis=1, keepdims=True) + EPS)
        nrm[r, :] = centred * inv
        invo[r, :] = jnp.broadcast_to(inv, (BAND, LANES))
        return 0

    lax.fori_loop(0, tokens // BAND, moments, 0)
    nrm_copy = pltpu.make_async_copy(nrm, nrmo, gos.at[0, 2])
    nrm_copy.start()
    for u in range(2, AHEAD_B):
        z_wait(u)
    for i in range(4, 8):
        to_runs(i, gs)
    perm[...] = run_matrix(tokens, True)
    for j in range(1, nx):
        vx(j).wait_recv()

    for c in range(width // LANES):
        part = vbuf[c * LANES:(c + 1) * LANES, :].astype(F32)
        vecs[:, c * LANES:(c + 1) * LANES] = part.T[0:8, :]

    def rounding(i, _):
        r = pl.ds(pl.multiple_of(i * BAND, BAND), BAND)
        rnd[r, :] = (nrm[r, :] * vecs[0:1, :] + vecs[1:2, :]).astype(BF16)
        return 0

    lax.fori_loop(0, tokens // BAND, rounding, 0)

    quads = nx // 2

    def r_own(i):
        src = rnd.at[:, pl.ds(pl.multiple_of((2 * i + core) * block, LANES), block)]
        return pltpu.make_async_copy(src, rcat.at[0:tokens, pl.ds(i * block, block)], ro.at[i])

    def r_mate(i):
        src = rnd.at[:, pl.ds(pl.multiple_of((2 * i + 1 - core) * block, LANES), block)]
        dst = rcat.at[tokens:2 * tokens, pl.ds(i * block, block)]
        return remote(src, dst, rs.at[i], rr.at[i], (mate, gy))

    for i in range(quads):
        r_own(i).start()
        r_mate(i).start()

    def e_copies(buf, send, recv, q, level):
        if level == 0:
            return [
                remote(buf.at[q, gy], buf.at[q, gy], send.at[q, j - 1], recv.at[q, j - 1], (gx, peer_y(j)))
                for j in range(1, ny)
            ]
        return [
            remote(buf.at[q, gx], buf.at[q, gx], send.at[q, j - 1], recv.at[q, j - 1], (peer_x(j), gy))
            for j in range(1, nx)
        ]

    def e_start(*a):
        for c in e_copies(*a):
            c.start()

    def e_wait(*a):
        for c in e_copies(*a):
            c.wait_recv()

    double = tokens // (2 * RUNS)

    def project(u):
        slot = lax.rem(u, 2 * GROUP)
        pj[slot] = jnp.dot(rnd[...], wv[u], preferred_element_type=F32)

    def vec(i, u):
        return vecs[i:i + 1, lanes_of(u)]

    def gates(u):
        slot = lax.rem(u, 2 * GROUP)
        gain, shift, vf, bf = (vec(i, u) for i in range(4))

        def step(i, carry):
            a, b = carry
            r = pl.ds(pl.multiple_of(i * 16, 16), 16)
            scaled = nrm[r, lanes_of(u)] * gain + shift
            f = jax.nn.sigmoid(pj[slot, r, LANES:2 * LANES] + vf * scaled + bf)
            pj[slot, r, LANES:2 * LANES] = f
            d = f * keep[r, :]
            inflow = (1.0 - f) * pj[slot, r, 0:LANES]
            for h in (0, 8):
                a = a * d[h:h + 8]
                b = d[h:h + 8] * b + inflow[h:h + 8]
            return a, b

        a, b = lax.fori_loop(0, double, step, (jnp.ones((RUNS, LANES), F32), jnp.zeros((RUNS, LANES), F32)), unroll=4)
        g, j = lax.rem(u // GROUP, 2), lax.rem(u, GROUP)
        ach[g, :, lanes_of(j)] = a
        bch[g, :, lanes_of(j)] = b

    def totals(q):
        g = lax.rem(q, 2)
        a, b = jnp.ones((1, glanes), F32), jnp.zeros((1, glanes), F32)
        for s in range(RUNS):
            one = ach[g, s:s + 1, :]
            a = a * one
            b = one * b + bch[g, s:s + 1, :]
        m1a[q, gy, 0:1, :] = a
        m1a[q, gy, 1:2, :] = b
        e_start(m1a, e1as, e1ar, q, 0)

    def totals_x(q):
        e_wait(m1a, e1as, e1ar, q, 0)
        a, b = jnp.ones((1, glanes), F32), jnp.zeros((1, glanes), F32)
        for s in range(ny):
            one = m1a[q, s, 0:1, :]
            a = a * one
            b = one * b + m1a[q, s, 1:2, :]
        m1b[q, gx, 0:1, :] = a
        m1b[q, gx, 1:2, :] = b
        e_start(m1b, e1bs, e1br, q, 1)

    def enter(q):
        e_wait(m1b, e1bs, e1br, q, 1)
        g = lax.rem(q, 2)
        s = jnp.zeros((1, glanes), F32)
        s = lax.fori_loop(0, gx, lambda i, s: m1b[q, i, 0:1, :] * s + m1b[q, i, 1:2, :], s)
        s = lax.fori_loop(0, gy, lambda i, s: m1a[q, i, 0:1, :] * s + m1a[q, i, 1:2, :], s)
        for r in range(RUNS):
            sin[g, r:r + 1, :] = s
            s = ach[g, r:r + 1, :] * s + bch[g, r:r + 1, :]

    def forward(u):
        slot = lax.rem(u, 2 * GROUP)
        g, j = lax.rem(u // GROUP, 2), lax.rem(u, GROUP)
        vr, br_ = vec(4, u), vec(5, u)
        zero = jnp.zeros((RUNS, LANES), F32)

        def step(i, carry):
            s, run, q, v4, v5 = carry
            r = pl.ds(pl.multiple_of(i * 16, 16), 16)
            f = pj[slot, r, LANES:2 * LANES]
            k = keep[r, :]
            inflow = (1.0 - f) * pj[slot, r, 0:LANES]
            prevs, states = [], []
            for h in (0, 8):
                prev = k[h:h + 8] * s
                s = f[h:h + 8] * prev + inflow[h:h + 8]
                prevs.append(prev)
                states.append(s)
            prev, state = jnp.concatenate(prevs, 0), jnp.concatenate(states, 0)
            x = xs[r, lanes_of(u)].astype(F32)
            up = gs[r, lanes_of(u)].astype(F32)
            reset = jax.nn.sigmoid(pj[slot, r, 2 * LANES:3 * LANES] + vr * prev + br_)
            rest = 1.0 - reset
            outs[r, lanes_of(j)] = (reset * state + rest * x).astype(BF16)
            rg = up * (state - x) * reset * rest
            gr = up * rest
            pj[slot, r, 2 * LANES:3 * LANES] = rg
            pv[slot, r, :] = prev
            grs[g, r, lanes_of(j)] = gr
            local = up * reset
            d, through = f * k, k * vr * rg
            for h in (0, 8):
                q = q + run * through[h:h + 8]
                run = run * d[h:h + 8]
                q = q + run * local[h:h + 8]
                v4 = v4 + rg[h:h + 8] * prev[h:h + 8]
                v5 = v5 + rg[h:h + 8]
            return s, run, q, v4, v5

        init = (sin[g, :, lanes_of(j)], jnp.ones((RUNS, LANES), F32), zero, zero, zero)
        _, _, q, v4, v5 = lax.fori_loop(0, double, step, init, unroll=4)
        qch[g, :, lanes_of(j)] = q
        vsum[4:5, lanes_of(u)] = jnp.sum(v4, axis=0, keepdims=True)
        vsum[5:6, lanes_of(u)] = jnp.sum(v5, axis=0, keepdims=True)

    def out_copy(q):
        c = pl.ds(pl.multiple_of(q * glanes, LANES), glanes)
        return pltpu.make_async_copy(stage.at[lax.rem(q, 2)], outp.at[:, c], gos.at[q, 0])

    def rest_copy(q):
        c = pl.ds(pl.multiple_of(q * glanes, LANES), glanes)
        return pltpu.make_async_copy(grs.at[lax.rem(q, 2)], grest.at[:, c], gos.at[q, 1])

    def forward_group(q):
        enter(q)
        pl.when(q >= 2)(lambda: (rest_copy(q - 2).wait(), out_copy(q - 2).wait())[0])
        lax.fori_loop(0, GROUP, lambda j, _: (forward(q * GROUP + j), 0)[1], 0)
        g = lax.rem(q, 2)
        s = jnp.zeros((1, glanes), F32)
        for r in reversed(range(RUNS)):
            s = ach[g, r:r + 1, :] * s + qch[g, r:r + 1, :]
        m2a[q, gy, 0:1, :] = s
        e_start(m2a, e2as, e2ar, q, 0)
        rest_copy(q).start()
        stage[g] = jnp.dot(perm[...], outs[...], preferred_element_type=F32).astype(BF16)
        out_copy(q).start()

    def grads_x(q):
        e_wait(m2a, e2as, e2ar, q, 0)
        s = jnp.zeros((1, glanes), F32)
        for r in reversed(range(ny)):
            s = m1a[q, r, 0:1, :] * s + m2a[q, r, 0:1, :]
        m2b[q, gx, 0:1, :] = s
        e_start(m2b, e2bs, e2br, q, 1)

    def enter_back(q):
        e_wait(m2b, e2bs, e2br, q, 1)
        g = lax.rem(q, 2)
        s = jnp.zeros((1, glanes), F32)

        def over_x(i, s):
            return m1b[q, nx - 1 - i, 0:1, :] * s + m2b[q, nx - 1 - i, 0:1, :]

        def over_y(i, s):
            return m1a[q, ny - 1 - i, 0:1, :] * s + m2a[q, ny - 1 - i, 0:1, :]

        s = lax.fori_loop(0, nx - 1 - gx, over_x, s)
        s = lax.fori_loop(0, ny - 1 - gy, over_y, s)
        for r in reversed(range(RUNS)):
            cin[g, r:r + 1, :] = s
            s = ach[g, r:r + 1, :] * s + qch[g, r:r + 1, :]

    def pg_own(u):
        return pltpu.make_async_copy(pgs.at[u], pg.at[u, 0:tokens], po.at[u])

    def pg_mate(u):
        return remote(pgs.at[u], pg.at[u, tokens:2 * tokens], ps.at[u], pr.at[u], (mate, gy))

    def backward(u):
        slot = lax.rem(u, 2 * GROUP)
        g, j = lax.rem(u // GROUP, 2), lax.rem(u, GROUP)
        gain, shift, vr = vec(0, u), vec(1, u), vec(4, u)
        zero = jnp.zeros((RUNS, LANES), F32)

        def step(i, carry):
            c, v2, v3 = carry
            r = pl.ds(pl.multiple_of((double - 1 - i) * 16, 16), 16)
            f = pj[slot, r, LANES:2 * LANES]
            k = keep[r, :]
            rg = pj[slot, r, 2 * LANES:3 * LANES]
            local = gs[r, lanes_of(u)].astype(F32) - grs[g, r, lanes_of(j)]
            d, through = f * k, k * vr * rg
            grads = [None, None]
            for h in (1, 0):
                part = slice(8 * h, 8 * h + 8)
                grads[h] = local[part] + c
                c = d[part] * grads[h] + through[part]
            grad = jnp.concatenate(grads, 0)
            cg = grad * (1.0 - f)
            fg = cg * (pv[slot, r, :] - pj[slot, r, 0:LANES]) * f
            scaled = nrm[r, lanes_of(u)] * gain + shift
            pgs[u, r, 0:LANES] = cg.astype(BF16)
            pgs[u, r, LANES:2 * LANES] = fg.astype(BF16)
            pgs[u, r, 2 * LANES:3 * LANES] = rg.astype(BF16)
            fs = fg * scaled
            return c, v2 + fs[0:8] + fs[8:16], v3 + fg[0:8] + fg[8:16]

        _, v2, v3 = lax.fori_loop(0, double, step, (cin[g, :, lanes_of(j)], zero, zero), unroll=4)
        vsum[2:3, lanes_of(u)] = jnp.sum(v2, axis=0, keepdims=True)
        vsum[3:4, lanes_of(u)] = jnp.sum(v3, axis=0, keepdims=True)
        pg_own(u).start()
        pg_mate(u).start()

    def backward_group(q):
        enter_back(q)
        lax.fori_loop(0, GROUP, lambda j, _: (backward(q * GROUP + j), 0)[1], 0)

    vsum[...] = jnp.zeros_like(vsum)

    def tick(k, _):
        u = k - 2
        q, m = u // GROUP, lax.rem(u, GROUP)
        pl.when(k + AHEAD_Z < units)(lambda: z_start(k + AHEAD_Z))
        pl.when(k + AHEAD_B < units)(lambda: z_wait(k + AHEAD_B))
        pl.when(k < units)(lambda: xy_wait(k))
        pl.when((k >= 1) & (k <= units))(lambda: diag_wait(k - 1))
        late = (u >= GROUP)
        pl.when(late & (m == 0))(lambda: totals_x(q - 1))
        pl.when(late & (m == 1))(lambda: forward_group(q - 1))
        pl.when(late & (m == 2))(lambda: grads_x(q - 1))
        pl.when(late & (m == 3))(lambda: backward_group(q - 1))

        @pl.when((u >= 0) & (u < units))
        def _():
            core_wait(u)
            keep_copy(u).start()
            project(u)
            gates(u)
            pl.when(m == GROUP - 1)(lambda: totals(q))

        return 0

    lax.fori_loop(0, units + 2 + GROUP, tick, 0)

    def drain(u, _):
        for j in range(1, ny):
            z_copy(u, j).wait_send()
        for i in range(3):
            band_copy(u, i).wait_send()
        for i in (0, 1):
            diag_copy(u, i).wait_send()
        for i in (1, 2, 3):
            core_copy(u, i).wait_send()
        keep_copy(u).wait()
        pg_own(u).wait()
        pg_mate(u).wait()
        return 0

    lax.fori_loop(0, units, drain, 0)

    def drain_group(q, _):
        for a in ((m1a, e1as, e1ar, q, 0), (m1b, e1bs, e1br, q, 1), (m2a, e2as, e2ar, q, 0), (m2b, e2bs, e2br, q, 1)):
            for c in e_copies(*a):
                c.wait_send()
        return 0

    lax.fori_loop(0, groups, drain_group, 0)
    for q in range(groups - 2, groups):
        rest_copy(q).wait()
        out_copy(q).wait()
    nrm_copy.wait()
    for j in range(1, ny):
        vz(j).wait_send()
    for j in range(1, nx):
        vx(j).wait_send()
    for i in range(quads):
        r_own(i).wait()
        r_mate(i).wait()


def front(nx, ny, tok, cot, keep, wsrc, vsrc):
    tokens, width = tok.shape
    units, rows, cols = wsrc.shape
    groups, glanes, block = units // GROUP, GROUP * LANES, rows * ny
    dma = pltpu.SemaphoreType.DMA
    any_, vmem = pl.BlockSpec(memory_space=pl.ANY), pl.BlockSpec(memory_space=pltpu.VMEM)
    msg = RUNS, glanes
    s = jax.ShapeDtypeStruct
    return pl.pallas_call(
        functools.partial(front_kernel, nx, ny, units),
        out_shape=(
            s((units, width, cols), BF16), s((units, 2 * tokens, cols), BF16), s((2 * tokens, width // 2), BF16),
            s((tokens, width), BF16), s((tokens, width), F32), s((tokens, width), F32), s((tokens, LANES), F32),
            s((8, width), F32), s((8, width), F32),
        ),
        in_specs=[any_, any_, vmem, any_, any_],
        out_specs=(any_,) * 6 + (vmem,) * 3,
        scratch_shapes=[
            pltpu.VMEM((units, width, cols), BF16),
            pltpu.VMEM((width, LANES), BF16),
            pltpu.VMEM((tokens, width), BF16),
            pltpu.VMEM((tokens, width), BF16),
            pltpu.VMEM((tokens, width), F32),
            pltpu.VMEM((tokens, width), BF16),
            pltpu.VMEM((2 * GROUP, tokens, cols), F32),
            pltpu.VMEM((2 * GROUP, tokens, LANES), F32),
            pltpu.VMEM((2, tokens, glanes), F32),
            pltpu.VMEM((tokens, glanes), BF16),
            pltpu.VMEM((units, tokens, cols), BF16),
            pltpu.VMEM((tokens, tokens), BF16),
            pltpu.VMEM((2, tokens, glanes), BF16),
            pltpu.VMEM((2,) + msg, F32), pltpu.VMEM((2,) + msg, F32), pltpu.VMEM((2,) + msg, F32),
            pltpu.VMEM((2,) + msg, F32), pltpu.VMEM((2,) + msg, F32),
            pltpu.VMEM((groups, ny) + msg, F32), pltpu.VMEM((groups, nx) + msg, F32),
            pltpu.VMEM((groups, ny) + msg, F32), pltpu.VMEM((groups, nx) + msg, F32),
            dma((units, ny - 1)), dma((units, ny - 1)), dma((units,)), dma((units, 3)), dma((units, 2)),
            dma((units, 2)), dma((units, 2)), dma((units, 3)), dma((units, 4)), dma((units,)),
            dma((ny - 1,)), dma((ny - 1,)), dma((nx - 1,)), dma((nx - 1,)), dma, dma((2,)),
            dma((nx // 2,)), dma((nx // 2,)), dma((nx // 2,)), dma((units,)), dma((units,)), dma((units,)),
            dma((groups, 3)),
            dma((groups, ny - 1)), dma((groups, ny - 1)), dma((groups, nx - 1)), dma((groups, nx - 1)),
            dma((groups, ny - 1)), dma((groups, ny - 1)), dma((groups, nx - 1)), dma((groups, nx - 1)),
        ],
        compiler_params=pltpu.CompilerParams(
            collective_id=0, has_side_effects=True, vmem_limit_bytes=61 * 2**20
        ),
        cost_estimate=pl.CostEstimate(
            flops=2 * tokens * width * units * cols, bytes_accessed=2 * width * units * cols, transcendentals=0
        ),
    )(tok, cot, keep, wsrc, vsrc)


def back_kernel(
    nx, ny, units,
    pg, rcat, wall, nrmi, inv, resti, vecs, vsum,
    igo, wgo, vgo,
    rt, rbuf, pgb, wb, sb, rd, rx, ry, rz, zb, sg, nrm, rest, vtot, vin, perm, outb,
    lds, pgl, wl, dsn, drc, xsn, xrc, ysn, yrc, zsn, zrc, vsn, vrc, ous,
):
    gx, gy, core, mate, xn, yn = place(ny)
    tokens, width = sg.shape
    cols = pgb.shape[2]
    block = zb.shape[1]
    half, rows = block // 2, block // ny
    diag = xn + yn - gx
    count = nx * ny
    me = gx * ny + gy

    barrier = pltpu.get_barrier_semaphore()

    def greet(j, _):
        to = lax.rem(me + j, count)
        pl.semaphore_signal(barrier, inc=1, device_id=(to // ny, lax.rem(to, ny)), device_id_type=MESH)
        return 0

    lax.fori_loop(1, count, greet, 0)

    def pg_load(u):
        return pltpu.make_async_copy(pg.at[u], pgb.at[lax.rem(u, 2)], pgl.at[lax.rem(u, 2)])

    def w_load(u):
        return pltpu.make_async_copy(wall.at[u], wb.at[lax.rem(u, 2)], wl.at[lax.rem(u, 2)])

    r_load = pltpu.make_async_copy(rcat, rbuf, lds.at[0])
    r_load.start()
    pg_load(0).start()
    w_load(0).start()
    nrm_load = pltpu.make_async_copy(nrmi, nrm, lds.at[1])
    rest_load = pltpu.make_async_copy(resti, rest, lds.at[2])
    nrm_load.start()
    rest_load.start()

    def rows_of(chip, part, n=half):
        return pl.ds(pl.multiple_of((chip // 2) * block + part * half, 16), n)

    def d_copy(u, i):
        return remote(
            sb.at[u, rows_of(diag, i)], rd.at[u, i * half:(i + 1) * half], dsn.at[u, i], drc.at[u, i], ((yn, xn)[i], gy)
        )

    def x_copy(u, i):
        return remote(sb.at[u, rows_of(xn, i)], rx.at[u, i * half:(i + 1) * half], xsn.at[u, i], xrc.at[u, i], (xn, gy))

    def y_copy(u, i):
        return remote(sb.at[u, rows_of(yn, i)], ry.at[u, i * half:(i + 1) * half], ysn.at[u, i], yrc.at[u, i], (yn, gy))

    def z_copy(u, j):
        to = lax.rem(gy + j, ny)
        src = zb.at[u, pl.ds(pl.multiple_of(to * rows, 16), rows)]
        return remote(src, rz.at[u, j - 1], zsn.at[u, j - 1], zrc.at[u, j - 1], (gx, to))

    r_load.wait()
    rt[...] = rbuf[...].T
    sg[...] = jnp.zeros_like(sg)
    pl.semaphore_wait(barrier, count - 1)

    def weigh(u):
        slot = lax.rem(u, 2)
        pg_load(u).wait()

        @pl.when(u + 1 < units)
        def _():
            pg_load(u + 1).start()

        sb[u] = jnp.dot(rt[...], pgb[slot], preferred_element_type=F32).astype(BF16)
        for i in (0, 1):
            d_copy(u, i).start()
        x_copy(u, 1).start()
        y_copy(u, 0).start()
        w_load(u).wait()

        @pl.when(u + 1 < units)
        def _():
            w_load(u + 1).start()

        mine = pgb[slot, 0:tokens, :]
        sg[...] += lax.dot_general(mine, wb[slot], (((1,), (1,)), ((), ())), preferred_element_type=F32)
        sg[:, lanes_of(u)] += pgb[slot, 0:tokens, LANES:2 * LANES].astype(F32) * vecs[2:3, lanes_of(u)]

    def fold(into, at, more):
        into[at] = (into[at].astype(F32) + more.astype(F32)).astype(BF16)

    def meet(u):
        for i in (0, 1):
            d_copy(u, i).wait_recv()
        own = sb.at[u]
        fold(own, (rows_of(xn, 0), slice(None)), rd[u, 0:half])
        x_copy(u, 0).start()
        fold(own, (rows_of(yn, 1), slice(None)), rd[u, half:block])
        y_copy(u, 1).start()

    def column(u):
        for i in (0, 1):
            x_copy(u, i).wait_recv()
            y_copy(u, i).wait_recv()
        total = sb[u, rows_of(gx, 0, block), :].astype(F32) + rx[u].astype(F32) + ry[u].astype(F32)
        zb[u] = total.astype(BF16)
        for j in range(1, ny):
            z_copy(u, j).start()

    def settle(u):
        r = pl.ds(pl.multiple_of(gy * rows, 16), rows)
        at = pl.ds(pl.multiple_of((gx // 2) * block + gy * rows, 16), rows)
        total = sb[u, at, :].astype(F32) + rx[u, r, :].astype(F32) + ry[u, r, :].astype(F32)
        for j in range(1, ny):
            z_copy(u, j).wait_recv()
        for j in range(1, ny):
            total = total + rz[u, j - 1].astype(F32)
        for i in range(3):
            wgo[:, lanes_of(u + i * units)] = total[:, i * LANES:(i + 1) * LANES]

    BAND = 32
    bands = tokens // BAND

    def finish(i, _):
        r = pl.ds(pl.multiple_of(i * BAND, BAND), BAND)
        s, z = sg[r, :], nrm[r, :]
        sz = s * z
        gain = vecs[0:1, :]
        vtot_rows[0][...] += jnp.sum(sz.reshape(BAND // 8, 8, width), axis=0)
        vtot_rows[1][...] += jnp.sum(s.reshape(BAND // 8, 8, width), axis=0)
        n = s * gain
        m1 = jnp.mean(n, axis=1, keepdims=True)
        m2 = jnp.mean(sz * gain, axis=1, keepdims=True)
        sg[r, :] = rest[r, :] + inv[r, 0:1] * (n - m1 - z * m2)
        return 0

    vtot_rows = (outb.at[0, 0:8, :], outb.at[0, 8:16, :])

    def v_copy(j):
        to = lax.rem(me + j, count)
        return remote(vtot.at[to // 2], vin.at[me], vsn.at[to], vrc.at[me], (to // ny, lax.rem(to, ny)))

    def v_recv(j):
        at = lax.rem(me + j, count)
        return remote(vtot.at[0], vin.at[at], vsn.at[at], vrc.at[at], (at // ny, lax.rem(at, ny)))

    def vectors_out():
        zero = jnp.zeros((2, LANES), F32)
        for c in range(width // LANES):
            at = slice(c * LANES, (c + 1) * LANES)
            top = [jnp.sum(v[:, at], axis=0, keepdims=True) for v in vtot_rows]
            vtot[c] = jnp.concatenate(top + [vsum[2:6, at], zero], 0)
        lax.fori_loop(1, count, lambda j, _: (v_copy(j).start(), 0)[1], 0)

    chunk = outb.shape[2] // 4

    def out_copy(c):
        return pltpu.make_async_copy(rest.at[:, pl.ds(c * chunk, chunk)], igo.at[:, pl.ds(c * chunk, chunk)], ous.at[c])

    def natural():
        perm[...] = run_matrix(tokens, True)
        for c in range(4):
            at = slice(c * chunk, (c + 1) * chunk)
            v = sg[:, at]
            high = v.astype(BF16)
            low = (v - high.astype(F32)).astype(BF16)
            rest[:, at] = jnp.dot(perm[...], high, preferred_element_type=F32) + jnp.dot(
                perm[...], low, preferred_element_type=F32
            )
            out_copy(c).start()

    LAG1, LAG2, LAG3 = 2, 4, 6

    def tick(k, _):
        pl.when(k < units)(lambda: weigh(k))
        pl.when((k >= LAG1) & (k < units + LAG1))(lambda: meet(k - LAG1))
        pl.when((k >= LAG2) & (k < units + LAG2))(lambda: column(k - LAG2))
        pl.when(k >= LAG3)(lambda: settle(k - LAG3))

        @pl.when(k == units)
        def _():
            nrm_load.wait()
            rest_load.wait()
            for v in vtot_rows:
                v[...] = jnp.zeros_like(v)
            lax.fori_loop(0, bands // 2, finish, 0)

        @pl.when(k == units + 1)
        def _():
            lax.fori_loop(bands // 2, bands, finish, 0)
            vectors_out()

        pl.when(k == units + 2)(natural)
        return 0

    lax.fori_loop(0, units + LAG3, tick, 0)

    lax.fori_loop(1, count, lambda j, _: (v_recv(j).wait_recv(), 0)[1], 0)
    vin[me] = vtot[me // 2]
    vgo[...] = lax.fori_loop(0, count, lambda j, s: s + vin[j], jnp.zeros((8, LANES), F32))

    def drain(u, _):
        for i in (0, 1):
            d_copy(u, i).wait_send()
            x_copy(u, i).wait_send()
            y_copy(u, i).wait_send()
        for j in range(1, ny):
            z_copy(u, j).wait_send()
        return 0

    lax.fori_loop(0, units, drain, 0)
    lax.fori_loop(1, count, lambda j, _: (v_copy(j).wait_send(), 0)[1], 0)
    for c in range(4):
        out_copy(c).wait()


def back(nx, ny, pg, rcat, wall, nrm, inv, rest, vecs, vsum):
    units, both, cols = pg.shape
    tokens, width = nrm.shape
    block = width // nx
    rows = block // ny
    dma = pltpu.SemaphoreType.DMA
    any_, vmem = pl.BlockSpec(memory_space=pl.ANY), pl.BlockSpec(memory_space=pltpu.VMEM)
    s = jax.ShapeDtypeStruct
    return pl.pallas_call(
        functools.partial(back_kernel, nx, ny, units),
        out_shape=(s((tokens, width), F32), s((rows, 3 * width), F32), s((8, LANES), F32)),
        in_specs=[any_, any_, any_, any_, vmem, any_, vmem, vmem],
        out_specs=(any_, vmem, vmem),
        scratch_shapes=[
            pltpu.VMEM((width // 2, both), BF16),
            pltpu.VMEM((both, width // 2), BF16),
            pltpu.VMEM((2, both, cols), BF16),
            pltpu.VMEM((2, width, cols), BF16),
            pltpu.VMEM((units, width // 2, cols), BF16),
            pltpu.VMEM((units, block, cols), BF16),
            pltpu.VMEM((units, block, cols), BF16),
            pltpu.VMEM((units, block, cols), BF16),
            pltpu.VMEM((units, ny - 1, rows, cols), BF16),
            pltpu.VMEM((units, block, cols), BF16),
            pltpu.VMEM((tokens, width), F32),
            pltpu.VMEM((tokens, width), F32),
            pltpu.VMEM((tokens, width), F32),
            pltpu.VMEM((width // LANES, 8, LANES), F32),
            pltpu.VMEM((nx * ny, 8, LANES), F32),
            pltpu.VMEM((tokens, tokens), BF16),
            pltpu.VMEM((1, 16, width), F32),
            dma((3,)), dma((2,)), dma((2,)),
            dma((units, 2)), dma((units, 2)), dma((units, 2)), dma((units, 2)), dma((units, 2)), dma((units, 2)),
            dma((units, ny - 1)), dma((units, ny - 1)), dma((nx * ny,)), dma((nx * ny,)), dma((4,)),
        ],
        compiler_params=pltpu.CompilerParams(
            collective_id=1, has_side_effects=True, vmem_limit_bytes=61 * 2**20
        ),
        cost_estimate=pl.CostEstimate(
            flops=4 * tokens * width * units * cols, bytes_accessed=2 * width * units * cols, transcendentals=0
        ),
    )(pg, rcat, wall, nrm, inv, rest, vecs, vsum)


def fast(nx, ny, tokens, reset_mask, weight, vectors, cotangent):
    count, width = tokens.shape
    rows = weight.shape[0]
    units, steps = width // LANES, count // RUNS
    keep = (1 - reset_mask).astype(F32).reshape(RUNS, steps).T.reshape(count, 1)
    keep = jnp.broadcast_to(keep, (count, LANES))
    wsrc = weight.reshape(rows, 3, units, LANES).transpose(2, 0, 1, 3).reshape(units, rows, 3 * LANES)
    vsrc = jnp.pad(vectors.T, ((0, 0), (0, LANES - 6)))
    wall, pg, rcat, outp, grest, nrm, inv, vecs, vsum = front(nx, ny, tokens, cotangent, keep, wsrc, vsrc)
    grad, weight_grad, tile = back(nx, ny, pg, rcat, wall, nrm, inv, grest, vecs, vsum)
    odd = lax.rem(lax.axis_index("gx") * ny + lax.axis_index("gy"), 2) == 1
    vector_grad = jnp.where(odd, tile[:6, rows:2 * rows], tile[:6, :rows])
    return outp, grad, weight_grad, vector_grad


def solution(mesh):
    placed = (
        P(("gx", "gy"), None),
        P(("gx", "gy")),
        P(("gx", "gy"), None),
        P(None, ("gx", "gy")),
        P(("gx", "gy"), None),
    )
    nx, ny = mesh.shape["gx"], mesh.shape["gy"]

    def body(tokens, reset_mask, weight, vectors, cotangent):
        whole_tiles = weight.shape[0] % 16 == 0 and tokens.shape[0] % 256 == 0
        if nx == 8 and whole_tiles and 2 * weight.shape[0] == LANES and tokens.shape[1] % 2048 == 0:
            return fast(nx, ny, tokens, reset_mask, weight, vectors, cotangent)
        return local(tokens, reset_mask, weight, vectors, cotangent)

    return jax.shard_map(
        body,
        mesh=mesh,
        in_specs=placed,
        out_specs=(
            P(("gx", "gy"), None),
            P(("gx", "gy"), None),
            P(("gx", "gy"), None),
            P(None, ("gx", "gy")),
        ),
        check_vma=False,
    )
```

```python
import functools

import jax
import jax.numpy as jnp
from jax import lax
from jax.experimental import pallas as pl
from jax.experimental.pallas import tpu as pltpu
from jax.sharding import PartitionSpec as P

MESH = pl.DeviceIdType.MESH
F32, BF16 = jnp.float32, jnp.bfloat16
LANES, RUNS, GROUP = 128, 8, 2
EPS = 1e-05


def place(ny):
    gx, gy = lax.axis_index("gx"), lax.axis_index("gy")
    core, xx, yy = lax.rem(gx, 2), lax.rem(gx // 2, 2), gx // 4
    return gx, gy, core, gx + 1 - 2 * core, gx + 2 - 4 * xx, gx + 4 - 8 * yy


def remote(src, dst, send, recv, to):
    return pltpu.make_async_remote_copy(
        src_ref=src, dst_ref=dst, send_sem=send, recv_sem=recv, device_id=to, device_id_type=MESH
    )


def lanes_of(b):
    return pl.ds(pl.multiple_of(b * LANES, LANES), LANES)


def run_matrix(tokens, back):
    steps = tokens // RUNS
    row = lax.broadcasted_iota(jnp.int32, (tokens, tokens), 0)
    col = lax.broadcasted_iota(jnp.int32, (tokens, tokens), 1)
    if back:
        hit = row == (col & (RUNS - 1)) * steps + (col >> 3)
    else:
        hit = col == (row & (RUNS - 1)) * steps + (row >> 3)
    return jnp.where(hit, 1.0, 0.0).astype(BF16)


def entering(value, axis, join, neutral, backward):
    count, mine = (lax.axis_size(axis), lax.axis_index(axis))
    pieces = jax.tree.map(lambda part: lax.all_gather(part, axis), value)
    if backward:
        pieces = jax.tree.map(lambda part: part[::-1], pieces)
        mine = count - 1 - mine
    subtotal = jax.tree.map(
        lambda part, zero: jnp.full_like(part, 0) + jnp.asarray(zero, part.dtype), value, neutral
    )

    def lap(position, subtotal):
        longer = join(subtotal, jax.tree.map(lambda part: part[position], pieces))
        return jax.tree.map(lambda new, old: jnp.where(position < mine, new, old), longer, subtotal)

    return lax.fori_loop(0, count - 1, lap, subtotal)


def from_behind(block, axis, distance):
    devices = range(lax.axis_size(axis))
    route = [(i - distance, i) for i in devices if i - distance in devices]
    return lax.ppermute(block, axis, route)


def compose(earlier, later):
    return (earlier[0] * later[0], later[0] * earlier[1] + later[1])


def local(tokens, reset_mask, weight, vectors, cotangent):
    width = weight.shape[1] // 3
    whole_weight, whole_vectors = (
        lax.all_gather(weight, ("gx", "gy"), axis=0, tiled=True),
        lax.all_gather(vectors, ("gx", "gy"), axis=1, tiled=True),
    )
    params = whole_vectors.astype(jnp.float32)
    gain = params[0]
    shift_bias = params[1]
    forget_peep = params[2]
    forget_bias = params[3]
    reset_peep = params[4]
    reset_bias = params[5]
    inputs = tokens.astype(jnp.float32)
    keep = (1 - reset_mask).astype(jnp.float32)[:, None]
    centred = inputs - jnp.mean(inputs, axis=1, keepdims=True)
    inv_std = lax.rsqrt(jnp.mean(centred * centred, axis=1, keepdims=True) + 1e-05)
    normed = centred * inv_std
    scaled = normed * gain + shift_bias
    rounded = scaled.astype(jnp.bfloat16)
    projected = jnp.dot(rounded, whole_weight, preferred_element_type=jnp.float32)
    candidate = projected[:, :width]
    forget_pre = projected[:, width : 2 * width]
    reset_pre = projected[:, 2 * width :]
    forget = jax.nn.sigmoid(forget_pre + forget_peep * scaled + forget_bias)
    decay = forget * keep
    inflow = (1.0 - forget) * candidate
    cum_decay, cum_state = lax.associative_scan(compose, (decay, inflow), axis=0)
    unit = (jnp.ones_like(cum_decay[-1]), jnp.zeros_like(cum_state[-1]))
    before = entering((cum_decay[-1], cum_state[-1]), ("gx", "gy"), compose, unit, False)
    state_in = before[1]
    state = cum_decay * state_in + cum_state
    previous = keep * jnp.concatenate([state_in[None], state[:-1]], 0)
    reset = jax.nn.sigmoid(reset_pre + reset_peep * previous + reset_bias)
    output = reset * state + (1.0 - reset) * inputs
    upstream = cotangent.astype(jnp.float32)
    reset_grad = upstream * (state - inputs) * reset * (1.0 - reset)
    through = keep * reset_peep * reset_grad
    next_decay, next_through = from_behind((decay[0], through[0]), ("gx", "gy"), -1)
    ahead = jnp.concatenate([decay[1:], next_decay[None]], 0)
    local_term = upstream * reset + jnp.concatenate([through[1:], next_through[None]], 0)
    flip_mult, flip_sum = lax.associative_scan(compose, (ahead[::-1], local_term[::-1]), axis=0)
    mult_back = flip_mult[::-1]
    sum_back = flip_sum[::-1]
    after = entering((mult_back[0], sum_back[0]), ("gx", "gy"), compose, unit, True)
    state_grad = mult_back * after[1] + sum_back
    candidate_grad = state_grad * (1.0 - forget)
    forget_grad = state_grad * (previous - candidate) * forget * (1.0 - forget)
    proj_grad = jnp.concatenate([candidate_grad, forget_grad, reset_grad], 1).astype(jnp.bfloat16)
    weight_grad = lax.psum_scatter(
        lax.dot_general(
            rounded, proj_grad, (((0,), (0,)), ((), ())), preferred_element_type=jnp.float32
        ),
        ("gx", "gy"),
        scatter_dimension=0,
        tiled=True,
    )
    scaled_grad = lax.dot_general(
        proj_grad,
        lax.all_gather(weight, ("gx", "gy"), axis=0, tiled=True),
        (((1,), (1,)), ((), ())),
        preferred_element_type=jnp.float32,
    )
    scaled_grad = scaled_grad + forget_grad * forget_peep
    vector_terms = jnp.stack(
        [
            jnp.sum(scaled_grad * normed, axis=0),
            jnp.sum(scaled_grad, axis=0),
            jnp.sum(forget_grad * scaled, axis=0),
            jnp.sum(forget_grad, axis=0),
            jnp.sum(reset_grad * previous, axis=0),
            jnp.sum(reset_grad, axis=0),
        ],
        0,
    )
    vector_grad = lax.psum_scatter(vector_terms, ("gx", "gy"), scatter_dimension=1, tiled=True)
    normed_grad = scaled_grad * gain
    input_grad = upstream * (1.0 - reset) + inv_std * (
        normed_grad
        - jnp.mean(normed_grad, axis=1, keepdims=True)
        - normed * jnp.mean(normed_grad * normed, axis=1, keepdims=True)
    )
    return (output.astype(jnp.bfloat16), input_grad, weight_grad, vector_grad)


SLOTS = 8
TOTALS, FORE, GRADS, BACK = 3, 5, 6, 8


def front_kernel(
    nx, ny, units,
    tok, cot, keep, wsrc, vsrc,
    wall, pg, rcat, outp, grest, nrmo, invo, vecs, vsum,
    wv, vbuf, xs, gs, nrm, rnd, pj, pv, grs, outs, pgs, perm, stage,
    ach, bch, qch, sin, cin, m1a, m1b, m2a, m2b,
    zs, zr, os, bs, br, dsn, dr, cs, cr, ws,
    vzs, vzr, vxs, vxr, vo, sts, rs, rr, ro, ps, pr, po, gos, e1as, e1ar, e1bs, e1br, e2as, e2ar, e2bs, e2br,
):
    gx, gy, core, mate, xn, yn = place(ny)
    tokens, width = xs.shape
    rows = wsrc.shape[1]
    block = rows * ny
    groups = units // GROUP
    glanes = GROUP * LANES
    diag = xn + yn - gx
    first = gx * block
    mine = first + gy * rows
    me = gx * ny + gy

    def peer_y(j):
        return lax.rem(gy + j, ny)

    def peer_x(j):
        return lax.rem(gx + j, nx)

    barrier = pltpu.get_barrier_semaphore()
    for j in range(1, ny):
        pl.semaphore_signal(barrier, inc=1, device_id=(gx, peer_y(j)), device_id_type=MESH)
    for j in range(1, nx):
        pl.semaphore_signal(barrier, inc=1, device_id=(peer_x(j), gy), device_id_type=MESH)

    def band(b, n=block):
        return pl.ds(pl.multiple_of(b, 16), n)

    chunks = width // glanes

    def stage_copy(i):
        src = tok if i < chunks else cot
        c = i % chunks
        return pltpu.make_async_copy(src.at[:, pl.ds(c * glanes, glanes)], stage.at[i % 2], sts.at[i % 2])

    stage_copy(0).start()
    stage_copy(1).start()

    def vz(j):
        return remote(vsrc, vbuf.at[me], vzs.at[j - 1], vzr.at[j - 1], (gx, peer_y(j)))

    def vx(j):
        part = vbuf.at[pl.ds(gx * ny, ny)]
        return remote(part, part, vxs.at[j - 1], vxr.at[j - 1], (peer_x(j), gy))

    own_vec = pltpu.make_async_copy(vsrc, vbuf.at[me], vo)

    def z_copy(u, j):
        return remote(wsrc.at[u], wv.at[u, band(mine, rows)], zs.at[u, j - 1], zr.at[u, j - 1], (gx, peer_y(j)))

    def own_copy(u):
        return pltpu.make_async_copy(wsrc.at[u], wv.at[u, band(mine, rows)], os.at[u])

    def band_copy(u, i):
        to = (mate, xn, yn)[i]
        recv = cr.at[u, 0] if i == 0 else br.at[u, i - 1]
        part = wv.at[u, band(first)]
        return remote(part, part, bs.at[u, i], recv, (to, gy))

    def diag_copy(u, i):
        at = (xn * block, yn * block + block // 2)[i]
        part = wv.at[u, band(at, block // 2)]
        return remote(part, part, dsn.at[u, i], dr.at[u, i], ((yn, xn)[i], gy))

    def core_copy(u, i):
        part = wv.at[u, band((None, xn, yn, diag)[i] * block)]
        return remote(part, part, cs.at[u, i - 1], cr.at[u, i], (mate, gy))

    def keep_copy(u):
        return pltpu.make_async_copy(wv.at[u], wall.at[u], ws.at[u])

    def z_start(u):
        own_copy(u).start()
        for j in range(1, ny):
            z_copy(u, j).start()

    def z_wait(u):
        own_copy(u).wait()
        for j in range(1, ny):
            z_copy(u, j).wait_recv()
        for i in (1, 2, 0):
            band_copy(u, i).start()

    def xy_wait(u):
        for i in (1, 2):
            band_copy(u, i).wait_recv()
        for i in (0, 1):
            diag_copy(u, i).start()
        for i in (1, 2):
            core_copy(u, i).start()

    def diag_wait(u):
        for i in (0, 1):
            diag_copy(u, i).wait_recv()
        core_copy(u, 3).start()

    def core_wait(u):
        band_copy(u, 0).wait_recv()
        for i in (1, 2, 3):
            core_copy(u, i).wait_recv()

    pl.semaphore_wait(barrier, nx + ny - 2)
    own_vec.start()
    for j in range(1, ny):
        vz(j).start()
    AHEAD_Z, AHEAD_B = 5, 3
    for u in range(AHEAD_Z):
        z_start(u)

    perm[...] = run_matrix(tokens, False)

    def to_runs(i, into):
        stage_copy(i).wait()
        c = i % chunks
        into[:, c * glanes:(c + 1) * glanes] = jnp.dot(
            perm[...], stage[i % 2], preferred_element_type=F32
        ).astype(BF16)
        if i + 2 < 2 * chunks:
            stage_copy(i + 2).start()

    for i in range(chunks):
        to_runs(i, xs)
    z_wait(0)
    own_vec.wait()
    for j in range(1, ny):
        vz(j).wait_recv()
    for j in range(1, nx):
        vx(j).start()
    z_wait(1)

    BAND = 32

    def moments(i, _):
        r = pl.ds(pl.multiple_of(i * BAND, BAND), BAND)
        x = xs[r, :].astype(F32)
        centred = x - jnp.mean(x, axis=1, keepdims=True)
        inv = lax.rsqrt(jnp.mean(centred * centred, axis=1, keepdims=True) + EPS)
        nrm[r, :] = centred * inv
        invo[r, :] = jnp.broadcast_to(inv, (BAND, LANES))
        return 0

    lax.fori_loop(0, tokens // BAND, moments, 0)
    nrm_copy = pltpu.make_async_copy(nrm, nrmo, gos.at[0, 2])
    nrm_copy.start()
    for u in range(2, AHEAD_B):
        z_wait(u)
    for i in range(chunks, 2 * chunks):
        to_runs(i, gs)
    perm[...] = run_matrix(tokens, True)
    for j in range(1, nx):
        vx(j).wait_recv()

    for c in range(width // LANES):
        part = vbuf[2 * c].astype(F32) + vbuf[2 * c + 1].astype(F32)
        vecs[:, c * LANES:(c + 1) * LANES] = part[0:8, :]

    def rounding(i, _):
        r = pl.ds(pl.multiple_of(i * BAND, BAND), BAND)
        rnd[r, :] = (nrm[r, :] * vecs[0:1, :] + vecs[1:2, :]).astype(BF16)
        return 0

    lax.fori_loop(0, tokens // BAND, rounding, 0)

    quads = nx // 2

    def r_own(i):
        src = rnd.at[:, pl.ds(pl.multiple_of((2 * i + core) * block, LANES), block)]
        return pltpu.make_async_copy(src, rcat.at[0:tokens, pl.ds(i * block, block)], ro.at[i])

    def r_mate(i):
        src = rnd.at[:, pl.ds(pl.multiple_of((2 * i + 1 - core) * block, LANES), block)]
        dst = rcat.at[tokens:2 * tokens, pl.ds(i * block, block)]
        return remote(src, dst, rs.at[i], rr.at[i], (mate, gy))

    for i in range(quads):
        r_own(i).start()
        r_mate(i).start()

    def e_copies(buf, send, recv, q, level):
        if level == 0:
            return [
                remote(buf.at[q, gy], buf.at[q, gy], send.at[q, j - 1], recv.at[q, j - 1], (gx, peer_y(j)))
                for j in range(1, ny)
            ]
        return [
            remote(buf.at[q, gx], buf.at[q, gx], send.at[q, j - 1], recv.at[q, j - 1], (peer_x(j), gy))
            for j in range(1, nx)
        ]

    def e_start(*a):
        for c in e_copies(*a):
            c.start()

    def e_wait(*a):
        for c in e_copies(*a):
            c.wait_recv()

    double = tokens // (2 * RUNS)

    def project(u):
        slot = lax.rem(u, SLOTS)
        pj[slot] = jnp.dot(rnd[...], wv[u], preferred_element_type=F32)

    def vec(i, u):
        return vecs[i:i + 1, lanes_of(u)]

    def gates(u):
        slot = lax.rem(u, SLOTS)
        gain, shift, vf, bf = (vec(i, u) for i in range(4))

        def step(i, carry):
            a, b = carry
            r = pl.ds(pl.multiple_of(i * 16, 16), 16)
            scaled = nrm[r, lanes_of(u)] * gain + shift
            f = jax.nn.sigmoid(pj[slot, r, LANES:2 * LANES] + vf * scaled + bf)
            pj[slot, r, LANES:2 * LANES] = f
            d = f * keep[r, :]
            inflow = (1.0 - f) * pj[slot, r, 0:LANES]
            for h in (0, 8):
                a = a * d[h:h + 8]
                b = d[h:h + 8] * b + inflow[h:h + 8]
            return a, b

        a, b = lax.fori_loop(0, double, step, (jnp.ones((RUNS, LANES), F32), jnp.zeros((RUNS, LANES), F32)), unroll=4)
        q, j = u // GROUP, lax.rem(u, GROUP)
        ach[q, :, lanes_of(j)] = a
        bch[q, :, lanes_of(j)] = b

    def totals(q):
        a, b = jnp.ones((1, glanes), F32), jnp.zeros((1, glanes), F32)
        for s in range(RUNS):
            one = ach[q, s:s + 1, :]
            a = a * one
            b = one * b + bch[q, s:s + 1, :]
        m1a[q, gy, 0:1, :] = a
        m1a[q, gy, 1:2, :] = b
        e_start(m1a, e1as, e1ar, q, 0)

    def totals_x(q):
        e_wait(m1a, e1as, e1ar, q, 0)
        a, b = jnp.ones((1, glanes), F32), jnp.zeros((1, glanes), F32)
        for s in range(ny):
            one = m1a[q, s, 0:1, :]
            a = a * one
            b = one * b + m1a[q, s, 1:2, :]
        m1b[q, gx, 0:1, :] = a
        m1b[q, gx, 1:2, :] = b
        e_start(m1b, e1bs, e1br, q, 1)

    def enter(q):
        e_wait(m1b, e1bs, e1br, q, 1)
        g = lax.rem(q, 2)
        s = jnp.zeros((1, glanes), F32)
        s = lax.fori_loop(0, gx, lambda i, s: m1b[q, i, 0:1, :] * s + m1b[q, i, 1:2, :], s)
        s = lax.fori_loop(0, gy, lambda i, s: m1a[q, i, 0:1, :] * s + m1a[q, i, 1:2, :], s)
        for r in range(RUNS):
            sin[q, r:r + 1, :] = s
            s = ach[q, r:r + 1, :] * s + bch[q, r:r + 1, :]

    def forward(u):
        slot = lax.rem(u, SLOTS)
        q, j = u // GROUP, lax.rem(u, GROUP)
        g = lax.rem(q, 2)
        vr, br_ = vec(4, u), vec(5, u)
        zero = jnp.zeros((RUNS, LANES), F32)

        def step(i, carry):
            s, run, t, v4, v5 = carry
            r = pl.ds(pl.multiple_of(i * 16, 16), 16)
            f = pj[slot, r, LANES:2 * LANES]
            k = keep[r, :]
            inflow = (1.0 - f) * pj[slot, r, 0:LANES]
            prevs, states = [], []
            for h in (0, 8):
                prev = k[h:h + 8] * s
                s = f[h:h + 8] * prev + inflow[h:h + 8]
                prevs.append(prev)
                states.append(s)
            prev, state = jnp.concatenate(prevs, 0), jnp.concatenate(states, 0)
            x = xs[r, lanes_of(u)].astype(F32)
            up = gs[r, lanes_of(u)].astype(F32)
            reset = jax.nn.sigmoid(pj[slot, r, 2 * LANES:3 * LANES] + vr * prev + br_)
            rest = 1.0 - reset
            outs[r, lanes_of(j)] = (reset * state + rest * x).astype(BF16)
            rg = up * (state - x) * reset * rest
            gr = up * rest
            pj[slot, r, 2 * LANES:3 * LANES] = rg
            pv[slot, r, :] = prev
            grs[g, r, lanes_of(j)] = gr
            local = up * reset
            d, through = f * k, k * vr * rg
            for h in (0, 8):
                t = t + run * through[h:h + 8]
                run = run * d[h:h + 8]
                t = t + run * local[h:h + 8]
                v4 = v4 + rg[h:h + 8] * prev[h:h + 8]
                v5 = v5 + rg[h:h + 8]
            return s, run, t, v4, v5

        init = (sin[q, :, lanes_of(j)], jnp.ones((RUNS, LANES), F32), zero, zero, zero)
        _, _, t, v4, v5 = lax.fori_loop(0, double, step, init, unroll=4)
        qch[q, :, lanes_of(j)] = t
        vsum[4:5, lanes_of(u)] = jnp.sum(v4, axis=0, keepdims=True)
        vsum[5:6, lanes_of(u)] = jnp.sum(v5, axis=0, keepdims=True)

    def out_copy(q):
        c = pl.ds(pl.multiple_of(q * glanes, LANES), glanes)
        return pltpu.make_async_copy(stage.at[lax.rem(q, 2)], outp.at[:, c], gos.at[q, 0])

    def rest_copy(q):
        c = pl.ds(pl.multiple_of(q * glanes, LANES), glanes)
        return pltpu.make_async_copy(grs.at[lax.rem(q, 2)], grest.at[:, c], gos.at[q, 1])

    def forward_group(q):
        enter(q)
        pl.when(q >= 2)(lambda: (rest_copy(q - 2).wait(), out_copy(q - 2).wait())[0])
        lax.fori_loop(0, GROUP, lambda j, _: (forward(q * GROUP + j), 0)[1], 0)
        g = lax.rem(q, 2)
        s = jnp.zeros((1, glanes), F32)
        for r in reversed(range(RUNS)):
            s = ach[q, r:r + 1, :] * s + qch[q, r:r + 1, :]
        m2a[q, gy, 0:1, :] = s
        e_start(m2a, e2as, e2ar, q, 0)
        rest_copy(q).start()
        stage[g] = jnp.dot(perm[...], outs[...], preferred_element_type=F32).astype(BF16)
        out_copy(q).start()

    def grads_x(q):
        e_wait(m2a, e2as, e2ar, q, 0)
        s = jnp.zeros((1, glanes), F32)
        for r in reversed(range(ny)):
            s = m1a[q, r, 0:1, :] * s + m2a[q, r, 0:1, :]
        m2b[q, gx, 0:1, :] = s
        e_start(m2b, e2bs, e2br, q, 1)

    def enter_back(q):
        e_wait(m2b, e2bs, e2br, q, 1)
        g = lax.rem(q, 2)
        s = jnp.zeros((1, glanes), F32)

        def over_x(i, s):
            return m1b[q, nx - 1 - i, 0:1, :] * s + m2b[q, nx - 1 - i, 0:1, :]

        def over_y(i, s):
            return m1a[q, ny - 1 - i, 0:1, :] * s + m2a[q, ny - 1 - i, 0:1, :]

        s = lax.fori_loop(0, nx - 1 - gx, over_x, s)
        s = lax.fori_loop(0, ny - 1 - gy, over_y, s)
        for r in reversed(range(RUNS)):
            cin[q, r:r + 1, :] = s
            s = ach[q, r:r + 1, :] * s + qch[q, r:r + 1, :]

    def pg_own(u):
        return pltpu.make_async_copy(pgs.at[u], pg.at[u, 0:tokens], po.at[u])

    def pg_mate(u):
        return remote(pgs.at[u], pg.at[u, tokens:2 * tokens], ps.at[u], pr.at[u], (mate, gy))

    def backward(u):
        slot = lax.rem(u, SLOTS)
        q, j = u // GROUP, lax.rem(u, GROUP)
        g = lax.rem(q, 2)
        gain, shift, vr = vec(0, u), vec(1, u), vec(4, u)
        zero = jnp.zeros((RUNS, LANES), F32)

        def step(i, carry):
            c, v2, v3 = carry
            r = pl.ds(pl.multiple_of((double - 1 - i) * 16, 16), 16)
            f = pj[slot, r, LANES:2 * LANES]
            k = keep[r, :]
            rg = pj[slot, r, 2 * LANES:3 * LANES]
            local = gs[r, lanes_of(u)].astype(F32) - grs[g, r, lanes_of(j)]
            d, through = f * k, k * vr * rg
            grads = [None, None]
            for h in (1, 0):
                part = slice(8 * h, 8 * h + 8)
                grads[h] = local[part] + c
                c = d[part] * grads[h] + through[part]
            grad = jnp.concatenate(grads, 0)
            cg = grad * (1.0 - f)
            fg = cg * (pv[slot, r, :] - pj[slot, r, 0:LANES]) * f
            scaled = nrm[r, lanes_of(u)] * gain + shift
            pgs[u, r, 0:LANES] = cg.astype(BF16)
            pgs[u, r, LANES:2 * LANES] = fg.astype(BF16)
            pgs[u, r, 2 * LANES:3 * LANES] = rg.astype(BF16)
            fs = fg * scaled
            return c, v2 + fs[0:8] + fs[8:16], v3 + fg[0:8] + fg[8:16]

        _, v2, v3 = lax.fori_loop(0, double, step, (cin[q, :, lanes_of(j)], zero, zero), unroll=4)
        vsum[2:3, lanes_of(u)] = jnp.sum(v2, axis=0, keepdims=True)
        vsum[3:4, lanes_of(u)] = jnp.sum(v3, axis=0, keepdims=True)
        pg_own(u).start()
        pg_mate(u).start()

    def backward_group(q):
        enter_back(q)
        lax.fori_loop(0, GROUP, lambda j, _: (backward(q * GROUP + j), 0)[1], 0)

    vsum[...] = jnp.zeros_like(vsum)

    def tick(k, _):
        u = k - 2
        q, m = u // GROUP, lax.rem(u, GROUP)
        pl.when(k + AHEAD_Z < units)(lambda: z_start(k + AHEAD_Z))
        pl.when(k + AHEAD_B < units)(lambda: z_wait(k + AHEAD_B))
        pl.when(k < units)(lambda: xy_wait(k))
        pl.when((k >= 1) & (k <= units))(lambda: diag_wait(k - 1))

        def event(lag, run):
            g = (u - lag) // GROUP
            pl.when((u >= lag) & (lax.rem(u - lag + GROUP, GROUP) == 0) & (g < groups))(lambda: run(g))

        event(BACK, backward_group)
        event(GRADS, grads_x)
        event(FORE, forward_group)
        event(TOTALS, totals_x)

        @pl.when((u >= 0) & (u < units))
        def _():
            core_wait(u)
            keep_copy(u).start()
            project(u)
            gates(u)
            pl.when(m == GROUP - 1)(lambda: totals(q))

        return 0

    lax.fori_loop(0, units + BACK - GROUP + 1 + 2, tick, 0)

    def drain(u, _):
        for j in range(1, ny):
            z_copy(u, j).wait_send()
        for i in range(3):
            band_copy(u, i).wait_send()
        for i in (0, 1):
            diag_copy(u, i).wait_send()
        for i in (1, 2, 3):
            core_copy(u, i).wait_send()
        keep_copy(u).wait()
        pg_own(u).wait()
        pg_mate(u).wait()
        return 0

    lax.fori_loop(0, units, drain, 0)

    def drain_group(q, _):
        for a in ((m1a, e1as, e1ar, q, 0), (m1b, e1bs, e1br, q, 1), (m2a, e2as, e2ar, q, 0), (m2b, e2bs, e2br, q, 1)):
            for c in e_copies(*a):
                c.wait_send()
        return 0

    lax.fori_loop(0, groups, drain_group, 0)
    for q in range(groups - 2, groups):
        rest_copy(q).wait()
        out_copy(q).wait()
    nrm_copy.wait()
    for j in range(1, ny):
        vz(j).wait_send()
    for j in range(1, nx):
        vx(j).wait_send()
    for i in range(quads):
        r_own(i).wait()
        r_mate(i).wait()


def front(nx, ny, tok, cot, keep, wsrc, vsrc):
    tokens, width = tok.shape
    units, rows, cols = wsrc.shape
    groups, glanes, block = units // GROUP, GROUP * LANES, rows * ny
    dma = pltpu.SemaphoreType.DMA
    any_, vmem = pl.BlockSpec(memory_space=pl.ANY), pl.BlockSpec(memory_space=pltpu.VMEM)
    msg = RUNS, glanes
    s = jax.ShapeDtypeStruct
    return pl.pallas_call(
        functools.partial(front_kernel, nx, ny, units),
        name="front",
        out_shape=(
            s((units, width, cols), BF16), s((units, 2 * tokens, cols), BF16), s((2 * tokens, width // 2), BF16),
            s((tokens, width), BF16), s((tokens, width), F32), s((tokens, width), F32), s((tokens, LANES), F32),
            s((8, width), F32), s((8, width), F32),
        ),
        in_specs=[any_, any_, vmem, any_, any_],
        out_specs=(any_,) * 6 + (vmem,) * 3,
        scratch_shapes=[
            pltpu.VMEM((units, width, cols), BF16),
            pltpu.VMEM((nx * ny, 16, LANES), BF16),
            pltpu.VMEM((tokens, width), BF16),
            pltpu.VMEM((tokens, width), BF16),
            pltpu.VMEM((tokens, width), F32),
            pltpu.VMEM((tokens, width), BF16),
            pltpu.VMEM((SLOTS, tokens, cols), F32),
            pltpu.VMEM((SLOTS, tokens, LANES), F32),
            pltpu.VMEM((2, tokens, glanes), F32),
            pltpu.VMEM((tokens, glanes), BF16),
            pltpu.VMEM((units, tokens, cols), BF16),
            pltpu.VMEM((tokens, tokens), BF16),
            pltpu.VMEM((2, tokens, glanes), BF16),
            *[pltpu.VMEM((groups,) + msg, F32)] * 5,
            pltpu.VMEM((groups, ny) + msg, F32), pltpu.VMEM((groups, nx) + msg, F32),
            pltpu.VMEM((groups, ny) + msg, F32), pltpu.VMEM((groups, nx) + msg, F32),
            dma((units, ny - 1)), dma((units, ny - 1)), dma((units,)), dma((units, 3)), dma((units, 2)),
            dma((units, 2)), dma((units, 2)), dma((units, 3)), dma((units, 4)), dma((units,)),
            dma((ny - 1,)), dma((ny - 1,)), dma((nx - 1,)), dma((nx - 1,)), dma, dma((2,)),
            dma((nx // 2,)), dma((nx // 2,)), dma((nx // 2,)), dma((units,)), dma((units,)), dma((units,)),
            dma((groups, 3)),
            dma((groups, ny - 1)), dma((groups, ny - 1)), dma((groups, nx - 1)), dma((groups, nx - 1)),
            dma((groups, ny - 1)), dma((groups, ny - 1)), dma((groups, nx - 1)), dma((groups, nx - 1)),
        ],
        compiler_params=pltpu.CompilerParams(
            collective_id=0, has_side_effects=True, vmem_limit_bytes=61 * 2**20
        ),
        cost_estimate=pl.CostEstimate(
            flops=2 * tokens * width * units * cols, bytes_accessed=2 * width * units * cols, transcendentals=0
        ),
    )(tok, cot, keep, wsrc, vsrc)


def back_kernel(
    nx, ny, units,
    pg, rcat, wall, nrmi, inv, resti, vecs, vsum,
    igo, wgo, vgo,
    rt, rbuf, pgb, wb, sb, rd, rx, ry, rz, zb, sg, nrm, rest, vtot, vin, perm, outb,
    lds, pgl, wl, dsn, drc, xsn, xrc, ysn, yrc, zsn, zrc, vsn, vrc, ous,
):
    gx, gy, core, mate, xn, yn = place(ny)
    tokens, width = sg.shape
    cols = pgb.shape[2]
    block = zb.shape[1]
    half, rows = block // 2, block // ny
    diag = xn + yn - gx
    count = nx * ny
    me = gx * ny + gy

    barrier = pltpu.get_barrier_semaphore()

    def greet(j, _):
        to = lax.rem(me + j, count)
        pl.semaphore_signal(barrier, inc=1, device_id=(to // ny, lax.rem(to, ny)), device_id_type=MESH)
        return 0

    lax.fori_loop(1, count, greet, 0)

    def pg_load(u):
        return pltpu.make_async_copy(pg.at[u], pgb.at[lax.rem(u, 2)], pgl.at[lax.rem(u, 2)])

    def w_load(u):
        return pltpu.make_async_copy(wall.at[u], wb.at[lax.rem(u, 2)], wl.at[lax.rem(u, 2)])

    r_load = pltpu.make_async_copy(rcat, rbuf, lds.at[0])
    r_load.start()
    pg_load(0).start()
    w_load(0).start()
    nrm_load = pltpu.make_async_copy(nrmi, nrm, lds.at[1])
    rest_load = pltpu.make_async_copy(resti, rest, lds.at[2])
    nrm_load.start()
    rest_load.start()

    def rows_of(chip, part, n=half):
        return pl.ds(pl.multiple_of((chip // 2) * block + part * half, 16), n)

    def d_copy(u, i):
        return remote(
            sb.at[u, rows_of(diag, i)], rd.at[u, i * half:(i + 1) * half], dsn.at[u, i], drc.at[u, i], ((yn, xn)[i], gy)
        )

    def x_copy(u, i):
        return remote(sb.at[u, rows_of(xn, i)], rx.at[u, i * half:(i + 1) * half], xsn.at[u, i], xrc.at[u, i], (xn, gy))

    def y_copy(u, i):
        return remote(sb.at[u, rows_of(yn, i)], ry.at[u, i * half:(i + 1) * half], ysn.at[u, i], yrc.at[u, i], (yn, gy))

    def z_copy(u, j):
        to = lax.rem(gy + j, ny)
        src = zb.at[u, pl.ds(pl.multiple_of(to * rows, 16), rows)]
        return remote(src, rz.at[u, j - 1], zsn.at[u, j - 1], zrc.at[u, j - 1], (gx, to))

    r_load.wait()
    rt[...] = rbuf[...].T
    sg[...] = jnp.zeros_like(sg)
    pl.semaphore_wait(barrier, count - 1)

    def weigh(u):
        slot = lax.rem(u, 2)
        pg_load(u).wait()

        @pl.when(u + 1 < units)
        def _():
            pg_load(u + 1).start()

        sb[u] = jnp.dot(rt[...], pgb[slot], preferred_element_type=F32).astype(BF16)
        for i in (0, 1):
            d_copy(u, i).start()
        x_copy(u, 1).start()
        y_copy(u, 0).start()
        w_load(u).wait()

        @pl.when(u + 1 < units)
        def _():
            w_load(u + 1).start()

        mine = pgb[slot, 0:tokens, :]
        sg[...] += lax.dot_general(mine, wb[slot], (((1,), (1,)), ((), ())), preferred_element_type=F32)
        sg[:, lanes_of(u)] += pgb[slot, 0:tokens, LANES:2 * LANES].astype(F32) * vecs[2:3, lanes_of(u)]

    def fold(into, at, more):
        into[at] = (into[at].astype(F32) + more.astype(F32)).astype(BF16)

    def meet(u):
        for i in (0, 1):
            d_copy(u, i).wait_recv()
        own = sb.at[u]
        fold(own, (rows_of(xn, 0), slice(None)), rd[u, 0:half])
        x_copy(u, 0).start()
        fold(own, (rows_of(yn, 1), slice(None)), rd[u, half:block])
        y_copy(u, 1).start()

    def column(u):
        for i in (0, 1):
            x_copy(u, i).wait_recv()
            y_copy(u, i).wait_recv()
        total = sb[u, rows_of(gx, 0, block), :].astype(F32) + rx[u].astype(F32) + ry[u].astype(F32)
        zb[u] = total.astype(BF16)
        for j in range(1, ny):
            z_copy(u, j).start()

    def settle(u):
        r = pl.ds(pl.multiple_of(gy * rows, 16), rows)
        at = pl.ds(pl.multiple_of((gx // 2) * block + gy * rows, 16), rows)
        total = sb[u, at, :].astype(F32) + rx[u, r, :].astype(F32) + ry[u, r, :].astype(F32)
        for j in range(1, ny):
            z_copy(u, j).wait_recv()
        for j in range(1, ny):
            total = total + rz[u, j - 1].astype(F32)
        for i in range(3):
            wgo[:, lanes_of(u + i * units)] = total[:, i * LANES:(i + 1) * LANES]

    BAND = 32
    bands = tokens // BAND

    def finish(i, _):
        r = pl.ds(pl.multiple_of(i * BAND, BAND), BAND)
        s, z = sg[r, :], nrm[r, :]
        sz = s * z
        gain = vecs[0:1, :]
        vtot_rows[0][...] += jnp.sum(sz.reshape(BAND // 8, 8, width), axis=0)
        vtot_rows[1][...] += jnp.sum(s.reshape(BAND // 8, 8, width), axis=0)
        n = s * gain
        m1 = jnp.mean(n, axis=1, keepdims=True)
        m2 = jnp.mean(sz * gain, axis=1, keepdims=True)
        sg[r, :] = rest[r, :] + inv[r, 0:1] * (n - m1 - z * m2)
        return 0

    vtot_rows = (outb.at[0, 0:8, :], outb.at[0, 8:16, :])

    def v_copy(j):
        to = lax.rem(me + j, count)
        return remote(vtot.at[to // 2], vin.at[me], vsn.at[to], vrc.at[me], (to // ny, lax.rem(to, ny)))

    def v_recv(j):
        at = lax.rem(me + j, count)
        return remote(vtot.at[0], vin.at[at], vsn.at[at], vrc.at[at], (at // ny, lax.rem(at, ny)))

    def vectors_out():
        zero = jnp.zeros((2, LANES), F32)
        for c in range(width // LANES):
            at = slice(c * LANES, (c + 1) * LANES)
            top = [jnp.sum(v[:, at], axis=0, keepdims=True) for v in vtot_rows]
            vtot[c] = jnp.concatenate(top + [vsum[2:6, at], zero], 0)
        lax.fori_loop(1, count, lambda j, _: (v_copy(j).start(), 0)[1], 0)

    chunk = outb.shape[2] // 4

    def out_copy(c):
        return pltpu.make_async_copy(rest.at[:, pl.ds(c * chunk, chunk)], igo.at[:, pl.ds(c * chunk, chunk)], ous.at[c])

    def natural():
        perm[...] = run_matrix(tokens, True)
        for c in range(4):
            at = slice(c * chunk, (c + 1) * chunk)
            v = sg[:, at]
            high = v.astype(BF16)
            low = (v - high.astype(F32)).astype(BF16)
            rest[:, at] = jnp.dot(perm[...], high, preferred_element_type=F32) + jnp.dot(
                perm[...], low, preferred_element_type=F32
            )
            out_copy(c).start()

    LAG1, LAG2, LAG3 = 2, 4, 6

    def tick(k, _):
        pl.when(k < units)(lambda: weigh(k))
        pl.when((k >= LAG1) & (k < units + LAG1))(lambda: meet(k - LAG1))
        pl.when((k >= LAG2) & (k < units + LAG2))(lambda: column(k - LAG2))
        pl.when(k >= LAG3)(lambda: settle(k - LAG3))

        @pl.when(k == units)
        def _():
            nrm_load.wait()
            rest_load.wait()
            for v in vtot_rows:
                v[...] = jnp.zeros_like(v)
            lax.fori_loop(0, bands // 2, finish, 0)

        @pl.when(k == units + 1)
        def _():
            lax.fori_loop(bands // 2, bands, finish, 0)
            vectors_out()

        pl.when(k == units + 2)(natural)
        return 0

    lax.fori_loop(0, units + LAG3, tick, 0)

    lax.fori_loop(1, count, lambda j, _: (v_recv(j).wait_recv(), 0)[1], 0)
    vin[me] = vtot[me // 2]
    vgo[...] = lax.fori_loop(0, count, lambda j, s: s + vin[j], jnp.zeros((8, LANES), F32))

    def drain(u, _):
        for i in (0, 1):
            d_copy(u, i).wait_send()
            x_copy(u, i).wait_send()
            y_copy(u, i).wait_send()
        for j in range(1, ny):
            z_copy(u, j).wait_send()
        return 0

    lax.fori_loop(0, units, drain, 0)
    lax.fori_loop(1, count, lambda j, _: (v_copy(j).wait_send(), 0)[1], 0)
    for c in range(4):
        out_copy(c).wait()


def back(nx, ny, pg, rcat, wall, nrm, inv, rest, vecs, vsum):
    units, both, cols = pg.shape
    tokens, width = nrm.shape
    block = width // nx
    rows = block // ny
    dma = pltpu.SemaphoreType.DMA
    any_, vmem = pl.BlockSpec(memory_space=pl.ANY), pl.BlockSpec(memory_space=pltpu.VMEM)
    s = jax.ShapeDtypeStruct
    return pl.pallas_call(
        functools.partial(back_kernel, nx, ny, units),
        name="back",
        out_shape=(s((tokens, width), F32), s((rows, 3 * width), F32), s((8, LANES), F32)),
        in_specs=[any_, any_, any_, any_, vmem, any_, vmem, vmem],
        out_specs=(any_, vmem, vmem),
        scratch_shapes=[
            pltpu.VMEM((width // 2, both), BF16),
            pltpu.VMEM((both, width // 2), BF16),
            pltpu.VMEM((2, both, cols), BF16),
            pltpu.VMEM((2, width, cols), BF16),
            pltpu.VMEM((units, width // 2, cols), BF16),
            pltpu.VMEM((units, block, cols), BF16),
            pltpu.VMEM((units, block, cols), BF16),
            pltpu.VMEM((units, block, cols), BF16),
            pltpu.VMEM((units, ny - 1, rows, cols), BF16),
            pltpu.VMEM((units, block, cols), BF16),
            pltpu.VMEM((tokens, width), F32),
            pltpu.VMEM((tokens, width), F32),
            pltpu.VMEM((tokens, width), F32),
            pltpu.VMEM((width // LANES, 8, LANES), F32),
            pltpu.VMEM((nx * ny, 8, LANES), F32),
            pltpu.VMEM((tokens, tokens), BF16),
            pltpu.VMEM((1, 16, width), F32),
            dma((3,)), dma((2,)), dma((2,)),
            dma((units, 2)), dma((units, 2)), dma((units, 2)), dma((units, 2)), dma((units, 2)), dma((units, 2)),
            dma((units, ny - 1)), dma((units, ny - 1)), dma((nx * ny,)), dma((nx * ny,)), dma((4,)),
        ],
        compiler_params=pltpu.CompilerParams(
            collective_id=1, has_side_effects=True, vmem_limit_bytes=61 * 2**20
        ),
        cost_estimate=pl.CostEstimate(
            flops=4 * tokens * width * units * cols, bytes_accessed=2 * width * units * cols, transcendentals=0
        ),
    )(pg, rcat, wall, nrm, inv, rest, vecs, vsum)


def fast(nx, ny, tokens, reset_mask, weight, vectors, cotangent):
    count, width = tokens.shape
    rows = weight.shape[0]
    units, steps = width // LANES, count // RUNS
    keep = (1 - reset_mask).astype(F32).reshape(RUNS, steps).T.reshape(count, 1)
    keep = jnp.broadcast_to(keep, (count, LANES))
    wsrc = weight.reshape(rows, 3, units, LANES).transpose(2, 0, 1, 3).reshape(units, rows, 3 * LANES)
    odd = lax.rem(lax.axis_index("gx") * ny + lax.axis_index("gy"), 2) == 1
    low, high = (jnp.pad(vectors, ((0, 10), side)) for side in ((0, rows), (rows, 0)))
    vsrc = jnp.where(odd, high, low)
    wall, pg, rcat, outp, grest, nrm, inv, vecs, vsum = front(nx, ny, tokens, cotangent, keep, wsrc, vsrc)
    grad, weight_grad, tile = back(nx, ny, pg, rcat, wall, nrm, inv, grest, vecs, vsum)
    vector_grad = jnp.where(odd, tile[:6, rows:2 * rows], tile[:6, :rows])
    return outp, grad, weight_grad, vector_grad


def solution(mesh):
    placed = (
        P(("gx", "gy"), None),
        P(("gx", "gy")),
        P(("gx", "gy"), None),
        P(None, ("gx", "gy")),
        P(("gx", "gy"), None),
    )
    nx, ny = mesh.shape["gx"], mesh.shape["gy"]

    def body(tokens, reset_mask, weight, vectors, cotangent):
        whole_tiles = weight.shape[0] % 16 == 0 and tokens.shape[0] % 256 == 0
        if nx == 8 and whole_tiles and 2 * weight.shape[0] == LANES and tokens.shape[1] % 2048 == 0:
            return fast(nx, ny, tokens, reset_mask, weight, vectors, cotangent)
        return local(tokens, reset_mask, weight, vectors, cotangent)

    return jax.shard_map(
        body,
        mesh=mesh,
        in_specs=placed,
        out_specs=(
            P(("gx", "gy"), None),
            P(("gx", "gy"), None),
            P(("gx", "gy"), None),
            P(None, ("gx", "gy")),
        ),
        check_vma=False,
    )
```

```python
import functools

import jax
import jax.numpy as jnp
from jax import lax
from jax.experimental import pallas as pl
from jax.experimental.pallas import tpu as pltpu
from jax.sharding import PartitionSpec as P

MESH = pl.DeviceIdType.MESH
F32, BF16 = jnp.float32, jnp.bfloat16
LANES, RUNS, GROUP = 128, 8, 2
EPS = 1e-05


def place(ny):
    gx, gy = lax.axis_index("gx"), lax.axis_index("gy")
    core, xx, yy = lax.rem(gx, 2), lax.rem(gx // 2, 2), gx // 4
    return gx, gy, core, gx + 1 - 2 * core, gx + 2 - 4 * xx, gx + 4 - 8 * yy


def remote(src, dst, send, recv, to):
    return pltpu.make_async_remote_copy(
        src_ref=src, dst_ref=dst, send_sem=send, recv_sem=recv, device_id=to, device_id_type=MESH
    )


def lanes_of(b):
    return pl.ds(pl.multiple_of(b * LANES, LANES), LANES)


def run_matrix(tokens, back):
    steps = tokens // RUNS
    row = lax.broadcasted_iota(jnp.int32, (tokens, tokens), 0)
    col = lax.broadcasted_iota(jnp.int32, (tokens, tokens), 1)
    if back:
        hit = row == (col & (RUNS - 1)) * steps + (col >> 3)
    else:
        hit = col == (row & (RUNS - 1)) * steps + (row >> 3)
    return jnp.where(hit, 1.0, 0.0).astype(BF16)


def entering(value, axis, join, neutral, backward):
    count, mine = (lax.axis_size(axis), lax.axis_index(axis))
    pieces = jax.tree.map(lambda part: lax.all_gather(part, axis), value)
    if backward:
        pieces = jax.tree.map(lambda part: part[::-1], pieces)
        mine = count - 1 - mine
    subtotal = jax.tree.map(
        lambda part, zero: jnp.full_like(part, 0) + jnp.asarray(zero, part.dtype), value, neutral
    )

    def lap(position, subtotal):
        longer = join(subtotal, jax.tree.map(lambda part: part[position], pieces))
        return jax.tree.map(lambda new, old: jnp.where(position < mine, new, old), longer, subtotal)

    return lax.fori_loop(0, count - 1, lap, subtotal)


def from_behind(block, axis, distance):
    devices = range(lax.axis_size(axis))
    route = [(i - distance, i) for i in devices if i - distance in devices]
    return lax.ppermute(block, axis, route)


def compose(earlier, later):
    return (earlier[0] * later[0], later[0] * earlier[1] + later[1])


def local(tokens, reset_mask, weight, vectors, cotangent):
    width = weight.shape[1] // 3
    whole_weight, whole_vectors = (
        lax.all_gather(weight, ("gx", "gy"), axis=0, tiled=True),
        lax.all_gather(vectors, ("gx", "gy"), axis=1, tiled=True),
    )
    params = whole_vectors.astype(jnp.float32)
    gain = params[0]
    shift_bias = params[1]
    forget_peep = params[2]
    forget_bias = params[3]
    reset_peep = params[4]
    reset_bias = params[5]
    inputs = tokens.astype(jnp.float32)
    keep = (1 - reset_mask).astype(jnp.float32)[:, None]
    centred = inputs - jnp.mean(inputs, axis=1, keepdims=True)
    inv_std = lax.rsqrt(jnp.mean(centred * centred, axis=1, keepdims=True) + 1e-05)
    normed = centred * inv_std
    scaled = normed * gain + shift_bias
    rounded = scaled.astype(jnp.bfloat16)
    projected = jnp.dot(rounded, whole_weight, preferred_element_type=jnp.float32)
    candidate = projected[:, :width]
    forget_pre = projected[:, width : 2 * width]
    reset_pre = projected[:, 2 * width :]
    forget = jax.nn.sigmoid(forget_pre + forget_peep * scaled + forget_bias)
    decay = forget * keep
    inflow = (1.0 - forget) * candidate
    cum_decay, cum_state = lax.associative_scan(compose, (decay, inflow), axis=0)
    unit = (jnp.ones_like(cum_decay[-1]), jnp.zeros_like(cum_state[-1]))
    before = entering((cum_decay[-1], cum_state[-1]), ("gx", "gy"), compose, unit, False)
    state_in = before[1]
    state = cum_decay * state_in + cum_state
    previous = keep * jnp.concatenate([state_in[None], state[:-1]], 0)
    reset = jax.nn.sigmoid(reset_pre + reset_peep * previous + reset_bias)
    output = reset * state + (1.0 - reset) * inputs
    upstream = cotangent.astype(jnp.float32)
    reset_grad = upstream * (state - inputs) * reset * (1.0 - reset)
    through = keep * reset_peep * reset_grad
    next_decay, next_through = from_behind((decay[0], through[0]), ("gx", "gy"), -1)
    ahead = jnp.concatenate([decay[1:], next_decay[None]], 0)
    local_term = upstream * reset + jnp.concatenate([through[1:], next_through[None]], 0)
    flip_mult, flip_sum = lax.associative_scan(compose, (ahead[::-1], local_term[::-1]), axis=0)
    mult_back = flip_mult[::-1]
    sum_back = flip_sum[::-1]
    after = entering((mult_back[0], sum_back[0]), ("gx", "gy"), compose, unit, True)
    state_grad = mult_back * after[1] + sum_back
    candidate_grad = state_grad * (1.0 - forget)
    forget_grad = state_grad * (previous - candidate) * forget * (1.0 - forget)
    proj_grad = jnp.concatenate([candidate_grad, forget_grad, reset_grad], 1).astype(jnp.bfloat16)
    weight_grad = lax.psum_scatter(
        lax.dot_general(
            rounded, proj_grad, (((0,), (0,)), ((), ())), preferred_element_type=jnp.float32
        ),
        ("gx", "gy"),
        scatter_dimension=0,
        tiled=True,
    )
    scaled_grad = lax.dot_general(
        proj_grad,
        lax.all_gather(weight, ("gx", "gy"), axis=0, tiled=True),
        (((1,), (1,)), ((), ())),
        preferred_element_type=jnp.float32,
    )
    scaled_grad = scaled_grad + forget_grad * forget_peep
    vector_terms = jnp.stack(
        [
            jnp.sum(scaled_grad * normed, axis=0),
            jnp.sum(scaled_grad, axis=0),
            jnp.sum(forget_grad * scaled, axis=0),
            jnp.sum(forget_grad, axis=0),
            jnp.sum(reset_grad * previous, axis=0),
            jnp.sum(reset_grad, axis=0),
        ],
        0,
    )
    vector_grad = lax.psum_scatter(vector_terms, ("gx", "gy"), scatter_dimension=1, tiled=True)
    normed_grad = scaled_grad * gain
    input_grad = upstream * (1.0 - reset) + inv_std * (
        normed_grad
        - jnp.mean(normed_grad, axis=1, keepdims=True)
        - normed * jnp.mean(normed_grad * normed, axis=1, keepdims=True)
    )
    return (output.astype(jnp.bfloat16), input_grad, weight_grad, vector_grad)


SLOTS, SEND, PAIR, ZSEND = 8, 8, 4, 4
TOTALS, FORE, GRADS, BACK, WEIGH = 3, 5, 6, 8, 10
LAG1, LAG2, LAG3 = 2, 4, 6
AHEAD_Z, AHEAD_B = 5, 3
BAND = 32


def layer_kernel(
    nx, ny, units,
    tok, cot, keep, wsrc, vsrc,
    wall, pgm, outp, igo, wgo, vgo,
    vbuf, vecs, xs, gs, means, invs, rnd, rt, rtm, wf, pj, pv, grs, outs, stage, perm, pgs,
    wb, sb, rd, rx, ry, rz, zb, sg, vsum, vrows, vtot, vin,
    ach, bch, qch, sin, cin, m1a, m1b, m2a, m2b,
    zs, zr, os, bs, br, dsn, dr, cs, cr, ws,
    vzs, vzr, vxs, vxr, vo, sts, rs, rr, ps, pr, pl_, wl, gos,
    e1as, e1ar, e1bs, e1br, e2as, e2ar, e2bs, e2br,
    fds, fdr, fxs, fxr, fys, fyr, fzs, fzr, vsn, vrc, ous,
):
    gx, gy, core, mate, xn, yn = place(ny)
    tokens, width = xs.shape
    rows = wsrc.shape[1]
    block = rows * ny
    half = block // 2
    groups = units // GROUP
    glanes = GROUP * LANES
    diag = xn + yn - gx
    first = gx * block
    mine = first + gy * rows
    count = nx * ny
    me = gx * ny + gy

    def peer_y(j):
        return lax.rem(gy + j, ny)

    def peer_x(j):
        return lax.rem(gx + j, nx)

    def each(n, run, start=0):
        lax.fori_loop(start, n, lambda i, _: (run(i), 0)[1], 0)

    barrier = pltpu.get_barrier_semaphore()

    def greet(j):
        to = lax.rem(me + j, count)
        pl.semaphore_signal(barrier, inc=1, device_id=(to // ny, lax.rem(to, ny)), device_id_type=MESH)

    each(count, greet, 1)

    def band(b, n=block):
        return pl.ds(pl.multiple_of(b, 16), n)

    chunks = width // glanes

    def stage_copy(i):
        src = tok if i < chunks else cot
        c = i % chunks
        return pltpu.make_async_copy(src.at[:, pl.ds(c * glanes, glanes)], stage.at[i % 2], sts.at[i % 2])

    stage_copy(0).start()
    stage_copy(1).start()

    def vz(j):
        return remote(vsrc, vbuf.at[me], vzs.at[j - 1], vzr.at[j - 1], (gx, peer_y(j)))

    def vx(j):
        part = vbuf.at[pl.ds(gx * ny, ny)]
        return remote(part, part, vxs.at[j - 1], vxr.at[j - 1], (peer_x(j), gy))

    own_vec = pltpu.make_async_copy(vsrc, vbuf.at[me], vo)

    def z_copy(u, j):
        return remote(wsrc.at[u], wall.at[u, band(mine, rows)], zs.at[u, j - 1], zr.at[u, j - 1], (gx, peer_y(j)))

    def own_copy(u):
        return pltpu.make_async_copy(wsrc.at[u], wall.at[u, band(mine, rows)], os.at[u])

    def band_copy(u, i):
        to = (mate, xn, yn)[i]
        recv = cr.at[u, 0] if i == 0 else br.at[u, i - 1]
        part = wall.at[u, band(first)]
        return remote(part, part, bs.at[u, i], recv, (to, gy))

    def diag_copy(u, i):
        part = wall.at[u, band((xn * block, yn * block + half)[i], half)]
        return remote(part, part, dsn.at[u, i], dr.at[u, i], ((yn, xn)[i], gy))

    def core_copy(u, i):
        part = wall.at[u, band((None, xn, yn, diag)[i] * block)]
        return remote(part, part, cs.at[u, i - 1], cr.at[u, i], (mate, gy))

    def z_start(u):
        own_copy(u).start()
        for j in range(1, ny):
            z_copy(u, j).start()

    def z_wait(u):
        own_copy(u).wait()
        for j in range(1, ny):
            z_copy(u, j).wait_recv()
        for i in (1, 2, 0):
            band_copy(u, i).start()

    def xy_wait(u):
        for i in (1, 2):
            band_copy(u, i).wait_recv()
        for i in (0, 1):
            diag_copy(u, i).start()
        for i in (1, 2):
            core_copy(u, i).start()

    def diag_wait(u):
        for i in (0, 1):
            diag_copy(u, i).wait_recv()
        core_copy(u, 3).start()

    def core_wait(u):
        band_copy(u, 0).wait_recv()
        for i in (1, 2, 3):
            core_copy(u, i).wait_recv()

    pl.semaphore_wait(barrier, count - 1)
    own_vec.start()
    for j in range(1, ny):
        vz(j).start()
    for u in range(AHEAD_Z):
        z_start(u)

    perm[...] = run_matrix(tokens, False)

    def to_runs(i, into):
        stage_copy(i).wait()
        c = i % chunks
        into[:, c * glanes:(c + 1) * glanes] = jnp.dot(
            perm[...], stage[i % 2], preferred_element_type=F32
        ).astype(BF16)
        if i + 2 < 2 * chunks:
            stage_copy(i + 2).start()

    for i in range(chunks):
        to_runs(i, xs)
    z_wait(0)
    own_vec.wait()
    for j in range(1, ny):
        vz(j).wait_recv()
    for j in range(1, nx):
        vx(j).start()
    z_wait(1)

    def moments(i):
        r = pl.ds(pl.multiple_of(i * BAND, BAND), BAND)
        x = xs[r, :].astype(F32)
        mean = jnp.mean(x, axis=1, keepdims=True)
        centred = x - mean
        inv = lax.rsqrt(jnp.mean(centred * centred, axis=1, keepdims=True) + EPS)
        means[r, :] = jnp.broadcast_to(mean, (BAND, LANES))
        invs[r, :] = jnp.broadcast_to(inv, (BAND, LANES))

    each(tokens // BAND, moments)
    for u in range(2, AHEAD_B):
        z_wait(u)
    for j in range(1, nx):
        vx(j).wait_recv()
    for c in range(width // LANES):
        part = vbuf[2 * c].astype(F32) + vbuf[2 * c + 1].astype(F32)
        vecs[:, c * LANES:(c + 1) * LANES] = part[0:8, :]

    def rounding(i):
        r = pl.ds(pl.multiple_of(i * BAND, BAND), BAND)
        normed = (xs[r, :].astype(F32) - means[r, 0:1]) * invs[r, 0:1]
        rnd[r, :] = (normed * vecs[0:1, :] + vecs[1:2, :]).astype(BF16)

    each(tokens // BAND, rounding)

    quads = nx // 2

    def turn(i):
        at = pl.ds(pl.multiple_of(i * block, 16), block)
        rt[at, 0:tokens] = rnd[:, pl.ds(pl.multiple_of((2 * i + core) * block, LANES), block)].T
        rtm[at, :] = rnd[:, pl.ds(pl.multiple_of((2 * i + 1 - core) * block, LANES), block)].T

    r_mate = remote(rtm, rt.at[:, tokens:2 * tokens], rs, rr, (mate, gy))

    def late_start():
        each(quads, turn)
        r_mate.start()
        for i in range(chunks, 2 * chunks):
            to_runs(i, gs)
        perm[...] = run_matrix(tokens, True)

    def e_copies(buf, send, recv, q, level):
        if level == 0:
            return [
                remote(buf.at[q, gy], buf.at[q, gy], send.at[q, j - 1], recv.at[q, j - 1], (gx, peer_y(j)))
                for j in range(1, ny)
            ]
        return [
            remote(buf.at[q, gx], buf.at[q, gx], send.at[q, j - 1], recv.at[q, j - 1], (peer_x(j), gy))
            for j in range(1, nx)
        ]

    def e_start(*a):
        for c in e_copies(*a):
            c.start()

    def e_wait(*a):
        for c in e_copies(*a):
            c.wait_recv()

    double = tokens // (2 * RUNS)

    def front_load(u):
        return pltpu.make_async_copy(wall.at[u], wf, ws)

    def project(u):
        front_load(u).wait()
        pj[lax.rem(u, SLOTS)] = jnp.dot(rnd[...], wf[...], preferred_element_type=F32)

    def vec(i, u):
        return vecs[i:i + 1, lanes_of(u)]

    def scale(u, r, gain, shift):
        return (xs[r, lanes_of(u)].astype(F32) - means[r, :]) * invs[r, :] * gain + shift

    def gates(u):
        slot = lax.rem(u, SLOTS)
        gain, shift, vf, bf = (vec(i, u) for i in range(4))

        def step(i, carry):
            a, b = carry
            r = pl.ds(pl.multiple_of(i * 16, 16), 16)
            f = jax.nn.sigmoid(pj[slot, r, LANES:2 * LANES] + vf * scale(u, r, gain, shift) + bf)
            pj[slot, r, LANES:2 * LANES] = f
            d = f * keep[r, :]
            inflow = (1.0 - f) * pj[slot, r, 0:LANES]
            for h in (0, 8):
                a = a * d[h:h + 8]
                b = d[h:h + 8] * b + inflow[h:h + 8]
            return a, b

        a, b = lax.fori_loop(0, double, step, (jnp.ones((RUNS, LANES), F32), jnp.zeros((RUNS, LANES), F32)), unroll=4)
        q, j = u // GROUP, lax.rem(u, GROUP)
        ach[q, :, lanes_of(j)] = a
        bch[q, :, lanes_of(j)] = b

    def totals(q):
        a, b = jnp.ones((1, glanes), F32), jnp.zeros((1, glanes), F32)
        for s in range(RUNS):
            one = ach[q, s:s + 1, :]
            a = a * one
            b = one * b + bch[q, s:s + 1, :]
        m1a[q, gy, 0:1, :] = a
        m1a[q, gy, 1:2, :] = b
        e_start(m1a, e1as, e1ar, q, 0)

    def totals_x(q):
        e_wait(m1a, e1as, e1ar, q, 0)
        a, b = jnp.ones((1, glanes), F32), jnp.zeros((1, glanes), F32)
        for s in range(ny):
            one = m1a[q, s, 0:1, :]
            a = a * one
            b = one * b + m1a[q, s, 1:2, :]
        m1b[q, gx, 0:1, :] = a
        m1b[q, gx, 1:2, :] = b
        e_start(m1b, e1bs, e1br, q, 1)

    def enter(q):
        e_wait(m1b, e1bs, e1br, q, 1)
        s = jnp.zeros((1, glanes), F32)
        s = lax.fori_loop(0, gx, lambda i, s: m1b[q, i, 0:1, :] * s + m1b[q, i, 1:2, :], s)
        s = lax.fori_loop(0, gy, lambda i, s: m1a[q, i, 0:1, :] * s + m1a[q, i, 1:2, :], s)
        for r in range(RUNS):
            sin[q, r:r + 1, :] = s
            s = ach[q, r:r + 1, :] * s + bch[q, r:r + 1, :]

    def forward(u):
        slot = lax.rem(u, SLOTS)
        q, j = u // GROUP, lax.rem(u, GROUP)
        vr, br_ = vec(4, u), vec(5, u)
        zero = jnp.zeros((RUNS, LANES), F32)

        def step(i, carry):
            s, run, t, v4, v5 = carry
            r = pl.ds(pl.multiple_of(i * 16, 16), 16)
            f = pj[slot, r, LANES:2 * LANES]
            k = keep[r, :]
            inflow = (1.0 - f) * pj[slot, r, 0:LANES]
            prevs, states = [], []
            for h in (0, 8):
                prev = k[h:h + 8] * s
                s = f[h:h + 8] * prev + inflow[h:h + 8]
                prevs.append(prev)
                states.append(s)
            prev, state = jnp.concatenate(prevs, 0), jnp.concatenate(states, 0)
            x = xs[r, lanes_of(u)].astype(F32)
            up = gs[r, lanes_of(u)].astype(F32)
            reset = jax.nn.sigmoid(pj[slot, r, 2 * LANES:3 * LANES] + vr * prev + br_)
            rest = 1.0 - reset
            outs[r, lanes_of(j)] = (reset * state + rest * x).astype(BF16)
            rg = up * (state - x) * reset * rest
            pj[slot, r, 2 * LANES:3 * LANES] = rg
            pv[slot, r, :] = prev
            grs[r, lanes_of(u)] = up * rest
            local = up * reset
            d, through = f * k, k * vr * rg
            for h in (0, 8):
                t = t + run * through[h:h + 8]
                run = run * d[h:h + 8]
                t = t + run * local[h:h + 8]
                v4 = v4 + rg[h:h + 8] * prev[h:h + 8]
                v5 = v5 + rg[h:h + 8]
            return s, run, t, v4, v5

        init = (sin[q, :, lanes_of(j)], jnp.ones((RUNS, LANES), F32), zero, zero, zero)
        _, _, t, v4, v5 = lax.fori_loop(0, double, step, init, unroll=4)
        qch[q, :, lanes_of(j)] = t
        vsum[4:5, lanes_of(u)] = jnp.sum(v4, axis=0, keepdims=True)
        vsum[5:6, lanes_of(u)] = jnp.sum(v5, axis=0, keepdims=True)

    def out_copy(q):
        c = pl.ds(pl.multiple_of(q * glanes, LANES), glanes)
        return pltpu.make_async_copy(stage.at[lax.rem(q, 2)], outp.at[:, c], gos.at[q])

    def forward_group(q):
        enter(q)
        pl.when(q >= 2)(lambda: out_copy(q - 2).wait())
        each(GROUP, lambda j: forward(q * GROUP + j))
        s = jnp.zeros((1, glanes), F32)
        for r in reversed(range(RUNS)):
            s = ach[q, r:r + 1, :] * s + qch[q, r:r + 1, :]
        m2a[q, gy, 0:1, :] = s
        e_start(m2a, e2as, e2ar, q, 0)
        stage[lax.rem(q, 2)] = jnp.dot(perm[...], outs[...], preferred_element_type=F32).astype(BF16)
        out_copy(q).start()

    def grads_x(q):
        e_wait(m2a, e2as, e2ar, q, 0)
        s = jnp.zeros((1, glanes), F32)
        for r in reversed(range(ny)):
            s = m1a[q, r, 0:1, :] * s + m2a[q, r, 0:1, :]
        m2b[q, gx, 0:1, :] = s
        e_start(m2b, e2bs, e2br, q, 1)

    def enter_back(q):
        e_wait(m2b, e2bs, e2br, q, 1)
        s = jnp.zeros((1, glanes), F32)

        def over_x(i, s):
            return m1b[q, nx - 1 - i, 0:1, :] * s + m2b[q, nx - 1 - i, 0:1, :]

        def over_y(i, s):
            return m1a[q, ny - 1 - i, 0:1, :] * s + m2a[q, ny - 1 - i, 0:1, :]

        s = lax.fori_loop(0, nx - 1 - gx, over_x, s)
        s = lax.fori_loop(0, ny - 1 - gy, over_y, s)
        for r in reversed(range(RUNS)):
            cin[q, r:r + 1, :] = s
            s = ach[q, r:r + 1, :] * s + qch[q, r:r + 1, :]

    def pg_mate(u):
        return remote(pgs.at[lax.rem(u, PAIR), 0:tokens], pgm.at[u], ps.at[u], pr.at[u], (mate, gy))

    def backward(u):
        slot, pair = lax.rem(u, SLOTS), lax.rem(u, PAIR)
        q, j = u // GROUP, lax.rem(u, GROUP)
        gain, shift, vr = vec(0, u), vec(1, u), vec(4, u)
        zero = jnp.zeros((RUNS, LANES), F32)

        def step(i, carry):
            c, v2, v3 = carry
            r = pl.ds(pl.multiple_of((double - 1 - i) * 16, 16), 16)
            f = pj[slot, r, LANES:2 * LANES]
            k = keep[r, :]
            rg = pj[slot, r, 2 * LANES:3 * LANES]
            local = gs[r, lanes_of(u)].astype(F32) - grs[r, lanes_of(u)]
            d, through = f * k, k * vr * rg
            grads = [None, None]
            for h in (1, 0):
                part = slice(8 * h, 8 * h + 8)
                grads[h] = local[part] + c
                c = d[part] * grads[h] + through[part]
            grad = jnp.concatenate(grads, 0)
            cg = grad * (1.0 - f)
            fg = cg * (pv[slot, r, :] - pj[slot, r, 0:LANES]) * f
            pgs[pair, r, 0:LANES] = cg.astype(BF16)
            pgs[pair, r, LANES:2 * LANES] = fg.astype(BF16)
            pgs[pair, r, 2 * LANES:3 * LANES] = rg.astype(BF16)
            fs = fg * scale(u, r, gain, shift)
            return c, v2 + fs[0:8] + fs[8:16], v3 + fg[0:8] + fg[8:16]

        _, v2, v3 = lax.fori_loop(0, double, step, (cin[q, :, lanes_of(j)], zero, zero), unroll=4)
        vsum[2:3, lanes_of(u)] = jnp.sum(v2, axis=0, keepdims=True)
        vsum[3:4, lanes_of(u)] = jnp.sum(v3, axis=0, keepdims=True)
        pg_mate(u).start()

    def backward_group(q):
        enter_back(q)
        each(GROUP, lambda j: backward(q * GROUP + j))

    def pg_load(u):
        return pltpu.make_async_copy(pgm.at[u], pgs.at[lax.rem(u, PAIR), tokens:2 * tokens], pl_)

    def back_load(u):
        return pltpu.make_async_copy(wall.at[u], wb, wl)

    def rows_of(chip, part, n=half):
        return pl.ds(pl.multiple_of((chip // 2) * block + part * half, 16), n)

    def sent(u):
        return sb.at[lax.rem(u, SEND)]

    def d_copy(u, i):
        return remote(
            sent(u).at[rows_of(diag, i)], rd.at[u, i * half:(i + 1) * half], fds.at[u, i], fdr.at[u, i], ((yn, xn)[i], gy)
        )

    def x_copy(u, i):
        return remote(sent(u).at[rows_of(xn, i)], rx.at[u, i * half:(i + 1) * half], fxs.at[u, i], fxr.at[u, i], (xn, gy))

    def y_copy(u, i):
        return remote(sent(u).at[rows_of(yn, i)], ry.at[u, i * half:(i + 1) * half], fys.at[u, i], fyr.at[u, i], (yn, gy))

    def f_copy(u, j):
        to = lax.rem(gy + j, ny)
        src = zb.at[lax.rem(u, ZSEND), pl.ds(pl.multiple_of(to * rows, 16), rows)]
        return remote(src, rz.at[u, j - 1], fzs.at[u, j - 1], fzr.at[u, j - 1], (gx, to))

    def next_loads(u):
        pg_mate(u).wait_recv()
        pg_load(u).start()
        back_load(u).start()

    def weigh(u):
        slot, pair = lax.rem(u, SEND), lax.rem(u, PAIR)

        @pl.when(u >= SEND)
        def _():
            for i in (0, 1):
                d_copy(u - SEND, i).wait_send()
                x_copy(u - SEND, i).wait_send()
                y_copy(u - SEND, i).wait_send()

        pg_load(u).wait()
        sb[slot] = jnp.dot(rt[...], pgs[pair], preferred_element_type=F32).astype(BF16)
        for i in (0, 1):
            d_copy(u, i).start()
        x_copy(u, 1).start()
        y_copy(u, 0).start()

    def spread(u):
        pair = lax.rem(u, PAIR)
        back_load(u).wait()
        own = pgs[pair, 0:tokens, :]
        sg[...] += lax.dot_general(own, wb[...], (((1,), (1,)), ((), ())), preferred_element_type=F32)
        sg[:, lanes_of(u)] += pgs[pair, 0:tokens, LANES:2 * LANES].astype(F32) * vecs[2:3, lanes_of(u)]
        pg_mate(u).wait_send()

    def fold(slot, r, more):
        sb[slot, r, :] = (sb[slot, r, :].astype(F32) + more.astype(F32)).astype(BF16)

    def meet(u):
        slot = lax.rem(u, SEND)
        for i in (0, 1):
            d_copy(u, i).wait_recv()
        fold(slot, rows_of(xn, 0), rd[u, 0:half])
        x_copy(u, 0).start()
        fold(slot, rows_of(yn, 1), rd[u, half:block])
        y_copy(u, 1).start()

    def column(u):
        slot, zslot = lax.rem(u, SEND), lax.rem(u, ZSEND)

        @pl.when(u >= ZSEND)
        def _():
            for j in range(1, ny):
                f_copy(u - ZSEND, j).wait_send()

        for i in (0, 1):
            x_copy(u, i).wait_recv()
            y_copy(u, i).wait_recv()
        total = sb[slot, rows_of(gx, 0, block), :].astype(F32) + rx[u].astype(F32) + ry[u].astype(F32)
        zb[zslot] = total.astype(BF16)
        for j in range(1, ny):
            f_copy(u, j).start()

    def settle(u):
        slot = lax.rem(u, SEND)
        r = pl.ds(pl.multiple_of(gy * rows, 16), rows)
        at = pl.ds(pl.multiple_of((gx // 2) * block + gy * rows, 16), rows)
        total = sb[slot, at, :].astype(F32) + rx[u, r, :].astype(F32) + ry[u, r, :].astype(F32)
        for j in range(1, ny):
            f_copy(u, j).wait_recv()
        for j in range(1, ny):
            total = total + rz[u, j - 1].astype(F32)
        for i in range(3):
            wgo[:, lanes_of(u + i * units)] = total[:, i * LANES:(i + 1) * LANES]

    bands = tokens // BAND

    def finish(i):
        r = pl.ds(pl.multiple_of(i * BAND, BAND), BAND)
        s = sg[r, :]
        inv = invs[r, 0:1]
        z = (xs[r, :].astype(F32) - means[r, 0:1]) * inv
        sz = s * z
        gain = vecs[0:1, :]
        vrows[0:8, :] += jnp.sum(sz.reshape(BAND // 8, 8, width), axis=0)
        vrows[8:16, :] += jnp.sum(s.reshape(BAND // 8, 8, width), axis=0)
        n = s * gain
        m1 = jnp.mean(n, axis=1, keepdims=True)
        m2 = jnp.mean(sz * gain, axis=1, keepdims=True)
        sg[r, :] = grs[r, :] + inv * (n - m1 - z * m2)

    def v_copy(j):
        to = lax.rem(me + j, count)
        return remote(vtot.at[to // 2], vin.at[me], vsn.at[to], vrc.at[me], (to // ny, lax.rem(to, ny)))

    def v_recv(j):
        at = lax.rem(me + j, count)
        return remote(vtot.at[0], vin.at[at], vsn.at[at], vrc.at[at], (at // ny, lax.rem(at, ny)))

    def vectors_out():
        zero = jnp.zeros((2, LANES), F32)
        for c in range(width // LANES):
            at = slice(c * LANES, (c + 1) * LANES)
            top = [jnp.sum(vrows[8 * v:8 * v + 8, at], axis=0, keepdims=True) for v in (0, 1)]
            vtot[c] = jnp.concatenate(top + [vsum[2:6, at], zero], 0)
        each(count, lambda j: v_copy(j).start(), 1)

    quarter = width // 4

    def grad_copy(c):
        return pltpu.make_async_copy(grs.at[:, pl.ds(c * quarter, quarter)], igo.at[:, pl.ds(c * quarter, quarter)], ous.at[c])

    def natural():
        for c in range(4):
            at = slice(c * quarter, (c + 1) * quarter)
            v = sg[:, at]
            high = v.astype(BF16)
            low = (v - high.astype(F32)).astype(BF16)
            grs[:, at] = jnp.dot(perm[...], high, preferred_element_type=F32) + jnp.dot(
                perm[...], low, preferred_element_type=F32
            )
            grad_copy(c).start()

    def tick(k, _):
        u = k - 3
        v = u - WEIGH
        pl.when(k + AHEAD_Z < units)(lambda: z_start(k + AHEAD_Z))
        pl.when(k + AHEAD_B < units)(lambda: z_wait(k + AHEAD_B))
        pl.when(k < units)(lambda: xy_wait(k))
        pl.when((k >= 1) & (k <= units))(lambda: diag_wait(k - 1))
        pl.when(k == 0)(late_start)

        pl.when((v >= LAG1) & (v < units + LAG1))(lambda: meet(v - LAG1))
        pl.when((v >= LAG2) & (v < units + LAG2))(lambda: column(v - LAG2))
        pl.when(v >= LAG3)(lambda: settle(v - LAG3))

        @pl.when(v == 0)
        def _():
            r_mate.wait_recv()
            sg[...] = jnp.zeros_like(sg)
            vrows[...] = jnp.zeros_like(vrows)

        @pl.when((v >= 0) & (v < units))
        def _():
            weigh(v)
            spread(v)

        pl.when((v >= -1) & (v < units - 1))(lambda: next_loads(v + 1))

        def event(lag, run):
            g = (u - lag) // GROUP
            pl.when((u >= lag) & (lax.rem(u - lag + GROUP, GROUP) == 0) & (g < groups))(lambda: run(g))

        event(BACK, backward_group)
        event(GRADS, grads_x)
        event(FORE, forward_group)
        event(TOTALS, totals_x)

        @pl.when((u >= 0) & (u < units))
        def _():
            project(u)

        @pl.when((u >= -1) & (u < units - 1))
        def _():
            core_wait(u + 1)
            front_load(u + 1).start()

        @pl.when((u >= 0) & (u < units))
        def _():
            gates(u)
            pl.when(lax.rem(u, GROUP) == GROUP - 1)(lambda: totals(u // GROUP))

        pl.when(v == units)(lambda: each(bands // 2, finish))

        @pl.when(v == units + 1)
        def _():
            each(bands, finish, bands // 2)
            vectors_out()

        pl.when(v == units + 2)(natural)
        return 0

    lax.fori_loop(0, units + WEIGH + 3 + LAG3, tick, 0)

    each(count, lambda j: v_recv(j).wait_recv(), 1)
    vin[me] = vtot[me // 2]
    vgo[...] = lax.fori_loop(0, count, lambda j, s: s + vin[j], jnp.zeros((8, LANES), F32))

    def drain(u):
        for j in range(1, ny):
            z_copy(u, j).wait_send()
        for i in range(3):
            band_copy(u, i).wait_send()
        for i in (0, 1):
            diag_copy(u, i).wait_send()
        for i in (1, 2, 3):
            core_copy(u, i).wait_send()

    each(units, drain)

    def drain_send(u):
        for i in (0, 1):
            d_copy(u, i).wait_send()
            x_copy(u, i).wait_send()
            y_copy(u, i).wait_send()

    each(units, drain_send, units - SEND)

    def drain_z(u):
        for j in range(1, ny):
            f_copy(u, j).wait_send()

    each(units, drain_z, units - ZSEND)

    def drain_group(q):
        for a in ((m1a, e1as, e1ar, q, 0), (m1b, e1bs, e1br, q, 1), (m2a, e2as, e2ar, q, 0), (m2b, e2bs, e2br, q, 1)):
            for c in e_copies(*a):
                c.wait_send()

    each(groups, drain_group)
    for q in range(groups - 2, groups):
        out_copy(q).wait()
    for j in range(1, ny):
        vz(j).wait_send()
    for j in range(1, nx):
        vx(j).wait_send()
    r_mate.wait_send()
    each(count, lambda j: v_copy(j).wait_send(), 1)
    for c in range(4):
        grad_copy(c).wait()


def layer(nx, ny, tok, cot, keep, wsrc, vsrc):
    tokens, width = tok.shape
    units, rows, cols = wsrc.shape
    groups, glanes, block, count = units // GROUP, GROUP * LANES, rows * ny, nx * ny
    dma = pltpu.SemaphoreType.DMA
    any_, vmem = pl.BlockSpec(memory_space=pl.ANY), pl.BlockSpec(memory_space=pltpu.VMEM)
    msg = RUNS, glanes
    s, v = jax.ShapeDtypeStruct, pltpu.VMEM
    return pl.pallas_call(
        functools.partial(layer_kernel, nx, ny, units),
        name="layer",
        out_shape=(
            s((units, width, cols), BF16), s((units, tokens, cols), BF16),
            s((tokens, width), BF16), s((tokens, width), F32), s((rows, 3 * width), F32), s((8, LANES), F32),
        ),
        in_specs=[any_, any_, vmem, any_, any_],
        out_specs=(any_,) * 4 + (vmem,) * 2,
        scratch_shapes=[
            v((count, 16, LANES), BF16), v((8, width), F32),
            v((tokens, width), BF16), v((tokens, width), BF16), v((tokens, LANES), F32), v((tokens, LANES), F32),
            v((tokens, width), BF16), v((width // 2, 2 * tokens), BF16), v((width // 2, tokens), BF16),
            v((width, cols), BF16),
            v((SLOTS, tokens, cols), F32), v((SLOTS, tokens, LANES), F32),
            v((tokens, width), F32), v((tokens, glanes), BF16), v((2, tokens, glanes), BF16),
            v((tokens, tokens), BF16), v((PAIR, 2 * tokens, cols), BF16),
            v((width, cols), BF16), v((SEND, width // 2, cols), BF16),
            v((units, block, cols), BF16), v((units, block, cols), BF16), v((units, block, cols), BF16),
            v((units, ny - 1, rows, cols), BF16), v((ZSEND, block, cols), BF16),
            v((tokens, width), F32), v((8, width), F32), v((16, width), F32),
            v((width // LANES, 8, LANES), F32), v((count, 8, LANES), F32),
            *[v((groups,) + msg, F32)] * 5,
            v((groups, ny) + msg, F32), v((groups, nx) + msg, F32),
            v((groups, ny) + msg, F32), v((groups, nx) + msg, F32),
            dma((units, ny - 1)), dma((units, ny - 1)), dma((units,)), dma((units, 3)), dma((units, 2)),
            dma((units, 2)), dma((units, 2)), dma((units, 3)), dma((units, 4)), dma,
            dma((ny - 1,)), dma((ny - 1,)), dma((nx - 1,)), dma((nx - 1,)), dma, dma((2,)),
            dma, dma, dma((units,)), dma((units,)), dma, dma, dma((groups,)),
            dma((groups, ny - 1)), dma((groups, ny - 1)), dma((groups, nx - 1)), dma((groups, nx - 1)),
            dma((groups, ny - 1)), dma((groups, ny - 1)), dma((groups, nx - 1)), dma((groups, nx - 1)),
            *[dma((units, 2))] * 6, dma((units, ny - 1)), dma((units, ny - 1)),
            dma((count,)), dma((count,)), dma((4,)),
        ],
        compiler_params=pltpu.CompilerParams(
            collective_id=0, has_side_effects=True, vmem_limit_bytes=62 * 2**20
        ),
        cost_estimate=pl.CostEstimate(
            flops=6 * tokens * width * units * cols, bytes_accessed=4 * width * units * cols, transcendentals=0
        ),
    )(tok, cot, keep, wsrc, vsrc)


def fast(nx, ny, tokens, reset_mask, weight, vectors, cotangent):
    count, width = tokens.shape
    rows = weight.shape[0]
    units, steps = width // LANES, count // RUNS
    keep = (1 - reset_mask).astype(F32).reshape(RUNS, steps).T.reshape(count, 1)
    keep = jnp.broadcast_to(keep, (count, LANES))
    wsrc = weight.reshape(rows, 3, units, LANES).transpose(2, 0, 1, 3).reshape(units, rows, 3 * LANES)
    odd = lax.rem(lax.axis_index("gx") * ny + lax.axis_index("gy"), 2) == 1
    low, high = (jnp.pad(vectors, ((0, 10), side)) for side in ((0, rows), (rows, 0)))
    vsrc = jnp.where(odd, high, low)
    _, _, outp, grad, weight_grad, tile = layer(nx, ny, tokens, cotangent, keep, wsrc, vsrc)
    vector_grad = jnp.where(odd, tile[:6, rows:2 * rows], tile[:6, :rows])
    return outp, grad, weight_grad, vector_grad


def solution(mesh):
    placed = (
        P(("gx", "gy"), None),
        P(("gx", "gy")),
        P(("gx", "gy"), None),
        P(None, ("gx", "gy")),
        P(("gx", "gy"), None),
    )
    nx, ny = mesh.shape["gx"], mesh.shape["gy"]

    def body(tokens, reset_mask, weight, vectors, cotangent):
        whole_tiles = weight.shape[0] % 16 == 0 and tokens.shape[0] % 256 == 0
        if nx == 8 and whole_tiles and 2 * weight.shape[0] == LANES and tokens.shape[1] % 2048 == 0:
            return fast(nx, ny, tokens, reset_mask, weight, vectors, cotangent)
        return local(tokens, reset_mask, weight, vectors, cotangent)

    return jax.shard_map(
        body,
        mesh=mesh,
        in_specs=placed,
        out_specs=(
            P(("gx", "gy"), None),
            P(("gx", "gy"), None),
            P(("gx", "gy"), None),
            P(None, ("gx", "gy")),
        ),
        check_vma=False,
    )
```

```python
import functools

import jax
import jax.numpy as jnp
from jax import lax
from jax.experimental import pallas as pl
from jax.experimental.pallas import tpu as pltpu
from jax.sharding import PartitionSpec as P

MESH = pl.DeviceIdType.MESH
F32, BF16 = jnp.float32, jnp.bfloat16
LANES, RUNS, GROUP = 128, 8, 2
EPS = 1e-05


def place(ny):
    gx, gy = lax.axis_index("gx"), lax.axis_index("gy")
    core, xx, yy = lax.rem(gx, 2), lax.rem(gx // 2, 2), gx // 4
    return gx, gy, core, gx + 1 - 2 * core, gx + 2 - 4 * xx, gx + 4 - 8 * yy


def remote(src, dst, send, recv, to):
    return pltpu.make_async_remote_copy(
        src_ref=src, dst_ref=dst, send_sem=send, recv_sem=recv, device_id=to, device_id_type=MESH
    )


def lanes_of(b):
    return pl.ds(pl.multiple_of(b * LANES, LANES), LANES)


def run_matrix(tokens, back):
    steps = tokens // RUNS
    row = lax.broadcasted_iota(jnp.int32, (tokens, tokens), 0)
    col = lax.broadcasted_iota(jnp.int32, (tokens, tokens), 1)
    if back:
        hit = row == (col & (RUNS - 1)) * steps + (col >> 3)
    else:
        hit = col == (row & (RUNS - 1)) * steps + (row >> 3)
    return jnp.where(hit, 1.0, 0.0).astype(BF16)


def entering(value, axis, join, neutral, backward):
    count, mine = (lax.axis_size(axis), lax.axis_index(axis))
    pieces = jax.tree.map(lambda part: lax.all_gather(part, axis), value)
    if backward:
        pieces = jax.tree.map(lambda part: part[::-1], pieces)
        mine = count - 1 - mine
    subtotal = jax.tree.map(
        lambda part, zero: jnp.full_like(part, 0) + jnp.asarray(zero, part.dtype), value, neutral
    )

    def lap(position, subtotal):
        longer = join(subtotal, jax.tree.map(lambda part: part[position], pieces))
        return jax.tree.map(lambda new, old: jnp.where(position < mine, new, old), longer, subtotal)

    return lax.fori_loop(0, count - 1, lap, subtotal)


def from_behind(block, axis, distance):
    devices = range(lax.axis_size(axis))
    route = [(i - distance, i) for i in devices if i - distance in devices]
    return lax.ppermute(block, axis, route)


def compose(earlier, later):
    return (earlier[0] * later[0], later[0] * earlier[1] + later[1])


def local(tokens, reset_mask, weight, vectors, cotangent):
    width = weight.shape[1] // 3
    whole_weight, whole_vectors = (
        lax.all_gather(weight, ("gx", "gy"), axis=0, tiled=True),
        lax.all_gather(vectors, ("gx", "gy"), axis=1, tiled=True),
    )
    params = whole_vectors.astype(jnp.float32)
    gain = params[0]
    shift_bias = params[1]
    forget_peep = params[2]
    forget_bias = params[3]
    reset_peep = params[4]
    reset_bias = params[5]
    inputs = tokens.astype(jnp.float32)
    keep = (1 - reset_mask).astype(jnp.float32)[:, None]
    centred = inputs - jnp.mean(inputs, axis=1, keepdims=True)
    inv_std = lax.rsqrt(jnp.mean(centred * centred, axis=1, keepdims=True) + 1e-05)
    normed = centred * inv_std
    scaled = normed * gain + shift_bias
    rounded = scaled.astype(jnp.bfloat16)
    projected = jnp.dot(rounded, whole_weight, preferred_element_type=jnp.float32)
    candidate = projected[:, :width]
    forget_pre = projected[:, width : 2 * width]
    reset_pre = projected[:, 2 * width :]
    forget = jax.nn.sigmoid(forget_pre + forget_peep * scaled + forget_bias)
    decay = forget * keep
    inflow = (1.0 - forget) * candidate
    cum_decay, cum_state = lax.associative_scan(compose, (decay, inflow), axis=0)
    unit = (jnp.ones_like(cum_decay[-1]), jnp.zeros_like(cum_state[-1]))
    before = entering((cum_decay[-1], cum_state[-1]), ("gx", "gy"), compose, unit, False)
    state_in = before[1]
    state = cum_decay * state_in + cum_state
    previous = keep * jnp.concatenate([state_in[None], state[:-1]], 0)
    reset = jax.nn.sigmoid(reset_pre + reset_peep * previous + reset_bias)
    output = reset * state + (1.0 - reset) * inputs
    upstream = cotangent.astype(jnp.float32)
    reset_grad = upstream * (state - inputs) * reset * (1.0 - reset)
    through = keep * reset_peep * reset_grad
    next_decay, next_through = from_behind((decay[0], through[0]), ("gx", "gy"), -1)
    ahead = jnp.concatenate([decay[1:], next_decay[None]], 0)
    local_term = upstream * reset + jnp.concatenate([through[1:], next_through[None]], 0)
    flip_mult, flip_sum = lax.associative_scan(compose, (ahead[::-1], local_term[::-1]), axis=0)
    mult_back = flip_mult[::-1]
    sum_back = flip_sum[::-1]
    after = entering((mult_back[0], sum_back[0]), ("gx", "gy"), compose, unit, True)
    state_grad = mult_back * after[1] + sum_back
    candidate_grad = state_grad * (1.0 - forget)
    forget_grad = state_grad * (previous - candidate) * forget * (1.0 - forget)
    proj_grad = jnp.concatenate([candidate_grad, forget_grad, reset_grad], 1).astype(jnp.bfloat16)
    weight_grad = lax.psum_scatter(
        lax.dot_general(
            rounded, proj_grad, (((0,), (0,)), ((), ())), preferred_element_type=jnp.float32
        ),
        ("gx", "gy"),
        scatter_dimension=0,
        tiled=True,
    )
    scaled_grad = lax.dot_general(
        proj_grad,
        lax.all_gather(weight, ("gx", "gy"), axis=0, tiled=True),
        (((1,), (1,)), ((), ())),
        preferred_element_type=jnp.float32,
    )
    scaled_grad = scaled_grad + forget_grad * forget_peep
    vector_terms = jnp.stack(
        [
            jnp.sum(scaled_grad * normed, axis=0),
            jnp.sum(scaled_grad, axis=0),
            jnp.sum(forget_grad * scaled, axis=0),
            jnp.sum(forget_grad, axis=0),
            jnp.sum(reset_grad * previous, axis=0),
            jnp.sum(reset_grad, axis=0),
        ],
        0,
    )
    vector_grad = lax.psum_scatter(vector_terms, ("gx", "gy"), scatter_dimension=1, tiled=True)
    normed_grad = scaled_grad * gain
    input_grad = upstream * (1.0 - reset) + inv_std * (
        normed_grad
        - jnp.mean(normed_grad, axis=1, keepdims=True)
        - normed * jnp.mean(normed_grad * normed, axis=1, keepdims=True)
    )
    return (output.astype(jnp.bfloat16), input_grad, weight_grad, vector_grad)


SLOTS, SEND, PAIR, ZSEND = 8, 8, 4, 4
TOTALS, FORE, GRADS, BACK, WEIGH = 3, 5, 6, 8, 10
LAG1, LAG2, LAG3 = 2, 4, 6
LAST = 6
AHEAD_Z, AHEAD_B = 4, 3
BAND = 32
ACROSS = ((10, (0, 3, 6)), (15, (8, 11, 13)))
ACROSS_SUM = ()
PACE, GATHER, MEET, SETTLE = 2, 7, 9, 11


def layer_kernel(
    nx, ny, units,
    tok, cot, mask, weight, vectors,
    wall, pgm, outp, igo, wgo, vgo,
    vbuf, vecs, xs, gs, means, invs, rnd, rt, rtm, wf, pj, pv, grs, outs, stage, perm, pgs,
    wb, sb, rd, rx, ry, rz, zb, sg, vsum, vrows, vtot, vin, cz, keep, wraw, wsrc, vsrc,
    ach, bch, qch, sin, cin, m1a, m1b, m2a, m2b,
    zs, zr, os, bs, br, dsn, dr, cs, cr, ws,
    vzs, vzr, vxs, vxr, vo, wls, sts, rs, rr, ps, pr, pl_, wl, gos,
    e1as, e1ar, e1bs, e1br, e2as, e2ar, e2bs, e2br,
    fds, fdr, fxs, fxr, fys, fyr, fzs, fzr, vsn, vrc, ous,
):
    gx, gy, core, mate, xn, yn = place(ny)
    tokens, width = xs.shape
    rows = wsrc.shape[1]
    cols = wsrc.shape[2]
    block = rows * ny
    half, short = ny // 2, rows // 2
    groups = units // GROUP
    glanes = GROUP * LANES
    diag = xn + yn - gx
    own, xq, yq, dq = gx // 2, xn // 2, yn // 2, diag // 2
    count = nx * ny
    me = gx * ny + gy

    def peer_y(j):
        return lax.rem(gy + j, ny)

    def peer_x(j):
        return lax.rem(gx + j, nx)

    def each(n, run, start=0):
        lax.fori_loop(start, n, lambda i, _: (run(i), 0)[1], 0)

    barrier = pltpu.get_barrier_semaphore()

    def greet(j):
        to = lax.rem(me + j, count)
        pl.semaphore_signal(barrier, inc=1, device_id=(to // ny, lax.rem(to, ny)), device_id_type=MESH)

    raw = pltpu.make_async_copy(weight, wraw, wls)
    raw.start()
    each(count, greet, 1)

    def among(u, some):
        hit = u < 0
        for s in some:
            hit = hit | (u == s)
        return hit

    across = tuple(c for c, _ in ACROSS)

    def straight(u, run):
        pl.when(jnp.logical_not(among(u, across)))(lambda: run(u))

    chunks = width // glanes

    def stage_copy(i):
        src = tok if i < chunks else cot
        c = i % chunks
        return pltpu.make_async_copy(src.at[:, pl.ds(c * glanes, glanes)], stage.at[i % 2], sts.at[i % 2])

    stage_copy(0).start()
    stage_copy(1).start()

    def vz(j):
        return remote(vsrc, vbuf.at[me], vzs.at[j - 1], vzr.at[j - 1], (gx, peer_y(j)))

    def vx(j):
        part = vbuf.at[pl.ds(gx * ny, ny)]
        return remote(part, part, vxs.at[j - 1], vxr.at[j - 1], (peer_x(j), gy))

    own_vec = pltpu.make_async_copy(vsrc, vbuf.at[me], vo)

    def z_copy(u, j):
        return remote(wsrc.at[u], wall.at[u, own, core, gy], zs.at[u, j - 1], zr.at[u, j - 1], (gx, peer_y(j)))

    def own_copy(u):
        return pltpu.make_async_copy(wsrc.at[u], wall.at[u, own, core, gy], os.at[u])

    def band_copy(u, i):
        to = (mate, xn, yn)[i]
        recv = cr.at[u, 0] if i == 0 else br.at[u, i - 1]
        part = wall.at[u, own, core]
        return remote(part, part, bs.at[u, i], recv, (to, gy))

    def diag_copy(u, i):
        part = wall.at[u, (xq, yq)[i], core, half * i:half * (i + 1)]
        return remote(part, part, dsn.at[u, i], dr.at[u, i], ((yn, xn)[i], gy))

    def core_copy(u, i):
        part = wall.at[u, (own, xq, yq, dq)[i], core]
        return remote(part, part, cs.at[u, i - 1], cr.at[u, i], (mate, gy))

    def z_start(u):
        own_copy(u).start()
        for j in range(1, ny):
            z_copy(u, j).start()

    def z_wait(u):
        own_copy(u).wait()
        for j in range(1, ny):
            z_copy(u, j).wait_recv()
        for i in (1, 2, 0):
            band_copy(u, i).start()

    def xy_wait(u):
        for i in (1, 2):
            band_copy(u, i).wait_recv()
        for i in (0, 1):
            diag_copy(u, i).start()
        for i in (1, 2):
            core_copy(u, i).start()

    def diag_wait(u):
        for i in (0, 1):
            diag_copy(u, i).wait_recv()
        core_copy(u, 3).start()

    def core_wait(u):
        band_copy(u, 0).wait_recv()
        for i in (1, 2, 3):
            core_copy(u, i).wait_recv()

    def a_copy(u, i):
        return remote(
            wsrc.at[u], wall.at[u, own, core, gy], bs.at[u, i], br.at[u, i - 1], ((None, xn, yn)[i], gy)
        )

    def a_diag(u, i):
        part = wall.at[u, (xq, yq)[i], core, gy, short * i:short * (i + 1)]
        return remote(part, part, dsn.at[u, i], dr.at[u, i], ((yn, xn)[i], gy))

    def a_z(u, j):
        part = wall.at[u, :, core, gy]
        return remote(part, part, zs.at[u, j - 1], zr.at[u, j - 1], (gx, peer_y(j)))

    def a_core(u):
        part = wall.at[u, :, core]
        return remote(part, part, bs.at[u, 0], cr.at[u, 0], (mate, gy))

    def a_start(u):
        own_copy(u).start()
        for i in (1, 2):
            a_copy(u, i).start()

    def a_turn(u):
        own_copy(u).wait()
        for i in (1, 2):
            a_copy(u, i).wait_recv()
        for i in (0, 1):
            a_diag(u, i).start()

    def a_meet(u):
        for i in (0, 1):
            a_diag(u, i).wait_recv()

    def a_share(u):
        for j in range(1, ny):
            a_z(u, j).wait_recv()
        a_core(u).start()

    zero = jnp.zeros((vectors.shape[0], LANES - rows), BF16)
    odd = lax.rem(me, 2) == 1
    tile = jnp.where(
        odd, jnp.concatenate([zero, vectors[...]], 1).astype(F32), jnp.concatenate([vectors[...], zero], 1).astype(F32)
    )
    pad = jnp.zeros((16 - vectors.shape[0], LANES), F32)
    vsrc[...] = jnp.concatenate([tile, pad], 0).astype(BF16)
    raw.wait()
    for u in range(units):
        for s in range(3):
            at = s * width + u * LANES
            wsrc[u, :, s * LANES:(s + 1) * LANES] = wraw[:, at:at + LANES]

    pl.semaphore_wait(barrier, count - 1)
    own_vec.start()
    for j in range(1, ny):
        vz(j).start()
    for u in across:
        a_start(u)
    for u in range(AHEAD_Z):
        z_start(u)

    def to_runs(i, into):
        stage_copy(i).wait()
        c = i % chunks
        into[:, c * glanes:(c + 1) * glanes] = jnp.dot(
            perm[...], stage[i % 2], preferred_element_type=F32
        ).astype(BF16)
        if i + 2 < 2 * chunks:
            stage_copy(i + 2).start()

    def moments(i):
        r = pl.ds(pl.multiple_of(i * BAND, BAND), BAND)
        x = xs[r, :].astype(F32)
        mean = jnp.mean(x, axis=1, keepdims=True)
        centred = x - mean
        inv = lax.rsqrt(jnp.mean(centred * centred, axis=1, keepdims=True) + EPS)
        means[r, :] = jnp.broadcast_to(mean, (BAND, LANES))
        invs[r, :] = jnp.broadcast_to(inv, (BAND, LANES))

    def rounding(i):
        r = pl.ds(pl.multiple_of(i * BAND, BAND), BAND)
        normed = (xs[r, :].astype(F32) - means[r, 0:1]) * invs[r, 0:1]
        rnd[r, :] = (normed * vecs[0:1, :] + vecs[1:2, :]).astype(BF16)

    quads = nx // 2

    def turn(i):
        at = pl.ds(pl.multiple_of(i * block, 16), block)
        rt[at, 0:tokens] = rnd[:, pl.ds(pl.multiple_of((2 * i + core) * block, LANES), block)].T
        rtm[at, :] = rnd[:, pl.ds(pl.multiple_of((2 * i + 1 - core) * block, LANES), block)].T

    r_mate = remote(rtm, rt.at[:, tokens:2 * tokens], rs, rr, (mate, gy))

    def gather_tick(k):
        pl.when(k + AHEAD_Z < units)(lambda: straight(k + AHEAD_Z, z_start))
        pl.when(k + AHEAD_B < units)(lambda: straight(k + AHEAD_B, z_wait))
        pl.when(k < units)(lambda: straight(k, xy_wait))
        pl.when((k >= 1) & (k <= units))(lambda: straight(k - 1, diag_wait))
        for c, times in ACROSS:
            for j, t in enumerate(times):
                pl.when(k == t)(lambda c=c, j=j: a_z(c, j + 1).start())
            pl.when(k == c + 1)(functools.partial(a_share, c))

    bands = tokens // BAND
    perm[...] = run_matrix(tokens, False)
    for i in range(chunks // 2):
        to_runs(i, xs)
    z_wait(0)
    for i in range(chunks // 2, chunks):
        to_runs(i, xs)
    own_vec.wait()
    for j in range(1, ny):
        vz(j).wait_recv()
    for j in range(1, nx):
        vx(j).start()
    for u in across:
        a_turn(u)
    z_wait(1)
    each(bands // 2, moments)
    for u in range(2, AHEAD_B):
        z_wait(u)
    for u in across:
        a_meet(u)
    gather_tick(0)
    each(bands, moments, bands // 2)
    for j in range(1, nx):
        vx(j).wait_recv()
    for c in range(width // LANES):
        part = vbuf[2 * c].astype(F32) + vbuf[2 * c + 1].astype(F32)
        vecs[:, c * LANES:(c + 1) * LANES] = part[0:8, :]
    each(bands // 2, rounding)
    gather_tick(1)
    each(bands, rounding, bands // 2)
    kept = (1 - mask[...]).astype(F32)
    keep[...] = jnp.dot(
        (perm[...].astype(F32) * kept).astype(BF16), jnp.ones((tokens, LANES), BF16), preferred_element_type=F32
    )
    for i in range(chunks, chunks + chunks // 2):
        to_runs(i, gs)
    gather_tick(2)
    straight(0, core_wait)

    def late_start():
        for i in range(chunks + chunks // 2, 2 * chunks):
            to_runs(i, gs)
        perm[...] = run_matrix(tokens, True)

    def late_turn():
        each(quads, turn)
        r_mate.start()

    def e_copies(buf, send, recv, q, level):
        if level == 0:
            return [
                remote(buf.at[q, gy], buf.at[q, gy], send.at[q, j - 1], recv.at[q, j - 1], (gx, peer_y(j)))
                for j in range(1, ny)
            ]
        return [
            remote(buf.at[q, gx], buf.at[q, gx], send.at[q, j - 1], recv.at[q, j - 1], (peer_x(j), gy))
            for j in range(1, nx)
        ]

    def e_start(*a):
        for c in e_copies(*a):
            c.start()

    def e_wait(*a):
        for c in e_copies(*a):
            c.wait_recv()

    double = tokens // (2 * RUNS)

    def front_load(u):
        return pltpu.make_async_copy(wall.at[u], wf, ws)

    def project(u):
        front_load(u).wait()
        pj[lax.rem(u, SLOTS)] = jnp.dot(rnd[...], wf[...].reshape(width, -1), preferred_element_type=F32)

    def vec(i, u):
        return vecs[i:i + 1, lanes_of(u)]

    def scale(u, r, gain, shift):
        return (xs[r, lanes_of(u)].astype(F32) - means[r, :]) * invs[r, :] * gain + shift

    def gates(u):
        slot = lax.rem(u, SLOTS)
        gain, shift, vf, bf = (vec(i, u) for i in range(4))

        def step(i, carry):
            a, b = carry
            r = pl.ds(pl.multiple_of(i * 16, 16), 16)
            f = jax.nn.sigmoid(pj[slot, r, LANES:2 * LANES] + vf * scale(u, r, gain, shift) + bf)
            pj[slot, r, LANES:2 * LANES] = f
            d = f * keep[r, :]
            inflow = (1.0 - f) * pj[slot, r, 0:LANES]
            for h in (0, 8):
                a = a * d[h:h + 8]
                b = d[h:h + 8] * b + inflow[h:h + 8]
            return a, b

        a, b = lax.fori_loop(0, double, step, (jnp.ones((RUNS, LANES), F32), jnp.zeros((RUNS, LANES), F32)), unroll=4)
        q, j = u // GROUP, lax.rem(u, GROUP)
        ach[q, :, lanes_of(j)] = a
        bch[q, :, lanes_of(j)] = b

    def totals(q):
        a, b = jnp.ones((1, glanes), F32), jnp.zeros((1, glanes), F32)
        for s in range(RUNS):
            one = ach[q, s:s + 1, :]
            a = a * one
            b = one * b + bch[q, s:s + 1, :]
        m1a[q, gy, 0:1, :] = a
        m1a[q, gy, 1:2, :] = b
        e_start(m1a, e1as, e1ar, q, 0)

    def totals_x(q):
        e_wait(m1a, e1as, e1ar, q, 0)
        a, b = jnp.ones((1, glanes), F32), jnp.zeros((1, glanes), F32)
        for s in range(ny):
            one = m1a[q, s, 0:1, :]
            a = a * one
            b = one * b + m1a[q, s, 1:2, :]
        m1b[q, gx, 0:1, :] = a
        m1b[q, gx, 1:2, :] = b
        e_start(m1b, e1bs, e1br, q, 1)

    def enter(q):
        e_wait(m1b, e1bs, e1br, q, 1)
        s = jnp.zeros((1, glanes), F32)
        s = lax.fori_loop(0, gx, lambda i, s: m1b[q, i, 0:1, :] * s + m1b[q, i, 1:2, :], s)
        s = lax.fori_loop(0, gy, lambda i, s: m1a[q, i, 0:1, :] * s + m1a[q, i, 1:2, :], s)
        for r in range(RUNS):
            sin[q, r:r + 1, :] = s
            s = ach[q, r:r + 1, :] * s + bch[q, r:r + 1, :]

    def forward(u):
        slot = lax.rem(u, SLOTS)
        q, j = u // GROUP, lax.rem(u, GROUP)
        vr, br_ = vec(4, u), vec(5, u)
        zero = jnp.zeros((RUNS, LANES), F32)

        def step(i, carry):
            s, run, t, v4, v5 = carry
            r = pl.ds(pl.multiple_of(i * 16, 16), 16)
            f = pj[slot, r, LANES:2 * LANES]
            k = keep[r, :]
            inflow = (1.0 - f) * pj[slot, r, 0:LANES]
            prevs, states = [], []
            for h in (0, 8):
                prev = k[h:h + 8] * s
                s = f[h:h + 8] * prev + inflow[h:h + 8]
                prevs.append(prev)
                states.append(s)
            prev, state = jnp.concatenate(prevs, 0), jnp.concatenate(states, 0)
            x = xs[r, lanes_of(u)].astype(F32)
            up = gs[r, lanes_of(u)].astype(F32)
            reset = jax.nn.sigmoid(pj[slot, r, 2 * LANES:3 * LANES] + vr * prev + br_)
            rest = 1.0 - reset
            outs[r, lanes_of(j)] = (reset * state + rest * x).astype(BF16)
            rg = up * (state - x) * reset * rest
            pj[slot, r, 2 * LANES:3 * LANES] = rg
            pv[slot, r, :] = prev
            grs[r, lanes_of(u)] = up * rest
            local = up * reset
            d, through = f * k, k * vr * rg
            for h in (0, 8):
                t = t + run * through[h:h + 8]
                run = run * d[h:h + 8]
                t = t + run * local[h:h + 8]
                v4 = v4 + rg[h:h + 8] * prev[h:h + 8]
                v5 = v5 + rg[h:h + 8]
            return s, run, t, v4, v5

        init = (sin[q, :, lanes_of(j)], jnp.ones((RUNS, LANES), F32), zero, zero, zero)
        _, _, t, v4, v5 = lax.fori_loop(0, double, step, init, unroll=4)
        qch[q, :, lanes_of(j)] = t
        vsum[4:5, lanes_of(u)] = jnp.sum(v4, axis=0, keepdims=True)
        vsum[5:6, lanes_of(u)] = jnp.sum(v5, axis=0, keepdims=True)

    def out_copy(q):
        c = pl.ds(pl.multiple_of(q * glanes, LANES), glanes)
        return pltpu.make_async_copy(stage.at[lax.rem(q, 2)], outp.at[:, c], gos.at[q])

    def forward_group(q):
        enter(q)
        pl.when(q >= 2)(lambda: out_copy(q - 2).wait())
        each(GROUP, lambda j: forward(q * GROUP + j))
        s = jnp.zeros((1, glanes), F32)
        for r in reversed(range(RUNS)):
            s = ach[q, r:r + 1, :] * s + qch[q, r:r + 1, :]
        m2a[q, gy, 0:1, :] = s
        e_start(m2a, e2as, e2ar, q, 0)
        stage[lax.rem(q, 2)] = jnp.dot(perm[...], outs[...], preferred_element_type=F32).astype(BF16)
        out_copy(q).start()

    def grads_x(q):
        e_wait(m2a, e2as, e2ar, q, 0)
        s = jnp.zeros((1, glanes), F32)
        for r in reversed(range(ny)):
            s = m1a[q, r, 0:1, :] * s + m2a[q, r, 0:1, :]
        m2b[q, gx, 0:1, :] = s
        e_start(m2b, e2bs, e2br, q, 1)

    def enter_back(q):
        e_wait(m2b, e2bs, e2br, q, 1)
        s = jnp.zeros((1, glanes), F32)

        def over_x(i, s):
            return m1b[q, nx - 1 - i, 0:1, :] * s + m2b[q, nx - 1 - i, 0:1, :]

        def over_y(i, s):
            return m1a[q, ny - 1 - i, 0:1, :] * s + m2a[q, ny - 1 - i, 0:1, :]

        s = lax.fori_loop(0, nx - 1 - gx, over_x, s)
        s = lax.fori_loop(0, ny - 1 - gy, over_y, s)
        for r in reversed(range(RUNS)):
            cin[q, r:r + 1, :] = s
            s = ach[q, r:r + 1, :] * s + qch[q, r:r + 1, :]

    def pg_mate(u):
        return remote(pgs.at[lax.rem(u, PAIR), 0:tokens], pgm.at[u], ps.at[u], pr.at[u], (mate, gy))

    def backward(u):
        slot, pair = lax.rem(u, SLOTS), lax.rem(u, PAIR)
        q, j = u // GROUP, lax.rem(u, GROUP)
        gain, shift, vr = vec(0, u), vec(1, u), vec(4, u)
        zero = jnp.zeros((RUNS, LANES), F32)

        def step(i, carry):
            c, v2, v3 = carry
            r = pl.ds(pl.multiple_of((double - 1 - i) * 16, 16), 16)
            f = pj[slot, r, LANES:2 * LANES]
            k = keep[r, :]
            rg = pj[slot, r, 2 * LANES:3 * LANES]
            local = gs[r, lanes_of(u)].astype(F32) - grs[r, lanes_of(u)]
            d, through = f * k, k * vr * rg
            grads = [None, None]
            for h in (1, 0):
                part = slice(8 * h, 8 * h + 8)
                grads[h] = local[part] + c
                c = d[part] * grads[h] + through[part]
            grad = jnp.concatenate(grads, 0)
            cg = grad * (1.0 - f)
            fg = cg * (pv[slot, r, :] - pj[slot, r, 0:LANES]) * f
            pgs[pair, r, 0:LANES] = cg.astype(BF16)
            pgs[pair, r, LANES:2 * LANES] = fg.astype(BF16)
            pgs[pair, r, 2 * LANES:3 * LANES] = rg.astype(BF16)
            fs = fg * scale(u, r, gain, shift)
            return c, v2 + fs[0:8] + fs[8:16], v3 + fg[0:8] + fg[8:16]

        _, v2, v3 = lax.fori_loop(0, double, step, (cin[q, :, lanes_of(j)], zero, zero), unroll=4)
        vsum[2:3, lanes_of(u)] = jnp.sum(v2, axis=0, keepdims=True)
        vsum[3:4, lanes_of(u)] = jnp.sum(v3, axis=0, keepdims=True)
        pg_mate(u).start()

    def backward_group(q):
        enter_back(q)
        each(GROUP, lambda j: backward(q * GROUP + j))

    def pg_load(u):
        return pltpu.make_async_copy(pgm.at[u], pgs.at[lax.rem(u, PAIR), tokens:2 * tokens], pl_)

    def back_load(u):
        return pltpu.make_async_copy(wall.at[u], wb, wl)

    def some(part):
        return pl.ds(part * half, half)

    def sent(u):
        return sb.at[lax.rem(u, SEND)]

    def d_copy(u, i):
        return remote(
            sent(u).at[dq, some(i)], rd.at[u, some(i)], fds.at[u, i], fdr.at[u, i], ((yn, xn)[i], gy)
        )

    def x_copy(u, i):
        return remote(sent(u).at[xq, some(i)], rx.at[u, some(i)], fxs.at[u, i], fxr.at[u, i], (xn, gy))

    def y_copy(u, i):
        return remote(sent(u).at[yq, some(i)], ry.at[u, some(i)], fys.at[u, i], fyr.at[u, i], (yn, gy))

    def f_copy(u, j):
        to = lax.rem(gy + j, ny)
        return remote(zb.at[lax.rem(u, ZSEND), to], rz.at[u, j - 1], fzs.at[u, j - 1], fzr.at[u, j - 1], (gx, to))

    def next_loads(u):
        pg_mate(u).wait_recv()
        pg_load(u).start()
        back_load(u).start()

    def weigh(u):
        slot, pair = lax.rem(u, SEND), lax.rem(u, PAIR)

        @pl.when((u >= SEND) & jnp.logical_not(among(u - SEND, ACROSS_SUM)))
        def _():
            for i in (0, 1):
                d_copy(u - SEND, i).wait_send()
                x_copy(u - SEND, i).wait_send()
                y_copy(u - SEND, i).wait_send()

        pg_load(u).wait()
        sb[slot] = jnp.dot(rt[...], pgs[pair], preferred_element_type=F32).astype(BF16).reshape(sb.shape[1:])

        @pl.when(jnp.logical_not(among(u, ACROSS_SUM)))
        def _():
            for i in (0, 1):
                d_copy(u, i).start()
            x_copy(u, 1).start()
            y_copy(u, 0).start()

    def spread(u):
        pair = lax.rem(u, PAIR)
        back_load(u).wait()
        mine = pgs[pair, 0:tokens, :]
        sg[...] += lax.dot_general(mine, wb[...].reshape(width, -1), (((1,), (1,)), ((), ())), preferred_element_type=F32)
        sg[:, lanes_of(u)] += pgs[pair, 0:tokens, LANES:2 * LANES].astype(F32) * vecs[2:3, lanes_of(u)]
        pg_mate(u).wait_send()

    def fold(ref, at, more):
        ref[at] = (ref[at].astype(F32) + more.astype(F32)).astype(BF16)

    def meet(u):
        slot = lax.rem(u, SEND)
        for i in (0, 1):
            d_copy(u, i).wait_recv()
        fold(sb, (slot, xq, some(0)), rd[u, 0:half])
        x_copy(u, 0).start()
        fold(sb, (slot, yq, some(1)), rd[u, half:ny])
        y_copy(u, 1).start()

    def column(u):
        slot, zslot = lax.rem(u, SEND), lax.rem(u, ZSEND)

        @pl.when((u >= ZSEND) & jnp.logical_not(among(u - ZSEND, ACROSS_SUM)))
        def _():
            for j in range(1, ny):
                f_copy(u - ZSEND, j).wait_send()

        for i in (0, 1):
            x_copy(u, i).wait_recv()
            y_copy(u, i).wait_recv()
        total = sb[slot, own].astype(F32) + rx[u].astype(F32) + ry[u].astype(F32)
        zb[zslot] = total.astype(BF16)
        for j in range(1, ny):
            f_copy(u, j).start()

    def settle(u):
        slot = lax.rem(u, SEND)
        total = sb[slot, own, gy].astype(F32) + rx[u, gy].astype(F32) + ry[u, gy].astype(F32)
        for j in range(1, ny):
            f_copy(u, j).wait_recv()
        for j in range(1, ny):
            total = total + rz[u, j - 1].astype(F32)
        place_sum(u, total)

    def place_sum(u, total):
        for i in range(3):
            wgo[:, lanes_of(u + i * units)] = total[:, i * LANES:(i + 1) * LANES]

    def part(i):
        return pl.ds(i * short, short)

    def b_z(u, j):
        to = peer_y(j)
        return remote(sent(u).at[:, to], (rd, rx, ry)[j - 1].at[u], fzs.at[u, j - 1], fzr.at[u, j - 1], (gx, to))

    def b_diag(u, n, i):
        return remote(cz.at[n, dq, part(i)], rz.at[u, 0, part(i)], fds.at[u, i], fdr.at[u, i], ((yn, xn)[i], gy))

    def b_x(u, n, i):
        return remote(cz.at[n, xq, part(i)], rz.at[u, 1, part(i)], fxs.at[u, i], fxr.at[u, i], (xn, gy))

    def b_y(u, n, i):
        return remote(cz.at[n, yq, part(i)], rz.at[u, 2, part(i)], fys.at[u, i], fyr.at[u, i], (yn, gy))

    def b_gather(u, n):
        for j in range(1, ny):
            b_z(u, j).wait()
            if u >= ZSEND and u - ZSEND not in ACROSS_SUM:
                f_copy(u - ZSEND, j).wait_send()
        total = sb[lax.rem(u, SEND), :, gy].astype(F32)
        for ref in (rd, rx, ry):
            total = total + ref[u].astype(F32)
        cz[n] = total.astype(BF16)
        for i in (0, 1):
            b_diag(u, n, i).start()
        b_x(u, n, 1).start()
        b_y(u, n, 0).start()

    def b_meet(u, n):
        for i in (0, 1):
            b_diag(u, n, i).wait_recv()
        fold(cz, (n, xq, part(0)), rz[u, 0, part(0)])
        b_x(u, n, 0).start()
        fold(cz, (n, yq, part(1)), rz[u, 0, part(1)])
        b_y(u, n, 1).start()

    def b_settle(u, n):
        for i in (0, 1):
            b_x(u, n, i).wait_recv()
            b_y(u, n, i).wait_recv()
        place_sum(u, cz[n, own].astype(F32) + rz[u, 1].astype(F32) + rz[u, 2].astype(F32))

    def b_drain(u, n):
        for i in (0, 1):
            b_diag(u, n, i).wait_send()
            b_x(u, n, i).wait_send()
            b_y(u, n, i).wait_send()

    def finish(i):
        r = pl.ds(pl.multiple_of(i * BAND, BAND), BAND)
        s = sg[r, :]
        inv = invs[r, 0:1]
        z = (xs[r, :].astype(F32) - means[r, 0:1]) * inv
        sz = s * z
        gain = vecs[0:1, :]
        vrows[0:8, :] += jnp.sum(sz.reshape(BAND // 8, 8, width), axis=0)
        vrows[8:16, :] += jnp.sum(s.reshape(BAND // 8, 8, width), axis=0)
        n = s * gain
        m1 = jnp.mean(n, axis=1, keepdims=True)
        m2 = jnp.mean(sz * gain, axis=1, keepdims=True)
        sg[r, :] = grs[r, :] + inv * (n - m1 - z * m2)

    def v_copy(j):
        to = lax.rem(me + j, count)
        return remote(vtot.at[to // 2], vin.at[me], vsn.at[to], vrc.at[me], (to // ny, lax.rem(to, ny)))

    def v_recv(j):
        at = lax.rem(me + j, count)
        return remote(vtot.at[0], vin.at[at], vsn.at[at], vrc.at[at], (at // ny, lax.rem(at, ny)))

    def vectors_out():
        zero = jnp.zeros((2, LANES), F32)
        for c in range(width // LANES):
            at = slice(c * LANES, (c + 1) * LANES)
            top = [jnp.sum(vrows[8 * v:8 * v + 8, at], axis=0, keepdims=True) for v in (0, 1)]
            vtot[c] = jnp.concatenate(top + [vsum[2:6, at], zero], 0)
        each(count, lambda j: v_copy(j).start(), 1)

    quarter = width // 4

    def grad_copy(c):
        return pltpu.make_async_copy(grs.at[:, pl.ds(c * quarter, quarter)], igo.at[:, pl.ds(c * quarter, quarter)], ous.at[c])

    def natural():
        for c in range(4):
            at = slice(c * quarter, (c + 1) * quarter)
            v = sg[:, at]
            high = v.astype(BF16)
            low = (v - high.astype(F32)).astype(BF16)
            grs[:, at] = jnp.dot(perm[...], high, preferred_element_type=F32) + jnp.dot(
                perm[...], low, preferred_element_type=F32
            )
            grad_copy(c).start()

    def tick(k, _):
        u = k - 3
        v = u - WEIGH
        gather_tick(k)
        pl.when(k == 3)(late_start)
        pl.when(k == 5)(late_turn)

        def summed(lag, run):
            w = v - lag
            pl.when((w >= 0) & (w < units) & jnp.logical_not(among(w, ACROSS_SUM)))(lambda: run(w))

        summed(LAG1, meet)
        summed(LAG2, column)
        summed(LAG3, settle)
        for n, c in enumerate(ACROSS_SUM):
            pl.when(v == c + GATHER)(functools.partial(b_gather, c, n))
            pl.when(v == c + MEET)(functools.partial(b_meet, c, n))
            pl.when(v == c + SETTLE)(functools.partial(b_settle, c, n))

        @pl.when(v == 0)
        def _():
            r_mate.wait_recv()
            sg[...] = jnp.zeros_like(sg)
            vrows[...] = jnp.zeros_like(vrows)

        @pl.when((v >= 0) & (v < units))
        def _():
            weigh(v)
            spread(v)

        for c in ACROSS_SUM:
            for j in range(1, ny):
                pl.when(v == c + PACE * (j - 1))(lambda c=c, j=j: b_z(c, j).start())

        pl.when((v >= -1) & (v < units - 1))(lambda: next_loads(v + 1))

        def event(lag, run):
            g = (u - lag) // GROUP
            pl.when((u >= lag) & (lax.rem(u - lag + GROUP, GROUP) == 0) & (g < groups))(lambda: run(g))

        event(BACK, backward_group)
        event(GRADS, grads_x)
        event(FORE, forward_group)
        event(TOTALS, totals_x)

        @pl.when((u >= 0) & (u < units))
        def _():
            project(u)

        @pl.when((u >= 0) & (u < units - 1))
        def _():
            straight(u + 1, core_wait)
            for c in across:
                pl.when(u + 1 == c)(lambda c=c: a_core(c).wait_recv())
            front_load(u + 1).start()

        @pl.when((u >= 0) & (u < units))
        def _():
            gates(u)
            pl.when(lax.rem(u, GROUP) == GROUP - 1)(lambda: totals(u // GROUP))

        pl.when(v == units)(lambda: each(bands // 2, finish))

        @pl.when(v == units + 1)
        def _():
            each(bands, finish, bands // 2)
            vectors_out()

        pl.when(v == units + 2)(natural)
        return 0

    front_load(0).start()
    lax.fori_loop(3, units + WEIGH + 3 + LAST, tick, 0)

    each(count, lambda j: v_recv(j).wait_recv(), 1)
    vin[me] = vtot[me // 2]
    vgo[...] = lax.fori_loop(0, count, lambda j, s: s + vin[j], jnp.zeros((8, LANES), F32))

    def drain(u):
        for j in range(1, ny):
            z_copy(u, j).wait_send()
        for i in range(3):
            band_copy(u, i).wait_send()
        for i in (0, 1):
            diag_copy(u, i).wait_send()
        for i in (1, 2, 3):
            core_copy(u, i).wait_send()

    each(units, lambda u: straight(u, drain))
    for c in across:
        for j in range(1, ny):
            a_z(c, j).wait_send()
        for i in (1, 2):
            a_copy(c, i).wait_send()
        for i in (0, 1):
            a_diag(c, i).wait_send()
        a_core(c).wait_send()
    for n, c in enumerate(ACROSS_SUM):
        b_drain(c, n)

    def drain_send(u):
        for i in (0, 1):
            d_copy(u, i).wait_send()
            x_copy(u, i).wait_send()
            y_copy(u, i).wait_send()

    each(units, lambda u: pl.when(jnp.logical_not(among(u, ACROSS_SUM)))(lambda: drain_send(u)), units - SEND)

    def drain_z(u):
        for j in range(1, ny):
            f_copy(u, j).wait_send()

    each(units, drain_z, units - ZSEND)

    def drain_group(q):
        for a in ((m1a, e1as, e1ar, q, 0), (m1b, e1bs, e1br, q, 1), (m2a, e2as, e2ar, q, 0), (m2b, e2bs, e2br, q, 1)):
            for c in e_copies(*a):
                c.wait_send()

    each(groups, drain_group)
    for q in range(groups - 2, groups):
        out_copy(q).wait()
    for j in range(1, ny):
        vz(j).wait_send()
    for j in range(1, nx):
        vx(j).wait_send()
    r_mate.wait_send()
    each(count, lambda j: v_copy(j).wait_send(), 1)
    for c in range(4):
        grad_copy(c).wait()


def layer(nx, ny, tok, cot, mask, weight, vectors):
    tokens, width = tok.shape
    rows, cols = weight.shape[0], 3 * LANES
    units = width // LANES
    groups, glanes, block, count = units // GROUP, GROUP * LANES, rows * ny, nx * ny
    dma = pltpu.SemaphoreType.DMA
    any_, vmem = pl.BlockSpec(memory_space=pl.ANY), pl.BlockSpec(memory_space=pltpu.VMEM)
    msg = RUNS, glanes
    s, v = jax.ShapeDtypeStruct, pltpu.VMEM
    return pl.pallas_call(
        functools.partial(layer_kernel, nx, ny, units),
        name="layer",
        out_shape=(
            s((units, nx // 2, 2, ny, rows, cols), BF16), s((units, tokens, cols), BF16),
            s((tokens, width), BF16), s((tokens, width), F32), s((rows, 3 * width), F32), s((8, LANES), F32),
        ),
        in_specs=[any_, any_, vmem, any_, vmem],
        out_specs=(any_,) * 4 + (vmem,) * 2,
        scratch_shapes=[
            v((count, 16, LANES), BF16), v((8, width), F32),
            v((tokens, width), BF16), v((tokens, width), BF16), v((tokens, LANES), F32), v((tokens, LANES), F32),
            v((tokens, width), BF16), v((width // 2, 2 * tokens), BF16), v((width // 2, tokens), BF16),
            v((nx // 2, 2, ny, rows, cols), BF16),
            v((SLOTS, tokens, cols), F32), v((SLOTS, tokens, LANES), F32),
            v((tokens, width), F32), v((tokens, glanes), BF16), v((2, tokens, glanes), BF16),
            v((tokens, tokens), BF16), v((PAIR, 2 * tokens, cols), BF16),
            v((nx // 2, 2, ny, rows, cols), BF16), v((SEND, nx // 2, ny, rows, cols), BF16),
            *[v((units, ny, rows, cols), BF16)] * 3,
            v((units, ny - 1, rows, cols), BF16), v((ZSEND, ny, rows, cols), BF16),
            v((tokens, width), F32), v((8, width), F32), v((16, width), F32),
            v((width // LANES, 8, LANES), F32), v((count, 8, LANES), F32),
            v((max(1, len(ACROSS_SUM)), nx // 2, rows, cols), BF16), v((tokens, LANES), F32),
            v((rows, 3 * width), BF16), v((units, rows, cols), BF16), v((16, LANES), BF16),
            *[v((groups,) + msg, F32)] * 5,
            v((groups, ny) + msg, F32), v((groups, nx) + msg, F32),
            v((groups, ny) + msg, F32), v((groups, nx) + msg, F32),
            dma((units, ny - 1)), dma((units, ny - 1)), dma((units,)), dma((units, 3)), dma((units, 2)),
            dma((units, 2)), dma((units, 2)), dma((units, 3)), dma((units, 4)), dma,
            dma((ny - 1,)), dma((ny - 1,)), dma((nx - 1,)), dma((nx - 1,)), dma, dma, dma((2,)),
            dma, dma, dma((units,)), dma((units,)), dma, dma, dma((groups,)),
            dma((groups, ny - 1)), dma((groups, ny - 1)), dma((groups, nx - 1)), dma((groups, nx - 1)),
            dma((groups, ny - 1)), dma((groups, ny - 1)), dma((groups, nx - 1)), dma((groups, nx - 1)),
            *[dma((units, 2))] * 6, dma((units, ny - 1)), dma((units, ny - 1)),
            dma((count,)), dma((count,)), dma((4,)),
        ],
        compiler_params=pltpu.CompilerParams(
            collective_id=0, has_side_effects=True, vmem_limit_bytes=62 * 2**20
        ),
        cost_estimate=pl.CostEstimate(
            flops=6 * tokens * width * units * cols, bytes_accessed=4 * width * units * cols, transcendentals=0
        ),
    )(tok, cot, mask, weight, vectors)


def fast(nx, ny, tokens, reset_mask, weight, vectors, cotangent):
    rows = weight.shape[0]
    odd = lax.rem(lax.axis_index("gx") * ny + lax.axis_index("gy"), 2) == 1
    mask = reset_mask.reshape(1, -1)
    _, _, outp, grad, weight_grad, tile = layer(nx, ny, tokens, cotangent, mask, weight, vectors)
    vector_grad = jnp.where(odd, tile[:6, rows:2 * rows], tile[:6, :rows])
    return outp, grad, weight_grad, vector_grad


def solution(mesh):
    placed = (
        P(("gx", "gy"), None),
        P(("gx", "gy")),
        P(("gx", "gy"), None),
        P(None, ("gx", "gy")),
        P(("gx", "gy"), None),
    )
    nx, ny = mesh.shape["gx"], mesh.shape["gy"]

    def body(tokens, reset_mask, weight, vectors, cotangent):
        whole_tiles = weight.shape[0] % 16 == 0 and tokens.shape[0] % 256 == 0
        if (nx, ny) == (8, 4) and whole_tiles and 2 * weight.shape[0] == LANES and tokens.shape[1] % 2048 == 0:
            return fast(nx, ny, tokens, reset_mask, weight, vectors, cotangent)
        return local(tokens, reset_mask, weight, vectors, cotangent)

    return jax.shard_map(
        body,
        mesh=mesh,
        in_specs=placed,
        out_specs=(
            P(("gx", "gy"), None),
            P(("gx", "gy"), None),
            P(("gx", "gy"), None),
            P(None, ("gx", "gy")),
        ),
        check_vma=False,
    )
```

```python
import functools

import jax
import jax.numpy as jnp
from jax import lax
from jax.experimental import pallas as pl
from jax.experimental.pallas import tpu as pltpu
from jax.sharding import PartitionSpec as P

MESH = pl.DeviceIdType.MESH
F32, BF16 = jnp.float32, jnp.bfloat16
LANES, RUNS, GROUP = 128, 8, 2
EPS = 1e-05


def place(ny):
    gx, gy = lax.axis_index("gx"), lax.axis_index("gy")
    core, xx, yy = lax.rem(gx, 2), lax.rem(gx // 2, 2), gx // 4
    return gx, gy, core, gx + 1 - 2 * core, gx + 2 - 4 * xx, gx + 4 - 8 * yy


def remote(src, dst, send, recv, to):
    return pltpu.make_async_remote_copy(
        src_ref=src, dst_ref=dst, send_sem=send, recv_sem=recv, device_id=to, device_id_type=MESH
    )


def lanes_of(b):
    return pl.ds(pl.multiple_of(b * LANES, LANES), LANES)


def run_matrix(tokens, back):
    steps = tokens // RUNS
    row = lax.broadcasted_iota(jnp.int32, (tokens, tokens), 0)
    col = lax.broadcasted_iota(jnp.int32, (tokens, tokens), 1)
    if back:
        hit = row == (col & (RUNS - 1)) * steps + (col >> 3)
    else:
        hit = col == (row & (RUNS - 1)) * steps + (row >> 3)
    return jnp.where(hit, 1.0, 0.0).astype(BF16)


def entering(value, axis, join, neutral, backward):
    count, mine = (lax.axis_size(axis), lax.axis_index(axis))
    pieces = jax.tree.map(lambda part: lax.all_gather(part, axis), value)
    if backward:
        pieces = jax.tree.map(lambda part: part[::-1], pieces)
        mine = count - 1 - mine
    subtotal = jax.tree.map(
        lambda part, zero: jnp.full_like(part, 0) + jnp.asarray(zero, part.dtype), value, neutral
    )

    def lap(position, subtotal):
        longer = join(subtotal, jax.tree.map(lambda part: part[position], pieces))
        return jax.tree.map(lambda new, old: jnp.where(position < mine, new, old), longer, subtotal)

    return lax.fori_loop(0, count - 1, lap, subtotal)


def from_behind(block, axis, distance):
    devices = range(lax.axis_size(axis))
    route = [(i - distance, i) for i in devices if i - distance in devices]
    return lax.ppermute(block, axis, route)


def compose(earlier, later):
    return (earlier[0] * later[0], later[0] * earlier[1] + later[1])


def local(tokens, reset_mask, weight, vectors, cotangent):
    width = weight.shape[1] // 3
    whole_weight, whole_vectors = (
        lax.all_gather(weight, ("gx", "gy"), axis=0, tiled=True),
        lax.all_gather(vectors, ("gx", "gy"), axis=1, tiled=True),
    )
    params = whole_vectors.astype(jnp.float32)
    gain = params[0]
    shift_bias = params[1]
    forget_peep = params[2]
    forget_bias = params[3]
    reset_peep = params[4]
    reset_bias = params[5]
    inputs = tokens.astype(jnp.float32)
    keep = (1 - reset_mask).astype(jnp.float32)[:, None]
    centred = inputs - jnp.mean(inputs, axis=1, keepdims=True)
    inv_std = lax.rsqrt(jnp.mean(centred * centred, axis=1, keepdims=True) + 1e-05)
    normed = centred * inv_std
    scaled = normed * gain + shift_bias
    rounded = scaled.astype(jnp.bfloat16)
    projected = jnp.dot(rounded, whole_weight, preferred_element_type=jnp.float32)
    candidate = projected[:, :width]
    forget_pre = projected[:, width : 2 * width]
    reset_pre = projected[:, 2 * width :]
    forget = jax.nn.sigmoid(forget_pre + forget_peep * scaled + forget_bias)
    decay = forget * keep
    inflow = (1.0 - forget) * candidate
    cum_decay, cum_state = lax.associative_scan(compose, (decay, inflow), axis=0)
    unit = (jnp.ones_like(cum_decay[-1]), jnp.zeros_like(cum_state[-1]))
    before = entering((cum_decay[-1], cum_state[-1]), ("gx", "gy"), compose, unit, False)
    state_in = before[1]
    state = cum_decay * state_in + cum_state
    previous = keep * jnp.concatenate([state_in[None], state[:-1]], 0)
    reset = jax.nn.sigmoid(reset_pre + reset_peep * previous + reset_bias)
    output = reset * state + (1.0 - reset) * inputs
    upstream = cotangent.astype(jnp.float32)
    reset_grad = upstream * (state - inputs) * reset * (1.0 - reset)
    through = keep * reset_peep * reset_grad
    next_decay, next_through = from_behind((decay[0], through[0]), ("gx", "gy"), -1)
    ahead = jnp.concatenate([decay[1:], next_decay[None]], 0)
    local_term = upstream * reset + jnp.concatenate([through[1:], next_through[None]], 0)
    flip_mult, flip_sum = lax.associative_scan(compose, (ahead[::-1], local_term[::-1]), axis=0)
    mult_back = flip_mult[::-1]
    sum_back = flip_sum[::-1]
    after = entering((mult_back[0], sum_back[0]), ("gx", "gy"), compose, unit, True)
    state_grad = mult_back * after[1] + sum_back
    candidate_grad = state_grad * (1.0 - forget)
    forget_grad = state_grad * (previous - candidate) * forget * (1.0 - forget)
    proj_grad = jnp.concatenate([candidate_grad, forget_grad, reset_grad], 1).astype(jnp.bfloat16)
    weight_grad = lax.psum_scatter(
        lax.dot_general(
            rounded, proj_grad, (((0,), (0,)), ((), ())), preferred_element_type=jnp.float32
        ),
        ("gx", "gy"),
        scatter_dimension=0,
        tiled=True,
    )
    scaled_grad = lax.dot_general(
        proj_grad,
        lax.all_gather(weight, ("gx", "gy"), axis=0, tiled=True),
        (((1,), (1,)), ((), ())),
        preferred_element_type=jnp.float32,
    )
    scaled_grad = scaled_grad + forget_grad * forget_peep
    vector_terms = jnp.stack(
        [
            jnp.sum(scaled_grad * normed, axis=0),
            jnp.sum(scaled_grad, axis=0),
            jnp.sum(forget_grad * scaled, axis=0),
            jnp.sum(forget_grad, axis=0),
            jnp.sum(reset_grad * previous, axis=0),
            jnp.sum(reset_grad, axis=0),
        ],
        0,
    )
    vector_grad = lax.psum_scatter(vector_terms, ("gx", "gy"), scatter_dimension=1, tiled=True)
    normed_grad = scaled_grad * gain
    input_grad = upstream * (1.0 - reset) + inv_std * (
        normed_grad
        - jnp.mean(normed_grad, axis=1, keepdims=True)
        - normed * jnp.mean(normed_grad * normed, axis=1, keepdims=True)
    )
    return (output.astype(jnp.bfloat16), input_grad, weight_grad, vector_grad)


SLOTS, SEND, PAIR, ZSEND = 8, 8, 4, 4
TOTALS, FORE, GRADS, BACK, WEIGH = 3, 5, 6, 8, 10
LAG1, LAG2, LAG3 = 2, 4, 6
LAST = 6
AHEAD_Z, AHEAD_B = 5, 3
BAND = 32
ACROSS = ((10, (0, 3, 6)), (15, (8, 11, 13)))
ACROSS_SUM = ()


def layer_kernel(
    nx, ny, units,
    tok, cot, mask, weight, vectors,
    wall, pgm, outp, igo, wgo, vgo,
    vbuf, vecs, xs, gs, means, invs, rnd, rt, rtm, wf, pj, pv, grs, outs, stage, perm, pgs,
    wb, sb, rd, rx, ry, rz, zb, sg, vsum, vrows, vtot, vin, cz, keep, wraw, wsrc, vsrc,
    ach, bch, qch, sin, cin, m1a, m1b, m2a, m2b,
    zs, zr, os, bs, br, dsn, dr, cs, cr, ws,
    vzs, vzr, vxs, vxr, vo, wls, sts, rs, rr, ps, pr, pl_, wl, gos,
    e1as, e1ar, e1bs, e1br, e2as, e2ar, e2bs, e2br,
    fds, fdr, fxs, fxr, fys, fyr, fzs, fzr, vsn, vrc, ous,
):
    gx, gy, core, mate, xn, yn = place(ny)
    tokens, width = xs.shape
    rows = wsrc.shape[1]
    cols = wsrc.shape[2]
    block = rows * ny
    half, short = ny // 2, rows // 2
    groups = units // GROUP
    glanes = GROUP * LANES
    diag = xn + yn - gx
    own, xq, yq, dq = gx // 2, xn // 2, yn // 2, diag // 2
    count = nx * ny
    me = gx * ny + gy

    def peer_y(j):
        return lax.rem(gy + j, ny)

    def peer_x(j):
        return lax.rem(gx + j, nx)

    def each(n, run, start=0):
        lax.fori_loop(start, n, lambda i, _: (run(i), 0)[1], 0)

    barrier = pltpu.get_barrier_semaphore()

    def greet(j):
        to = lax.rem(me + j, count)
        pl.semaphore_signal(barrier, inc=1, device_id=(to // ny, lax.rem(to, ny)), device_id_type=MESH)

    raw = pltpu.make_async_copy(weight, wraw, wls)
    raw.start()
    each(count, greet, 1)

    def among(u, some):
        hit = u < 0
        for s in some:
            hit = hit | (u == s)
        return hit

    across = tuple(c for c, _ in ACROSS)
    turned = tuple(c for c, _, _ in ACROSS_SUM)

    def straight(u, run):
        pl.when(jnp.logical_not(among(u, across)))(lambda: run(u))

    chunks = width // glanes

    def stage_copy(i):
        src = tok if i < chunks else cot
        c = i % chunks
        return pltpu.make_async_copy(src.at[:, pl.ds(c * glanes, glanes)], stage.at[i % 2], sts.at[i % 2])

    stage_copy(0).start()
    stage_copy(1).start()

    def vz(j):
        return remote(vsrc, vbuf.at[me], vzs.at[j - 1], vzr.at[j - 1], (gx, peer_y(j)))

    def vx(j):
        part = vbuf.at[pl.ds(gx * ny, ny)]
        return remote(part, part, vxs.at[j - 1], vxr.at[j - 1], (peer_x(j), gy))

    own_vec = pltpu.make_async_copy(vsrc, vbuf.at[me], vo)

    def z_copy(u, j):
        return remote(wsrc.at[u], wall.at[u, own, core, gy], zs.at[u, j - 1], zr.at[u, j - 1], (gx, peer_y(j)))

    def own_copy(u):
        return pltpu.make_async_copy(wsrc.at[u], wall.at[u, own, core, gy], os.at[u])

    def band_copy(u, i):
        to = (mate, xn, yn)[i]
        recv = cr.at[u, 0] if i == 0 else br.at[u, i - 1]
        part = wall.at[u, own, core]
        return remote(part, part, bs.at[u, i], recv, (to, gy))

    def diag_copy(u, i):
        part = wall.at[u, (xq, yq)[i], core, half * i:half * (i + 1)]
        return remote(part, part, dsn.at[u, i], dr.at[u, i], ((yn, xn)[i], gy))

    def core_copy(u, i):
        part = wall.at[u, (own, xq, yq, dq)[i], core]
        return remote(part, part, cs.at[u, i - 1], cr.at[u, i], (mate, gy))

    def z_start(u):
        own_copy(u).start()
        for j in range(1, ny):
            z_copy(u, j).start()

    def z_wait(u):
        own_copy(u).wait()
        for j in range(1, ny):
            z_copy(u, j).wait_recv()
        for i in (1, 2, 0):
            band_copy(u, i).start()

    def xy_wait(u):
        for i in (1, 2):
            band_copy(u, i).wait_recv()
        for i in (0, 1):
            diag_copy(u, i).start()
        for i in (1, 2):
            core_copy(u, i).start()

    def diag_wait(u):
        for i in (0, 1):
            diag_copy(u, i).wait_recv()
        core_copy(u, 3).start()

    def core_wait(u):
        band_copy(u, 0).wait_recv()
        for i in (1, 2, 3):
            core_copy(u, i).wait_recv()

    def a_copy(u, i):
        return remote(
            wsrc.at[u], wall.at[u, own, core, gy], bs.at[u, i], br.at[u, i - 1], ((None, xn, yn)[i], gy)
        )

    def a_diag(u, i):
        part = wall.at[u, (xq, yq)[i], core, gy, short * i:short * (i + 1)]
        return remote(part, part, dsn.at[u, i], dr.at[u, i], ((yn, xn)[i], gy))

    def a_z(u, j):
        part = wall.at[u, :, core, gy]
        return remote(part, part, zs.at[u, j - 1], zr.at[u, j - 1], (gx, peer_y(j)))

    def a_core(u):
        part = wall.at[u, :, core]
        return remote(part, part, bs.at[u, 0], cr.at[u, 0], (mate, gy))

    def a_start(u):
        own_copy(u).start()
        for i in (1, 2):
            a_copy(u, i).start()

    def a_turn(u):
        own_copy(u).wait()
        for i in (1, 2):
            a_copy(u, i).wait_recv()
        for i in (0, 1):
            a_diag(u, i).start()

    def a_meet(u):
        for i in (0, 1):
            a_diag(u, i).wait_recv()

    def a_share(u):
        for j in range(1, ny):
            a_z(u, j).wait_recv()
        a_core(u).start()

    zero = jnp.zeros((vectors.shape[0], LANES - rows), BF16)
    odd = lax.rem(me, 2) == 1
    tile = jnp.where(
        odd, jnp.concatenate([zero, vectors[...]], 1).astype(F32), jnp.concatenate([vectors[...], zero], 1).astype(F32)
    )
    pad = jnp.zeros((16 - vectors.shape[0], LANES), F32)
    vsrc[...] = jnp.concatenate([tile, pad], 0).astype(BF16)
    raw.wait()
    for u in range(units):
        for s in range(3):
            at = s * width + u * LANES
            wsrc[u, :, s * LANES:(s + 1) * LANES] = wraw[:, at:at + LANES]

    pl.semaphore_wait(barrier, count - 1)
    own_vec.start()
    for j in range(1, ny):
        vz(j).start()
    for u in across:
        a_start(u)
    z_start(0)

    def to_runs(i, into):
        stage_copy(i).wait()
        c = i % chunks
        into[:, c * glanes:(c + 1) * glanes] = jnp.dot(
            perm[...], stage[i % 2], preferred_element_type=F32
        ).astype(BF16)
        if i + 2 < 2 * chunks:
            stage_copy(i + 2).start()

    def moments(i):
        r = pl.ds(pl.multiple_of(i * BAND, BAND), BAND)
        x = xs[r, :].astype(F32)
        mean = jnp.mean(x, axis=1, keepdims=True)
        centred = x - mean
        inv = lax.rsqrt(jnp.mean(centred * centred, axis=1, keepdims=True) + EPS)
        means[r, :] = jnp.broadcast_to(mean, (BAND, LANES))
        invs[r, :] = jnp.broadcast_to(inv, (BAND, LANES))

    def rounding(i):
        r = pl.ds(pl.multiple_of(i * BAND, BAND), BAND)
        normed = (xs[r, :].astype(F32) - means[r, 0:1]) * invs[r, 0:1]
        rnd[r, :] = (normed * vecs[0:1, :] + vecs[1:2, :]).astype(BF16)

    quads = nx // 2

    def turn(i):
        at = pl.ds(pl.multiple_of(i * block, 16), block)
        rt[at, 0:tokens] = rnd[:, pl.ds(pl.multiple_of((2 * i + core) * block, LANES), block)].T
        rtm[at, :] = rnd[:, pl.ds(pl.multiple_of((2 * i + 1 - core) * block, LANES), block)].T

    r_mate = remote(rtm, rt.at[:, tokens:2 * tokens], rs, rr, (mate, gy))

    def gather_tick(k):
        pl.when(k + AHEAD_Z < units)(lambda: straight(k + AHEAD_Z, z_start))
        pl.when(k + AHEAD_B < units)(lambda: straight(k + AHEAD_B, z_wait))
        pl.when(k < units)(lambda: straight(k, xy_wait))
        pl.when((k >= 1) & (k <= units))(lambda: straight(k - 1, diag_wait))
        for c, times in ACROSS:
            for j, t in enumerate(times):
                pl.when(k == t)(lambda c=c, j=j: a_z(c, j + 1).start())
            pl.when(k == c + 1)(functools.partial(a_share, c))

    bands = tokens // BAND
    perm[...] = run_matrix(tokens, False)
    for i in range(chunks // 2):
        to_runs(i, xs)
    z_wait(0)
    z_start(1)
    z_start(2)
    for i in range(chunks // 2, chunks):
        to_runs(i, xs)
    own_vec.wait()
    for j in range(1, ny):
        vz(j).wait_recv()
    for j in range(1, nx):
        vx(j).start()
    for u in across:
        a_turn(u)
    z_wait(1)
    for u in range(3, AHEAD_Z):
        z_start(u)
    each(bands // 2, moments)
    for u in range(2, AHEAD_B):
        z_wait(u)
    for u in across:
        a_meet(u)
    gather_tick(0)
    each(bands, moments, bands // 2)
    for j in range(1, nx):
        vx(j).wait_recv()
    for c in range(width // LANES):
        part = vbuf[2 * c].astype(F32) + vbuf[2 * c + 1].astype(F32)
        vecs[:, c * LANES:(c + 1) * LANES] = part[0:8, :]
    each(bands // 2, rounding)
    gather_tick(1)
    each(bands, rounding, bands // 2)
    kept = (1 - mask[...]).astype(F32)
    keep[...] = jnp.dot(
        (perm[...].astype(F32) * kept).astype(BF16), jnp.ones((tokens, LANES), BF16), preferred_element_type=F32
    )
    for i in range(chunks, chunks + chunks // 2):
        to_runs(i, gs)
    gather_tick(2)
    straight(0, core_wait)

    def late_start():
        for i in range(chunks + chunks // 2, 2 * chunks):
            to_runs(i, gs)
        perm[...] = run_matrix(tokens, True)

    def late_turn():
        each(quads, turn)
        r_mate.start()

    def e_copies(buf, send, recv, q, level):
        if level == 0:
            return [
                remote(buf.at[q, gy], buf.at[q, gy], send.at[q, j - 1], recv.at[q, j - 1], (gx, peer_y(j)))
                for j in range(1, ny)
            ]
        return [
            remote(buf.at[q, gx], buf.at[q, gx], send.at[q, j - 1], recv.at[q, j - 1], (peer_x(j), gy))
            for j in range(1, nx)
        ]

    def e_start(*a):
        for c in e_copies(*a):
            c.start()

    def e_wait(*a):
        for c in e_copies(*a):
            c.wait_recv()

    double = tokens // (2 * RUNS)

    def front_load(u):
        return pltpu.make_async_copy(wall.at[u], wf, ws)

    def project(u):
        front_load(u).wait()
        pj[lax.rem(u, SLOTS)] = jnp.dot(rnd[...], wf[...].reshape(width, -1), preferred_element_type=F32)

    def vec(i, u):
        return vecs[i:i + 1, lanes_of(u)]

    def scale(u, r, gain, shift):
        return (xs[r, lanes_of(u)].astype(F32) - means[r, :]) * invs[r, :] * gain + shift

    def gates(u):
        slot = lax.rem(u, SLOTS)
        gain, shift, vf, bf = (vec(i, u) for i in range(4))

        def step(i, carry):
            a, b = carry
            r = pl.ds(pl.multiple_of(i * 16, 16), 16)
            f = jax.nn.sigmoid(pj[slot, r, LANES:2 * LANES] + vf * scale(u, r, gain, shift) + bf)
            pj[slot, r, LANES:2 * LANES] = f
            d = f * keep[r, :]
            inflow = (1.0 - f) * pj[slot, r, 0:LANES]
            for h in (0, 8):
                a = a * d[h:h + 8]
                b = d[h:h + 8] * b + inflow[h:h + 8]
            return a, b

        a, b = lax.fori_loop(0, double, step, (jnp.ones((RUNS, LANES), F32), jnp.zeros((RUNS, LANES), F32)), unroll=4)
        q, j = u // GROUP, lax.rem(u, GROUP)
        ach[q, :, lanes_of(j)] = a
        bch[q, :, lanes_of(j)] = b

    def totals(q):
        a, b = jnp.ones((1, glanes), F32), jnp.zeros((1, glanes), F32)
        for s in range(RUNS):
            one = ach[q, s:s + 1, :]
            a = a * one
            b = one * b + bch[q, s:s + 1, :]
        m1a[q, gy, 0:1, :] = a
        m1a[q, gy, 1:2, :] = b
        e_start(m1a, e1as, e1ar, q, 0)

    def totals_x(q):
        e_wait(m1a, e1as, e1ar, q, 0)
        a, b = jnp.ones((1, glanes), F32), jnp.zeros((1, glanes), F32)
        for s in range(ny):
            one = m1a[q, s, 0:1, :]
            a = a * one
            b = one * b + m1a[q, s, 1:2, :]
        m1b[q, gx, 0:1, :] = a
        m1b[q, gx, 1:2, :] = b
        e_start(m1b, e1bs, e1br, q, 1)

    def enter(q):
        e_wait(m1b, e1bs, e1br, q, 1)
        s = jnp.zeros((1, glanes), F32)
        s = lax.fori_loop(0, gx, lambda i, s: m1b[q, i, 0:1, :] * s + m1b[q, i, 1:2, :], s)
        s = lax.fori_loop(0, gy, lambda i, s: m1a[q, i, 0:1, :] * s + m1a[q, i, 1:2, :], s)
        for r in range(RUNS):
            sin[q, r:r + 1, :] = s
            s = ach[q, r:r + 1, :] * s + bch[q, r:r + 1, :]

    def forward(u):
        slot = lax.rem(u, SLOTS)
        q, j = u // GROUP, lax.rem(u, GROUP)
        vr, br_ = vec(4, u), vec(5, u)
        zero = jnp.zeros((RUNS, LANES), F32)

        def step(i, carry):
            s, run, t, v4, v5 = carry
            r = pl.ds(pl.multiple_of(i * 16, 16), 16)
            f = pj[slot, r, LANES:2 * LANES]
            k = keep[r, :]
            inflow = (1.0 - f) * pj[slot, r, 0:LANES]
            prevs, states = [], []
            for h in (0, 8):
                prev = k[h:h + 8] * s
                s = f[h:h + 8] * prev + inflow[h:h + 8]
                prevs.append(prev)
                states.append(s)
            prev, state = jnp.concatenate(prevs, 0), jnp.concatenate(states, 0)
            x = xs[r, lanes_of(u)].astype(F32)
            up = gs[r, lanes_of(u)].astype(F32)
            reset = jax.nn.sigmoid(pj[slot, r, 2 * LANES:3 * LANES] + vr * prev + br_)
            rest = 1.0 - reset
            outs[r, lanes_of(j)] = (reset * state + rest * x).astype(BF16)
            rg = up * (state - x) * reset * rest
            pj[slot, r, 2 * LANES:3 * LANES] = rg
            pv[slot, r, :] = prev
            grs[r, lanes_of(u)] = up * rest
            local = up * reset
            d, through = f * k, k * vr * rg
            for h in (0, 8):
                t = t + run * through[h:h + 8]
                run = run * d[h:h + 8]
                t = t + run * local[h:h + 8]
                v4 = v4 + rg[h:h + 8] * prev[h:h + 8]
                v5 = v5 + rg[h:h + 8]
            return s, run, t, v4, v5

        init = (sin[q, :, lanes_of(j)], jnp.ones((RUNS, LANES), F32), zero, zero, zero)
        _, _, t, v4, v5 = lax.fori_loop(0, double, step, init, unroll=4)
        qch[q, :, lanes_of(j)] = t
        vsum[4:5, lanes_of(u)] = jnp.sum(v4, axis=0, keepdims=True)
        vsum[5:6, lanes_of(u)] = jnp.sum(v5, axis=0, keepdims=True)

    def out_copy(q):
        c = pl.ds(pl.multiple_of(q * glanes, LANES), glanes)
        return pltpu.make_async_copy(stage.at[lax.rem(q, 2)], outp.at[:, c], gos.at[q])

    def forward_group(q):
        enter(q)
        pl.when(q >= 2)(lambda: out_copy(q - 2).wait())
        each(GROUP, lambda j: forward(q * GROUP + j))
        s = jnp.zeros((1, glanes), F32)
        for r in reversed(range(RUNS)):
            s = ach[q, r:r + 1, :] * s + qch[q, r:r + 1, :]
        m2a[q, gy, 0:1, :] = s
        e_start(m2a, e2as, e2ar, q, 0)
        stage[lax.rem(q, 2)] = jnp.dot(perm[...], outs[...], preferred_element_type=F32).astype(BF16)
        out_copy(q).start()

    def grads_x(q):
        e_wait(m2a, e2as, e2ar, q, 0)
        s = jnp.zeros((1, glanes), F32)
        for r in reversed(range(ny)):
            s = m1a[q, r, 0:1, :] * s + m2a[q, r, 0:1, :]
        m2b[q, gx, 0:1, :] = s
        e_start(m2b, e2bs, e2br, q, 1)

    def enter_back(q):
        e_wait(m2b, e2bs, e2br, q, 1)
        s = jnp.zeros((1, glanes), F32)

        def over_x(i, s):
            return m1b[q, nx - 1 - i, 0:1, :] * s + m2b[q, nx - 1 - i, 0:1, :]

        def over_y(i, s):
            return m1a[q, ny - 1 - i, 0:1, :] * s + m2a[q, ny - 1 - i, 0:1, :]

        s = lax.fori_loop(0, nx - 1 - gx, over_x, s)
        s = lax.fori_loop(0, ny - 1 - gy, over_y, s)
        for r in reversed(range(RUNS)):
            cin[q, r:r + 1, :] = s
            s = ach[q, r:r + 1, :] * s + qch[q, r:r + 1, :]

    def pg_mate(u):
        return remote(pgs.at[lax.rem(u, PAIR), 0:tokens], pgm.at[u], ps.at[u], pr.at[u], (mate, gy))

    def backward(u):
        slot, pair = lax.rem(u, SLOTS), lax.rem(u, PAIR)
        q, j = u // GROUP, lax.rem(u, GROUP)
        gain, shift, vr = vec(0, u), vec(1, u), vec(4, u)
        zero = jnp.zeros((RUNS, LANES), F32)

        def step(i, carry):
            c, v2, v3 = carry
            r = pl.ds(pl.multiple_of((double - 1 - i) * 16, 16), 16)
            f = pj[slot, r, LANES:2 * LANES]
            k = keep[r, :]
            rg = pj[slot, r, 2 * LANES:3 * LANES]
            local = gs[r, lanes_of(u)].astype(F32) - grs[r, lanes_of(u)]
            d, through = f * k, k * vr * rg
            grads = [None, None]
            for h in (1, 0):
                part = slice(8 * h, 8 * h + 8)
                grads[h] = local[part] + c
                c = d[part] * grads[h] + through[part]
            grad = jnp.concatenate(grads, 0)
            cg = grad * (1.0 - f)
            fg = cg * (pv[slot, r, :] - pj[slot, r, 0:LANES]) * f
            pgs[pair, r, 0:LANES] = cg.astype(BF16)
            pgs[pair, r, LANES:2 * LANES] = fg.astype(BF16)
            pgs[pair, r, 2 * LANES:3 * LANES] = rg.astype(BF16)
            fs = fg * scale(u, r, gain, shift)
            return c, v2 + fs[0:8] + fs[8:16], v3 + fg[0:8] + fg[8:16]

        _, v2, v3 = lax.fori_loop(0, double, step, (cin[q, :, lanes_of(j)], zero, zero), unroll=4)
        vsum[2:3, lanes_of(u)] = jnp.sum(v2, axis=0, keepdims=True)
        vsum[3:4, lanes_of(u)] = jnp.sum(v3, axis=0, keepdims=True)
        pg_mate(u).start()

    def backward_group(q):
        enter_back(q)
        each(GROUP, lambda j: backward(q * GROUP + j))

    def pg_load(u):
        return pltpu.make_async_copy(pgm.at[u], pgs.at[lax.rem(u, PAIR), tokens:2 * tokens], pl_)

    def back_load(u):
        return pltpu.make_async_copy(wall.at[u], wb, wl)

    def some(part):
        return pl.ds(part * half, half)

    def sent(u):
        return sb.at[lax.rem(u, SEND)]

    def d_copy(u, i):
        return remote(
            sent(u).at[dq, some(i)], rd.at[u, some(i)], fds.at[u, i], fdr.at[u, i], ((yn, xn)[i], gy)
        )

    def x_copy(u, i):
        return remote(sent(u).at[xq, some(i)], rx.at[u, some(i)], fxs.at[u, i], fxr.at[u, i], (xn, gy))

    def y_copy(u, i):
        return remote(sent(u).at[yq, some(i)], ry.at[u, some(i)], fys.at[u, i], fyr.at[u, i], (yn, gy))

    def f_copy(u, j):
        to = lax.rem(gy + j, ny)
        return remote(zb.at[lax.rem(u, ZSEND), to], rz.at[u, j - 1], fzs.at[u, j - 1], fzr.at[u, j - 1], (gx, to))

    def next_loads(u):
        pg_mate(u).wait_recv()
        pg_load(u).start()
        back_load(u).start()

    def weigh(u):
        slot, pair = lax.rem(u, SEND), lax.rem(u, PAIR)

        @pl.when((u >= SEND) & jnp.logical_not(among(u - SEND, turned)))
        def _():
            for i in (0, 1):
                d_copy(u - SEND, i).wait_send()
                x_copy(u - SEND, i).wait_send()
                y_copy(u - SEND, i).wait_send()

        pg_load(u).wait()
        sb[slot] = jnp.dot(rt[...], pgs[pair], preferred_element_type=F32).astype(BF16).reshape(sb.shape[1:])

        @pl.when(jnp.logical_not(among(u, turned)))
        def _():
            for i in (0, 1):
                d_copy(u, i).start()
            x_copy(u, 1).start()
            y_copy(u, 0).start()

    def spread(u):
        pair = lax.rem(u, PAIR)
        back_load(u).wait()
        mine = pgs[pair, 0:tokens, :]
        sg[...] += lax.dot_general(mine, wb[...].reshape(width, -1), (((1,), (1,)), ((), ())), preferred_element_type=F32)
        sg[:, lanes_of(u)] += pgs[pair, 0:tokens, LANES:2 * LANES].astype(F32) * vecs[2:3, lanes_of(u)]
        pg_mate(u).wait_send()

    def fold(ref, at, more):
        ref[at] = (ref[at].astype(F32) + more.astype(F32)).astype(BF16)

    def meet(u):
        slot = lax.rem(u, SEND)
        for i in (0, 1):
            d_copy(u, i).wait_recv()
        fold(sb, (slot, xq, some(0)), rd[u, 0:half])
        x_copy(u, 0).start()
        fold(sb, (slot, yq, some(1)), rd[u, half:ny])
        y_copy(u, 1).start()

    def column(u):
        slot, zslot = lax.rem(u, SEND), lax.rem(u, ZSEND)

        @pl.when((u >= ZSEND) & jnp.logical_not(among(u - ZSEND, turned)))
        def _():
            for j in range(1, ny):
                f_copy(u - ZSEND, j).wait_send()

        for i in (0, 1):
            x_copy(u, i).wait_recv()
            y_copy(u, i).wait_recv()
        total = sb[slot, own].astype(F32) + rx[u].astype(F32) + ry[u].astype(F32)
        zb[zslot] = total.astype(BF16)
        for j in range(1, ny):
            f_copy(u, j).start()

    def settle(u):
        slot = lax.rem(u, SEND)
        total = sb[slot, own, gy].astype(F32) + rx[u, gy].astype(F32) + ry[u, gy].astype(F32)
        for j in range(1, ny):
            f_copy(u, j).wait_recv()
        for j in range(1, ny):
            total = total + rz[u, j - 1].astype(F32)
        place_sum(u, total)

    def place_sum(u, total):
        for i in range(3):
            wgo[:, lanes_of(u + i * units)] = total[:, i * LANES:(i + 1) * LANES]

    def part(i):
        return pl.ds(i * short, short)

    def b_z(u, j):
        to = peer_y(j)
        return remote(sent(u).at[:, to], (rd, rx, ry)[j - 1].at[u], fzs.at[u, j - 1], fzr.at[u, j - 1], (gx, to))

    def b_diag(u, n, i):
        return remote(cz.at[n, dq, part(i)], rz.at[u, 0, part(i)], fds.at[u, i], fdr.at[u, i], ((yn, xn)[i], gy))

    def b_x(u, n, i):
        return remote(cz.at[n, xq, part(i)], rz.at[u, 1, part(i)], fxs.at[u, i], fxr.at[u, i], (xn, gy))

    def b_y(u, n, i):
        return remote(cz.at[n, yq, part(i)], rz.at[u, 2, part(i)], fys.at[u, i], fyr.at[u, i], (yn, gy))

    def b_gather(u, n):
        for j in range(1, ny):
            b_z(u, j).wait()
            if u >= ZSEND and u - ZSEND not in turned:
                f_copy(u - ZSEND, j).wait_send()
        total = sb[lax.rem(u, SEND), :, gy].astype(F32)
        for ref in (rd, rx, ry):
            total = total + ref[u].astype(F32)
        cz[n] = total.astype(BF16)
        for i in (0, 1):
            b_diag(u, n, i).start()
        b_x(u, n, 1).start()
        b_y(u, n, 0).start()

    def b_meet(u, n):
        for i in (0, 1):
            b_diag(u, n, i).wait_recv()
        fold(cz, (n, xq, part(0)), rz[u, 0, part(0)])
        b_x(u, n, 0).start()
        fold(cz, (n, yq, part(1)), rz[u, 0, part(1)])
        b_y(u, n, 1).start()

    def b_settle(u, n):
        for i in (0, 1):
            b_x(u, n, i).wait_recv()
            b_y(u, n, i).wait_recv()
        place_sum(u, cz[n, own].astype(F32) + rz[u, 1].astype(F32) + rz[u, 2].astype(F32))

    def b_drain(u, n):
        for i in (0, 1):
            b_diag(u, n, i).wait_send()
            b_x(u, n, i).wait_send()
            b_y(u, n, i).wait_send()

    def finish(i):
        r = pl.ds(pl.multiple_of(i * BAND, BAND), BAND)
        s = sg[r, :]
        inv = invs[r, 0:1]
        z = (xs[r, :].astype(F32) - means[r, 0:1]) * inv
        sz = s * z
        gain = vecs[0:1, :]
        vrows[0:8, :] += jnp.sum(sz.reshape(BAND // 8, 8, width), axis=0)
        vrows[8:16, :] += jnp.sum(s.reshape(BAND // 8, 8, width), axis=0)
        n = s * gain
        m1 = jnp.mean(n, axis=1, keepdims=True)
        m2 = jnp.mean(sz * gain, axis=1, keepdims=True)
        sg[r, :] = grs[r, :] + inv * (n - m1 - z * m2)

    def v_copy(j):
        to = lax.rem(me + j, count)
        return remote(vtot.at[to // 2], vin.at[me], vsn.at[to], vrc.at[me], (to // ny, lax.rem(to, ny)))

    def v_recv(j):
        at = lax.rem(me + j, count)
        return remote(vtot.at[0], vin.at[at], vsn.at[at], vrc.at[at], (at // ny, lax.rem(at, ny)))

    def vectors_out():
        zero = jnp.zeros((2, LANES), F32)
        for c in range(width // LANES):
            at = slice(c * LANES, (c + 1) * LANES)
            top = [jnp.sum(vrows[8 * v:8 * v + 8, at], axis=0, keepdims=True) for v in (0, 1)]
            vtot[c] = jnp.concatenate(top + [vsum[2:6, at], zero], 0)
        each(count, lambda j: v_copy(j).start(), 1)

    quarter = width // 4

    def grad_copy(c):
        return pltpu.make_async_copy(grs.at[:, pl.ds(c * quarter, quarter)], igo.at[:, pl.ds(c * quarter, quarter)], ous.at[c])

    def natural():
        for c in range(4):
            at = slice(c * quarter, (c + 1) * quarter)
            v = sg[:, at]
            high = v.astype(BF16)
            low = (v - high.astype(F32)).astype(BF16)
            grs[:, at] = jnp.dot(perm[...], high, preferred_element_type=F32) + jnp.dot(
                perm[...], low, preferred_element_type=F32
            )
            grad_copy(c).start()

    def tick(k, _):
        u = k - 3
        v = u - WEIGH
        gather_tick(k)
        pl.when(k == 3)(late_start)
        pl.when(k == 5)(late_turn)

        def summed(lag, run):
            w = v - lag
            pl.when((w >= 0) & (w < units) & jnp.logical_not(among(w, turned)))(lambda: run(w))

        summed(LAG1, meet)
        summed(LAG2, column)
        summed(LAG3, settle)
        for n, (c, _, steps) in enumerate(ACROSS_SUM):
            for t, run in zip(steps, (b_gather, b_meet, b_settle)):
                pl.when(v == t)(functools.partial(run, c, n))

        @pl.when(v == 0)
        def _():
            r_mate.wait_recv()
            sg[...] = jnp.zeros_like(sg)
            vrows[...] = jnp.zeros_like(vrows)

        @pl.when((v >= 0) & (v < units))
        def _():
            weigh(v)
            spread(v)

        for c, times, _ in ACROSS_SUM:
            for j, t in enumerate(times):
                pl.when(v == t)(lambda c=c, j=j: b_z(c, j + 1).start())

        pl.when((v >= -1) & (v < units - 1))(lambda: next_loads(v + 1))

        def event(lag, run):
            g = (u - lag) // GROUP
            pl.when((u >= lag) & (lax.rem(u - lag + GROUP, GROUP) == 0) & (g < groups))(lambda: run(g))

        event(BACK, backward_group)
        event(GRADS, grads_x)
        event(FORE, forward_group)
        event(TOTALS, totals_x)

        @pl.when((u >= 0) & (u < units))
        def _():
            project(u)

        @pl.when((u >= 0) & (u < units - 1))
        def _():
            straight(u + 1, core_wait)
            for c in across:
                pl.when(u + 1 == c)(lambda c=c: a_core(c).wait_recv())
            front_load(u + 1).start()

        @pl.when((u >= 0) & (u < units))
        def _():
            gates(u)
            pl.when(lax.rem(u, GROUP) == GROUP - 1)(lambda: totals(u // GROUP))

        pl.when(v == units)(lambda: each(bands // 2, finish))

        @pl.when(v == units + 1)
        def _():
            each(bands, finish, bands // 2)
            vectors_out()

        pl.when(v == units + 2)(natural)
        return 0

    front_load(0).start()
    lax.fori_loop(3, units + WEIGH + 3 + LAST, tick, 0)

    each(count, lambda j: v_recv(j).wait_recv(), 1)
    vin[me] = vtot[me // 2]
    vgo[...] = lax.fori_loop(0, count, lambda j, s: s + vin[j], jnp.zeros((8, LANES), F32))

    def drain(u):
        for j in range(1, ny):
            z_copy(u, j).wait_send()
        for i in range(3):
            band_copy(u, i).wait_send()
        for i in (0, 1):
            diag_copy(u, i).wait_send()
        for i in (1, 2, 3):
            core_copy(u, i).wait_send()

    each(units, lambda u: straight(u, drain))
    for c in across:
        for j in range(1, ny):
            a_z(c, j).wait_send()
        for i in (1, 2):
            a_copy(c, i).wait_send()
        for i in (0, 1):
            a_diag(c, i).wait_send()
        a_core(c).wait_send()
    for n, c in enumerate(turned):
        b_drain(c, n)

    def drain_send(u):
        for i in (0, 1):
            d_copy(u, i).wait_send()
            x_copy(u, i).wait_send()
            y_copy(u, i).wait_send()

    each(units, lambda u: pl.when(jnp.logical_not(among(u, turned)))(lambda: drain_send(u)), units - SEND)

    def drain_z(u):
        for j in range(1, ny):
            f_copy(u, j).wait_send()

    each(units, drain_z, units - ZSEND)

    def drain_group(q):
        for a in ((m1a, e1as, e1ar, q, 0), (m1b, e1bs, e1br, q, 1), (m2a, e2as, e2ar, q, 0), (m2b, e2bs, e2br, q, 1)):
            for c in e_copies(*a):
                c.wait_send()

    each(groups, drain_group)
    for q in range(groups - 2, groups):
        out_copy(q).wait()
    for j in range(1, ny):
        vz(j).wait_send()
    for j in range(1, nx):
        vx(j).wait_send()
    r_mate.wait_send()
    each(count, lambda j: v_copy(j).wait_send(), 1)
    for c in range(4):
        grad_copy(c).wait()


def layer(nx, ny, tok, cot, mask, weight, vectors):
    tokens, width = tok.shape
    rows, cols = weight.shape[0], 3 * LANES
    units = width // LANES
    groups, glanes, block, count = units // GROUP, GROUP * LANES, rows * ny, nx * ny
    dma = pltpu.SemaphoreType.DMA
    any_, vmem = pl.BlockSpec(memory_space=pl.ANY), pl.BlockSpec(memory_space=pltpu.VMEM)
    msg = RUNS, glanes
    s, v = jax.ShapeDtypeStruct, pltpu.VMEM
    return pl.pallas_call(
        functools.partial(layer_kernel, nx, ny, units),
        name="layer",
        out_shape=(
            s((units, nx // 2, 2, ny, rows, cols), BF16), s((units, tokens, cols), BF16),
            s((tokens, width), BF16), s((tokens, width), F32), s((rows, 3 * width), F32), s((8, LANES), F32),
        ),
        in_specs=[any_, any_, vmem, any_, vmem],
        out_specs=(any_,) * 4 + (vmem,) * 2,
        scratch_shapes=[
            v((count, 16, LANES), BF16), v((8, width), F32),
            v((tokens, width), BF16), v((tokens, width), BF16), v((tokens, LANES), F32), v((tokens, LANES), F32),
            v((tokens, width), BF16), v((width // 2, 2 * tokens), BF16), v((width // 2, tokens), BF16),
            v((nx // 2, 2, ny, rows, cols), BF16),
            v((SLOTS, tokens, cols), F32), v((SLOTS, tokens, LANES), F32),
            v((tokens, width), F32), v((tokens, glanes), BF16), v((2, tokens, glanes), BF16),
            v((tokens, tokens), BF16), v((PAIR, 2 * tokens, cols), BF16),
            v((nx // 2, 2, ny, rows, cols), BF16), v((SEND, nx // 2, ny, rows, cols), BF16),
            *[v((units, ny, rows, cols), BF16)] * 3,
            v((units, ny - 1, rows, cols), BF16), v((ZSEND, ny, rows, cols), BF16),
            v((tokens, width), F32), v((8, width), F32), v((16, width), F32),
            v((width // LANES, 8, LANES), F32), v((count, 8, LANES), F32),
            v((max(1, len(ACROSS_SUM)), nx // 2, rows, cols), BF16), v((tokens, LANES), F32),
            v((rows, 3 * width), BF16), v((units, rows, cols), BF16), v((16, LANES), BF16),
            *[v((groups,) + msg, F32)] * 5,
            v((groups, ny, 2, glanes), F32), v((groups, nx, 2, glanes), F32),
            v((groups, ny, 1, glanes), F32), v((groups, nx, 1, glanes), F32),
            dma((units, ny - 1)), dma((units, ny - 1)), dma((units,)), dma((units, 3)), dma((units, 2)),
            dma((units, 2)), dma((units, 2)), dma((units, 3)), dma((units, 4)), dma,
            dma((ny - 1,)), dma((ny - 1,)), dma((nx - 1,)), dma((nx - 1,)), dma, dma, dma((2,)),
            dma, dma, dma((units,)), dma((units,)), dma, dma, dma((groups,)),
            dma((groups, ny - 1)), dma((groups, ny - 1)), dma((groups, nx - 1)), dma((groups, nx - 1)),
            dma((groups, ny - 1)), dma((groups, ny - 1)), dma((groups, nx - 1)), dma((groups, nx - 1)),
            *[dma((units, 2))] * 6, dma((units, ny - 1)), dma((units, ny - 1)),
            dma((count,)), dma((count,)), dma((4,)),
        ],
        compiler_params=pltpu.CompilerParams(
            collective_id=0, has_side_effects=True, vmem_limit_bytes=62 * 2**20
        ),
        cost_estimate=pl.CostEstimate(
            flops=6 * tokens * width * units * cols, bytes_accessed=4 * width * units * cols, transcendentals=0
        ),
    )(tok, cot, mask, weight, vectors)


def fast(nx, ny, tokens, reset_mask, weight, vectors, cotangent):
    rows = weight.shape[0]
    odd = lax.rem(lax.axis_index("gx") * ny + lax.axis_index("gy"), 2) == 1
    mask = reset_mask.reshape(1, -1)
    _, _, outp, grad, weight_grad, tile = layer(nx, ny, tokens, cotangent, mask, weight, vectors)
    vector_grad = jnp.where(odd, tile[:6, rows:2 * rows], tile[:6, :rows])
    return outp, grad, weight_grad, vector_grad


def solution(mesh):
    placed = (
        P(("gx", "gy"), None),
        P(("gx", "gy")),
        P(("gx", "gy"), None),
        P(None, ("gx", "gy")),
        P(("gx", "gy"), None),
    )
    nx, ny = mesh.shape["gx"], mesh.shape["gy"]

    def body(tokens, reset_mask, weight, vectors, cotangent):
        whole_tiles = weight.shape[0] % 16 == 0 and tokens.shape[0] % 256 == 0
        if (nx, ny) == (8, 4) and whole_tiles and 2 * weight.shape[0] == LANES and tokens.shape[1] % 2048 == 0:
            return fast(nx, ny, tokens, reset_mask, weight, vectors, cotangent)
        return local(tokens, reset_mask, weight, vectors, cotangent)

    return jax.shard_map(
        body,
        mesh=mesh,
        in_specs=placed,
        out_specs=(
            P(("gx", "gy"), None),
            P(("gx", "gy"), None),
            P(("gx", "gy"), None),
            P(None, ("gx", "gy")),
        ),
        check_vma=False,
    )
```

```python
import functools

import jax
import jax.numpy as jnp
from jax import lax
from jax.experimental import pallas as pl
from jax.experimental.pallas import tpu as pltpu
from jax.sharding import PartitionSpec as P

MESH = pl.DeviceIdType.MESH
F32, BF16 = jnp.float32, jnp.bfloat16
LANES, RUNS, GROUP = 128, 8, 2
EPS = 1e-05


def place(ny):
    gx, gy = lax.axis_index("gx"), lax.axis_index("gy")
    core, xx, yy = lax.rem(gx, 2), lax.rem(gx // 2, 2), gx // 4
    return gx, gy, core, gx + 1 - 2 * core, gx + 2 - 4 * xx, gx + 4 - 8 * yy


def remote(src, dst, send, recv, to):
    return pltpu.make_async_remote_copy(
        src_ref=src, dst_ref=dst, send_sem=send, recv_sem=recv, device_id=to, device_id_type=MESH
    )


def lanes_of(b):
    return pl.ds(pl.multiple_of(b * LANES, LANES), LANES)


def run_matrix(tokens, back):
    steps = tokens // RUNS
    row = lax.broadcasted_iota(jnp.int32, (tokens, tokens), 0)
    col = lax.broadcasted_iota(jnp.int32, (tokens, tokens), 1)
    if back:
        hit = row == (col & (RUNS - 1)) * steps + (col >> 3)
    else:
        hit = col == (row & (RUNS - 1)) * steps + (row >> 3)
    return jnp.where(hit, 1.0, 0.0).astype(BF16)


def entering(value, axis, join, neutral, backward):
    count, mine = (lax.axis_size(axis), lax.axis_index(axis))
    pieces = jax.tree.map(lambda part: lax.all_gather(part, axis), value)
    if backward:
        pieces = jax.tree.map(lambda part: part[::-1], pieces)
        mine = count - 1 - mine
    subtotal = jax.tree.map(
        lambda part, zero: jnp.full_like(part, 0) + jnp.asarray(zero, part.dtype), value, neutral
    )

    def lap(position, subtotal):
        longer = join(subtotal, jax.tree.map(lambda part: part[position], pieces))
        return jax.tree.map(lambda new, old: jnp.where(position < mine, new, old), longer, subtotal)

    return lax.fori_loop(0, count - 1, lap, subtotal)


def from_behind(block, axis, distance):
    devices = range(lax.axis_size(axis))
    route = [(i - distance, i) for i in devices if i - distance in devices]
    return lax.ppermute(block, axis, route)


def compose(earlier, later):
    return (earlier[0] * later[0], later[0] * earlier[1] + later[1])


def local(tokens, reset_mask, weight, vectors, cotangent):
    width = weight.shape[1] // 3
    whole_weight, whole_vectors = (
        lax.all_gather(weight, ("gx", "gy"), axis=0, tiled=True),
        lax.all_gather(vectors, ("gx", "gy"), axis=1, tiled=True),
    )
    params = whole_vectors.astype(jnp.float32)
    gain = params[0]
    shift_bias = params[1]
    forget_peep = params[2]
    forget_bias = params[3]
    reset_peep = params[4]
    reset_bias = params[5]
    inputs = tokens.astype(jnp.float32)
    keep = (1 - reset_mask).astype(jnp.float32)[:, None]
    centred = inputs - jnp.mean(inputs, axis=1, keepdims=True)
    inv_std = lax.rsqrt(jnp.mean(centred * centred, axis=1, keepdims=True) + 1e-05)
    normed = centred * inv_std
    scaled = normed * gain + shift_bias
    rounded = scaled.astype(jnp.bfloat16)
    projected = jnp.dot(rounded, whole_weight, preferred_element_type=jnp.float32)
    candidate = projected[:, :width]
    forget_pre = projected[:, width : 2 * width]
    reset_pre = projected[:, 2 * width :]
    forget = jax.nn.sigmoid(forget_pre + forget_peep * scaled + forget_bias)
    decay = forget * keep
    inflow = (1.0 - forget) * candidate
    cum_decay, cum_state = lax.associative_scan(compose, (decay, inflow), axis=0)
    unit = (jnp.ones_like(cum_decay[-1]), jnp.zeros_like(cum_state[-1]))
    before = entering((cum_decay[-1], cum_state[-1]), ("gx", "gy"), compose, unit, False)
    state_in = before[1]
    state = cum_decay * state_in + cum_state
    previous = keep * jnp.concatenate([state_in[None], state[:-1]], 0)
    reset = jax.nn.sigmoid(reset_pre + reset_peep * previous + reset_bias)
    output = reset * state + (1.0 - reset) * inputs
    upstream = cotangent.astype(jnp.float32)
    reset_grad = upstream * (state - inputs) * reset * (1.0 - reset)
    through = keep * reset_peep * reset_grad
    next_decay, next_through = from_behind((decay[0], through[0]), ("gx", "gy"), -1)
    ahead = jnp.concatenate([decay[1:], next_decay[None]], 0)
    local_term = upstream * reset + jnp.concatenate([through[1:], next_through[None]], 0)
    flip_mult, flip_sum = lax.associative_scan(compose, (ahead[::-1], local_term[::-1]), axis=0)
    mult_back = flip_mult[::-1]
    sum_back = flip_sum[::-1]
    after = entering((mult_back[0], sum_back[0]), ("gx", "gy"), compose, unit, True)
    state_grad = mult_back * after[1] + sum_back
    candidate_grad = state_grad * (1.0 - forget)
    forget_grad = state_grad * (previous - candidate) * forget * (1.0 - forget)
    proj_grad = jnp.concatenate([candidate_grad, forget_grad, reset_grad], 1).astype(jnp.bfloat16)
    weight_grad = lax.psum_scatter(
        lax.dot_general(
            rounded, proj_grad, (((0,), (0,)), ((), ())), preferred_element_type=jnp.float32
        ),
        ("gx", "gy"),
        scatter_dimension=0,
        tiled=True,
    )
    scaled_grad = lax.dot_general(
        proj_grad,
        lax.all_gather(weight, ("gx", "gy"), axis=0, tiled=True),
        (((1,), (1,)), ((), ())),
        preferred_element_type=jnp.float32,
    )
    scaled_grad = scaled_grad + forget_grad * forget_peep
    vector_terms = jnp.stack(
        [
            jnp.sum(scaled_grad * normed, axis=0),
            jnp.sum(scaled_grad, axis=0),
            jnp.sum(forget_grad * scaled, axis=0),
            jnp.sum(forget_grad, axis=0),
            jnp.sum(reset_grad * previous, axis=0),
            jnp.sum(reset_grad, axis=0),
        ],
        0,
    )
    vector_grad = lax.psum_scatter(vector_terms, ("gx", "gy"), scatter_dimension=1, tiled=True)
    normed_grad = scaled_grad * gain
    input_grad = upstream * (1.0 - reset) + inv_std * (
        normed_grad
        - jnp.mean(normed_grad, axis=1, keepdims=True)
        - normed * jnp.mean(normed_grad * normed, axis=1, keepdims=True)
    )
    return (output.astype(jnp.bfloat16), input_grad, weight_grad, vector_grad)


SLOTS, SEND, PAIR, ZSEND = 8, 8, 4, 4
TOTALS, FORE, GRADS, BACK, WEIGH = 2, 4, 5, 7, 9
LAG1, LAG2, LAG3 = 2, 4, 6
LAST = 6
AHEAD_Z, AHEAD_B = 5, 3
BAND = 32
ACROSS = ((10, (0, 3, 6)), (15, (8, 11, 13)))
ACROSS_SUM = ()


def layer_kernel(
    nx, ny, units,
    tok, cot, mask, weight, vectors,
    wall, pgm, outp, igo, wgo, vgo,
    vbuf, vecs, xs, gs, means, invs, rnd, rt, rtm, wf, pj, pv, grs, outs, stage, perm, pgs,
    wb, sb, rd, rx, ry, rz, zb, sg, vsum, vrows, vtot, vin, cz, keep, wraw, wsrc, vsrc,
    ach, bch, qch, sin, cin, m1a, m1b, m2a, m2b,
    zs, zr, os, bs, br, dsn, dr, cs, cr, ws,
    vzs, vzr, vxs, vxr, vo, wls, sts, rs, rr, ps, pr, pl_, wl, gos,
    e1as, e1ar, e1bs, e1br, e2as, e2ar, e2bs, e2br,
    fds, fdr, fxs, fxr, fys, fyr, fzs, fzr, vsn, vrc, ous,
):
    gx, gy, core, mate, xn, yn = place(ny)
    tokens, width = xs.shape
    rows = wsrc.shape[1]
    cols = wsrc.shape[2]
    block = rows * ny
    half, short = ny // 2, rows // 2
    groups = units // GROUP
    glanes = GROUP * LANES
    diag = xn + yn - gx
    own, xq, yq, dq = gx // 2, xn // 2, yn // 2, diag // 2
    count = nx * ny
    me = gx * ny + gy

    def peer_y(j):
        return lax.rem(gy + j, ny)

    def peer_x(j):
        return lax.rem(gx + j, nx)

    def each(n, run, start=0):
        lax.fori_loop(start, n, lambda i, _: (run(i), 0)[1], 0)

    barrier = pltpu.get_barrier_semaphore()

    def greet(j):
        to = lax.rem(me + j, count)
        pl.semaphore_signal(barrier, inc=1, device_id=(to // ny, lax.rem(to, ny)), device_id_type=MESH)

    raw = pltpu.make_async_copy(weight, wraw, wls)
    raw.start()
    each(count, greet, 1)

    def among(u, some):
        hit = u < 0
        for s in some:
            hit = hit | (u == s)
        return hit

    across = tuple(c for c, _ in ACROSS)
    turned = tuple(c for c, _, _ in ACROSS_SUM)

    def straight(u, run):
        pl.when(jnp.logical_not(among(u, across)))(lambda: run(u))

    chunks = width // glanes

    tok_load = pltpu.make_async_copy(tok, xs, sts.at[0])
    cot_load = pltpu.make_async_copy(cot, gs, sts.at[1])
    tok_load.start()
    cot_load.start()

    def vz(j):
        return remote(vsrc, vbuf.at[me], vzs.at[j - 1], vzr.at[j - 1], (gx, peer_y(j)))

    def vx(j):
        part = vbuf.at[pl.ds(gx * ny, ny)]
        return remote(part, part, vxs.at[j - 1], vxr.at[j - 1], (peer_x(j), gy))

    own_vec = pltpu.make_async_copy(vsrc, vbuf.at[me], vo)

    def z_copy(u, j):
        return remote(wsrc.at[u], wall.at[u, own, core, gy], zs.at[u, j - 1], zr.at[u, j - 1], (gx, peer_y(j)))

    def own_copy(u):
        return pltpu.make_async_copy(wsrc.at[u], wall.at[u, own, core, gy], os.at[u])

    def band_copy(u, i):
        to = (mate, xn, yn)[i]
        recv = cr.at[u, 0] if i == 0 else br.at[u, i - 1]
        part = wall.at[u, own, core]
        return remote(part, part, bs.at[u, i], recv, (to, gy))

    def diag_copy(u, i):
        part = wall.at[u, (xq, yq)[i], core, half * i:half * (i + 1)]
        return remote(part, part, dsn.at[u, i], dr.at[u, i], ((yn, xn)[i], gy))

    def core_copy(u, i):
        part = wall.at[u, (own, xq, yq, dq)[i], core]
        return remote(part, part, cs.at[u, i - 1], cr.at[u, i], (mate, gy))

    def z_start(u):
        own_copy(u).start()
        for j in range(1, ny):
            z_copy(u, j).start()

    def z_wait(u):
        own_copy(u).wait()
        for j in range(1, ny):
            z_copy(u, j).wait_recv()
        for i in (1, 2, 0):
            band_copy(u, i).start()

    def xy_wait(u):
        for i in (1, 2):
            band_copy(u, i).wait_recv()
        for i in (0, 1):
            diag_copy(u, i).start()
        for i in (1, 2):
            core_copy(u, i).start()

    def diag_wait(u):
        for i in (0, 1):
            diag_copy(u, i).wait_recv()
        core_copy(u, 3).start()

    def core_wait(u):
        band_copy(u, 0).wait_recv()
        for i in (1, 2, 3):
            core_copy(u, i).wait_recv()

    def a_copy(u, i):
        return remote(
            wsrc.at[u], wall.at[u, own, core, gy], bs.at[u, i], br.at[u, i - 1], ((None, xn, yn)[i], gy)
        )

    def a_diag(u, i):
        part = wall.at[u, (xq, yq)[i], core, gy, short * i:short * (i + 1)]
        return remote(part, part, dsn.at[u, i], dr.at[u, i], ((yn, xn)[i], gy))

    def a_z(u, j):
        part = wall.at[u, :, core, gy]
        return remote(part, part, zs.at[u, j - 1], zr.at[u, j - 1], (gx, peer_y(j)))

    def a_core(u):
        part = wall.at[u, :, core]
        return remote(part, part, bs.at[u, 0], cr.at[u, 0], (mate, gy))

    def a_start(u):
        own_copy(u).start()
        for i in (1, 2):
            a_copy(u, i).start()

    def a_turn(u):
        own_copy(u).wait()
        for i in (1, 2):
            a_copy(u, i).wait_recv()
        for i in (0, 1):
            a_diag(u, i).start()

    def a_meet(u):
        for i in (0, 1):
            a_diag(u, i).wait_recv()

    def a_share(u):
        for j in range(1, ny):
            a_z(u, j).wait_recv()
        a_core(u).start()

    zero = jnp.zeros((vectors.shape[0], LANES - rows), BF16)
    odd = lax.rem(me, 2) == 1
    tile = jnp.where(
        odd, jnp.concatenate([zero, vectors[...]], 1).astype(F32), jnp.concatenate([vectors[...], zero], 1).astype(F32)
    )
    pad = jnp.zeros((16 - vectors.shape[0], LANES), F32)
    vsrc[...] = jnp.concatenate([tile, pad], 0).astype(BF16)
    raw.wait()
    for u in range(units):
        for s in range(3):
            at = s * width + u * LANES
            wsrc[u, :, s * LANES:(s + 1) * LANES] = wraw[:, at:at + LANES]

    pl.semaphore_wait(barrier, count - 1)
    own_vec.start()
    for j in range(1, ny):
        vz(j).start()
    for u in across:
        a_start(u)
    z_start(0)

    def to_runs(i, into):
        at = slice(i * glanes, (i + 1) * glanes)
        into[:, at] = jnp.dot(perm[...], into[:, at], preferred_element_type=F32).astype(BF16)

    def moments(i):
        r = pl.ds(pl.multiple_of(i * BAND, BAND), BAND)
        x = xs[r, :].astype(F32)
        mean = jnp.mean(x, axis=1, keepdims=True)
        centred = x - mean
        inv = lax.rsqrt(jnp.mean(centred * centred, axis=1, keepdims=True) + EPS)
        means[r, :] = jnp.broadcast_to(mean, (BAND, LANES))
        invs[r, :] = jnp.broadcast_to(inv, (BAND, LANES))

    def rounding(i):
        r = pl.ds(pl.multiple_of(i * BAND, BAND), BAND)
        normed = (xs[r, :].astype(F32) - means[r, 0:1]) * invs[r, 0:1]
        rnd[r, :] = (normed * vecs[0:1, :] + vecs[1:2, :]).astype(BF16)

    quads = nx // 2

    def turn(i):
        at = pl.ds(pl.multiple_of(i * block, 16), block)
        rt[at, 0:tokens] = rnd[:, pl.ds(pl.multiple_of((2 * i + core) * block, LANES), block)].T
        rtm[at, :] = rnd[:, pl.ds(pl.multiple_of((2 * i + 1 - core) * block, LANES), block)].T

    r_mate = remote(rtm, rt.at[:, tokens:2 * tokens], rs, rr, (mate, gy))

    def gather_tick(k):
        pl.when(k + AHEAD_Z < units)(lambda: straight(k + AHEAD_Z, z_start))
        pl.when(k + AHEAD_B < units)(lambda: straight(k + AHEAD_B, z_wait))
        pl.when(k < units)(lambda: straight(k, xy_wait))
        pl.when((k >= 1) & (k <= units))(lambda: straight(k - 1, diag_wait))
        for c, times in ACROSS:
            for j, t in enumerate(times):
                pl.when(k == t)(lambda c=c, j=j: a_z(c, j + 1).start())
            pl.when(k == c + 1)(functools.partial(a_share, c))

    bands = tokens // BAND
    perm[...] = run_matrix(tokens, False)
    tok_load.wait()
    for i in range(chunks // 2):
        to_runs(i, xs)
    z_wait(0)
    z_start(1)
    z_start(2)
    for i in range(chunks // 2, chunks):
        to_runs(i, xs)
    own_vec.wait()
    for j in range(1, ny):
        vz(j).wait_recv()
    for j in range(1, nx):
        vx(j).start()
    for u in across:
        a_turn(u)
    z_wait(1)
    for u in range(3, AHEAD_Z):
        z_start(u)
    each(bands // 2, moments)
    for u in range(2, AHEAD_B):
        z_wait(u)
    for u in across:
        a_meet(u)
    gather_tick(0)
    each(bands, moments, bands // 2)
    for j in range(1, nx):
        vx(j).wait_recv()
    for c in range(width // LANES):
        part = vbuf[2 * c].astype(F32) + vbuf[2 * c + 1].astype(F32)
        vecs[:, c * LANES:(c + 1) * LANES] = part[0:8, :]
    each(bands // 2, rounding)
    gather_tick(1)
    each(bands, rounding, bands // 2)
    kept = (1 - mask[...]).astype(F32)
    keep[...] = jnp.dot(
        (perm[...].astype(F32) * kept).astype(BF16), jnp.ones((tokens, LANES), BF16), preferred_element_type=F32
    )
    cot_load.wait()
    for i in range(chunks // 2):
        to_runs(i, gs)
    gather_tick(2)
    straight(0, core_wait)

    def late_start():
        for i in range(chunks // 2, chunks):
            to_runs(i, gs)
        perm[...] = run_matrix(tokens, True)

    def late_turn():
        each(quads, turn)
        r_mate.start()

    def e_copies(buf, send, recv, q, level):
        if level == 0:
            return [
                remote(buf.at[q, gy], buf.at[q, gy], send.at[q, j - 1], recv.at[q, j - 1], (gx, peer_y(j)))
                for j in range(1, ny)
            ]
        return [
            remote(buf.at[q, gx], buf.at[q, gx], send.at[q, j - 1], recv.at[q, j - 1], (peer_x(j), gy))
            for j in range(1, nx)
        ]

    def e_start(*a):
        for c in e_copies(*a):
            c.start()

    def e_wait(*a):
        for c in e_copies(*a):
            c.wait_recv()

    double = tokens // (2 * RUNS)

    def front_load(u):
        return pltpu.make_async_copy(wall.at[u], wf, ws)

    def project(u):
        front_load(u).wait()
        pj[lax.rem(u, SLOTS)] = jnp.dot(rnd[...], wf[...].reshape(width, -1), preferred_element_type=F32)

    def vec(i, u):
        return vecs[i:i + 1, lanes_of(u)]

    def scale(u, r, gain, shift):
        return (xs[r, lanes_of(u)].astype(F32) - means[r, :]) * invs[r, :] * gain + shift

    def gates(u):
        slot = lax.rem(u, SLOTS)
        gain, shift, vf, bf = (vec(i, u) for i in range(4))

        def step(i, carry):
            a, b = carry
            r = pl.ds(pl.multiple_of(i * 16, 16), 16)
            f = jax.nn.sigmoid(pj[slot, r, LANES:2 * LANES] + vf * scale(u, r, gain, shift) + bf)
            pj[slot, r, LANES:2 * LANES] = f
            d = f * keep[r, :]
            inflow = (1.0 - f) * pj[slot, r, 0:LANES]
            for h in (0, 8):
                a = a * d[h:h + 8]
                b = d[h:h + 8] * b + inflow[h:h + 8]
            return a, b

        a, b = lax.fori_loop(0, double, step, (jnp.ones((RUNS, LANES), F32), jnp.zeros((RUNS, LANES), F32)), unroll=4)
        q, j = u // GROUP, lax.rem(u, GROUP)
        ach[q, :, lanes_of(j)] = a
        bch[q, :, lanes_of(j)] = b

    def totals(q):
        a, b = jnp.ones((1, glanes), F32), jnp.zeros((1, glanes), F32)
        for s in range(RUNS):
            one = ach[q, s:s + 1, :]
            a = a * one
            b = one * b + bch[q, s:s + 1, :]
        m1a[q, gy, 0:1, :] = a
        m1a[q, gy, 1:2, :] = b
        e_start(m1a, e1as, e1ar, q, 0)

    def totals_x(q):
        e_wait(m1a, e1as, e1ar, q, 0)
        a, b = jnp.ones((1, glanes), F32), jnp.zeros((1, glanes), F32)
        for s in range(ny):
            one = m1a[q, s, 0:1, :]
            a = a * one
            b = one * b + m1a[q, s, 1:2, :]
        m1b[q, gx, 0:1, :] = a
        m1b[q, gx, 1:2, :] = b
        e_start(m1b, e1bs, e1br, q, 1)

    def enter(q):
        e_wait(m1b, e1bs, e1br, q, 1)
        s = jnp.zeros((1, glanes), F32)
        s = lax.fori_loop(0, gx, lambda i, s: m1b[q, i, 0:1, :] * s + m1b[q, i, 1:2, :], s)
        s = lax.fori_loop(0, gy, lambda i, s: m1a[q, i, 0:1, :] * s + m1a[q, i, 1:2, :], s)
        for r in range(RUNS):
            sin[q, r:r + 1, :] = s
            s = ach[q, r:r + 1, :] * s + bch[q, r:r + 1, :]

    def forward(u):
        slot = lax.rem(u, SLOTS)
        q, j = u // GROUP, lax.rem(u, GROUP)
        vr, br_ = vec(4, u), vec(5, u)
        zero = jnp.zeros((RUNS, LANES), F32)

        def step(i, carry):
            s, run, t, v4, v5 = carry
            r = pl.ds(pl.multiple_of(i * 16, 16), 16)
            f = pj[slot, r, LANES:2 * LANES]
            k = keep[r, :]
            inflow = (1.0 - f) * pj[slot, r, 0:LANES]
            prevs, states = [], []
            for h in (0, 8):
                prev = k[h:h + 8] * s
                s = f[h:h + 8] * prev + inflow[h:h + 8]
                prevs.append(prev)
                states.append(s)
            prev, state = jnp.concatenate(prevs, 0), jnp.concatenate(states, 0)
            x = xs[r, lanes_of(u)].astype(F32)
            up = gs[r, lanes_of(u)].astype(F32)
            reset = jax.nn.sigmoid(pj[slot, r, 2 * LANES:3 * LANES] + vr * prev + br_)
            rest = 1.0 - reset
            outs[r, lanes_of(j)] = (reset * state + rest * x).astype(BF16)
            rg = up * (state - x) * reset * rest
            pj[slot, r, 2 * LANES:3 * LANES] = rg
            pv[slot, r, :] = prev
            grs[r, lanes_of(u)] = up * rest
            local = up * reset
            d, through = f * k, k * vr * rg
            for h in (0, 8):
                t = t + run * through[h:h + 8]
                run = run * d[h:h + 8]
                t = t + run * local[h:h + 8]
                v4 = v4 + rg[h:h + 8] * prev[h:h + 8]
                v5 = v5 + rg[h:h + 8]
            return s, run, t, v4, v5

        init = (sin[q, :, lanes_of(j)], jnp.ones((RUNS, LANES), F32), zero, zero, zero)
        _, _, t, v4, v5 = lax.fori_loop(0, double, step, init, unroll=4)
        qch[q, :, lanes_of(j)] = t
        vsum[4:5, lanes_of(u)] = jnp.sum(v4, axis=0, keepdims=True)
        vsum[5:6, lanes_of(u)] = jnp.sum(v5, axis=0, keepdims=True)

    def out_copy(q):
        c = pl.ds(pl.multiple_of(q * glanes, LANES), glanes)
        return pltpu.make_async_copy(stage.at[lax.rem(q, 2)], outp.at[:, c], gos.at[q])

    def forward_group(q):
        enter(q)
        pl.when(q >= 2)(lambda: out_copy(q - 2).wait())
        each(GROUP, lambda j: forward(q * GROUP + j))
        s = jnp.zeros((1, glanes), F32)
        for r in reversed(range(RUNS)):
            s = ach[q, r:r + 1, :] * s + qch[q, r:r + 1, :]
        m2a[q, gy, 0:1, :] = s
        e_start(m2a, e2as, e2ar, q, 0)
        stage[lax.rem(q, 2)] = jnp.dot(perm[...], outs[...], preferred_element_type=F32).astype(BF16)
        out_copy(q).start()

    def grads_x(q):
        e_wait(m2a, e2as, e2ar, q, 0)
        s = jnp.zeros((1, glanes), F32)
        for r in reversed(range(ny)):
            s = m1a[q, r, 0:1, :] * s + m2a[q, r, 0:1, :]
        m2b[q, gx, 0:1, :] = s
        e_start(m2b, e2bs, e2br, q, 1)

    def enter_back(q):
        e_wait(m2b, e2bs, e2br, q, 1)
        s = jnp.zeros((1, glanes), F32)

        def over_x(i, s):
            return m1b[q, nx - 1 - i, 0:1, :] * s + m2b[q, nx - 1 - i, 0:1, :]

        def over_y(i, s):
            return m1a[q, ny - 1 - i, 0:1, :] * s + m2a[q, ny - 1 - i, 0:1, :]

        s = lax.fori_loop(0, nx - 1 - gx, over_x, s)
        s = lax.fori_loop(0, ny - 1 - gy, over_y, s)
        for r in reversed(range(RUNS)):
            cin[q, r:r + 1, :] = s
            s = ach[q, r:r + 1, :] * s + qch[q, r:r + 1, :]

    def pg_mate(u):
        return remote(pgs.at[lax.rem(u, PAIR), 0:tokens], pgm.at[u], ps.at[u], pr.at[u], (mate, gy))

    def backward(u):
        slot, pair = lax.rem(u, SLOTS), lax.rem(u, PAIR)
        q, j = u // GROUP, lax.rem(u, GROUP)
        gain, shift, vr = vec(0, u), vec(1, u), vec(4, u)
        zero = jnp.zeros((RUNS, LANES), F32)

        def step(i, carry):
            c, v2, v3 = carry
            r = pl.ds(pl.multiple_of((double - 1 - i) * 16, 16), 16)
            f = pj[slot, r, LANES:2 * LANES]
            k = keep[r, :]
            rg = pj[slot, r, 2 * LANES:3 * LANES]
            local = gs[r, lanes_of(u)].astype(F32) - grs[r, lanes_of(u)]
            d, through = f * k, k * vr * rg
            grads = [None, None]
            for h in (1, 0):
                part = slice(8 * h, 8 * h + 8)
                grads[h] = local[part] + c
                c = d[part] * grads[h] + through[part]
            grad = jnp.concatenate(grads, 0)
            cg = grad * (1.0 - f)
            fg = cg * (pv[slot, r, :] - pj[slot, r, 0:LANES]) * f
            pgs[pair, r, 0:LANES] = cg.astype(BF16)
            pgs[pair, r, LANES:2 * LANES] = fg.astype(BF16)
            pgs[pair, r, 2 * LANES:3 * LANES] = rg.astype(BF16)
            fs = fg * scale(u, r, gain, shift)
            return c, v2 + fs[0:8] + fs[8:16], v3 + fg[0:8] + fg[8:16]

        _, v2, v3 = lax.fori_loop(0, double, step, (cin[q, :, lanes_of(j)], zero, zero), unroll=4)
        vsum[2:3, lanes_of(u)] = jnp.sum(v2, axis=0, keepdims=True)
        vsum[3:4, lanes_of(u)] = jnp.sum(v3, axis=0, keepdims=True)
        pg_mate(u).start()

    def backward_group(q):
        enter_back(q)
        each(GROUP, lambda j: backward(q * GROUP + j))
        drain_group(q)

    def pg_load(u):
        return pltpu.make_async_copy(pgm.at[u], pgs.at[lax.rem(u, PAIR), tokens:2 * tokens], pl_)

    def back_load(u):
        return pltpu.make_async_copy(wall.at[u], wb, wl)

    def some(part):
        return pl.ds(part * half, half)

    def sent(u):
        return sb.at[lax.rem(u, SEND)]

    def d_copy(u, i):
        return remote(
            sent(u).at[dq, some(i)], rd.at[u, some(i)], fds.at[u, i], fdr.at[u, i], ((yn, xn)[i], gy)
        )

    def x_copy(u, i):
        return remote(sent(u).at[xq, some(i)], rx.at[u, some(i)], fxs.at[u, i], fxr.at[u, i], (xn, gy))

    def y_copy(u, i):
        return remote(sent(u).at[yq, some(i)], ry.at[u, some(i)], fys.at[u, i], fyr.at[u, i], (yn, gy))

    def f_copy(u, j):
        to = lax.rem(gy + j, ny)
        return remote(zb.at[lax.rem(u, ZSEND), to], rz.at[u, j - 1], fzs.at[u, j - 1], fzr.at[u, j - 1], (gx, to))

    def next_loads(u):
        pg_mate(u).wait_recv()
        pg_load(u).start()
        back_load(u).start()

    def weigh(u):
        slot, pair = lax.rem(u, SEND), lax.rem(u, PAIR)

        @pl.when((u >= SEND) & jnp.logical_not(among(u - SEND, turned)))
        def _():
            for i in (0, 1):
                d_copy(u - SEND, i).wait_send()
                x_copy(u - SEND, i).wait_send()
                y_copy(u - SEND, i).wait_send()

        pg_load(u).wait()
        sb[slot] = jnp.dot(rt[...], pgs[pair], preferred_element_type=F32).astype(BF16).reshape(sb.shape[1:])

        @pl.when(jnp.logical_not(among(u, turned)))
        def _():
            for i in (0, 1):
                d_copy(u, i).start()
            x_copy(u, 1).start()
            y_copy(u, 0).start()

    def spread(u):
        pair = lax.rem(u, PAIR)
        back_load(u).wait()
        mine = pgs[pair, 0:tokens, :]
        sg[...] += lax.dot_general(mine, wb[...].reshape(width, -1), (((1,), (1,)), ((), ())), preferred_element_type=F32)
        sg[:, lanes_of(u)] += pgs[pair, 0:tokens, LANES:2 * LANES].astype(F32) * vecs[2:3, lanes_of(u)]
        pg_mate(u).wait_send()

    def fold(ref, at, more):
        ref[at] = (ref[at].astype(F32) + more.astype(F32)).astype(BF16)

    def meet(u):
        slot = lax.rem(u, SEND)
        for i in (0, 1):
            d_copy(u, i).wait_recv()
        fold(sb, (slot, xq, some(0)), rd[u, 0:half])
        x_copy(u, 0).start()
        fold(sb, (slot, yq, some(1)), rd[u, half:ny])
        y_copy(u, 1).start()

    def column(u):
        slot, zslot = lax.rem(u, SEND), lax.rem(u, ZSEND)

        @pl.when((u >= ZSEND) & jnp.logical_not(among(u - ZSEND, turned)))
        def _():
            for j in range(1, ny):
                f_copy(u - ZSEND, j).wait_send()

        for i in (0, 1):
            x_copy(u, i).wait_recv()
            y_copy(u, i).wait_recv()
        total = sb[slot, own].astype(F32) + rx[u].astype(F32) + ry[u].astype(F32)
        zb[zslot] = total.astype(BF16)
        for j in range(1, ny):
            f_copy(u, j).start()

    def settle(u):
        slot = lax.rem(u, SEND)
        total = sb[slot, own, gy].astype(F32) + rx[u, gy].astype(F32) + ry[u, gy].astype(F32)
        for j in range(1, ny):
            f_copy(u, j).wait_recv()
        for j in range(1, ny):
            total = total + rz[u, j - 1].astype(F32)
        place_sum(u, total)

    def place_sum(u, total):
        for i in range(3):
            wgo[:, lanes_of(u + i * units)] = total[:, i * LANES:(i + 1) * LANES]

    def part(i):
        return pl.ds(i * short, short)

    def b_z(u, j):
        to = peer_y(j)
        return remote(sent(u).at[:, to], (rd, rx, ry)[j - 1].at[u], fzs.at[u, j - 1], fzr.at[u, j - 1], (gx, to))

    def b_diag(u, n, i):
        return remote(cz.at[n, dq, part(i)], rz.at[u, 0, part(i)], fds.at[u, i], fdr.at[u, i], ((yn, xn)[i], gy))

    def b_x(u, n, i):
        return remote(cz.at[n, xq, part(i)], rz.at[u, 1, part(i)], fxs.at[u, i], fxr.at[u, i], (xn, gy))

    def b_y(u, n, i):
        return remote(cz.at[n, yq, part(i)], rz.at[u, 2, part(i)], fys.at[u, i], fyr.at[u, i], (yn, gy))

    def b_gather(u, n):
        for j in range(1, ny):
            b_z(u, j).wait()
            if u >= ZSEND and u - ZSEND not in turned:
                f_copy(u - ZSEND, j).wait_send()
        total = sb[lax.rem(u, SEND), :, gy].astype(F32)
        for ref in (rd, rx, ry):
            total = total + ref[u].astype(F32)
        cz[n] = total.astype(BF16)
        for i in (0, 1):
            b_diag(u, n, i).start()
        b_x(u, n, 1).start()
        b_y(u, n, 0).start()

    def b_meet(u, n):
        for i in (0, 1):
            b_diag(u, n, i).wait_recv()
        fold(cz, (n, xq, part(0)), rz[u, 0, part(0)])
        b_x(u, n, 0).start()
        fold(cz, (n, yq, part(1)), rz[u, 0, part(1)])
        b_y(u, n, 1).start()

    def b_settle(u, n):
        for i in (0, 1):
            b_x(u, n, i).wait_recv()
            b_y(u, n, i).wait_recv()
        place_sum(u, cz[n, own].astype(F32) + rz[u, 1].astype(F32) + rz[u, 2].astype(F32))

    def b_drain(u, n):
        for i in (0, 1):
            b_diag(u, n, i).wait_send()
            b_x(u, n, i).wait_send()
            b_y(u, n, i).wait_send()

    def finish(i):
        r = pl.ds(pl.multiple_of(i * BAND, BAND), BAND)
        s = sg[r, :]
        inv = invs[r, 0:1]
        z = (xs[r, :].astype(F32) - means[r, 0:1]) * inv
        sz = s * z
        gain = vecs[0:1, :]
        vrows[0:8, :] += jnp.sum(sz.reshape(BAND // 8, 8, width), axis=0)
        vrows[8:16, :] += jnp.sum(s.reshape(BAND // 8, 8, width), axis=0)
        n = s * gain
        m1 = jnp.mean(n, axis=1, keepdims=True)
        m2 = jnp.mean(sz * gain, axis=1, keepdims=True)
        sg[r, :] = grs[r, :] + inv * (n - m1 - z * m2)

    def v_copy(j):
        to = lax.rem(me + j, count)
        return remote(vtot.at[to // 2], vin.at[me], vsn.at[to], vrc.at[me], (to // ny, lax.rem(to, ny)))

    def v_recv(j):
        at = lax.rem(me + j, count)
        return remote(vtot.at[0], vin.at[at], vsn.at[at], vrc.at[at], (at // ny, lax.rem(at, ny)))

    def vectors_out():
        zero = jnp.zeros((2, LANES), F32)
        for c in range(width // LANES):
            at = slice(c * LANES, (c + 1) * LANES)
            top = [jnp.sum(vrows[8 * v:8 * v + 8, at], axis=0, keepdims=True) for v in (0, 1)]
            vtot[c] = jnp.concatenate(top + [vsum[2:6, at], zero], 0)
        each(count, lambda j: v_copy(j).start(), 1)

    quarter = width // 4

    def grad_copy(c):
        return pltpu.make_async_copy(grs.at[:, pl.ds(c * quarter, quarter)], igo.at[:, pl.ds(c * quarter, quarter)], ous.at[c])

    def natural():
        for c in range(4):
            at = slice(c * quarter, (c + 1) * quarter)
            v = sg[:, at]
            high = v.astype(BF16)
            low = (v - high.astype(F32)).astype(BF16)
            grs[:, at] = jnp.dot(perm[...], high, preferred_element_type=F32) + jnp.dot(
                perm[...], low, preferred_element_type=F32
            )
            grad_copy(c).start()

    def drain(u):
        for j in range(1, ny):
            z_copy(u, j).wait_send()
        for i in range(3):
            band_copy(u, i).wait_send()
        for i in (0, 1):
            diag_copy(u, i).wait_send()
        for i in (1, 2, 3):
            core_copy(u, i).wait_send()

    def drain_group(q):
        for a in ((m1a, e1as, e1ar, q, 0), (m1b, e1bs, e1br, q, 1), (m2a, e2as, e2ar, q, 0), (m2b, e2bs, e2br, q, 1)):
            for c in e_copies(*a):
                c.wait_send()

    def drain_first():
        for c in across:
            for j in range(1, ny):
                a_z(c, j).wait_send()
            for i in (1, 2):
                a_copy(c, i).wait_send()
            for i in (0, 1):
                a_diag(c, i).wait_send()
            a_core(c).wait_send()
        for j in range(1, ny):
            vz(j).wait_send()
        for j in range(1, nx):
            vx(j).wait_send()
        r_mate.wait_send()

    def vectors_in():
        each(count, lambda j: v_recv(j).wait_recv(), 1)
        vin[me] = vtot[me // 2]
        total = lax.fori_loop(0, count, lambda j, s: s + vin[j], jnp.zeros((8, LANES), F32))
        vgo[...] = jnp.where(odd, total[0:6, rows:2 * rows], total[0:6, 0:rows])
        each(count, lambda j: v_copy(j).wait_send(), 1)

    def tick(k, _):
        u = k - 3
        v = u - WEIGH
        gather_tick(k)
        pl.when(k == 3)(late_start)
        pl.when(k == 5)(late_turn)

        def summed(lag, run):
            w = v - lag
            pl.when((w >= 0) & (w < units) & jnp.logical_not(among(w, turned)))(lambda: run(w))

        summed(LAG1, meet)
        summed(LAG2, column)
        summed(LAG3, settle)
        for n, (c, _, steps) in enumerate(ACROSS_SUM):
            for t, run in zip(steps, (b_gather, b_meet, b_settle)):
                pl.when(v == t)(functools.partial(run, c, n))

        @pl.when(v == 0)
        def _():
            r_mate.wait_recv()
            sg[...] = jnp.zeros_like(sg)
            vrows[...] = jnp.zeros_like(vrows)

        @pl.when((v >= 0) & (v < units))
        def _():
            weigh(v)
            spread(v)

        for c, times, _ in ACROSS_SUM:
            for j, t in enumerate(times):
                pl.when(v == t)(lambda c=c, j=j: b_z(c, j + 1).start())

        pl.when((v >= -1) & (v < units - 1))(lambda: next_loads(v + 1))

        def event(lag, run):
            g = (u - lag) // GROUP
            pl.when((u >= lag) & (lax.rem(u - lag + GROUP, GROUP) == 0) & (g < groups))(lambda: run(g))

        event(BACK, backward_group)
        event(GRADS, grads_x)
        event(FORE, forward_group)
        event(TOTALS, totals_x)

        @pl.when((u >= 0) & (u < units))
        def _():
            project(u)

        @pl.when((u >= 0) & (u < units - 1))
        def _():
            straight(u + 1, core_wait)
            for c in across:
                pl.when(u + 1 == c)(lambda c=c: a_core(c).wait_recv())
            front_load(u + 1).start()

        @pl.when((u >= 0) & (u < units))
        def _():
            gates(u)
            pl.when(lax.rem(u, GROUP) == GROUP - 1)(lambda: totals(u // GROUP))

        pl.when(v == units)(lambda: each(bands // 2, finish))

        @pl.when(v == units + 1)
        def _():
            each(bands, finish, bands // 2)
            vectors_out()

        pl.when(v == units + 2)(natural)
        pl.when(v == units + 3)(vectors_in)
        w = k - units - 1

        @pl.when((w >= 0) & (w < units))
        def _():
            straight(w, drain)

        pl.when(w == 4)(drain_first)
        return 0

    front_load(0).start()
    lax.fori_loop(3, units + WEIGH + 3 + LAST, tick, 0)

    for n, c in enumerate(turned):
        b_drain(c, n)

    def drain_send(u):
        for i in (0, 1):
            d_copy(u, i).wait_send()
            x_copy(u, i).wait_send()
            y_copy(u, i).wait_send()

    each(units, lambda u: pl.when(jnp.logical_not(among(u, turned)))(lambda: drain_send(u)), units - SEND)

    def drain_z(u):
        for j in range(1, ny):
            f_copy(u, j).wait_send()

    each(units, drain_z, units - ZSEND)

    for q in range(groups - 2, groups):
        out_copy(q).wait()
    for c in range(4):
        grad_copy(c).wait()


def layer(nx, ny, tok, cot, mask, weight, vectors):
    tokens, width = tok.shape
    rows, cols = weight.shape[0], 3 * LANES
    units = width // LANES
    groups, glanes, block, count = units // GROUP, GROUP * LANES, rows * ny, nx * ny
    dma = pltpu.SemaphoreType.DMA
    any_, vmem = pl.BlockSpec(memory_space=pl.ANY), pl.BlockSpec(memory_space=pltpu.VMEM)
    msg = RUNS, glanes
    s, v = jax.ShapeDtypeStruct, pltpu.VMEM
    return pl.pallas_call(
        functools.partial(layer_kernel, nx, ny, units),
        name="layer",
        out_shape=(
            s((units, nx // 2, 2, ny, rows, cols), BF16), s((units, tokens, cols), BF16),
            s((tokens, width), BF16), s((tokens, width), F32), s((rows, 3 * width), F32), s(vectors.shape, F32),
        ),
        in_specs=[any_, any_, vmem, any_, vmem],
        out_specs=(any_,) * 4 + (vmem,) * 2,
        scratch_shapes=[
            v((count, 16, LANES), BF16), v((8, width), F32),
            v((tokens, width), BF16), v((tokens, width), BF16), v((tokens, LANES), F32), v((tokens, LANES), F32),
            v((tokens, width), BF16), v((width // 2, 2 * tokens), BF16), v((width // 2, tokens), BF16),
            v((nx // 2, 2, ny, rows, cols), BF16),
            v((SLOTS, tokens, cols), F32), v((SLOTS, tokens, LANES), F32),
            v((tokens, width), F32), v((tokens, glanes), BF16), v((2, tokens, glanes), BF16),
            v((tokens, tokens), BF16), v((PAIR, 2 * tokens, cols), BF16),
            v((nx // 2, 2, ny, rows, cols), BF16), v((SEND, nx // 2, ny, rows, cols), BF16),
            *[v((units, ny, rows, cols), BF16)] * 3,
            v((units, ny - 1, rows, cols), BF16), v((ZSEND, ny, rows, cols), BF16),
            v((tokens, width), F32), v((8, width), F32), v((16, width), F32),
            v((width // LANES, 8, LANES), F32), v((count, 8, LANES), F32),
            v((max(1, len(ACROSS_SUM)), nx // 2, rows, cols), BF16), v((tokens, LANES), F32),
            v((rows, 3 * width), BF16), v((units, rows, cols), BF16), v((16, LANES), BF16),
            *[v((groups,) + msg, F32)] * 5,
            v((groups, ny, 2, glanes), F32), v((groups, nx, 2, glanes), F32),
            v((groups, ny, 1, glanes), F32), v((groups, nx, 1, glanes), F32),
            dma((units, ny - 1)), dma((units, ny - 1)), dma((units,)), dma((units, 3)), dma((units, 2)),
            dma((units, 2)), dma((units, 2)), dma((units, 3)), dma((units, 4)), dma,
            dma((ny - 1,)), dma((ny - 1,)), dma((nx - 1,)), dma((nx - 1,)), dma, dma, dma((2,)),
            dma, dma, dma((units,)), dma((units,)), dma, dma, dma((groups,)),
            dma((groups, ny - 1)), dma((groups, ny - 1)), dma((groups, nx - 1)), dma((groups, nx - 1)),
            dma((groups, ny - 1)), dma((groups, ny - 1)), dma((groups, nx - 1)), dma((groups, nx - 1)),
            *[dma((units, 2))] * 6, dma((units, ny - 1)), dma((units, ny - 1)),
            dma((count,)), dma((count,)), dma((4,)),
        ],
        compiler_params=pltpu.CompilerParams(
            collective_id=0, has_side_effects=True, vmem_limit_bytes=62 * 2**20
        ),
        cost_estimate=pl.CostEstimate(
            flops=6 * tokens * width * units * cols, bytes_accessed=4 * width * units * cols, transcendentals=0
        ),
    )(tok, cot, mask, weight, vectors)


def fast(nx, ny, tokens, reset_mask, weight, vectors, cotangent):
    mask = reset_mask.reshape(1, -1)
    return layer(nx, ny, tokens, cotangent, mask, weight, vectors)[2:]


def solution(mesh):
    placed = (
        P(("gx", "gy"), None),
        P(("gx", "gy")),
        P(("gx", "gy"), None),
        P(None, ("gx", "gy")),
        P(("gx", "gy"), None),
    )
    nx, ny = mesh.shape["gx"], mesh.shape["gy"]

    def body(tokens, reset_mask, weight, vectors, cotangent):
        whole_tiles = weight.shape[0] % 16 == 0 and tokens.shape[0] % 256 == 0
        if (nx, ny) == (8, 4) and whole_tiles and 2 * weight.shape[0] == LANES and tokens.shape[1] % 2048 == 0:
            return fast(nx, ny, tokens, reset_mask, weight, vectors, cotangent)
        return local(tokens, reset_mask, weight, vectors, cotangent)

    return jax.shard_map(
        body,
        mesh=mesh,
        in_specs=placed,
        out_specs=(
            P(("gx", "gy"), None),
            P(("gx", "gy"), None),
            P(("gx", "gy"), None),
            P(None, ("gx", "gy")),
        ),
        check_vma=False,
    )
```

```python
import functools

import jax
import jax.numpy as jnp
from jax import lax
from jax.experimental import pallas as pl
from jax.experimental.pallas import tpu as pltpu
from jax.sharding import PartitionSpec as P

MESH = pl.DeviceIdType.MESH
F32, BF16 = jnp.float32, jnp.bfloat16
LANES, RUNS, GROUP = 128, 8, 2
EPS = 1e-05


def place(ny):
    gx, gy = lax.axis_index("gx"), lax.axis_index("gy")
    core, xx, yy = lax.rem(gx, 2), lax.rem(gx // 2, 2), gx // 4
    return gx, gy, core, gx + 1 - 2 * core, gx + 2 - 4 * xx, gx + 4 - 8 * yy


def remote(src, dst, send, recv, to):
    return pltpu.make_async_remote_copy(
        src_ref=src, dst_ref=dst, send_sem=send, recv_sem=recv, device_id=to, device_id_type=MESH
    )


def lanes_of(b):
    return pl.ds(pl.multiple_of(b * LANES, LANES), LANES)


def run_matrix(tokens, back):
    steps = tokens // RUNS
    row = lax.broadcasted_iota(jnp.int32, (tokens, tokens), 0)
    col = lax.broadcasted_iota(jnp.int32, (tokens, tokens), 1)
    if back:
        hit = row == (col & (RUNS - 1)) * steps + (col >> 3)
    else:
        hit = col == (row & (RUNS - 1)) * steps + (row >> 3)
    return jnp.where(hit, 1.0, 0.0).astype(BF16)


def entering(value, axis, join, neutral, backward):
    count, mine = (lax.axis_size(axis), lax.axis_index(axis))
    pieces = jax.tree.map(lambda part: lax.all_gather(part, axis), value)
    if backward:
        pieces = jax.tree.map(lambda part: part[::-1], pieces)
        mine = count - 1 - mine
    subtotal = jax.tree.map(
        lambda part, zero: jnp.full_like(part, 0) + jnp.asarray(zero, part.dtype), value, neutral
    )

    def lap(position, subtotal):
        longer = join(subtotal, jax.tree.map(lambda part: part[position], pieces))
        return jax.tree.map(lambda new, old: jnp.where(position < mine, new, old), longer, subtotal)

    return lax.fori_loop(0, count - 1, lap, subtotal)


def from_behind(block, axis, distance):
    devices = range(lax.axis_size(axis))
    route = [(i - distance, i) for i in devices if i - distance in devices]
    return lax.ppermute(block, axis, route)


def compose(earlier, later):
    return (earlier[0] * later[0], later[0] * earlier[1] + later[1])


def local(tokens, reset_mask, weight, vectors, cotangent):
    width = weight.shape[1] // 3
    whole_weight, whole_vectors = (
        lax.all_gather(weight, ("gx", "gy"), axis=0, tiled=True),
        lax.all_gather(vectors, ("gx", "gy"), axis=1, tiled=True),
    )
    params = whole_vectors.astype(jnp.float32)
    gain = params[0]
    shift_bias = params[1]
    forget_peep = params[2]
    forget_bias = params[3]
    reset_peep = params[4]
    reset_bias = params[5]
    inputs = tokens.astype(jnp.float32)
    keep = (1 - reset_mask).astype(jnp.float32)[:, None]
    centred = inputs - jnp.mean(inputs, axis=1, keepdims=True)
    inv_std = lax.rsqrt(jnp.mean(centred * centred, axis=1, keepdims=True) + 1e-05)
    normed = centred * inv_std
    scaled = normed * gain + shift_bias
    rounded = scaled.astype(jnp.bfloat16)
    projected = jnp.dot(rounded, whole_weight, preferred_element_type=jnp.float32)
    candidate = projected[:, :width]
    forget_pre = projected[:, width : 2 * width]
    reset_pre = projected[:, 2 * width :]
    forget = jax.nn.sigmoid(forget_pre + forget_peep * scaled + forget_bias)
    decay = forget * keep
    inflow = (1.0 - forget) * candidate
    cum_decay, cum_state = lax.associative_scan(compose, (decay, inflow), axis=0)
    unit = (jnp.ones_like(cum_decay[-1]), jnp.zeros_like(cum_state[-1]))
    before = entering((cum_decay[-1], cum_state[-1]), ("gx", "gy"), compose, unit, False)
    state_in = before[1]
    state = cum_decay * state_in + cum_state
    previous = keep * jnp.concatenate([state_in[None], state[:-1]], 0)
    reset = jax.nn.sigmoid(reset_pre + reset_peep * previous + reset_bias)
    output = reset * state + (1.0 - reset) * inputs
    upstream = cotangent.astype(jnp.float32)
    reset_grad = upstream * (state - inputs) * reset * (1.0 - reset)
    through = keep * reset_peep * reset_grad
    next_decay, next_through = from_behind((decay[0], through[0]), ("gx", "gy"), -1)
    ahead = jnp.concatenate([decay[1:], next_decay[None]], 0)
    local_term = upstream * reset + jnp.concatenate([through[1:], next_through[None]], 0)
    flip_mult, flip_sum = lax.associative_scan(compose, (ahead[::-1], local_term[::-1]), axis=0)
    mult_back = flip_mult[::-1]
    sum_back = flip_sum[::-1]
    after = entering((mult_back[0], sum_back[0]), ("gx", "gy"), compose, unit, True)
    state_grad = mult_back * after[1] + sum_back
    candidate_grad = state_grad * (1.0 - forget)
    forget_grad = state_grad * (previous - candidate) * forget * (1.0 - forget)
    proj_grad = jnp.concatenate([candidate_grad, forget_grad, reset_grad], 1).astype(jnp.bfloat16)
    weight_grad = lax.psum_scatter(
        lax.dot_general(
            rounded, proj_grad, (((0,), (0,)), ((), ())), preferred_element_type=jnp.float32
        ),
        ("gx", "gy"),
        scatter_dimension=0,
        tiled=True,
    )
    scaled_grad = lax.dot_general(
        proj_grad,
        lax.all_gather(weight, ("gx", "gy"), axis=0, tiled=True),
        (((1,), (1,)), ((), ())),
        preferred_element_type=jnp.float32,
    )
    scaled_grad = scaled_grad + forget_grad * forget_peep
    vector_terms = jnp.stack(
        [
            jnp.sum(scaled_grad * normed, axis=0),
            jnp.sum(scaled_grad, axis=0),
            jnp.sum(forget_grad * scaled, axis=0),
            jnp.sum(forget_grad, axis=0),
            jnp.sum(reset_grad * previous, axis=0),
            jnp.sum(reset_grad, axis=0),
        ],
        0,
    )
    vector_grad = lax.psum_scatter(vector_terms, ("gx", "gy"), scatter_dimension=1, tiled=True)
    normed_grad = scaled_grad * gain
    input_grad = upstream * (1.0 - reset) + inv_std * (
        normed_grad
        - jnp.mean(normed_grad, axis=1, keepdims=True)
        - normed * jnp.mean(normed_grad * normed, axis=1, keepdims=True)
    )
    return (output.astype(jnp.bfloat16), input_grad, weight_grad, vector_grad)


SLOTS, SEND, PAIR, ZSEND = 8, 8, 4, 4
TOTALS, FORE, GRADS, BACK, WEIGH = 2, 4, 5, 7, 9
LAG1, LAG2, LAG3 = 2, 4, 6
LAST = 6
AHEAD_Z, AHEAD_B = 5, 3
BAND = 32
ACROSS = ((10, (0, 3, 5)), (14, (6, 8, 10)), (15, (11, 13, 15)))
ACROSS_SUM = ()


def layer_kernel(
    nx, ny, units,
    tok, cot, mask, weight, vectors,
    wall, pgm, outp, igo, wgo, vgo,
    vbuf, vecs, xs, gs, means, invs, rnd, rt, rtm, wf, pj, pv, grs, outs, stage, perm, pgs,
    wb, sb, rd, rx, ry, rz, zb, sg, vsum, vrows, vtot, vin, cz, keep, wraw, wsrc, vsrc,
    ach, bch, qch, sin, cin, m1a, m1b, m2a, m2b,
    zs, zr, os, bs, br, dsn, dr, cs, cr, ws,
    vzs, vzr, vxs, vxr, vo, wls, sts, rs, rr, ps, pr, pl_, wl, gos,
    e1as, e1ar, e1bs, e1br, e2as, e2ar, e2bs, e2br,
    fds, fdr, fxs, fxr, fys, fyr, fzs, fzr, vsn, vrc, ous,
):
    gx, gy, core, mate, xn, yn = place(ny)
    tokens, width = xs.shape
    rows = wsrc.shape[1]
    cols = wsrc.shape[2]
    block = rows * ny
    half, short = ny // 2, rows // 2
    groups = units // GROUP
    glanes = GROUP * LANES
    diag = xn + yn - gx
    own, xq, yq, dq = gx // 2, xn // 2, yn // 2, diag // 2
    count = nx * ny
    me = gx * ny + gy

    def peer_y(j):
        return lax.rem(gy + j, ny)

    def peer_x(j):
        return lax.rem(gx + j, nx)

    def each(n, run, start=0):
        lax.fori_loop(start, n, lambda i, _: (run(i), 0)[1], 0)

    barrier = pltpu.get_barrier_semaphore()

    def greet(j):
        to = lax.rem(me + j, count)
        pl.semaphore_signal(barrier, inc=1, device_id=(to // ny, lax.rem(to, ny)), device_id_type=MESH)

    raw = pltpu.make_async_copy(weight, wraw, wls)
    raw.start()
    each(count, greet, 1)

    def among(u, some):
        hit = u < 0
        for s in some:
            hit = hit | (u == s)
        return hit

    across = tuple(c for c, _ in ACROSS)
    turned = tuple(c for c, _, _ in ACROSS_SUM)

    def straight(u, run):
        pl.when(jnp.logical_not(among(u, across)))(lambda: run(u))

    chunks = width // glanes

    tok_load = pltpu.make_async_copy(tok, xs, sts.at[0])
    cot_load = pltpu.make_async_copy(cot, gs, sts.at[1])
    tok_load.start()
    cot_load.start()

    def vz(j):
        return remote(vsrc, vbuf.at[me], vzs.at[j - 1], vzr.at[j - 1], (gx, peer_y(j)))

    def vx(j):
        part = vbuf.at[pl.ds(gx * ny, ny)]
        return remote(part, part, vxs.at[j - 1], vxr.at[j - 1], (peer_x(j), gy))

    own_vec = pltpu.make_async_copy(vsrc, vbuf.at[me], vo)

    def z_copy(u, j):
        return remote(wsrc.at[u], wall.at[u, own, core, gy], zs.at[u, j - 1], zr.at[u, j - 1], (gx, peer_y(j)))

    def own_copy(u):
        return pltpu.make_async_copy(wsrc.at[u], wall.at[u, own, core, gy], os.at[u])

    def band_copy(u, i):
        to = (mate, xn, yn)[i]
        recv = cr.at[u, 0] if i == 0 else br.at[u, i - 1]
        part = wall.at[u, own, core]
        return remote(part, part, bs.at[u, i], recv, (to, gy))

    def diag_copy(u, i):
        part = wall.at[u, (xq, yq)[i], core, half * i:half * (i + 1)]
        return remote(part, part, dsn.at[u, i], dr.at[u, i], ((yn, xn)[i], gy))

    def core_copy(u, i):
        part = wall.at[u, (own, xq, yq, dq)[i], core]
        return remote(part, part, cs.at[u, i - 1], cr.at[u, i], (mate, gy))

    def z_start(u):
        own_copy(u).start()
        for j in range(1, ny):
            z_copy(u, j).start()

    def z_wait(u):
        own_copy(u).wait()
        for j in range(1, ny):
            z_copy(u, j).wait_recv()
        for i in (1, 2, 0):
            band_copy(u, i).start()

    def xy_wait(u):
        for i in (1, 2):
            band_copy(u, i).wait_recv()
        for i in (0, 1):
            diag_copy(u, i).start()
        for i in (1, 2):
            core_copy(u, i).start()

    def diag_wait(u):
        for i in (0, 1):
            diag_copy(u, i).wait_recv()
        core_copy(u, 3).start()

    def core_wait(u):
        band_copy(u, 0).wait_recv()
        for i in (1, 2, 3):
            core_copy(u, i).wait_recv()

    def a_copy(u, i):
        return remote(
            wsrc.at[u], wall.at[u, own, core, gy], bs.at[u, i], br.at[u, i - 1], ((None, xn, yn)[i], gy)
        )

    def a_diag(u, i):
        part = wall.at[u, (xq, yq)[i], core, gy, short * i:short * (i + 1)]
        return remote(part, part, dsn.at[u, i], dr.at[u, i], ((yn, xn)[i], gy))

    def a_up(u, h):
        part = wall.at[u, :, core, gy - h]
        return remote(part, part, zs.at[u, h], zr.at[u, h], (gx, lax.rem(gy + 1, ny)))

    def a_down(u, h):
        part = wall.at[u, :, core, gy + h]
        return remote(part, part, cs.at[u, h], cr.at[u, h + 1], (gx, lax.rem(gy + ny - 1, ny)))

    def a_landed(u, h):
        pl.when(gy > h)(lambda: a_up(u, h).wait_recv())
        pl.when(gy + h + 1 < ny)(lambda: a_down(u, h).wait_recv())

    def a_hop(u, h):
        if h:
            a_landed(u, h - 1)
        pl.when((gy + 1 < ny) & (gy >= h))(lambda: a_up(u, h).start())
        pl.when((gy >= 1) & (gy + h < ny))(lambda: a_down(u, h).start())

    def a_left(u, h):
        pl.when((gy + 1 < ny) & (gy >= h))(lambda: a_up(u, h).wait_send())
        pl.when((gy >= 1) & (gy + h < ny))(lambda: a_down(u, h).wait_send())

    def a_core(u):
        part = wall.at[u, :, core]
        return remote(part, part, bs.at[u, 0], cr.at[u, 0], (mate, gy))

    def a_start(u):
        own_copy(u).start()
        for i in (1, 2):
            a_copy(u, i).start()

    def a_turn(u):
        own_copy(u).wait()
        for i in (1, 2):
            a_copy(u, i).wait_recv()
        for i in (0, 1):
            a_diag(u, i).start()

    def a_meet(u):
        for i in (0, 1):
            a_diag(u, i).wait_recv()

    def a_share(u):
        a_landed(u, ny - 2)
        a_core(u).start()

    zero = jnp.zeros((vectors.shape[0], LANES - rows), BF16)
    odd = lax.rem(me, 2) == 1
    tile = jnp.where(
        odd, jnp.concatenate([zero, vectors[...]], 1).astype(F32), jnp.concatenate([vectors[...], zero], 1).astype(F32)
    )
    pad = jnp.zeros((16 - vectors.shape[0], LANES), F32)
    vsrc[...] = jnp.concatenate([tile, pad], 0).astype(BF16)
    raw.wait()
    for u in range(units):
        for s in range(3):
            at = s * width + u * LANES
            wsrc[u, :, s * LANES:(s + 1) * LANES] = wraw[:, at:at + LANES]

    pl.semaphore_wait(barrier, count - 1)
    own_vec.start()
    for j in range(1, ny):
        vz(j).start()
    for u in across:
        a_start(u)
    z_start(0)

    def to_runs(i, into):
        at = slice(i * glanes, (i + 1) * glanes)
        into[:, at] = jnp.dot(perm[...], into[:, at], preferred_element_type=F32).astype(BF16)

    def moments(i):
        r = pl.ds(pl.multiple_of(i * BAND, BAND), BAND)
        x = xs[r, :].astype(F32)
        mean = jnp.mean(x, axis=1, keepdims=True)
        centred = x - mean
        inv = lax.rsqrt(jnp.mean(centred * centred, axis=1, keepdims=True) + EPS)
        means[r, :] = jnp.broadcast_to(mean, (BAND, LANES))
        invs[r, :] = jnp.broadcast_to(inv, (BAND, LANES))

    def rounding(i):
        r = pl.ds(pl.multiple_of(i * BAND, BAND), BAND)
        normed = (xs[r, :].astype(F32) - means[r, 0:1]) * invs[r, 0:1]
        rnd[r, :] = (normed * vecs[0:1, :] + vecs[1:2, :]).astype(BF16)

    quads = nx // 2

    def turn(i):
        at = pl.ds(pl.multiple_of(i * block, 16), block)
        rt[at, 0:tokens] = rnd[:, pl.ds(pl.multiple_of((2 * i + core) * block, LANES), block)].T
        rtm[at, :] = rnd[:, pl.ds(pl.multiple_of((2 * i + 1 - core) * block, LANES), block)].T

    r_mate = remote(rtm, rt.at[:, tokens:2 * tokens], rs, rr, (mate, gy))

    def gather_tick(k):
        pl.when(k + AHEAD_Z < units)(lambda: straight(k + AHEAD_Z, z_start))
        pl.when(k + AHEAD_B < units)(lambda: straight(k + AHEAD_B, z_wait))
        pl.when(k < units)(lambda: straight(k, xy_wait))
        pl.when((k >= 1) & (k <= units))(lambda: straight(k - 1, diag_wait))
        for c, times in ACROSS:
            for j, t in enumerate(times):
                pl.when(k == t)(functools.partial(a_hop, c, j))
            pl.when(k == c + 1)(functools.partial(a_share, c))

    bands = tokens // BAND
    perm[...] = run_matrix(tokens, False)
    tok_load.wait()
    for i in range(chunks // 2):
        to_runs(i, xs)
    z_wait(0)
    z_start(1)
    z_start(2)
    for i in range(chunks // 2, chunks):
        to_runs(i, xs)
    own_vec.wait()
    for j in range(1, ny):
        vz(j).wait_recv()
    for j in range(1, nx):
        vx(j).start()
    for u in across:
        a_turn(u)
    z_wait(1)
    for u in range(3, AHEAD_Z):
        z_start(u)
    each(bands // 2, moments)
    for u in range(2, AHEAD_B):
        z_wait(u)
    for u in across:
        a_meet(u)
    gather_tick(0)
    each(bands, moments, bands // 2)
    for j in range(1, nx):
        vx(j).wait_recv()
    for c in range(width // LANES):
        part = vbuf[2 * c].astype(F32) + vbuf[2 * c + 1].astype(F32)
        vecs[:, c * LANES:(c + 1) * LANES] = part[0:8, :]
    each(bands // 2, rounding)
    gather_tick(1)
    each(bands, rounding, bands // 2)
    kept = (1 - mask[...]).astype(F32)
    keep[...] = jnp.dot(
        (perm[...].astype(F32) * kept).astype(BF16), jnp.ones((tokens, LANES), BF16), preferred_element_type=F32
    )
    cot_load.wait()
    for i in range(chunks // 2):
        to_runs(i, gs)
    gather_tick(2)
    straight(0, core_wait)

    def late_start():
        for i in range(chunks // 2, chunks):
            to_runs(i, gs)
        perm[...] = run_matrix(tokens, True)

    def late_turn():
        each(quads, turn)
        r_mate.start()

    def e_copies(buf, send, recv, q, level):
        if level == 0:
            return [
                remote(buf.at[q, gy], buf.at[q, gy], send.at[q, j - 1], recv.at[q, j - 1], (gx, peer_y(j)))
                for j in range(1, ny)
            ]
        return [
            remote(buf.at[q, gx], buf.at[q, gx], send.at[q, j - 1], recv.at[q, j - 1], (peer_x(j), gy))
            for j in range(1, nx)
        ]

    def e_start(*a):
        for c in e_copies(*a):
            c.start()

    def e_wait(*a):
        for c in e_copies(*a):
            c.wait_recv()

    double = tokens // (2 * RUNS)

    def front_load(u):
        return pltpu.make_async_copy(wall.at[u], wf, ws)

    def project(u):
        front_load(u).wait()
        pj[lax.rem(u, SLOTS)] = jnp.dot(rnd[...], wf[...].reshape(width, -1), preferred_element_type=F32)

    def vec(i, u):
        return vecs[i:i + 1, lanes_of(u)]

    def scale(u, r, gain, shift):
        return (xs[r, lanes_of(u)].astype(F32) - means[r, :]) * invs[r, :] * gain + shift

    def gates(u):
        slot = lax.rem(u, SLOTS)
        gain, shift, vf, bf = (vec(i, u) for i in range(4))

        def step(i, carry):
            a, b = carry
            r = pl.ds(pl.multiple_of(i * 16, 16), 16)
            f = jax.nn.sigmoid(pj[slot, r, LANES:2 * LANES] + vf * scale(u, r, gain, shift) + bf)
            pj[slot, r, LANES:2 * LANES] = f
            d = f * keep[r, :]
            inflow = (1.0 - f) * pj[slot, r, 0:LANES]
            for h in (0, 8):
                a = a * d[h:h + 8]
                b = d[h:h + 8] * b + inflow[h:h + 8]
            return a, b

        a, b = lax.fori_loop(0, double, step, (jnp.ones((RUNS, LANES), F32), jnp.zeros((RUNS, LANES), F32)), unroll=4)
        q, j = u // GROUP, lax.rem(u, GROUP)
        ach[q, :, lanes_of(j)] = a
        bch[q, :, lanes_of(j)] = b

    def totals(q):
        a, b = jnp.ones((1, glanes), F32), jnp.zeros((1, glanes), F32)
        for s in range(RUNS):
            one = ach[q, s:s + 1, :]
            a = a * one
            b = one * b + bch[q, s:s + 1, :]
        m1a[q, gy, 0:1, :] = a
        m1a[q, gy, 1:2, :] = b
        e_start(m1a, e1as, e1ar, q, 0)

    def totals_x(q):
        e_wait(m1a, e1as, e1ar, q, 0)
        a, b = jnp.ones((1, glanes), F32), jnp.zeros((1, glanes), F32)
        for s in range(ny):
            one = m1a[q, s, 0:1, :]
            a = a * one
            b = one * b + m1a[q, s, 1:2, :]
        m1b[q, gx, 0:1, :] = a
        m1b[q, gx, 1:2, :] = b
        e_start(m1b, e1bs, e1br, q, 1)

    def enter(q):
        e_wait(m1b, e1bs, e1br, q, 1)
        s = jnp.zeros((1, glanes), F32)
        s = lax.fori_loop(0, gx, lambda i, s: m1b[q, i, 0:1, :] * s + m1b[q, i, 1:2, :], s)
        s = lax.fori_loop(0, gy, lambda i, s: m1a[q, i, 0:1, :] * s + m1a[q, i, 1:2, :], s)
        for r in range(RUNS):
            sin[q, r:r + 1, :] = s
            s = ach[q, r:r + 1, :] * s + bch[q, r:r + 1, :]

    def forward(u):
        slot = lax.rem(u, SLOTS)
        q, j = u // GROUP, lax.rem(u, GROUP)
        vr, br_ = vec(4, u), vec(5, u)
        zero = jnp.zeros((RUNS, LANES), F32)

        def step(i, carry):
            s, run, t, v4, v5 = carry
            r = pl.ds(pl.multiple_of(i * 16, 16), 16)
            f = pj[slot, r, LANES:2 * LANES]
            k = keep[r, :]
            inflow = (1.0 - f) * pj[slot, r, 0:LANES]
            prevs, states = [], []
            for h in (0, 8):
                prev = k[h:h + 8] * s
                s = f[h:h + 8] * prev + inflow[h:h + 8]
                prevs.append(prev)
                states.append(s)
            prev, state = jnp.concatenate(prevs, 0), jnp.concatenate(states, 0)
            x = xs[r, lanes_of(u)].astype(F32)
            up = gs[r, lanes_of(u)].astype(F32)
            reset = jax.nn.sigmoid(pj[slot, r, 2 * LANES:3 * LANES] + vr * prev + br_)
            rest = 1.0 - reset
            outs[r, lanes_of(j)] = (reset * state + rest * x).astype(BF16)
            rg = up * (state - x) * reset * rest
            pj[slot, r, 2 * LANES:3 * LANES] = rg
            pv[slot, r, :] = prev
            grs[r, lanes_of(u)] = up * rest
            local = up * reset
            d, through = f * k, k * vr * rg
            for h in (0, 8):
                t = t + run * through[h:h + 8]
                run = run * d[h:h + 8]
                t = t + run * local[h:h + 8]
                v4 = v4 + rg[h:h + 8] * prev[h:h + 8]
                v5 = v5 + rg[h:h + 8]
            return s, run, t, v4, v5

        init = (sin[q, :, lanes_of(j)], jnp.ones((RUNS, LANES), F32), zero, zero, zero)
        _, _, t, v4, v5 = lax.fori_loop(0, double, step, init, unroll=4)
        qch[q, :, lanes_of(j)] = t
        vsum[4:5, lanes_of(u)] = jnp.sum(v4, axis=0, keepdims=True)
        vsum[5:6, lanes_of(u)] = jnp.sum(v5, axis=0, keepdims=True)

    def out_copy(q):
        c = pl.ds(pl.multiple_of(q * glanes, LANES), glanes)
        return pltpu.make_async_copy(stage.at[lax.rem(q, 2)], outp.at[:, c], gos.at[q])

    def forward_group(q):
        enter(q)
        pl.when(q >= 2)(lambda: out_copy(q - 2).wait())
        each(GROUP, lambda j: forward(q * GROUP + j))
        s = jnp.zeros((1, glanes), F32)
        for r in reversed(range(RUNS)):
            s = ach[q, r:r + 1, :] * s + qch[q, r:r + 1, :]
        m2a[q, gy, 0:1, :] = s
        e_start(m2a, e2as, e2ar, q, 0)
        stage[lax.rem(q, 2)] = jnp.dot(perm[...], outs[...], preferred_element_type=F32).astype(BF16)
        out_copy(q).start()

    def grads_x(q):
        e_wait(m2a, e2as, e2ar, q, 0)
        s = jnp.zeros((1, glanes), F32)
        for r in reversed(range(ny)):
            s = m1a[q, r, 0:1, :] * s + m2a[q, r, 0:1, :]
        m2b[q, gx, 0:1, :] = s
        e_start(m2b, e2bs, e2br, q, 1)

    def enter_back(q):
        e_wait(m2b, e2bs, e2br, q, 1)
        s = jnp.zeros((1, glanes), F32)

        def over_x(i, s):
            return m1b[q, nx - 1 - i, 0:1, :] * s + m2b[q, nx - 1 - i, 0:1, :]

        def over_y(i, s):
            return m1a[q, ny - 1 - i, 0:1, :] * s + m2a[q, ny - 1 - i, 0:1, :]

        s = lax.fori_loop(0, nx - 1 - gx, over_x, s)
        s = lax.fori_loop(0, ny - 1 - gy, over_y, s)
        for r in reversed(range(RUNS)):
            cin[q, r:r + 1, :] = s
            s = ach[q, r:r + 1, :] * s + qch[q, r:r + 1, :]

    def pg_mate(u):
        return remote(pgs.at[lax.rem(u, PAIR), 0:tokens], pgm.at[u], ps.at[u], pr.at[u], (mate, gy))

    def backward(u):
        slot, pair = lax.rem(u, SLOTS), lax.rem(u, PAIR)
        q, j = u // GROUP, lax.rem(u, GROUP)
        gain, shift, vr = vec(0, u), vec(1, u), vec(4, u)
        zero = jnp.zeros((RUNS, LANES), F32)

        def step(i, carry):
            c, v2, v3 = carry
            r = pl.ds(pl.multiple_of((double - 1 - i) * 16, 16), 16)
            f = pj[slot, r, LANES:2 * LANES]
            k = keep[r, :]
            rg = pj[slot, r, 2 * LANES:3 * LANES]
            local = gs[r, lanes_of(u)].astype(F32) - grs[r, lanes_of(u)]
            d, through = f * k, k * vr * rg
            grads = [None, None]
            for h in (1, 0):
                part = slice(8 * h, 8 * h + 8)
                grads[h] = local[part] + c
                c = d[part] * grads[h] + through[part]
            grad = jnp.concatenate(grads, 0)
            cg = grad * (1.0 - f)
            fg = cg * (pv[slot, r, :] - pj[slot, r, 0:LANES]) * f
            pgs[pair, r, 0:LANES] = cg.astype(BF16)
            pgs[pair, r, LANES:2 * LANES] = fg.astype(BF16)
            pgs[pair, r, 2 * LANES:3 * LANES] = rg.astype(BF16)
            fs = fg * scale(u, r, gain, shift)
            return c, v2 + fs[0:8] + fs[8:16], v3 + fg[0:8] + fg[8:16]

        _, v2, v3 = lax.fori_loop(0, double, step, (cin[q, :, lanes_of(j)], zero, zero), unroll=4)
        vsum[2:3, lanes_of(u)] = jnp.sum(v2, axis=0, keepdims=True)
        vsum[3:4, lanes_of(u)] = jnp.sum(v3, axis=0, keepdims=True)
        pg_mate(u).start()

    def backward_group(q):
        enter_back(q)
        each(GROUP, lambda j: backward(q * GROUP + j))
        drain_group(q)

    def pg_load(u):
        return pltpu.make_async_copy(pgm.at[u], pgs.at[lax.rem(u, PAIR), tokens:2 * tokens], pl_)

    def back_load(u):
        return pltpu.make_async_copy(wall.at[u], wb, wl)

    def some(part):
        return pl.ds(part * half, half)

    def sent(u):
        return sb.at[lax.rem(u, SEND)]

    def d_copy(u, i):
        return remote(
            sent(u).at[dq, some(i)], rd.at[u, some(i)], fds.at[u, i], fdr.at[u, i], ((yn, xn)[i], gy)
        )

    def x_copy(u, i):
        return remote(sent(u).at[xq, some(i)], rx.at[u, some(i)], fxs.at[u, i], fxr.at[u, i], (xn, gy))

    def y_copy(u, i):
        return remote(sent(u).at[yq, some(i)], ry.at[u, some(i)], fys.at[u, i], fyr.at[u, i], (yn, gy))

    def f_copy(u, j):
        to = lax.rem(gy + j, ny)
        return remote(zb.at[lax.rem(u, ZSEND), to], rz.at[u, j - 1], fzs.at[u, j - 1], fzr.at[u, j - 1], (gx, to))

    def next_loads(u):
        pg_mate(u).wait_recv()
        pg_load(u).start()
        back_load(u).start()

    def weigh(u):
        slot, pair = lax.rem(u, SEND), lax.rem(u, PAIR)

        @pl.when((u >= SEND) & jnp.logical_not(among(u - SEND, turned)))
        def _():
            for i in (0, 1):
                d_copy(u - SEND, i).wait_send()
                x_copy(u - SEND, i).wait_send()
                y_copy(u - SEND, i).wait_send()

        pg_load(u).wait()
        sb[slot] = jnp.dot(rt[...], pgs[pair], preferred_element_type=F32).astype(BF16).reshape(sb.shape[1:])

        @pl.when(jnp.logical_not(among(u, turned)))
        def _():
            for i in (0, 1):
                d_copy(u, i).start()
            x_copy(u, 1).start()
            y_copy(u, 0).start()

    def spread(u):
        pair = lax.rem(u, PAIR)
        back_load(u).wait()
        mine = pgs[pair, 0:tokens, :]
        sg[...] += lax.dot_general(mine, wb[...].reshape(width, -1), (((1,), (1,)), ((), ())), preferred_element_type=F32)
        sg[:, lanes_of(u)] += pgs[pair, 0:tokens, LANES:2 * LANES].astype(F32) * vecs[2:3, lanes_of(u)]
        pg_mate(u).wait_send()

    def fold(ref, at, more):
        ref[at] = (ref[at].astype(F32) + more.astype(F32)).astype(BF16)

    def meet(u):
        slot = lax.rem(u, SEND)
        for i in (0, 1):
            d_copy(u, i).wait_recv()
        fold(sb, (slot, xq, some(0)), rd[u, 0:half])
        x_copy(u, 0).start()
        fold(sb, (slot, yq, some(1)), rd[u, half:ny])
        y_copy(u, 1).start()

    def column(u):
        slot, zslot = lax.rem(u, SEND), lax.rem(u, ZSEND)

        @pl.when((u >= ZSEND) & jnp.logical_not(among(u - ZSEND, turned)))
        def _():
            for j in range(1, ny):
                f_copy(u - ZSEND, j).wait_send()

        for i in (0, 1):
            x_copy(u, i).wait_recv()
            y_copy(u, i).wait_recv()
        total = sb[slot, own].astype(F32) + rx[u].astype(F32) + ry[u].astype(F32)
        zb[zslot] = total.astype(BF16)
        for j in range(1, ny):
            f_copy(u, j).start()

    def settle(u):
        slot = lax.rem(u, SEND)
        total = sb[slot, own, gy].astype(F32) + rx[u, gy].astype(F32) + ry[u, gy].astype(F32)
        for j in range(1, ny):
            f_copy(u, j).wait_recv()
        for j in range(1, ny):
            total = total + rz[u, j - 1].astype(F32)
        place_sum(u, total)

    def place_sum(u, total):
        for i in range(3):
            wgo[:, lanes_of(u + i * units)] = total[:, i * LANES:(i + 1) * LANES]

    def part(i):
        return pl.ds(i * short, short)

    def b_z(u, j):
        to = peer_y(j)
        return remote(sent(u).at[:, to], (rd, rx, ry)[j - 1].at[u], fzs.at[u, j - 1], fzr.at[u, j - 1], (gx, to))

    def b_diag(u, n, i):
        return remote(cz.at[n, dq, part(i)], rz.at[u, 0, part(i)], fds.at[u, i], fdr.at[u, i], ((yn, xn)[i], gy))

    def b_x(u, n, i):
        return remote(cz.at[n, xq, part(i)], rz.at[u, 1, part(i)], fxs.at[u, i], fxr.at[u, i], (xn, gy))

    def b_y(u, n, i):
        return remote(cz.at[n, yq, part(i)], rz.at[u, 2, part(i)], fys.at[u, i], fyr.at[u, i], (yn, gy))

    def b_gather(u, n):
        for j in range(1, ny):
            b_z(u, j).wait()
            if u >= ZSEND and u - ZSEND not in turned:
                f_copy(u - ZSEND, j).wait_send()
        total = sb[lax.rem(u, SEND), :, gy].astype(F32)
        for ref in (rd, rx, ry):
            total = total + ref[u].astype(F32)
        cz[n] = total.astype(BF16)
        for i in (0, 1):
            b_diag(u, n, i).start()
        b_x(u, n, 1).start()
        b_y(u, n, 0).start()

    def b_meet(u, n):
        for i in (0, 1):
            b_diag(u, n, i).wait_recv()
        fold(cz, (n, xq, part(0)), rz[u, 0, part(0)])
        b_x(u, n, 0).start()
        fold(cz, (n, yq, part(1)), rz[u, 0, part(1)])
        b_y(u, n, 1).start()

    def b_settle(u, n):
        for i in (0, 1):
            b_x(u, n, i).wait_recv()
            b_y(u, n, i).wait_recv()
        place_sum(u, cz[n, own].astype(F32) + rz[u, 1].astype(F32) + rz[u, 2].astype(F32))

    def b_drain(u, n):
        for i in (0, 1):
            b_diag(u, n, i).wait_send()
            b_x(u, n, i).wait_send()
            b_y(u, n, i).wait_send()

    def finish(i):
        r = pl.ds(pl.multiple_of(i * BAND, BAND), BAND)
        s = sg[r, :]
        inv = invs[r, 0:1]
        z = (xs[r, :].astype(F32) - means[r, 0:1]) * inv
        sz = s * z
        gain = vecs[0:1, :]
        vrows[0:8, :] += jnp.sum(sz.reshape(BAND // 8, 8, width), axis=0)
        vrows[8:16, :] += jnp.sum(s.reshape(BAND // 8, 8, width), axis=0)
        n = s * gain
        m1 = jnp.mean(n, axis=1, keepdims=True)
        m2 = jnp.mean(sz * gain, axis=1, keepdims=True)
        sg[r, :] = grs[r, :] + inv * (n - m1 - z * m2)

    def v_copy(j):
        to = lax.rem(me + j, count)
        return remote(vtot.at[to // 2], vin.at[me], vsn.at[to], vrc.at[me], (to // ny, lax.rem(to, ny)))

    def v_recv(j):
        at = lax.rem(me + j, count)
        return remote(vtot.at[0], vin.at[at], vsn.at[at], vrc.at[at], (at // ny, lax.rem(at, ny)))

    def vectors_out():
        zero = jnp.zeros((2, LANES), F32)
        for c in range(width // LANES):
            at = slice(c * LANES, (c + 1) * LANES)
            top = [jnp.sum(vrows[8 * v:8 * v + 8, at], axis=0, keepdims=True) for v in (0, 1)]
            vtot[c] = jnp.concatenate(top + [vsum[2:6, at], zero], 0)
        each(count, lambda j: v_copy(j).start(), 1)

    quarter = width // 4

    def grad_copy(c):
        return pltpu.make_async_copy(grs.at[:, pl.ds(c * quarter, quarter)], igo.at[:, pl.ds(c * quarter, quarter)], ous.at[c])

    def natural():
        for c in range(4):
            at = slice(c * quarter, (c + 1) * quarter)
            v = sg[:, at]
            high = v.astype(BF16)
            low = (v - high.astype(F32)).astype(BF16)
            grs[:, at] = jnp.dot(perm[...], high, preferred_element_type=F32) + jnp.dot(
                perm[...], low, preferred_element_type=F32
            )
            grad_copy(c).start()

    def drain(u):
        for j in range(1, ny):
            z_copy(u, j).wait_send()
        for i in range(3):
            band_copy(u, i).wait_send()
        for i in (0, 1):
            diag_copy(u, i).wait_send()
        for i in (1, 2, 3):
            core_copy(u, i).wait_send()

    def drain_group(q):
        for a in ((m1a, e1as, e1ar, q, 0), (m1b, e1bs, e1br, q, 1), (m2a, e2as, e2ar, q, 0), (m2b, e2bs, e2br, q, 1)):
            for c in e_copies(*a):
                c.wait_send()

    def drain_first():
        for c in across:
            for h in range(ny - 1):
                a_left(c, h)
            for i in (1, 2):
                a_copy(c, i).wait_send()
            for i in (0, 1):
                a_diag(c, i).wait_send()
            a_core(c).wait_send()
        for j in range(1, ny):
            vz(j).wait_send()
        for j in range(1, nx):
            vx(j).wait_send()
        r_mate.wait_send()

    def vectors_in():
        each(count, lambda j: v_recv(j).wait_recv(), 1)
        vin[me] = vtot[me // 2]
        total = lax.fori_loop(0, count, lambda j, s: s + vin[j], jnp.zeros((8, LANES), F32))
        vgo[...] = jnp.where(odd, total[0:6, rows:2 * rows], total[0:6, 0:rows])
        each(count, lambda j: v_copy(j).wait_send(), 1)

    def tick(k, _):
        u = k - 3
        v = u - WEIGH
        gather_tick(k)
        pl.when(k == 3)(late_start)
        pl.when(k == 5)(late_turn)

        def summed(lag, run):
            w = v - lag
            pl.when((w >= 0) & (w < units) & jnp.logical_not(among(w, turned)))(lambda: run(w))

        summed(LAG1, meet)
        summed(LAG2, column)
        summed(LAG3, settle)
        for n, (c, _, steps) in enumerate(ACROSS_SUM):
            for t, run in zip(steps, (b_gather, b_meet, b_settle)):
                pl.when(v == t)(functools.partial(run, c, n))

        @pl.when(v == 0)
        def _():
            r_mate.wait_recv()
            sg[...] = jnp.zeros_like(sg)
            vrows[...] = jnp.zeros_like(vrows)

        @pl.when((v >= 0) & (v < units))
        def _():
            weigh(v)
            spread(v)

        for c, times, _ in ACROSS_SUM:
            for j, t in enumerate(times):
                pl.when(v == t)(lambda c=c, j=j: b_z(c, j + 1).start())

        pl.when((v >= -1) & (v < units - 1))(lambda: next_loads(v + 1))

        def event(lag, run):
            g = (u - lag) // GROUP
            pl.when((u >= lag) & (lax.rem(u - lag + GROUP, GROUP) == 0) & (g < groups))(lambda: run(g))

        event(BACK, backward_group)
        event(GRADS, grads_x)
        event(FORE, forward_group)
        event(TOTALS, totals_x)

        @pl.when((u >= 0) & (u < units))
        def _():
            project(u)

        @pl.when((u >= 0) & (u < units - 1))
        def _():
            straight(u + 1, core_wait)
            for c in across:
                pl.when(u + 1 == c)(lambda c=c: a_core(c).wait_recv())
            front_load(u + 1).start()

        @pl.when((u >= 0) & (u < units))
        def _():
            gates(u)
            pl.when(lax.rem(u, GROUP) == GROUP - 1)(lambda: totals(u // GROUP))

        pl.when(v == units)(lambda: each(bands // 2, finish))

        @pl.when(v == units + 1)
        def _():
            each(bands, finish, bands // 2)
            vectors_out()

        pl.when(v == units + 2)(natural)
        pl.when(v == units + 3)(vectors_in)
        w = k - units - 1

        @pl.when((w >= 0) & (w < units))
        def _():
            straight(w, drain)

        pl.when(w == 4)(drain_first)
        return 0

    front_load(0).start()
    lax.fori_loop(3, units + WEIGH + 3 + LAST, tick, 0)

    for n, c in enumerate(turned):
        b_drain(c, n)

    def drain_send(u):
        for i in (0, 1):
            d_copy(u, i).wait_send()
            x_copy(u, i).wait_send()
            y_copy(u, i).wait_send()

    each(units, lambda u: pl.when(jnp.logical_not(among(u, turned)))(lambda: drain_send(u)), units - SEND)

    def drain_z(u):
        for j in range(1, ny):
            f_copy(u, j).wait_send()

    each(units, drain_z, units - ZSEND)

    for q in range(groups - 2, groups):
        out_copy(q).wait()
    for c in range(4):
        grad_copy(c).wait()


def layer(nx, ny, tok, cot, mask, weight, vectors):
    tokens, width = tok.shape
    rows, cols = weight.shape[0], 3 * LANES
    units = width // LANES
    groups, glanes, block, count = units // GROUP, GROUP * LANES, rows * ny, nx * ny
    dma = pltpu.SemaphoreType.DMA
    any_, vmem = pl.BlockSpec(memory_space=pl.ANY), pl.BlockSpec(memory_space=pltpu.VMEM)
    msg = RUNS, glanes
    s, v = jax.ShapeDtypeStruct, pltpu.VMEM
    return pl.pallas_call(
        functools.partial(layer_kernel, nx, ny, units),
        name="layer",
        out_shape=(
            s((units, nx // 2, 2, ny, rows, cols), BF16), s((units, tokens, cols), BF16),
            s((tokens, width), BF16), s((tokens, width), F32), s((rows, 3 * width), F32), s(vectors.shape, F32),
        ),
        in_specs=[any_, any_, vmem, any_, vmem],
        out_specs=(any_,) * 4 + (vmem,) * 2,
        scratch_shapes=[
            v((count, 16, LANES), BF16), v((8, width), F32),
            v((tokens, width), BF16), v((tokens, width), BF16), v((tokens, LANES), F32), v((tokens, LANES), F32),
            v((tokens, width), BF16), v((width // 2, 2 * tokens), BF16), v((width // 2, tokens), BF16),
            v((nx // 2, 2, ny, rows, cols), BF16),
            v((SLOTS, tokens, cols), F32), v((SLOTS, tokens, LANES), F32),
            v((tokens, width), F32), v((tokens, glanes), BF16), v((2, tokens, glanes), BF16),
            v((tokens, tokens), BF16), v((PAIR, 2 * tokens, cols), BF16),
            v((nx // 2, 2, ny, rows, cols), BF16), v((SEND, nx // 2, ny, rows, cols), BF16),
            *[v((units, ny, rows, cols), BF16)] * 3,
            v((units, ny - 1, rows, cols), BF16), v((ZSEND, ny, rows, cols), BF16),
            v((tokens, width), F32), v((8, width), F32), v((16, width), F32),
            v((width // LANES, 8, LANES), F32), v((count, 8, LANES), F32),
            v((max(1, len(ACROSS_SUM)), nx // 2, rows, cols), BF16), v((tokens, LANES), F32),
            v((rows, 3 * width), BF16), v((units, rows, cols), BF16), v((16, LANES), BF16),
            *[v((groups,) + msg, F32)] * 5,
            v((groups, ny, 2, glanes), F32), v((groups, nx, 2, glanes), F32),
            v((groups, ny, 1, glanes), F32), v((groups, nx, 1, glanes), F32),
            dma((units, ny - 1)), dma((units, ny - 1)), dma((units,)), dma((units, 3)), dma((units, 2)),
            dma((units, 2)), dma((units, 2)), dma((units, 3)), dma((units, 4)), dma,
            dma((ny - 1,)), dma((ny - 1,)), dma((nx - 1,)), dma((nx - 1,)), dma, dma, dma((2,)),
            dma, dma, dma((units,)), dma((units,)), dma, dma, dma((groups,)),
            dma((groups, ny - 1)), dma((groups, ny - 1)), dma((groups, nx - 1)), dma((groups, nx - 1)),
            dma((groups, ny - 1)), dma((groups, ny - 1)), dma((groups, nx - 1)), dma((groups, nx - 1)),
            *[dma((units, 2))] * 6, dma((units, ny - 1)), dma((units, ny - 1)),
            dma((count,)), dma((count,)), dma((4,)),
        ],
        compiler_params=pltpu.CompilerParams(
            collective_id=0, has_side_effects=True, vmem_limit_bytes=62 * 2**20
        ),
        cost_estimate=pl.CostEstimate(
            flops=6 * tokens * width * units * cols, bytes_accessed=4 * width * units * cols, transcendentals=0
        ),
    )(tok, cot, mask, weight, vectors)


def fast(nx, ny, tokens, reset_mask, weight, vectors, cotangent):
    mask = reset_mask.reshape(1, -1)
    return layer(nx, ny, tokens, cotangent, mask, weight, vectors)[2:]


def solution(mesh):
    placed = (
        P(("gx", "gy"), None),
        P(("gx", "gy")),
        P(("gx", "gy"), None),
        P(None, ("gx", "gy")),
        P(("gx", "gy"), None),
    )
    nx, ny = mesh.shape["gx"], mesh.shape["gy"]

    def body(tokens, reset_mask, weight, vectors, cotangent):
        whole_tiles = weight.shape[0] % 16 == 0 and tokens.shape[0] % 256 == 0
        if (nx, ny) == (8, 4) and whole_tiles and 2 * weight.shape[0] == LANES and tokens.shape[1] % 2048 == 0:
            return fast(nx, ny, tokens, reset_mask, weight, vectors, cotangent)
        return local(tokens, reset_mask, weight, vectors, cotangent)

    return jax.shard_map(
        body,
        mesh=mesh,
        in_specs=placed,
        out_specs=(
            P(("gx", "gy"), None),
            P(("gx", "gy"), None),
            P(("gx", "gy"), None),
            P(None, ("gx", "gy")),
        ),
        check_vma=False,
    )
```

```python
import functools

import jax
import jax.numpy as jnp
from jax import lax
from jax.experimental import pallas as pl
from jax.experimental.pallas import tpu as pltpu
from jax.sharding import PartitionSpec as P

MESH = pl.DeviceIdType.MESH
F32, BF16 = jnp.float32, jnp.bfloat16
LANES, RUNS, GROUP = 128, 8, 2
EPS = 1e-05


def place(ny):
    gx, gy = lax.axis_index("gx"), lax.axis_index("gy")
    core, xx, yy = lax.rem(gx, 2), lax.rem(gx // 2, 2), gx // 4
    return gx, gy, core, gx + 1 - 2 * core, gx + 2 - 4 * xx, gx + 4 - 8 * yy


def remote(src, dst, send, recv, to):
    return pltpu.make_async_remote_copy(
        src_ref=src, dst_ref=dst, send_sem=send, recv_sem=recv, device_id=to, device_id_type=MESH
    )


def lanes_of(b):
    return pl.ds(pl.multiple_of(b * LANES, LANES), LANES)


def run_matrix(tokens, back):
    steps = tokens // RUNS
    row = lax.broadcasted_iota(jnp.int32, (tokens, tokens), 0)
    col = lax.broadcasted_iota(jnp.int32, (tokens, tokens), 1)
    if back:
        hit = row == (col & (RUNS - 1)) * steps + (col >> 3)
    else:
        hit = col == (row & (RUNS - 1)) * steps + (row >> 3)
    return jnp.where(hit, 1.0, 0.0).astype(BF16)


def entering(value, axis, join, neutral, backward):
    count, mine = (lax.axis_size(axis), lax.axis_index(axis))
    pieces = jax.tree.map(lambda part: lax.all_gather(part, axis), value)
    if backward:
        pieces = jax.tree.map(lambda part: part[::-1], pieces)
        mine = count - 1 - mine
    subtotal = jax.tree.map(
        lambda part, zero: jnp.full_like(part, 0) + jnp.asarray(zero, part.dtype), value, neutral
    )

    def lap(position, subtotal):
        longer = join(subtotal, jax.tree.map(lambda part: part[position], pieces))
        return jax.tree.map(lambda new, old: jnp.where(position < mine, new, old), longer, subtotal)

    return lax.fori_loop(0, count - 1, lap, subtotal)


def from_behind(block, axis, distance):
    devices = range(lax.axis_size(axis))
    route = [(i - distance, i) for i in devices if i - distance in devices]
    return lax.ppermute(block, axis, route)


def compose(earlier, later):
    return (earlier[0] * later[0], later[0] * earlier[1] + later[1])


def local(tokens, reset_mask, weight, vectors, cotangent):
    width = weight.shape[1] // 3
    whole_weight, whole_vectors = (
        lax.all_gather(weight, ("gx", "gy"), axis=0, tiled=True),
        lax.all_gather(vectors, ("gx", "gy"), axis=1, tiled=True),
    )
    params = whole_vectors.astype(jnp.float32)
    gain = params[0]
    shift_bias = params[1]
    forget_peep = params[2]
    forget_bias = params[3]
    reset_peep = params[4]
    reset_bias = params[5]
    inputs = tokens.astype(jnp.float32)
    keep = (1 - reset_mask).astype(jnp.float32)[:, None]
    centred = inputs - jnp.mean(inputs, axis=1, keepdims=True)
    inv_std = lax.rsqrt(jnp.mean(centred * centred, axis=1, keepdims=True) + 1e-05)
    normed = centred * inv_std
    scaled = normed * gain + shift_bias
    rounded = scaled.astype(jnp.bfloat16)
    projected = jnp.dot(rounded, whole_weight, preferred_element_type=jnp.float32)
    candidate = projected[:, :width]
    forget_pre = projected[:, width : 2 * width]
    reset_pre = projected[:, 2 * width :]
    forget = jax.nn.sigmoid(forget_pre + forget_peep * scaled + forget_bias)
    decay = forget * keep
    inflow = (1.0 - forget) * candidate
    cum_decay, cum_state = lax.associative_scan(compose, (decay, inflow), axis=0)
    unit = (jnp.ones_like(cum_decay[-1]), jnp.zeros_like(cum_state[-1]))
    before = entering((cum_decay[-1], cum_state[-1]), ("gx", "gy"), compose, unit, False)
    state_in = before[1]
    state = cum_decay * state_in + cum_state
    previous = keep * jnp.concatenate([state_in[None], state[:-1]], 0)
    reset = jax.nn.sigmoid(reset_pre + reset_peep * previous + reset_bias)
    output = reset * state + (1.0 - reset) * inputs
    upstream = cotangent.astype(jnp.float32)
    reset_grad = upstream * (state - inputs) * reset * (1.0 - reset)
    through = keep * reset_peep * reset_grad
    next_decay, next_through = from_behind((decay[0], through[0]), ("gx", "gy"), -1)
    ahead = jnp.concatenate([decay[1:], next_decay[None]], 0)
    local_term = upstream * reset + jnp.concatenate([through[1:], next_through[None]], 0)
    flip_mult, flip_sum = lax.associative_scan(compose, (ahead[::-1], local_term[::-1]), axis=0)
    mult_back = flip_mult[::-1]
    sum_back = flip_sum[::-1]
    after = entering((mult_back[0], sum_back[0]), ("gx", "gy"), compose, unit, True)
    state_grad = mult_back * after[1] + sum_back
    candidate_grad = state_grad * (1.0 - forget)
    forget_grad = state_grad * (previous - candidate) * forget * (1.0 - forget)
    proj_grad = jnp.concatenate([candidate_grad, forget_grad, reset_grad], 1).astype(jnp.bfloat16)
    weight_grad = lax.psum_scatter(
        lax.dot_general(
            rounded, proj_grad, (((0,), (0,)), ((), ())), preferred_element_type=jnp.float32
        ),
        ("gx", "gy"),
        scatter_dimension=0,
        tiled=True,
    )
    scaled_grad = lax.dot_general(
        proj_grad,
        lax.all_gather(weight, ("gx", "gy"), axis=0, tiled=True),
        (((1,), (1,)), ((), ())),
        preferred_element_type=jnp.float32,
    )
    scaled_grad = scaled_grad + forget_grad * forget_peep
    vector_terms = jnp.stack(
        [
            jnp.sum(scaled_grad * normed, axis=0),
            jnp.sum(scaled_grad, axis=0),
            jnp.sum(forget_grad * scaled, axis=0),
            jnp.sum(forget_grad, axis=0),
            jnp.sum(reset_grad * previous, axis=0),
            jnp.sum(reset_grad, axis=0),
        ],
        0,
    )
    vector_grad = lax.psum_scatter(vector_terms, ("gx", "gy"), scatter_dimension=1, tiled=True)
    normed_grad = scaled_grad * gain
    input_grad = upstream * (1.0 - reset) + inv_std * (
        normed_grad
        - jnp.mean(normed_grad, axis=1, keepdims=True)
        - normed * jnp.mean(normed_grad * normed, axis=1, keepdims=True)
    )
    return (output.astype(jnp.bfloat16), input_grad, weight_grad, vector_grad)


SLOTS, SEND, PAIR, ZSEND = 8, 8, 4, 4
TOTALS, FORE, GRADS, BACK, WEIGH = 2, 4, 5, 7, 9
LAG1, LAG2, LAG3 = 2, 4, 6
LAST = 6
AHEAD_Z, AHEAD_B = 5, 3
BAND = 32
ACROSS = ((10, (0, 3, 5)), (14, (6, 8, 10)), (15, (11, 13, 15)))
ACROSS_SUM = ()


def layer_kernel(
    nx, ny, units,
    tok, cot, mask, weight, vectors,
    wall, pgm, outp, igo, wgo, vgo,
    vbuf, vecs, xs, gs, means, invs, rnd, rt, rtm, wf, pj, pv, grs, outs, stage, perm, pgs,
    wb, sb, rd, rx, ry, rz, zb, sg, vsum, vrows, vtot, vin, cz, keep, wraw, wsrc, vsrc,
    ach, bch, qch, sin, cin, m1a, m1b, m2a, m2b,
    zs, zr, os, bs, br, dsn, dr, cs, cr, ws,
    vzs, vzr, vxs, vxr, vo, wls, sts, rs, rr, ps, pr, pl_, wl, gos,
    e1as, e1ar, e1bs, e1br, e2as, e2ar, e2bs, e2br,
    fds, fdr, fxs, fxr, fys, fyr, fzs, fzr, vsn, vrc, ous,
):
    gx, gy, core, mate, xn, yn = place(ny)
    tokens, width = xs.shape
    rows = wsrc.shape[1]
    cols = wsrc.shape[2]
    block = rows * ny
    half, short = ny // 2, rows // 2
    groups = units // GROUP
    glanes = GROUP * LANES
    diag = xn + yn - gx
    own, xq, yq, dq = gx // 2, xn // 2, yn // 2, diag // 2
    count = nx * ny
    me = gx * ny + gy

    def peer_y(j):
        return lax.rem(gy + j, ny)

    def peer_x(j):
        return lax.rem(gx + j, nx)

    def each(n, run, start=0):
        lax.fori_loop(start, n, lambda i, _: (run(i), 0)[1], 0)

    barrier = pltpu.get_barrier_semaphore()

    def greet(j):
        to = lax.rem(me + j, count)
        pl.semaphore_signal(barrier, inc=1, device_id=(to // ny, lax.rem(to, ny)), device_id_type=MESH)

    raw = pltpu.make_async_copy(weight, wraw, wls)
    raw.start()
    each(count, greet, 1)

    def among(u, some):
        hit = u < 0
        for s in some:
            hit = hit | (u == s)
        return hit

    across = tuple(c for c, _ in ACROSS)
    turned = tuple(c for c, _, _ in ACROSS_SUM)

    def straight(u, run):
        pl.when(jnp.logical_not(among(u, across)))(lambda: run(u))

    chunks = width // glanes

    tok_load = pltpu.make_async_copy(tok, xs, sts.at[0])
    cot_load = pltpu.make_async_copy(cot, gs, sts.at[1])
    tok_load.start()
    cot_load.start()

    def vz(j):
        return remote(vsrc, vbuf.at[me], vzs.at[j - 1], vzr.at[j - 1], (gx, peer_y(j)))

    def vx(j):
        part = vbuf.at[pl.ds(gx * ny, ny)]
        return remote(part, part, vxs.at[j - 1], vxr.at[j - 1], (peer_x(j), gy))

    own_vec = pltpu.make_async_copy(vsrc, vbuf.at[me], vo)

    def z_copy(u, j):
        return remote(wsrc.at[u], wall.at[u, own, core, gy], zs.at[u, j - 1], zr.at[u, j - 1], (gx, peer_y(j)))

    def own_copy(u):
        return pltpu.make_async_copy(wsrc.at[u], wall.at[u, own, core, gy], os.at[u])

    def band_copy(u, i):
        to = (mate, xn, yn)[i]
        recv = cr.at[u, 0] if i == 0 else br.at[u, i - 1]
        part = wall.at[u, own, core]
        return remote(part, part, bs.at[u, i], recv, (to, gy))

    def diag_copy(u, i):
        part = wall.at[u, (xq, yq)[i], core, half * i:half * (i + 1)]
        return remote(part, part, dsn.at[u, i], dr.at[u, i], ((yn, xn)[i], gy))

    def core_copy(u, i):
        part = wall.at[u, (own, xq, yq, dq)[i], core]
        return remote(part, part, cs.at[u, i - 1], cr.at[u, i], (mate, gy))

    def z_start(u):
        own_copy(u).start()
        for j in range(1, ny):
            z_copy(u, j).start()

    def z_wait(u):
        own_copy(u).wait()
        for j in range(1, ny):
            z_copy(u, j).wait_recv()
        for i in (1, 2, 0):
            band_copy(u, i).start()

    def xy_wait(u):
        for i in (1, 2):
            band_copy(u, i).wait_recv()
        for i in (0, 1):
            diag_copy(u, i).start()
        for i in (1, 2):
            core_copy(u, i).start()

    def diag_wait(u):
        for i in (0, 1):
            diag_copy(u, i).wait_recv()
        core_copy(u, 3).start()

    def core_wait(u):
        band_copy(u, 0).wait_recv()
        for i in (1, 2, 3):
            core_copy(u, i).wait_recv()

    def a_copy(u, i):
        return remote(
            wsrc.at[u], wall.at[u, own, core, gy], bs.at[u, i], br.at[u, i - 1], ((None, xn, yn)[i], gy)
        )

    def a_diag(u, i):
        part = wall.at[u, (xq, yq)[i], core, gy, short * i:short * (i + 1)]
        return remote(part, part, dsn.at[u, i], dr.at[u, i], ((yn, xn)[i], gy))

    def a_up(u, h):
        part = wall.at[u, :, core, gy - h]
        return remote(part, part, zs.at[u, h], zr.at[u, h], (gx, lax.rem(gy + 1, ny)))

    def a_down(u, h):
        part = wall.at[u, :, core, gy + h]
        return remote(part, part, cs.at[u, h], cr.at[u, h + 1], (gx, lax.rem(gy + ny - 1, ny)))

    def a_landed(u, h):
        pl.when(gy > h)(lambda: a_up(u, h).wait_recv())
        pl.when(gy + h + 1 < ny)(lambda: a_down(u, h).wait_recv())

    def a_hop(u, h):
        if h:
            a_landed(u, h - 1)
        pl.when((gy + 1 < ny) & (gy >= h))(lambda: a_up(u, h).start())
        pl.when((gy >= 1) & (gy + h < ny))(lambda: a_down(u, h).start())

    def a_left(u, h):
        pl.when((gy + 1 < ny) & (gy >= h))(lambda: a_up(u, h).wait_send())
        pl.when((gy >= 1) & (gy + h < ny))(lambda: a_down(u, h).wait_send())

    def a_core(u):
        part = wall.at[u, :, core]
        return remote(part, part, bs.at[u, 0], cr.at[u, 0], (mate, gy))

    def a_start(u):
        own_copy(u).start()
        for i in (1, 2):
            a_copy(u, i).start()

    def a_turn(u):
        own_copy(u).wait()
        for i in (1, 2):
            a_copy(u, i).wait_recv()
        for i in (0, 1):
            a_diag(u, i).start()

    def a_meet(u):
        for i in (0, 1):
            a_diag(u, i).wait_recv()

    def a_share(u):
        a_landed(u, ny - 2)
        a_core(u).start()

    zero = jnp.zeros((vectors.shape[0], LANES - rows), BF16)
    odd = lax.rem(me, 2) == 1
    tile = jnp.where(
        odd, jnp.concatenate([zero, vectors[...]], 1).astype(F32), jnp.concatenate([vectors[...], zero], 1).astype(F32)
    )
    pad = jnp.zeros((16 - vectors.shape[0], LANES), F32)
    vsrc[...] = jnp.concatenate([tile, pad], 0).astype(BF16)
    raw.wait()
    for u in range(units):
        for s in range(3):
            at = s * width + u * LANES
            wsrc[u, :, s * LANES:(s + 1) * LANES] = wraw[:, at:at + LANES]

    pl.semaphore_wait(barrier, count - 1)
    own_vec.start()
    for j in range(1, ny):
        vz(j).start()
    for u in across:
        a_start(u)
    z_start(0)

    def to_runs(i, into):
        at = slice(i * glanes, (i + 1) * glanes)
        into[:, at] = jnp.dot(perm[...], into[:, at], preferred_element_type=F32).astype(BF16)

    def moments(i):
        r = pl.ds(pl.multiple_of(i * BAND, BAND), BAND)
        x = xs[r, :].astype(F32)
        mean = jnp.mean(x, axis=1, keepdims=True)
        centred = x - mean
        inv = lax.rsqrt(jnp.mean(centred * centred, axis=1, keepdims=True) + EPS)
        means[r, :] = jnp.broadcast_to(mean, (BAND, LANES))
        invs[r, :] = jnp.broadcast_to(inv, (BAND, LANES))

    def rounding(i):
        r = pl.ds(pl.multiple_of(i * BAND, BAND), BAND)
        normed = (xs[r, :].astype(F32) - means[r, 0:1]) * invs[r, 0:1]
        rnd[r, :] = (normed * vecs[0:1, :] + vecs[1:2, :]).astype(BF16)

    quads = nx // 2

    def turn(i):
        at = pl.ds(pl.multiple_of(i * block, 16), block)
        rt[at, 0:tokens] = rnd[:, pl.ds(pl.multiple_of((2 * i + core) * block, LANES), block)].T
        rtm[at, :] = rnd[:, pl.ds(pl.multiple_of((2 * i + 1 - core) * block, LANES), block)].T

    r_mate = remote(rtm, rt.at[:, tokens:2 * tokens], rs, rr, (mate, gy))

    def gather_tick(k):
        pl.when(k + AHEAD_Z < units)(lambda: straight(k + AHEAD_Z, z_start))
        pl.when(k + AHEAD_B < units)(lambda: straight(k + AHEAD_B, z_wait))
        pl.when(k < units)(lambda: straight(k, xy_wait))
        pl.when((k >= 1) & (k <= units))(lambda: straight(k - 1, diag_wait))
        for c, times in ACROSS:
            for j, t in enumerate(times):
                pl.when(k == t)(functools.partial(a_hop, c, j))
            pl.when(k == c + 1)(functools.partial(a_share, c))

    bands = tokens // BAND
    perm[...] = run_matrix(tokens, False)
    tok_load.wait()
    for i in range(chunks // 2):
        to_runs(i, xs)
    z_wait(0)
    z_start(1)
    z_start(2)
    for i in range(chunks // 2, chunks):
        to_runs(i, xs)
    own_vec.wait()
    for j in range(1, ny):
        vz(j).wait_recv()
    for j in range(1, nx):
        vx(j).start()
    for u in across:
        a_turn(u)
    z_wait(1)
    for u in range(3, AHEAD_Z):
        z_start(u)
    each(bands // 2, moments)
    for u in range(2, AHEAD_B):
        z_wait(u)
    for u in across:
        a_meet(u)
    gather_tick(0)
    each(bands, moments, bands // 2)
    for j in range(1, nx):
        vx(j).wait_recv()
    for c in range(width // LANES):
        part = vbuf[2 * c].astype(F32) + vbuf[2 * c + 1].astype(F32)
        vecs[:, c * LANES:(c + 1) * LANES] = part[0:8, :]
    each(bands // 2, rounding)
    gather_tick(1)
    each(bands, rounding, bands // 2)
    kept = (1 - mask[...]).astype(F32)
    keep[...] = jnp.dot(
        (perm[...].astype(F32) * kept).astype(BF16), jnp.ones((tokens, LANES), BF16), preferred_element_type=F32
    )
    cot_load.wait()
    for i in range(chunks // 2):
        to_runs(i, gs)
    gather_tick(2)
    straight(0, core_wait)

    def late_start():
        for i in range(chunks // 2, chunks):
            to_runs(i, gs)
        perm[...] = run_matrix(tokens, True)

    def late_turn():
        each(quads, turn)
        r_mate.start()

    def e_copies(buf, send, recv, q, level):
        if level == 0:
            return [
                remote(buf.at[q, gy], buf.at[q, gy], send.at[q, j - 1], recv.at[q, j - 1], (gx, peer_y(j)))
                for j in range(1, ny)
            ]
        return [
            remote(buf.at[q, gx], buf.at[q, gx], send.at[q, j - 1], recv.at[q, j - 1], (peer_x(j), gy))
            for j in range(1, nx)
        ]

    def e_start(*a):
        for c in e_copies(*a):
            c.start()

    def e_wait(*a):
        for c in e_copies(*a):
            c.wait_recv()

    double = tokens // (2 * RUNS)

    def side(u):
        return pl.ds(pl.multiple_of(lax.rem(u, 2) * cols, LANES), cols)

    def front_load(u):
        return pltpu.make_async_copy(wall.at[u], wf.at[:, :, :, :, side(u)], ws.at[lax.rem(u, 2)])

    def project(u):
        front_load(u - 1).wait()
        front_load(u).wait()
        both = jnp.dot(rnd[...], wf[...].reshape(width, -1), preferred_element_type=F32)
        pj[lax.rem(u - 1, SLOTS)] = both[:, :cols]
        pj[lax.rem(u, SLOTS)] = both[:, cols:]

    def vec(i, u):
        return vecs[i:i + 1, lanes_of(u)]

    def scale(u, r, gain, shift):
        return (xs[r, lanes_of(u)].astype(F32) - means[r, :]) * invs[r, :] * gain + shift

    def gates(u):
        slot = lax.rem(u, SLOTS)
        gain, shift, vf, bf = (vec(i, u) for i in range(4))

        def step(i, carry):
            a, b = carry
            r = pl.ds(pl.multiple_of(i * 16, 16), 16)
            f = jax.nn.sigmoid(pj[slot, r, LANES:2 * LANES] + vf * scale(u, r, gain, shift) + bf)
            pj[slot, r, LANES:2 * LANES] = f
            d = f * keep[r, :]
            inflow = (1.0 - f) * pj[slot, r, 0:LANES]
            for h in (0, 8):
                a = a * d[h:h + 8]
                b = d[h:h + 8] * b + inflow[h:h + 8]
            return a, b

        a, b = lax.fori_loop(0, double, step, (jnp.ones((RUNS, LANES), F32), jnp.zeros((RUNS, LANES), F32)), unroll=4)
        q, j = u // GROUP, lax.rem(u, GROUP)
        ach[q, :, lanes_of(j)] = a
        bch[q, :, lanes_of(j)] = b

    def totals(q):
        a, b = jnp.ones((1, glanes), F32), jnp.zeros((1, glanes), F32)
        for s in range(RUNS):
            one = ach[q, s:s + 1, :]
            a = a * one
            b = one * b + bch[q, s:s + 1, :]
        m1a[q, gy, 0:1, :] = a
        m1a[q, gy, 1:2, :] = b
        e_start(m1a, e1as, e1ar, q, 0)

    def totals_x(q):
        e_wait(m1a, e1as, e1ar, q, 0)
        a, b = jnp.ones((1, glanes), F32), jnp.zeros((1, glanes), F32)
        for s in range(ny):
            one = m1a[q, s, 0:1, :]
            a = a * one
            b = one * b + m1a[q, s, 1:2, :]
        m1b[q, gx, 0:1, :] = a
        m1b[q, gx, 1:2, :] = b
        e_start(m1b, e1bs, e1br, q, 1)

    def enter(q):
        e_wait(m1b, e1bs, e1br, q, 1)
        s = jnp.zeros((1, glanes), F32)
        s = lax.fori_loop(0, gx, lambda i, s: m1b[q, i, 0:1, :] * s + m1b[q, i, 1:2, :], s)
        s = lax.fori_loop(0, gy, lambda i, s: m1a[q, i, 0:1, :] * s + m1a[q, i, 1:2, :], s)
        for r in range(RUNS):
            sin[q, r:r + 1, :] = s
            s = ach[q, r:r + 1, :] * s + bch[q, r:r + 1, :]

    def forward(u):
        slot = lax.rem(u, SLOTS)
        q, j = u // GROUP, lax.rem(u, GROUP)
        vr, br_ = vec(4, u), vec(5, u)
        zero = jnp.zeros((RUNS, LANES), F32)

        def step(i, carry):
            s, run, t, v4, v5 = carry
            r = pl.ds(pl.multiple_of(i * 16, 16), 16)
            f = pj[slot, r, LANES:2 * LANES]
            k = keep[r, :]
            inflow = (1.0 - f) * pj[slot, r, 0:LANES]
            prevs, states = [], []
            for h in (0, 8):
                prev = k[h:h + 8] * s
                s = f[h:h + 8] * prev + inflow[h:h + 8]
                prevs.append(prev)
                states.append(s)
            prev, state = jnp.concatenate(prevs, 0), jnp.concatenate(states, 0)
            x = xs[r, lanes_of(u)].astype(F32)
            up = gs[r, lanes_of(u)].astype(F32)
            reset = jax.nn.sigmoid(pj[slot, r, 2 * LANES:3 * LANES] + vr * prev + br_)
            rest = 1.0 - reset
            outs[r, lanes_of(j)] = (reset * state + rest * x).astype(BF16)
            rg = up * (state - x) * reset * rest
            pj[slot, r, 2 * LANES:3 * LANES] = rg
            pv[slot, r, :] = prev
            grs[r, lanes_of(u)] = up * rest
            local = up * reset
            d, through = f * k, k * vr * rg
            for h in (0, 8):
                t = t + run * through[h:h + 8]
                run = run * d[h:h + 8]
                t = t + run * local[h:h + 8]
                v4 = v4 + rg[h:h + 8] * prev[h:h + 8]
                v5 = v5 + rg[h:h + 8]
            return s, run, t, v4, v5

        init = (sin[q, :, lanes_of(j)], jnp.ones((RUNS, LANES), F32), zero, zero, zero)
        _, _, t, v4, v5 = lax.fori_loop(0, double, step, init, unroll=4)
        qch[q, :, lanes_of(j)] = t
        vsum[4:5, lanes_of(u)] = jnp.sum(v4, axis=0, keepdims=True)
        vsum[5:6, lanes_of(u)] = jnp.sum(v5, axis=0, keepdims=True)

    def out_copy(q):
        c = pl.ds(pl.multiple_of(q * glanes, LANES), glanes)
        return pltpu.make_async_copy(stage.at[lax.rem(q, 2)], outp.at[:, c], gos.at[q])

    def forward_group(q):
        enter(q)
        pl.when(q >= 2)(lambda: out_copy(q - 2).wait())
        each(GROUP, lambda j: forward(q * GROUP + j))
        s = jnp.zeros((1, glanes), F32)
        for r in reversed(range(RUNS)):
            s = ach[q, r:r + 1, :] * s + qch[q, r:r + 1, :]
        m2a[q, gy, 0:1, :] = s
        e_start(m2a, e2as, e2ar, q, 0)
        stage[lax.rem(q, 2)] = jnp.dot(perm[...], outs[...], preferred_element_type=F32).astype(BF16)
        out_copy(q).start()

    def grads_x(q):
        e_wait(m2a, e2as, e2ar, q, 0)
        s = jnp.zeros((1, glanes), F32)
        for r in reversed(range(ny)):
            s = m1a[q, r, 0:1, :] * s + m2a[q, r, 0:1, :]
        m2b[q, gx, 0:1, :] = s
        e_start(m2b, e2bs, e2br, q, 1)

    def enter_back(q):
        e_wait(m2b, e2bs, e2br, q, 1)
        s = jnp.zeros((1, glanes), F32)

        def over_x(i, s):
            return m1b[q, nx - 1 - i, 0:1, :] * s + m2b[q, nx - 1 - i, 0:1, :]

        def over_y(i, s):
            return m1a[q, ny - 1 - i, 0:1, :] * s + m2a[q, ny - 1 - i, 0:1, :]

        s = lax.fori_loop(0, nx - 1 - gx, over_x, s)
        s = lax.fori_loop(0, ny - 1 - gy, over_y, s)
        for r in reversed(range(RUNS)):
            cin[q, r:r + 1, :] = s
            s = ach[q, r:r + 1, :] * s + qch[q, r:r + 1, :]

    def pg_mate(u):
        return remote(pgs.at[lax.rem(u, PAIR), 0:tokens], pgm.at[u], ps.at[u], pr.at[u], (mate, gy))

    def backward(u):
        slot, pair = lax.rem(u, SLOTS), lax.rem(u, PAIR)
        q, j = u // GROUP, lax.rem(u, GROUP)
        gain, shift, vr = vec(0, u), vec(1, u), vec(4, u)
        zero = jnp.zeros((RUNS, LANES), F32)

        def step(i, carry):
            c, v2, v3 = carry
            r = pl.ds(pl.multiple_of((double - 1 - i) * 16, 16), 16)
            f = pj[slot, r, LANES:2 * LANES]
            k = keep[r, :]
            rg = pj[slot, r, 2 * LANES:3 * LANES]
            local = gs[r, lanes_of(u)].astype(F32) - grs[r, lanes_of(u)]
            d, through = f * k, k * vr * rg
            grads = [None, None]
            for h in (1, 0):
                part = slice(8 * h, 8 * h + 8)
                grads[h] = local[part] + c
                c = d[part] * grads[h] + through[part]
            grad = jnp.concatenate(grads, 0)
            cg = grad * (1.0 - f)
            fg = cg * (pv[slot, r, :] - pj[slot, r, 0:LANES]) * f
            pgs[pair, r, 0:LANES] = cg.astype(BF16)
            pgs[pair, r, LANES:2 * LANES] = fg.astype(BF16)
            pgs[pair, r, 2 * LANES:3 * LANES] = rg.astype(BF16)
            fs = fg * scale(u, r, gain, shift)
            return c, v2 + fs[0:8] + fs[8:16], v3 + fg[0:8] + fg[8:16]

        _, v2, v3 = lax.fori_loop(0, double, step, (cin[q, :, lanes_of(j)], zero, zero), unroll=4)
        vsum[2:3, lanes_of(u)] = jnp.sum(v2, axis=0, keepdims=True)
        vsum[3:4, lanes_of(u)] = jnp.sum(v3, axis=0, keepdims=True)
        pg_mate(u).start()

    def backward_group(q):
        enter_back(q)
        each(GROUP, lambda j: backward(q * GROUP + j))
        drain_group(q)

    def pg_load(u):
        return pltpu.make_async_copy(pgm.at[u], pgs.at[lax.rem(u, PAIR), tokens:2 * tokens], pl_)

    def back_load(u):
        return pltpu.make_async_copy(wall.at[u], wb, wl)

    def some(part):
        return pl.ds(part * half, half)

    def sent(u):
        return sb.at[lax.rem(u, SEND)]

    def d_copy(u, i):
        return remote(
            sent(u).at[dq, some(i)], rd.at[u, some(i)], fds.at[u, i], fdr.at[u, i], ((yn, xn)[i], gy)
        )

    def x_copy(u, i):
        return remote(sent(u).at[xq, some(i)], rx.at[u, some(i)], fxs.at[u, i], fxr.at[u, i], (xn, gy))

    def y_copy(u, i):
        return remote(sent(u).at[yq, some(i)], ry.at[u, some(i)], fys.at[u, i], fyr.at[u, i], (yn, gy))

    def f_copy(u, j):
        to = lax.rem(gy + j, ny)
        return remote(zb.at[lax.rem(u, ZSEND), to], rz.at[u, j - 1], fzs.at[u, j - 1], fzr.at[u, j - 1], (gx, to))

    def next_loads(u):
        pg_mate(u).wait_recv()
        pg_load(u).start()
        back_load(u).start()

    def weigh(u):
        slot, pair = lax.rem(u, SEND), lax.rem(u, PAIR)

        @pl.when((u >= SEND) & jnp.logical_not(among(u - SEND, turned)))
        def _():
            for i in (0, 1):
                d_copy(u - SEND, i).wait_send()
                x_copy(u - SEND, i).wait_send()
                y_copy(u - SEND, i).wait_send()

        pg_load(u).wait()
        sb[slot] = jnp.dot(rt[...], pgs[pair], preferred_element_type=F32).astype(BF16).reshape(sb.shape[1:])

        @pl.when(jnp.logical_not(among(u, turned)))
        def _():
            for i in (0, 1):
                d_copy(u, i).start()
            x_copy(u, 1).start()
            y_copy(u, 0).start()

    def spread(u):
        pair = lax.rem(u, PAIR)
        back_load(u).wait()
        mine = pgs[pair, 0:tokens, :]
        sg[...] += lax.dot_general(mine, wb[...].reshape(width, -1), (((1,), (1,)), ((), ())), preferred_element_type=F32)
        sg[:, lanes_of(u)] += pgs[pair, 0:tokens, LANES:2 * LANES].astype(F32) * vecs[2:3, lanes_of(u)]
        pg_mate(u).wait_send()

    def fold(ref, at, more):
        ref[at] = (ref[at].astype(F32) + more.astype(F32)).astype(BF16)

    def meet(u):
        slot = lax.rem(u, SEND)
        for i in (0, 1):
            d_copy(u, i).wait_recv()
        fold(sb, (slot, xq, some(0)), rd[u, 0:half])
        x_copy(u, 0).start()
        fold(sb, (slot, yq, some(1)), rd[u, half:ny])
        y_copy(u, 1).start()

    def column(u):
        slot, zslot = lax.rem(u, SEND), lax.rem(u, ZSEND)

        @pl.when((u >= ZSEND) & jnp.logical_not(among(u - ZSEND, turned)))
        def _():
            for j in range(1, ny):
                f_copy(u - ZSEND, j).wait_send()

        for i in (0, 1):
            x_copy(u, i).wait_recv()
            y_copy(u, i).wait_recv()
        total = sb[slot, own].astype(F32) + rx[u].astype(F32) + ry[u].astype(F32)
        zb[zslot] = total.astype(BF16)
        for j in range(1, ny):
            f_copy(u, j).start()

    def settle(u):
        slot = lax.rem(u, SEND)
        total = sb[slot, own, gy].astype(F32) + rx[u, gy].astype(F32) + ry[u, gy].astype(F32)
        for j in range(1, ny):
            f_copy(u, j).wait_recv()
        for j in range(1, ny):
            total = total + rz[u, j - 1].astype(F32)
        place_sum(u, total)

    def place_sum(u, total):
        for i in range(3):
            wgo[:, lanes_of(u + i * units)] = total[:, i * LANES:(i + 1) * LANES]

    def part(i):
        return pl.ds(i * short, short)

    def b_z(u, j):
        to = peer_y(j)
        return remote(sent(u).at[:, to], (rd, rx, ry)[j - 1].at[u], fzs.at[u, j - 1], fzr.at[u, j - 1], (gx, to))

    def b_diag(u, n, i):
        return remote(cz.at[n, dq, part(i)], rz.at[u, 0, part(i)], fds.at[u, i], fdr.at[u, i], ((yn, xn)[i], gy))

    def b_x(u, n, i):
        return remote(cz.at[n, xq, part(i)], rz.at[u, 1, part(i)], fxs.at[u, i], fxr.at[u, i], (xn, gy))

    def b_y(u, n, i):
        return remote(cz.at[n, yq, part(i)], rz.at[u, 2, part(i)], fys.at[u, i], fyr.at[u, i], (yn, gy))

    def b_gather(u, n):
        for j in range(1, ny):
            b_z(u, j).wait()
            if u >= ZSEND and u - ZSEND not in turned:
                f_copy(u - ZSEND, j).wait_send()
        total = sb[lax.rem(u, SEND), :, gy].astype(F32)
        for ref in (rd, rx, ry):
            total = total + ref[u].astype(F32)
        cz[n] = total.astype(BF16)
        for i in (0, 1):
            b_diag(u, n, i).start()
        b_x(u, n, 1).start()
        b_y(u, n, 0).start()

    def b_meet(u, n):
        for i in (0, 1):
            b_diag(u, n, i).wait_recv()
        fold(cz, (n, xq, part(0)), rz[u, 0, part(0)])
        b_x(u, n, 0).start()
        fold(cz, (n, yq, part(1)), rz[u, 0, part(1)])
        b_y(u, n, 1).start()

    def b_settle(u, n):
        for i in (0, 1):
            b_x(u, n, i).wait_recv()
            b_y(u, n, i).wait_recv()
        place_sum(u, cz[n, own].astype(F32) + rz[u, 1].astype(F32) + rz[u, 2].astype(F32))

    def b_drain(u, n):
        for i in (0, 1):
            b_diag(u, n, i).wait_send()
            b_x(u, n, i).wait_send()
            b_y(u, n, i).wait_send()

    def finish(i):
        r = pl.ds(pl.multiple_of(i * BAND, BAND), BAND)
        s = sg[r, :]
        inv = invs[r, 0:1]
        z = (xs[r, :].astype(F32) - means[r, 0:1]) * inv
        sz = s * z
        gain = vecs[0:1, :]
        vrows[0:8, :] += jnp.sum(sz.reshape(BAND // 8, 8, width), axis=0)
        vrows[8:16, :] += jnp.sum(s.reshape(BAND // 8, 8, width), axis=0)
        n = s * gain
        m1 = jnp.mean(n, axis=1, keepdims=True)
        m2 = jnp.mean(sz * gain, axis=1, keepdims=True)
        sg[r, :] = grs[r, :] + inv * (n - m1 - z * m2)

    def v_copy(j):
        to = lax.rem(me + j, count)
        return remote(vtot.at[to // 2], vin.at[me], vsn.at[to], vrc.at[me], (to // ny, lax.rem(to, ny)))

    def v_recv(j):
        at = lax.rem(me + j, count)
        return remote(vtot.at[0], vin.at[at], vsn.at[at], vrc.at[at], (at // ny, lax.rem(at, ny)))

    def vectors_out():
        zero = jnp.zeros((2, LANES), F32)
        for c in range(width // LANES):
            at = slice(c * LANES, (c + 1) * LANES)
            top = [jnp.sum(vrows[8 * v:8 * v + 8, at], axis=0, keepdims=True) for v in (0, 1)]
            vtot[c] = jnp.concatenate(top + [vsum[2:6, at], zero], 0)
        each(count, lambda j: v_copy(j).start(), 1)

    quarter = width // 4

    def grad_copy(c):
        return pltpu.make_async_copy(grs.at[:, pl.ds(c * quarter, quarter)], igo.at[:, pl.ds(c * quarter, quarter)], ous.at[c])

    def natural():
        for c in range(4):
            at = slice(c * quarter, (c + 1) * quarter)
            v = sg[:, at]
            high = v.astype(BF16)
            low = (v - high.astype(F32)).astype(BF16)
            grs[:, at] = jnp.dot(perm[...], high, preferred_element_type=F32) + jnp.dot(
                perm[...], low, preferred_element_type=F32
            )
            grad_copy(c).start()

    def drain(u):
        for j in range(1, ny):
            z_copy(u, j).wait_send()
        for i in range(3):
            band_copy(u, i).wait_send()
        for i in (0, 1):
            diag_copy(u, i).wait_send()
        for i in (1, 2, 3):
            core_copy(u, i).wait_send()

    def drain_group(q):
        for a in ((m1a, e1as, e1ar, q, 0), (m1b, e1bs, e1br, q, 1), (m2a, e2as, e2ar, q, 0), (m2b, e2bs, e2br, q, 1)):
            for c in e_copies(*a):
                c.wait_send()

    def drain_first():
        for c in across:
            for h in range(ny - 1):
                a_left(c, h)
            for i in (1, 2):
                a_copy(c, i).wait_send()
            for i in (0, 1):
                a_diag(c, i).wait_send()
            a_core(c).wait_send()
        for j in range(1, ny):
            vz(j).wait_send()
        for j in range(1, nx):
            vx(j).wait_send()
        r_mate.wait_send()

    def vectors_in():
        each(count, lambda j: v_recv(j).wait_recv(), 1)
        vin[me] = vtot[me // 2]
        total = lax.fori_loop(0, count, lambda j, s: s + vin[j], jnp.zeros((8, LANES), F32))
        vgo[...] = jnp.where(odd, total[0:6, rows:2 * rows], total[0:6, 0:rows])
        each(count, lambda j: v_copy(j).wait_send(), 1)

    def tick(k, _):
        u = k - 3
        v = u - WEIGH
        gather_tick(k)
        pl.when(k == 3)(late_start)
        pl.when(k == 5)(late_turn)

        def summed(lag, run):
            w = v - lag
            pl.when((w >= 0) & (w < units) & jnp.logical_not(among(w, turned)))(lambda: run(w))

        summed(LAG1, meet)
        summed(LAG2, column)
        summed(LAG3, settle)
        for n, (c, _, steps) in enumerate(ACROSS_SUM):
            for t, run in zip(steps, (b_gather, b_meet, b_settle)):
                pl.when(v == t)(functools.partial(run, c, n))

        @pl.when(v == 0)
        def _():
            r_mate.wait_recv()
            sg[...] = jnp.zeros_like(sg)
            vrows[...] = jnp.zeros_like(vrows)

        @pl.when((v >= 0) & (v < units))
        def _():
            weigh(v)
            spread(v)

        for c, times, _ in ACROSS_SUM:
            for j, t in enumerate(times):
                pl.when(v == t)(lambda c=c, j=j: b_z(c, j + 1).start())

        pl.when((v >= -1) & (v < units - 1))(lambda: next_loads(v + 1))

        def event(lag, run):
            g = (u - lag) // GROUP
            pl.when((u >= lag) & (lax.rem(u - lag + GROUP, GROUP) == 0) & (g < groups))(lambda: run(g))

        event(BACK, backward_group)
        event(GRADS, grads_x)
        event(FORE, forward_group)
        event(TOTALS, totals_x)

        paired = (u >= 0) & (u < units) & (lax.rem(u, 2) == 1)

        @pl.when(paired)
        def _():
            project(u)

        @pl.when((u >= 0) & (u < units - 1))
        def _():
            straight(u + 1, core_wait)
            for c in across:
                pl.when(u + 1 == c)(lambda c=c: a_core(c).wait_recv())
            front_load(u + 1).start()

        @pl.when(paired)
        def _():
            gates(u - 1)
            gates(u)
            totals(u // GROUP)

        pl.when(v == units)(lambda: each(bands // 2, finish))

        @pl.when(v == units + 1)
        def _():
            each(bands, finish, bands // 2)
            vectors_out()

        pl.when(v == units + 2)(natural)
        pl.when(v == units + 3)(vectors_in)
        w = k - units - 1

        @pl.when((w >= 0) & (w < units))
        def _():
            straight(w, drain)

        pl.when(w == 4)(drain_first)
        return 0

    front_load(0).start()
    lax.fori_loop(3, units + WEIGH + 3 + LAST, tick, 0)

    for n, c in enumerate(turned):
        b_drain(c, n)

    def drain_send(u):
        for i in (0, 1):
            d_copy(u, i).wait_send()
            x_copy(u, i).wait_send()
            y_copy(u, i).wait_send()

    each(units, lambda u: pl.when(jnp.logical_not(among(u, turned)))(lambda: drain_send(u)), units - SEND)

    def drain_z(u):
        for j in range(1, ny):
            f_copy(u, j).wait_send()

    each(units, drain_z, units - ZSEND)

    for q in range(groups - 2, groups):
        out_copy(q).wait()
    for c in range(4):
        grad_copy(c).wait()


def layer(nx, ny, tok, cot, mask, weight, vectors):
    tokens, width = tok.shape
    rows, cols = weight.shape[0], 3 * LANES
    units = width // LANES
    groups, glanes, block, count = units // GROUP, GROUP * LANES, rows * ny, nx * ny
    dma = pltpu.SemaphoreType.DMA
    any_, vmem = pl.BlockSpec(memory_space=pl.ANY), pl.BlockSpec(memory_space=pltpu.VMEM)
    msg = RUNS, glanes
    s, v = jax.ShapeDtypeStruct, pltpu.VMEM
    return pl.pallas_call(
        functools.partial(layer_kernel, nx, ny, units),
        name="layer",
        out_shape=(
            s((units, nx // 2, 2, ny, rows, cols), BF16), s((units, tokens, cols), BF16),
            s((tokens, width), BF16), s((tokens, width), F32), s((rows, 3 * width), F32), s(vectors.shape, F32),
        ),
        in_specs=[any_, any_, vmem, any_, vmem],
        out_specs=(any_,) * 4 + (vmem,) * 2,
        scratch_shapes=[
            v((count, 16, LANES), BF16), v((8, width), F32),
            v((tokens, width), BF16), v((tokens, width), BF16), v((tokens, LANES), F32), v((tokens, LANES), F32),
            v((tokens, width), BF16), v((width // 2, 2 * tokens), BF16), v((width // 2, tokens), BF16),
            v((nx // 2, 2, ny, rows, 2 * cols), BF16),
            v((SLOTS, tokens, cols), F32), v((SLOTS, tokens, LANES), F32),
            v((tokens, width), F32), v((tokens, glanes), BF16), v((2, tokens, glanes), BF16),
            v((tokens, tokens), BF16), v((PAIR, 2 * tokens, cols), BF16),
            v((nx // 2, 2, ny, rows, cols), BF16), v((SEND, nx // 2, ny, rows, cols), BF16),
            *[v((units, ny, rows, cols), BF16)] * 3,
            v((units, ny - 1, rows, cols), BF16), v((ZSEND, ny, rows, cols), BF16),
            v((tokens, width), F32), v((8, width), F32), v((16, width), F32),
            v((width // LANES, 8, LANES), F32), v((count, 8, LANES), F32),
            v((max(1, len(ACROSS_SUM)), nx // 2, rows, cols), BF16), v((tokens, LANES), F32),
            v((rows, 3 * width), BF16), v((units, rows, cols), BF16), v((16, LANES), BF16),
            *[v((groups,) + msg, F32)] * 5,
            v((groups, ny, 2, glanes), F32), v((groups, nx, 2, glanes), F32),
            v((groups, ny, 1, glanes), F32), v((groups, nx, 1, glanes), F32),
            dma((units, ny - 1)), dma((units, ny - 1)), dma((units,)), dma((units, 3)), dma((units, 2)),
            dma((units, 2)), dma((units, 2)), dma((units, 3)), dma((units, 4)), dma((2,)),
            dma((ny - 1,)), dma((ny - 1,)), dma((nx - 1,)), dma((nx - 1,)), dma, dma, dma((2,)),
            dma, dma, dma((units,)), dma((units,)), dma, dma, dma((groups,)),
            dma((groups, ny - 1)), dma((groups, ny - 1)), dma((groups, nx - 1)), dma((groups, nx - 1)),
            dma((groups, ny - 1)), dma((groups, ny - 1)), dma((groups, nx - 1)), dma((groups, nx - 1)),
            *[dma((units, 2))] * 6, dma((units, ny - 1)), dma((units, ny - 1)),
            dma((count,)), dma((count,)), dma((4,)),
        ],
        compiler_params=pltpu.CompilerParams(
            collective_id=0, has_side_effects=True, vmem_limit_bytes=62 * 2**20
        ),
        cost_estimate=pl.CostEstimate(
            flops=6 * tokens * width * units * cols, bytes_accessed=4 * width * units * cols, transcendentals=0
        ),
    )(tok, cot, mask, weight, vectors)


def fast(nx, ny, tokens, reset_mask, weight, vectors, cotangent):
    mask = reset_mask.reshape(1, -1)
    return layer(nx, ny, tokens, cotangent, mask, weight, vectors)[2:]


def solution(mesh):
    placed = (
        P(("gx", "gy"), None),
        P(("gx", "gy")),
        P(("gx", "gy"), None),
        P(None, ("gx", "gy")),
        P(("gx", "gy"), None),
    )
    nx, ny = mesh.shape["gx"], mesh.shape["gy"]

    def body(tokens, reset_mask, weight, vectors, cotangent):
        whole_tiles = weight.shape[0] % 16 == 0 and tokens.shape[0] % 256 == 0
        if (nx, ny) == (8, 4) and whole_tiles and 2 * weight.shape[0] == LANES and tokens.shape[1] % 2048 == 0:
            return fast(nx, ny, tokens, reset_mask, weight, vectors, cotangent)
        return local(tokens, reset_mask, weight, vectors, cotangent)

    return jax.shard_map(
        body,
        mesh=mesh,
        in_specs=placed,
        out_specs=(
            P(("gx", "gy"), None),
            P(("gx", "gy"), None),
            P(("gx", "gy"), None),
            P(None, ("gx", "gy")),
        ),
        check_vma=False,
    )
```

```python
import functools

import jax
import jax.numpy as jnp
from jax import lax
from jax.experimental import pallas as pl
from jax.experimental.pallas import tpu as pltpu
from jax.sharding import PartitionSpec as P

MESH = pl.DeviceIdType.MESH
F32, BF16 = jnp.float32, jnp.bfloat16
LANES, RUNS, GROUP = 128, 8, 2
EPS = 1e-05


def place(ny):
    gx, gy = lax.axis_index("gx"), lax.axis_index("gy")
    core, xx, yy = lax.rem(gx, 2), lax.rem(gx // 2, 2), gx // 4
    return gx, gy, core, gx + 1 - 2 * core, gx + 2 - 4 * xx, gx + 4 - 8 * yy


def remote(src, dst, send, recv, to):
    return pltpu.make_async_remote_copy(
        src_ref=src, dst_ref=dst, send_sem=send, recv_sem=recv, device_id=to, device_id_type=MESH
    )


def lanes_of(b):
    return pl.ds(pl.multiple_of(b * LANES, LANES), LANES)


def run_matrix(tokens, back):
    steps = tokens // RUNS
    row = lax.broadcasted_iota(jnp.int32, (tokens, tokens), 0)
    col = lax.broadcasted_iota(jnp.int32, (tokens, tokens), 1)
    if back:
        hit = row == (col & (RUNS - 1)) * steps + (col >> 3)
    else:
        hit = col == (row & (RUNS - 1)) * steps + (row >> 3)
    return jnp.where(hit, 1.0, 0.0).astype(BF16)


def entering(value, axis, join, neutral, backward):
    count, mine = (lax.axis_size(axis), lax.axis_index(axis))
    pieces = jax.tree.map(lambda part: lax.all_gather(part, axis), value)
    if backward:
        pieces = jax.tree.map(lambda part: part[::-1], pieces)
        mine = count - 1 - mine
    subtotal = jax.tree.map(
        lambda part, zero: jnp.full_like(part, 0) + jnp.asarray(zero, part.dtype), value, neutral
    )

    def lap(position, subtotal):
        longer = join(subtotal, jax.tree.map(lambda part: part[position], pieces))
        return jax.tree.map(lambda new, old: jnp.where(position < mine, new, old), longer, subtotal)

    return lax.fori_loop(0, count - 1, lap, subtotal)


def from_behind(block, axis, distance):
    devices = range(lax.axis_size(axis))
    route = [(i - distance, i) for i in devices if i - distance in devices]
    return lax.ppermute(block, axis, route)


def compose(earlier, later):
    return (earlier[0] * later[0], later[0] * earlier[1] + later[1])


def local(tokens, reset_mask, weight, vectors, cotangent):
    width = weight.shape[1] // 3
    whole_weight, whole_vectors = (
        lax.all_gather(weight, ("gx", "gy"), axis=0, tiled=True),
        lax.all_gather(vectors, ("gx", "gy"), axis=1, tiled=True),
    )
    params = whole_vectors.astype(jnp.float32)
    gain = params[0]
    shift_bias = params[1]
    forget_peep = params[2]
    forget_bias = params[3]
    reset_peep = params[4]
    reset_bias = params[5]
    inputs = tokens.astype(jnp.float32)
    keep = (1 - reset_mask).astype(jnp.float32)[:, None]
    centred = inputs - jnp.mean(inputs, axis=1, keepdims=True)
    inv_std = lax.rsqrt(jnp.mean(centred * centred, axis=1, keepdims=True) + 1e-05)
    normed = centred * inv_std
    scaled = normed * gain + shift_bias
    rounded = scaled.astype(jnp.bfloat16)
    projected = jnp.dot(rounded, whole_weight, preferred_element_type=jnp.float32)
    candidate = projected[:, :width]
    forget_pre = projected[:, width : 2 * width]
    reset_pre = projected[:, 2 * width :]
    forget = jax.nn.sigmoid(forget_pre + forget_peep * scaled + forget_bias)
    decay = forget * keep
    inflow = (1.0 - forget) * candidate
    cum_decay, cum_state = lax.associative_scan(compose, (decay, inflow), axis=0)
    unit = (jnp.ones_like(cum_decay[-1]), jnp.zeros_like(cum_state[-1]))
    before = entering((cum_decay[-1], cum_state[-1]), ("gx", "gy"), compose, unit, False)
    state_in = before[1]
    state = cum_decay * state_in + cum_state
    previous = keep * jnp.concatenate([state_in[None], state[:-1]], 0)
    reset = jax.nn.sigmoid(reset_pre + reset_peep * previous + reset_bias)
    output = reset * state + (1.0 - reset) * inputs
    upstream = cotangent.astype(jnp.float32)
    reset_grad = upstream * (state - inputs) * reset * (1.0 - reset)
    through = keep * reset_peep * reset_grad
    next_decay, next_through = from_behind((decay[0], through[0]), ("gx", "gy"), -1)
    ahead = jnp.concatenate([decay[1:], next_decay[None]], 0)
    local_term = upstream * reset + jnp.concatenate([through[1:], next_through[None]], 0)
    flip_mult, flip_sum = lax.associative_scan(compose, (ahead[::-1], local_term[::-1]), axis=0)
    mult_back = flip_mult[::-1]
    sum_back = flip_sum[::-1]
    after = entering((mult_back[0], sum_back[0]), ("gx", "gy"), compose, unit, True)
    state_grad = mult_back * after[1] + sum_back
    candidate_grad = state_grad * (1.0 - forget)
    forget_grad = state_grad * (previous - candidate) * forget * (1.0 - forget)
    proj_grad = jnp.concatenate([candidate_grad, forget_grad, reset_grad], 1).astype(jnp.bfloat16)
    weight_grad = lax.psum_scatter(
        lax.dot_general(
            rounded, proj_grad, (((0,), (0,)), ((), ())), preferred_element_type=jnp.float32
        ),
        ("gx", "gy"),
        scatter_dimension=0,
        tiled=True,
    )
    scaled_grad = lax.dot_general(
        proj_grad,
        lax.all_gather(weight, ("gx", "gy"), axis=0, tiled=True),
        (((1,), (1,)), ((), ())),
        preferred_element_type=jnp.float32,
    )
    scaled_grad = scaled_grad + forget_grad * forget_peep
    vector_terms = jnp.stack(
        [
            jnp.sum(scaled_grad * normed, axis=0),
            jnp.sum(scaled_grad, axis=0),
            jnp.sum(forget_grad * scaled, axis=0),
            jnp.sum(forget_grad, axis=0),
            jnp.sum(reset_grad * previous, axis=0),
            jnp.sum(reset_grad, axis=0),
        ],
        0,
    )
    vector_grad = lax.psum_scatter(vector_terms, ("gx", "gy"), scatter_dimension=1, tiled=True)
    normed_grad = scaled_grad * gain
    input_grad = upstream * (1.0 - reset) + inv_std * (
        normed_grad
        - jnp.mean(normed_grad, axis=1, keepdims=True)
        - normed * jnp.mean(normed_grad * normed, axis=1, keepdims=True)
    )
    return (output.astype(jnp.bfloat16), input_grad, weight_grad, vector_grad)


SLOTS, SEND, PAIR, ZSEND = 8, 8, 4, 4
TOTALS, FORE, GRADS, BACK, WEIGH = 2, 4, 5, 7, 9
LAG1, LAG2, LAG3 = 2, 4, 6
LAST = 6
AHEAD_Z, AHEAD_B = 6, 3
BAND = 32
ACROSS = ((10, (0, 3, 5)), (14, (6, 8, 10)), (15, (11, 13, 15)))
ACROSS_SUM = ()


def layer_kernel(
    nx, ny, units,
    tok, cot, mask, weight, vectors,
    wall, pgm, outp, igo, wgo, vgo,
    vbuf, vecs, xs, gs, means, invs, rnd, rt, rtm, wf, pj, pv, grs, outs, stage, perm, pgs,
    wb, sb, rd, rx, ry, rz, zb, sg, vsum, vrows, vtot, vin, cz, keep, wraw, wsrc, vsrc,
    ach, bch, qch, sin, cin, m1a, m1b, m2a, m2b,
    zs, zr, os, bs, br, dsn, dr, cs, cr, ws,
    vzs, vzr, vxs, vxr, vo, wls, sts, rs, rr, ps, pr, pl_, wl, gos,
    e1as, e1ar, e1bs, e1br, e2as, e2ar, e2bs, e2br,
    fds, fdr, fxs, fxr, fys, fyr, fzs, fzr, vsn, vrc, ous,
):
    gx, gy, core, mate, xn, yn = place(ny)
    tokens, width = xs.shape
    rows = wsrc.shape[1]
    cols = wsrc.shape[2]
    block = rows * ny
    half, short = ny // 2, rows // 2
    groups = units // GROUP
    glanes = GROUP * LANES
    diag = xn + yn - gx
    own, xq, yq, dq = gx // 2, xn // 2, yn // 2, diag // 2
    count = nx * ny
    me = gx * ny + gy

    def peer_y(j):
        return lax.rem(gy + j, ny)

    def peer_x(j):
        return lax.rem(gx + j, nx)

    def each(n, run, start=0):
        lax.fori_loop(start, n, lambda i, _: (run(i), 0)[1], 0)

    barrier = pltpu.get_barrier_semaphore()

    def greet(j):
        to = lax.rem(me + j, count)
        pl.semaphore_signal(barrier, inc=1, device_id=(to // ny, lax.rem(to, ny)), device_id_type=MESH)

    raw = pltpu.make_async_copy(weight, wraw, wls)
    raw.start()
    each(count, greet, 1)

    def among(u, some):
        hit = u < 0
        for s in some:
            hit = hit | (u == s)
        return hit

    across = tuple(c for c, _ in ACROSS)
    turned = tuple(c for c, _, _ in ACROSS_SUM)

    def straight(u, run):
        pl.when(jnp.logical_not(among(u, across)))(lambda: run(u))

    chunks = width // glanes

    tok_load = pltpu.make_async_copy(tok, xs, sts.at[0])
    cot_load = pltpu.make_async_copy(cot, gs, sts.at[1])
    tok_load.start()
    cot_load.start()

    def vz(j):
        return remote(vsrc, vbuf.at[me], vzs.at[j - 1], vzr.at[j - 1], (gx, peer_y(j)))

    def vx(j):
        part = vbuf.at[pl.ds(gx * ny, ny)]
        return remote(part, part, vxs.at[j - 1], vxr.at[j - 1], (peer_x(j), gy))

    own_vec = pltpu.make_async_copy(vsrc, vbuf.at[me], vo)

    def z_copy(u, j):
        return remote(wsrc.at[u], wall.at[u, own, core, gy], zs.at[u, j - 1], zr.at[u, j - 1], (gx, peer_y(j)))

    def own_copy(u):
        return pltpu.make_async_copy(wsrc.at[u], wall.at[u, own, core, gy], os.at[u])

    def band_copy(u, i):
        to = (mate, xn, yn)[i]
        recv = cr.at[u, 0] if i == 0 else br.at[u, i - 1]
        part = wall.at[u, own, core]
        return remote(part, part, bs.at[u, i], recv, (to, gy))

    def diag_copy(u, i):
        part = wall.at[u, (xq, yq)[i], core, half * i:half * (i + 1)]
        return remote(part, part, dsn.at[u, i], dr.at[u, i], ((yn, xn)[i], gy))

    def core_copy(u, i):
        part = wall.at[u, (own, xq, yq, dq)[i], core]
        return remote(part, part, cs.at[u, i - 1], cr.at[u, i], (mate, gy))

    def z_start(u):
        own_copy(u).start()
        for j in range(1, ny):
            z_copy(u, j).start()

    def z_wait(u):
        own_copy(u).wait()
        for j in range(1, ny):
            z_copy(u, j).wait_recv()
        for i in (1, 2, 0):
            band_copy(u, i).start()

    def xy_wait(u):
        for i in (1, 2):
            band_copy(u, i).wait_recv()
        for i in (0, 1):
            diag_copy(u, i).start()
        for i in (1, 2):
            core_copy(u, i).start()

    def diag_wait(u):
        for i in (0, 1):
            diag_copy(u, i).wait_recv()
        core_copy(u, 3).start()

    def core_wait(u):
        band_copy(u, 0).wait_recv()
        for i in (1, 2, 3):
            core_copy(u, i).wait_recv()

    def a_copy(u, i):
        return remote(
            wsrc.at[u], wall.at[u, own, core, gy], bs.at[u, i], br.at[u, i - 1], ((None, xn, yn)[i], gy)
        )

    def a_diag(u, i):
        part = wall.at[u, (xq, yq)[i], core, gy, short * i:short * (i + 1)]
        return remote(part, part, dsn.at[u, i], dr.at[u, i], ((yn, xn)[i], gy))

    def a_up(u, h):
        part = wall.at[u, :, core, gy - h]
        return remote(part, part, zs.at[u, h], zr.at[u, h], (gx, lax.rem(gy + 1, ny)))

    def a_down(u, h):
        part = wall.at[u, :, core, gy + h]
        return remote(part, part, cs.at[u, h], cr.at[u, h + 1], (gx, lax.rem(gy + ny - 1, ny)))

    def a_landed(u, h):
        pl.when(gy > h)(lambda: a_up(u, h).wait_recv())
        pl.when(gy + h + 1 < ny)(lambda: a_down(u, h).wait_recv())

    def a_hop(u, h):
        if h:
            a_landed(u, h - 1)
        pl.when((gy + 1 < ny) & (gy >= h))(lambda: a_up(u, h).start())
        pl.when((gy >= 1) & (gy + h < ny))(lambda: a_down(u, h).start())

    def a_left(u, h):
        pl.when((gy + 1 < ny) & (gy >= h))(lambda: a_up(u, h).wait_send())
        pl.when((gy >= 1) & (gy + h < ny))(lambda: a_down(u, h).wait_send())

    def a_core(u):
        part = wall.at[u, :, core]
        return remote(part, part, bs.at[u, 0], cr.at[u, 0], (mate, gy))

    def a_start(u):
        own_copy(u).start()
        for i in (1, 2):
            a_copy(u, i).start()

    def a_turn(u):
        own_copy(u).wait()
        for i in (1, 2):
            a_copy(u, i).wait_recv()
        for i in (0, 1):
            a_diag(u, i).start()

    def a_meet(u):
        for i in (0, 1):
            a_diag(u, i).wait_recv()

    def a_share(u):
        a_landed(u, ny - 2)
        a_core(u).start()

    zero = jnp.zeros((vectors.shape[0], LANES - rows), BF16)
    odd = lax.rem(me, 2) == 1
    tile = jnp.where(
        odd, jnp.concatenate([zero, vectors[...]], 1).astype(F32), jnp.concatenate([vectors[...], zero], 1).astype(F32)
    )
    pad = jnp.zeros((16 - vectors.shape[0], LANES), F32)
    vsrc[...] = jnp.concatenate([tile, pad], 0).astype(BF16)
    raw.wait()
    for u in range(units):
        for s in range(3):
            at = s * width + u * LANES
            wsrc[u, :, s * LANES:(s + 1) * LANES] = wraw[:, at:at + LANES]

    pl.semaphore_wait(barrier, count - 1)
    own_vec.start()
    for j in range(1, ny):
        vz(j).start()
    for u in across:
        a_start(u)
    z_start(0)

    def to_runs(i, into):
        at = slice(i * glanes, (i + 1) * glanes)
        into[:, at] = jnp.dot(perm[...], into[:, at], preferred_element_type=F32).astype(BF16)

    def moments(i):
        r = pl.ds(pl.multiple_of(i * BAND, BAND), BAND)
        x = xs[r, :].astype(F32)
        mean = jnp.mean(x, axis=1, keepdims=True)
        centred = x - mean
        inv = lax.rsqrt(jnp.mean(centred * centred, axis=1, keepdims=True) + EPS)
        means[r, :] = jnp.broadcast_to(mean, (BAND, LANES))
        invs[r, :] = jnp.broadcast_to(inv, (BAND, LANES))

    def rounding(i):
        r = pl.ds(pl.multiple_of(i * BAND, BAND), BAND)
        normed = (xs[r, :].astype(F32) - means[r, 0:1]) * invs[r, 0:1]
        rnd[r, :] = (normed * vecs[0:1, :] + vecs[1:2, :]).astype(BF16)

    quads = nx // 2

    def turn(i):
        at = pl.ds(pl.multiple_of(i * block, 16), block)
        rt[at, 0:tokens] = rnd[:, pl.ds(pl.multiple_of((2 * i + core) * block, LANES), block)].T
        rtm[at, :] = rnd[:, pl.ds(pl.multiple_of((2 * i + 1 - core) * block, LANES), block)].T

    r_mate = remote(rtm, rt.at[:, tokens:2 * tokens], rs, rr, (mate, gy))

    def gather_tick(k):
        pl.when(k + AHEAD_Z < units)(lambda: straight(k + AHEAD_Z, z_start))
        pl.when(k + AHEAD_B < units)(lambda: straight(k + AHEAD_B, z_wait))
        pl.when(k < units)(lambda: straight(k, xy_wait))
        pl.when((k >= 1) & (k <= units))(lambda: straight(k - 1, diag_wait))
        for c, times in ACROSS:
            for j, t in enumerate(times):
                pl.when(k == t)(functools.partial(a_hop, c, j))
            pl.when(k == c + 1)(functools.partial(a_share, c))

    bands = tokens // BAND
    perm[...] = run_matrix(tokens, False)
    tok_load.wait()
    for i in range(chunks // 2):
        to_runs(i, xs)
    z_wait(0)
    z_start(1)
    z_start(2)
    for i in range(chunks // 2, chunks):
        to_runs(i, xs)
    own_vec.wait()
    for j in range(1, ny):
        vz(j).wait_recv()
    for j in range(1, nx):
        vx(j).start()
    for u in across:
        a_turn(u)
    z_wait(1)
    for u in range(3, AHEAD_Z):
        z_start(u)
    each(bands // 2, moments)
    for u in range(2, AHEAD_B):
        z_wait(u)
    for u in across:
        a_meet(u)
    gather_tick(0)
    each(bands, moments, bands // 2)
    for j in range(1, nx):
        vx(j).wait_recv()
    for c in range(width // LANES):
        part = vbuf[2 * c].astype(F32) + vbuf[2 * c + 1].astype(F32)
        vecs[:, c * LANES:(c + 1) * LANES] = part[0:8, :]
    each(bands // 2, rounding)
    gather_tick(1)
    each(bands, rounding, bands // 2)
    kept = (1 - mask[...]).astype(F32)
    keep[...] = jnp.dot(
        (perm[...].astype(F32) * kept).astype(BF16), jnp.ones((tokens, LANES), BF16), preferred_element_type=F32
    )
    cot_load.wait()
    for i in range(chunks // 2):
        to_runs(i, gs)
    gather_tick(2)
    straight(0, core_wait)

    def late_start():
        for i in range(chunks // 2, chunks):
            to_runs(i, gs)
        perm[...] = run_matrix(tokens, True)

    def late_turn():
        each(quads, turn)
        r_mate.start()

    def e_copies(buf, send, recv, q, level):
        if level == 0:
            return [
                remote(buf.at[q, gy], buf.at[q, gy], send.at[q, j - 1], recv.at[q, j - 1], (gx, peer_y(j)))
                for j in range(1, ny)
            ]
        return [
            remote(buf.at[q, gx], buf.at[q, gx], send.at[q, j - 1], recv.at[q, j - 1], (peer_x(j), gy))
            for j in range(1, nx)
        ]

    def e_start(*a):
        for c in e_copies(*a):
            c.start()

    def e_wait(*a):
        for c in e_copies(*a):
            c.wait_recv()

    double = tokens // (2 * RUNS)

    def side(u):
        return pl.ds(pl.multiple_of(lax.rem(u, 2) * cols, LANES), cols)

    def front_load(u):
        return pltpu.make_async_copy(wall.at[u], wf.at[:, :, :, :, side(u)], ws.at[lax.rem(u, 2)])

    def project(u):
        front_load(u - 1).wait()
        front_load(u).wait()
        both = jnp.dot(rnd[...], wf[...].reshape(width, -1), preferred_element_type=F32)
        pj[lax.rem(u - 1, SLOTS)] = both[:, :cols]
        pj[lax.rem(u, SLOTS)] = both[:, cols:]

    def vec(i, u):
        return vecs[i:i + 1, lanes_of(u)]

    def scale(u, r, gain, shift):
        return (xs[r, lanes_of(u)].astype(F32) - means[r, :]) * invs[r, :] * gain + shift

    def gates(u):
        slot = lax.rem(u, SLOTS)
        gain, shift, vf, bf = (vec(i, u) for i in range(4))

        def step(i, carry):
            a, b = carry
            r = pl.ds(pl.multiple_of(i * 16, 16), 16)
            f = jax.nn.sigmoid(pj[slot, r, LANES:2 * LANES] + vf * scale(u, r, gain, shift) + bf)
            pj[slot, r, LANES:2 * LANES] = f
            d = f * keep[r, :]
            inflow = (1.0 - f) * pj[slot, r, 0:LANES]
            for h in (0, 8):
                a = a * d[h:h + 8]
                b = d[h:h + 8] * b + inflow[h:h + 8]
            return a, b

        a, b = lax.fori_loop(0, double, step, (jnp.ones((RUNS, LANES), F32), jnp.zeros((RUNS, LANES), F32)), unroll=4)
        q, j = u // GROUP, lax.rem(u, GROUP)
        ach[q, :, lanes_of(j)] = a
        bch[q, :, lanes_of(j)] = b

    def totals(q):
        a, b = jnp.ones((1, glanes), F32), jnp.zeros((1, glanes), F32)
        for s in range(RUNS):
            one = ach[q, s:s + 1, :]
            a = a * one
            b = one * b + bch[q, s:s + 1, :]
        m1a[q, gy, 0:1, :] = a
        m1a[q, gy, 1:2, :] = b
        e_start(m1a, e1as, e1ar, q, 0)

    def totals_x(q):
        e_wait(m1a, e1as, e1ar, q, 0)
        a, b = jnp.ones((1, glanes), F32), jnp.zeros((1, glanes), F32)
        for s in range(ny):
            one = m1a[q, s, 0:1, :]
            a = a * one
            b = one * b + m1a[q, s, 1:2, :]
        m1b[q, gx, 0:1, :] = a
        m1b[q, gx, 1:2, :] = b
        e_start(m1b, e1bs, e1br, q, 1)

    def enter(q):
        e_wait(m1b, e1bs, e1br, q, 1)
        s = jnp.zeros((1, glanes), F32)
        s = lax.fori_loop(0, gx, lambda i, s: m1b[q, i, 0:1, :] * s + m1b[q, i, 1:2, :], s)
        s = lax.fori_loop(0, gy, lambda i, s: m1a[q, i, 0:1, :] * s + m1a[q, i, 1:2, :], s)
        for r in range(RUNS):
            sin[q, r:r + 1, :] = s
            s = ach[q, r:r + 1, :] * s + bch[q, r:r + 1, :]

    def forward(u):
        slot = lax.rem(u, SLOTS)
        q, j = u // GROUP, lax.rem(u, GROUP)
        vr, br_ = vec(4, u), vec(5, u)
        zero = jnp.zeros((RUNS, LANES), F32)

        def step(i, carry):
            s, run, t, v4, v5 = carry
            r = pl.ds(pl.multiple_of(i * 16, 16), 16)
            f = pj[slot, r, LANES:2 * LANES]
            k = keep[r, :]
            inflow = (1.0 - f) * pj[slot, r, 0:LANES]
            prevs, states = [], []
            for h in (0, 8):
                prev = k[h:h + 8] * s
                s = f[h:h + 8] * prev + inflow[h:h + 8]
                prevs.append(prev)
                states.append(s)
            prev, state = jnp.concatenate(prevs, 0), jnp.concatenate(states, 0)
            x = xs[r, lanes_of(u)].astype(F32)
            up = gs[r, lanes_of(u)].astype(F32)
            reset = jax.nn.sigmoid(pj[slot, r, 2 * LANES:3 * LANES] + vr * prev + br_)
            rest = 1.0 - reset
            outs[r, lanes_of(j)] = (reset * state + rest * x).astype(BF16)
            rg = up * (state - x) * reset * rest
            pj[slot, r, 2 * LANES:3 * LANES] = rg
            pv[slot, r, :] = prev
            grs[r, lanes_of(u)] = up * rest
            local = up * reset
            d, through = f * k, k * vr * rg
            for h in (0, 8):
                t = t + run * through[h:h + 8]
                run = run * d[h:h + 8]
                t = t + run * local[h:h + 8]
                v4 = v4 + rg[h:h + 8] * prev[h:h + 8]
                v5 = v5 + rg[h:h + 8]
            return s, run, t, v4, v5

        init = (sin[q, :, lanes_of(j)], jnp.ones((RUNS, LANES), F32), zero, zero, zero)
        _, _, t, v4, v5 = lax.fori_loop(0, double, step, init, unroll=4)
        qch[q, :, lanes_of(j)] = t
        vsum[4:5, lanes_of(u)] = jnp.sum(v4, axis=0, keepdims=True)
        vsum[5:6, lanes_of(u)] = jnp.sum(v5, axis=0, keepdims=True)

    def out_copy(q):
        c = pl.ds(pl.multiple_of(q * glanes, LANES), glanes)
        return pltpu.make_async_copy(stage.at[lax.rem(q, 2)], outp.at[:, c], gos.at[q])

    def forward_group(q):
        enter(q)
        pl.when(q >= 2)(lambda: out_copy(q - 2).wait())
        each(GROUP, lambda j: forward(q * GROUP + j))
        s = jnp.zeros((1, glanes), F32)
        for r in reversed(range(RUNS)):
            s = ach[q, r:r + 1, :] * s + qch[q, r:r + 1, :]
        m2a[q, gy, 0:1, :] = s
        e_start(m2a, e2as, e2ar, q, 0)
        stage[lax.rem(q, 2)] = jnp.dot(perm[...], outs[...], preferred_element_type=F32).astype(BF16)
        out_copy(q).start()

    def grads_x(q):
        e_wait(m2a, e2as, e2ar, q, 0)
        s = jnp.zeros((1, glanes), F32)
        for r in reversed(range(ny)):
            s = m1a[q, r, 0:1, :] * s + m2a[q, r, 0:1, :]
        m2b[q, gx, 0:1, :] = s
        e_start(m2b, e2bs, e2br, q, 1)

    def enter_back(q):
        e_wait(m2b, e2bs, e2br, q, 1)
        s = jnp.zeros((1, glanes), F32)

        def over_x(i, s):
            return m1b[q, nx - 1 - i, 0:1, :] * s + m2b[q, nx - 1 - i, 0:1, :]

        def over_y(i, s):
            return m1a[q, ny - 1 - i, 0:1, :] * s + m2a[q, ny - 1 - i, 0:1, :]

        s = lax.fori_loop(0, nx - 1 - gx, over_x, s)
        s = lax.fori_loop(0, ny - 1 - gy, over_y, s)
        for r in reversed(range(RUNS)):
            cin[q, r:r + 1, :] = s
            s = ach[q, r:r + 1, :] * s + qch[q, r:r + 1, :]

    def pg_mate(u):
        return remote(pgs.at[lax.rem(u, PAIR), 0:tokens], pgm.at[u], ps.at[u], pr.at[u], (mate, gy))

    def backward(u):
        slot, pair = lax.rem(u, SLOTS), lax.rem(u, PAIR)
        q, j = u // GROUP, lax.rem(u, GROUP)
        gain, shift, vr = vec(0, u), vec(1, u), vec(4, u)
        zero = jnp.zeros((RUNS, LANES), F32)

        def step(i, carry):
            c, v2, v3 = carry
            r = pl.ds(pl.multiple_of((double - 1 - i) * 16, 16), 16)
            f = pj[slot, r, LANES:2 * LANES]
            k = keep[r, :]
            rg = pj[slot, r, 2 * LANES:3 * LANES]
            local = gs[r, lanes_of(u)].astype(F32) - grs[r, lanes_of(u)]
            d, through = f * k, k * vr * rg
            grads = [None, None]
            for h in (1, 0):
                part = slice(8 * h, 8 * h + 8)
                grads[h] = local[part] + c
                c = d[part] * grads[h] + through[part]
            grad = jnp.concatenate(grads, 0)
            cg = grad * (1.0 - f)
            fg = cg * (pv[slot, r, :] - pj[slot, r, 0:LANES]) * f
            pgs[pair, r, 0:LANES] = cg.astype(BF16)
            pgs[pair, r, LANES:2 * LANES] = fg.astype(BF16)
            pgs[pair, r, 2 * LANES:3 * LANES] = rg.astype(BF16)
            fs = fg * scale(u, r, gain, shift)
            return c, v2 + fs[0:8] + fs[8:16], v3 + fg[0:8] + fg[8:16]

        _, v2, v3 = lax.fori_loop(0, double, step, (cin[q, :, lanes_of(j)], zero, zero), unroll=4)
        vsum[2:3, lanes_of(u)] = jnp.sum(v2, axis=0, keepdims=True)
        vsum[3:4, lanes_of(u)] = jnp.sum(v3, axis=0, keepdims=True)
        pg_mate(u).start()

    def backward_group(q):
        enter_back(q)
        each(GROUP, lambda j: backward(q * GROUP + j))
        drain_group(q)

    def pg_load(u):
        return pltpu.make_async_copy(pgm.at[u], pgs.at[lax.rem(u, PAIR), tokens:2 * tokens], pl_)

    def back_load(u):
        return pltpu.make_async_copy(wall.at[u], wb, wl)

    def some(part):
        return pl.ds(part * half, half)

    def sent(u):
        return sb.at[lax.rem(u, SEND)]

    def d_copy(u, i):
        return remote(
            sent(u).at[dq, some(i)], rd.at[u, some(i)], fds.at[u, i], fdr.at[u, i], ((yn, xn)[i], gy)
        )

    def x_copy(u, i):
        return remote(sent(u).at[xq, some(i)], rx.at[u, some(i)], fxs.at[u, i], fxr.at[u, i], (xn, gy))

    def y_copy(u, i):
        return remote(sent(u).at[yq, some(i)], ry.at[u, some(i)], fys.at[u, i], fyr.at[u, i], (yn, gy))

    def f_copy(u, j):
        to = lax.rem(gy + j, ny)
        return remote(zb.at[lax.rem(u, ZSEND), to], rz.at[u, j - 1], fzs.at[u, j - 1], fzr.at[u, j - 1], (gx, to))

    def next_loads(u):
        pg_mate(u).wait_recv()
        pg_load(u).start()
        back_load(u).start()

    def weigh(u):
        slot, pair = lax.rem(u, SEND), lax.rem(u, PAIR)

        @pl.when((u >= SEND) & jnp.logical_not(among(u - SEND, turned)))
        def _():
            for i in (0, 1):
                d_copy(u - SEND, i).wait_send()
                x_copy(u - SEND, i).wait_send()
                y_copy(u - SEND, i).wait_send()

        pg_load(u).wait()
        sb[slot] = jnp.dot(rt[...], pgs[pair], preferred_element_type=F32).astype(BF16).reshape(sb.shape[1:])

        @pl.when(jnp.logical_not(among(u, turned)))
        def _():
            for i in (0, 1):
                d_copy(u, i).start()
            x_copy(u, 1).start()
            y_copy(u, 0).start()

    def spread(u):
        pair = lax.rem(u, PAIR)
        back_load(u).wait()
        mine = pgs[pair, 0:tokens, :]
        sg[...] += lax.dot_general(mine, wb[...].reshape(width, -1), (((1,), (1,)), ((), ())), preferred_element_type=F32)
        sg[:, lanes_of(u)] += pgs[pair, 0:tokens, LANES:2 * LANES].astype(F32) * vecs[2:3, lanes_of(u)]
        pg_mate(u).wait_send()

    def fold(ref, at, more):
        ref[at] = (ref[at].astype(F32) + more.astype(F32)).astype(BF16)

    def meet(u):
        slot = lax.rem(u, SEND)
        for i in (0, 1):
            d_copy(u, i).wait_recv()
        fold(sb, (slot, xq, some(0)), rd[u, 0:half])
        x_copy(u, 0).start()
        fold(sb, (slot, yq, some(1)), rd[u, half:ny])
        y_copy(u, 1).start()

    def column(u):
        slot, zslot = lax.rem(u, SEND), lax.rem(u, ZSEND)

        @pl.when((u >= ZSEND) & jnp.logical_not(among(u - ZSEND, turned)))
        def _():
            for j in range(1, ny):
                f_copy(u - ZSEND, j).wait_send()

        for i in (0, 1):
            x_copy(u, i).wait_recv()
            y_copy(u, i).wait_recv()
        total = sb[slot, own].astype(F32) + rx[u].astype(F32) + ry[u].astype(F32)
        zb[zslot] = total.astype(BF16)
        for j in range(1, ny):
            f_copy(u, j).start()

    def settle(u):
        slot = lax.rem(u, SEND)
        total = sb[slot, own, gy].astype(F32) + rx[u, gy].astype(F32) + ry[u, gy].astype(F32)
        for j in range(1, ny):
            f_copy(u, j).wait_recv()
        for j in range(1, ny):
            total = total + rz[u, j - 1].astype(F32)
        place_sum(u, total)

    def place_sum(u, total):
        for i in range(3):
            wgo[:, lanes_of(u + i * units)] = total[:, i * LANES:(i + 1) * LANES]

    def part(i):
        return pl.ds(i * short, short)

    def b_z(u, j):
        to = peer_y(j)
        return remote(sent(u).at[:, to], (rd, rx, ry)[j - 1].at[u], fzs.at[u, j - 1], fzr.at[u, j - 1], (gx, to))

    def b_diag(u, n, i):
        return remote(cz.at[n, dq, part(i)], rz.at[u, 0, part(i)], fds.at[u, i], fdr.at[u, i], ((yn, xn)[i], gy))

    def b_x(u, n, i):
        return remote(cz.at[n, xq, part(i)], rz.at[u, 1, part(i)], fxs.at[u, i], fxr.at[u, i], (xn, gy))

    def b_y(u, n, i):
        return remote(cz.at[n, yq, part(i)], rz.at[u, 2, part(i)], fys.at[u, i], fyr.at[u, i], (yn, gy))

    def b_gather(u, n):
        for j in range(1, ny):
            b_z(u, j).wait()
            if u >= ZSEND and u - ZSEND not in turned:
                f_copy(u - ZSEND, j).wait_send()
        total = sb[lax.rem(u, SEND), :, gy].astype(F32)
        for ref in (rd, rx, ry):
            total = total + ref[u].astype(F32)
        cz[n] = total.astype(BF16)
        for i in (0, 1):
            b_diag(u, n, i).start()
        b_x(u, n, 1).start()
        b_y(u, n, 0).start()

    def b_meet(u, n):
        for i in (0, 1):
            b_diag(u, n, i).wait_recv()
        fold(cz, (n, xq, part(0)), rz[u, 0, part(0)])
        b_x(u, n, 0).start()
        fold(cz, (n, yq, part(1)), rz[u, 0, part(1)])
        b_y(u, n, 1).start()

    def b_settle(u, n):
        for i in (0, 1):
            b_x(u, n, i).wait_recv()
            b_y(u, n, i).wait_recv()
        place_sum(u, cz[n, own].astype(F32) + rz[u, 1].astype(F32) + rz[u, 2].astype(F32))

    def b_drain(u, n):
        for i in (0, 1):
            b_diag(u, n, i).wait_send()
            b_x(u, n, i).wait_send()
            b_y(u, n, i).wait_send()

    def finish(i):
        r = pl.ds(pl.multiple_of(i * BAND, BAND), BAND)
        s = sg[r, :]
        inv = invs[r, 0:1]
        z = (xs[r, :].astype(F32) - means[r, 0:1]) * inv
        sz = s * z
        gain = vecs[0:1, :]
        vrows[0:8, :] += jnp.sum(sz.reshape(BAND // 8, 8, width), axis=0)
        vrows[8:16, :] += jnp.sum(s.reshape(BAND // 8, 8, width), axis=0)
        n = s * gain
        m1 = jnp.mean(n, axis=1, keepdims=True)
        m2 = jnp.mean(sz * gain, axis=1, keepdims=True)
        sg[r, :] = grs[r, :] + inv * (n - m1 - z * m2)

    def v_copy(j):
        to = lax.rem(me + j, count)
        return remote(vtot.at[to // 2], vin.at[me], vsn.at[to], vrc.at[me], (to // ny, lax.rem(to, ny)))

    def v_recv(j):
        at = lax.rem(me + j, count)
        return remote(vtot.at[0], vin.at[at], vsn.at[at], vrc.at[at], (at // ny, lax.rem(at, ny)))

    def vectors_out():
        zero = jnp.zeros((2, LANES), F32)
        for c in range(width // LANES):
            at = slice(c * LANES, (c + 1) * LANES)
            top = [jnp.sum(vrows[8 * v:8 * v + 8, at], axis=0, keepdims=True) for v in (0, 1)]
            vtot[c] = jnp.concatenate(top + [vsum[2:6, at], zero], 0)
        each(count, lambda j: v_copy(j).start(), 1)

    quarter = width // 4

    def grad_copy(c):
        return pltpu.make_async_copy(grs.at[:, pl.ds(c * quarter, quarter)], igo.at[:, pl.ds(c * quarter, quarter)], ous.at[c])

    def natural():
        for c in range(4):
            at = slice(c * quarter, (c + 1) * quarter)
            v = sg[:, at]
            high = v.astype(BF16)
            low = (v - high.astype(F32)).astype(BF16)
            grs[:, at] = jnp.dot(perm[...], high, preferred_element_type=F32) + jnp.dot(
                perm[...], low, preferred_element_type=F32
            )
            grad_copy(c).start()

    def drain(u):
        for j in range(1, ny):
            z_copy(u, j).wait_send()
        for i in range(3):
            band_copy(u, i).wait_send()
        for i in (0, 1):
            diag_copy(u, i).wait_send()
        for i in (1, 2, 3):
            core_copy(u, i).wait_send()

    def drain_group(q):
        for a in ((m1a, e1as, e1ar, q, 0), (m1b, e1bs, e1br, q, 1), (m2a, e2as, e2ar, q, 0), (m2b, e2bs, e2br, q, 1)):
            for c in e_copies(*a):
                c.wait_send()

    def drain_first():
        for c in across:
            for h in range(ny - 1):
                a_left(c, h)
            for i in (1, 2):
                a_copy(c, i).wait_send()
            for i in (0, 1):
                a_diag(c, i).wait_send()
            a_core(c).wait_send()
        for j in range(1, ny):
            vz(j).wait_send()
        for j in range(1, nx):
            vx(j).wait_send()
        r_mate.wait_send()

    def vectors_in():
        each(count, lambda j: v_recv(j).wait_recv(), 1)
        vin[me] = vtot[me // 2]
        total = lax.fori_loop(0, count, lambda j, s: s + vin[j], jnp.zeros((8, LANES), F32))
        vgo[...] = jnp.where(odd, total[0:6, rows:2 * rows], total[0:6, 0:rows])
        each(count, lambda j: v_copy(j).wait_send(), 1)

    def tick(k, _):
        u = k - 3
        v = u - WEIGH
        gather_tick(k)
        pl.when(k == 3)(late_start)
        pl.when(k == 5)(late_turn)

        def summed(lag, run):
            w = v - lag
            pl.when((w >= 0) & (w < units) & jnp.logical_not(among(w, turned)))(lambda: run(w))

        summed(LAG1, meet)
        summed(LAG2, column)
        summed(LAG3, settle)
        for n, (c, _, steps) in enumerate(ACROSS_SUM):
            for t, run in zip(steps, (b_gather, b_meet, b_settle)):
                pl.when(v == t)(functools.partial(run, c, n))

        @pl.when(v == 0)
        def _():
            r_mate.wait_recv()
            sg[...] = jnp.zeros_like(sg)
            vrows[...] = jnp.zeros_like(vrows)

        @pl.when((v >= 0) & (v < units))
        def _():
            weigh(v)
            spread(v)

        for c, times, _ in ACROSS_SUM:
            for j, t in enumerate(times):
                pl.when(v == t)(lambda c=c, j=j: b_z(c, j + 1).start())

        pl.when((v >= -1) & (v < units - 1))(lambda: next_loads(v + 1))

        def event(lag, run):
            g = (u - lag) // GROUP
            pl.when((u >= lag) & (lax.rem(u - lag + GROUP, GROUP) == 0) & (g < groups))(lambda: run(g))

        event(BACK, backward_group)
        event(GRADS, grads_x)
        event(FORE, forward_group)
        event(TOTALS, totals_x)

        paired = (u >= 0) & (u < units) & (lax.rem(u, 2) == 1)

        @pl.when(paired)
        def _():
            project(u)

        @pl.when((u >= 0) & (u < units - 1))
        def _():
            straight(u + 1, core_wait)
            for c in across:
                pl.when(u + 1 == c)(lambda c=c: a_core(c).wait_recv())
            front_load(u + 1).start()

        @pl.when(paired)
        def _():
            gates(u - 1)
            gates(u)
            totals(u // GROUP)

        pl.when(v == units)(lambda: each(bands // 2, finish))

        @pl.when(v == units + 1)
        def _():
            each(bands, finish, bands // 2)
            vectors_out()

        pl.when(v == units + 2)(natural)
        pl.when(v == units + 3)(vectors_in)
        w = k - units - 1

        @pl.when((w >= 0) & (w < units))
        def _():
            straight(w, drain)

        pl.when(w == 4)(drain_first)
        return 0

    front_load(0).start()
    lax.fori_loop(3, units + WEIGH + 3 + LAST, tick, 0)

    for n, c in enumerate(turned):
        b_drain(c, n)

    def drain_send(u):
        for i in (0, 1):
            d_copy(u, i).wait_send()
            x_copy(u, i).wait_send()
            y_copy(u, i).wait_send()

    each(units, lambda u: pl.when(jnp.logical_not(among(u, turned)))(lambda: drain_send(u)), units - SEND)

    def drain_z(u):
        for j in range(1, ny):
            f_copy(u, j).wait_send()

    each(units, drain_z, units - ZSEND)

    for q in range(groups - 2, groups):
        out_copy(q).wait()
    for c in range(4):
        grad_copy(c).wait()


def layer(nx, ny, tok, cot, mask, weight, vectors):
    tokens, width = tok.shape
    rows, cols = weight.shape[0], 3 * LANES
    units = width // LANES
    groups, glanes, block, count = units // GROUP, GROUP * LANES, rows * ny, nx * ny
    dma = pltpu.SemaphoreType.DMA
    any_, vmem = pl.BlockSpec(memory_space=pl.ANY), pl.BlockSpec(memory_space=pltpu.VMEM)
    msg = RUNS, glanes
    s, v = jax.ShapeDtypeStruct, pltpu.VMEM
    return pl.pallas_call(
        functools.partial(layer_kernel, nx, ny, units),
        name="layer",
        out_shape=(
            s((units, nx // 2, 2, ny, rows, cols), BF16), s((units, tokens, cols), BF16),
            s((tokens, width), BF16), s((tokens, width), F32), s((rows, 3 * width), F32), s(vectors.shape, F32),
        ),
        in_specs=[any_, any_, vmem, any_, vmem],
        out_specs=(any_,) * 4 + (vmem,) * 2,
        scratch_shapes=[
            v((count, 16, LANES), BF16), v((8, width), F32),
            v((tokens, width), BF16), v((tokens, width), BF16), v((tokens, LANES), F32), v((tokens, LANES), F32),
            v((tokens, width), BF16), v((width // 2, 2 * tokens), BF16), v((width // 2, tokens), BF16),
            v((nx // 2, 2, ny, rows, 2 * cols), BF16),
            v((SLOTS, tokens, cols), F32), v((SLOTS, tokens, LANES), F32),
            v((tokens, width), F32), v((tokens, glanes), BF16), v((2, tokens, glanes), BF16),
            v((tokens, tokens), BF16), v((PAIR, 2 * tokens, cols), BF16),
            v((nx // 2, 2, ny, rows, cols), BF16), v((SEND, nx // 2, ny, rows, cols), BF16),
            *[v((units, ny, rows, cols), BF16)] * 3,
            v((units, ny - 1, rows, cols), BF16), v((ZSEND, ny, rows, cols), BF16),
            v((tokens, width), F32), v((8, width), F32), v((16, width), F32),
            v((width // LANES, 8, LANES), F32), v((count, 8, LANES), F32),
            v((max(1, len(ACROSS_SUM)), nx // 2, rows, cols), BF16), v((tokens, LANES), F32),
            v((rows, 3 * width), BF16), v((units, rows, cols), BF16), v((16, LANES), BF16),
            *[v((groups,) + msg, F32)] * 5,
            v((groups, ny, 2, glanes), F32), v((groups, nx, 2, glanes), F32),
            v((groups, ny, 1, glanes), F32), v((groups, nx, 1, glanes), F32),
            dma((units, ny - 1)), dma((units, ny - 1)), dma((units,)), dma((units, 3)), dma((units, 2)),
            dma((units, 2)), dma((units, 2)), dma((units, 3)), dma((units, 4)), dma((2,)),
            dma((ny - 1,)), dma((ny - 1,)), dma((nx - 1,)), dma((nx - 1,)), dma, dma, dma((2,)),
            dma, dma, dma((units,)), dma((units,)), dma, dma, dma((groups,)),
            dma((groups, ny - 1)), dma((groups, ny - 1)), dma((groups, nx - 1)), dma((groups, nx - 1)),
            dma((groups, ny - 1)), dma((groups, ny - 1)), dma((groups, nx - 1)), dma((groups, nx - 1)),
            *[dma((units, 2))] * 6, dma((units, ny - 1)), dma((units, ny - 1)),
            dma((count,)), dma((count,)), dma((4,)),
        ],
        compiler_params=pltpu.CompilerParams(
            collective_id=0, has_side_effects=True, vmem_limit_bytes=62 * 2**20
        ),
        cost_estimate=pl.CostEstimate(
            flops=6 * tokens * width * units * cols, bytes_accessed=4 * width * units * cols, transcendentals=0
        ),
    )(tok, cot, mask, weight, vectors)


def fast(nx, ny, tokens, reset_mask, weight, vectors, cotangent):
    mask = reset_mask.reshape(1, -1)
    return layer(nx, ny, tokens, cotangent, mask, weight, vectors)[2:]


def solution(mesh):
    placed = (
        P(("gx", "gy"), None),
        P(("gx", "gy")),
        P(("gx", "gy"), None),
        P(None, ("gx", "gy")),
        P(("gx", "gy"), None),
    )
    nx, ny = mesh.shape["gx"], mesh.shape["gy"]

    def body(tokens, reset_mask, weight, vectors, cotangent):
        whole_tiles = weight.shape[0] % 16 == 0 and tokens.shape[0] % 256 == 0
        if (nx, ny) == (8, 4) and whole_tiles and 2 * weight.shape[0] == LANES and tokens.shape[1] % 2048 == 0:
            return fast(nx, ny, tokens, reset_mask, weight, vectors, cotangent)
        return local(tokens, reset_mask, weight, vectors, cotangent)

    return jax.shard_map(
        body,
        mesh=mesh,
        in_specs=placed,
        out_specs=(
            P(("gx", "gy"), None),
            P(("gx", "gy"), None),
            P(("gx", "gy"), None),
            P(None, ("gx", "gy")),
        ),
        check_vma=False,
    )
```
